32 devices in a mesh: dp: 4 (over y, core), seq: 8 (over z, x).
Axes of the slice: x: 2, y: 2, z: 4, core: 2. Of those that a mesh axis runs over, the one named last changes fastest.
Arguments:
- tokens: float32 [4, 1024, 1152], P('dp', 'seq'), may hold values from -6 to 6
- cotangent: float32 [4, 1024, 1152], P('dp', 'seq'), may hold values from -6 to 6
- routes: int32 [4, 1024, 1], P('dp', 'seq'), may hold values from 0 to 3; in each aligned block of 128 rows (0 to 127, 128 to 255, ..., all dimensions but the last counted through in order) at most 56 rows name the same one
- mixer_gain: bfloat16 [1152], replicated, may hold values from 0.5 to 1.5
- input_proj: bfloat16 [2, 1152, 2304], P(None, None, ('dp', 'seq')), may hold values from -0.1875 to 0.1875
- conv_weight: bfloat16 [4, 2304], P(None, ('dp', 'seq')), may hold values from -3 to 3
- conv_bias: bfloat16 [2304], P(('dp', 'seq')), may hold values from -1.5 to 1.5
- select_proj: bfloat16 [104, 2304], P(None, ('dp', 'seq')), may hold values from -0.125 to 0.125
- step_proj: bfloat16 [72, 2304], P(None, ('dp', 'seq')), may hold values from -0.75 to 0.75
- step_bias: bfloat16 [2304], P(('dp', 'seq')), may hold values from -5 to -2
- decay_log: bfloat16 [16, 2304], P(None, ('dp', 'seq')), may hold values from -4 to 2
- skip_gain: bfloat16 [2304], P(('dp', 'seq')), may hold values from 0.5 to 1.5
- output_proj: bfloat16 [2304, 1152], P(('dp', 'seq')), may hold values from -0.25 to 0.25
- expert_gain: bfloat16 [1152], replicated, may hold values from 0.5 to 1.5
- router: bfloat16 [4, 1152], replicated, may hold values from -0.125 to 0.125
- expert_up: bfloat16 [1152, 12288], P('seq', 'dp'), may hold values from -0.1875 to 0.1875
- expert_down: bfloat16 [12288, 1152], P('dp', 'seq'), may hold values from -0.21875 to 0.21875
Outputs:
- output: float32 [4, 1024, 1152], P('dp', 'seq')
- input_grad: float32 [4, 1024, 1152], P('dp', 'seq')
- grad_mixer_gain: float32 [1152], replicated
- grad_input_proj: float32 [2, 1152, 2304], P(None, None, ('dp', 'seq'))
- grad_conv_weight: float32 [4, 2304], P(None, ('dp', 'seq'))
- grad_conv_bias: float32 [2304], P(('dp', 'seq'))
- grad_select_proj: float32 [104, 2304], P(None, ('dp', 'seq'))
- grad_step_proj: float32 [72, 2304], P(None, ('dp', 'seq'))
- grad_step_bias: float32 [2304], P(('dp', 'seq'))
- grad_decay_log: float32 [16, 2304], P(None, ('dp', 'seq'))
- grad_skip_gain: float32 [2304], P(('dp', 'seq'))
- grad_output_proj: float32 [2304, 1152], P(('dp', 'seq'))
- grad_expert_gain: float32 [1152], replicated
- grad_router: float32 [4, 1152], replicated
- grad_expert_up: float32 [1152, 12288], P('seq', 'dp')
- grad_expert_down: float32 [12288, 1152], P('dp', 'seq')
The draws below stay inside these ranges and needn't reach their ends.
Inputs may be any that keep to these rules, and one draw needn't show every extreme that they name: `routes`: among the tokens of one sequence block (128 consecutive tokens of a sequence, starting at a multiple of 128) no expert is the route of more than 56 tokens; in every draw some block sends exactly 56 tokens to one expert.
All inputs are finite; a program needn't handle non-finite values.
Results may differ from the reference program's by a relative error of at most 0.015.
Values may be sent and summed in bfloat16 or wider, within the bound.
A program may use at most 192 MiB of HBM per device.

```python
import math
import jax
import jax.numpy as jnp
import numpy as np
from jax import lax

D = 1152
DI = 2304
STATE = 16
RANK = 72
KERNEL = 4
FF = 3072
EXPERTS = 4
TOK_DEV = 128
CAP = 56
LENGTH = 1024
SEQS = 4


def shard_levels(own_key, extent, cuts, least, high):
    factor_of = 1.0
    for dim, blocks in cuts:
        steps = jax.random.uniform(jax.random.fold_in(jax.random.fold_in(own_key, 6), dim), (blocks,), jnp.float32, least / len(cuts), high / len(cuts))
        factor_of = factor_of * jnp.repeat(jnp.exp(steps), extent[dim] // blocks).reshape((-1,) + (1,) * (len(extent) - 1 - dim))
    return factor_of


def assign_block(stream_key, own, number, rows, amount, top, limit, skew):
    ranking = jax.random.permutation(stream_key, amount)
    heavy_load, ordinary = portions_of(amount, rows * top, limit, skew, True), portions_of(amount, rows * top, limit, skew, False)
    places = jnp.arange(amount)

    def named(tallies, offset_by):
        used = int((tallies > 0).sum())
        fixed = max(1, used // 4)
        shifted = fixed + (places - fixed + offset_by * (used - fixed)) % max(1, amount - fixed)
        return jnp.zeros((amount,), jnp.int32).at[ranking[jnp.where(places < fixed, places, shifted)]].set(jnp.asarray(tallies, jnp.int32))

    tallies = jnp.where(number % 4 == 0, named(heavy_load, number // 4), named(ordinary, number - number // 4 - 1))
    mixed = jax.random.permutation(jax.random.fold_in(own, 3), amount)
    giver, sink = mixed[0:amount // 2 * 2:2], mixed[1:amount // 2 * 2:2]
    margin = jnp.minimum(tallies[giver] - 1, limit - tallies[sink]) // 2
    margin = jnp.where((giver == ranking[0]) | (sink == ranking[0]) | (tallies[sink] == 0), 0, jnp.maximum(margin, 0))
    shifted = jax.random.randint(jax.random.fold_in(own, 4), (amount // 2,), 0, 1 << 20) % (margin + 1)
    tallies = tallies.at[giver].add(-shifted).at[sink].add(shifted)
    items = jnp.searchsorted(jnp.cumsum(tallies), jnp.arange(rows * top), side="right").astype(jnp.int32)
    grid = items.reshape(top, rows).T
    grid = grid[jax.random.permutation(jax.random.fold_in(own, 1), rows)]
    offset_by = jax.random.randint(jax.random.fold_in(own, 2), (rows, 1), 0, top)
    return jnp.take_along_axis(grid, (jnp.arange(top)[None, :] + offset_by) % top, axis=1)


def portions_of(number_of, total, most, lean, full):
    loads = [(1 << 20) // math.isqrt(grade ** lean) + 1 for grade in range(1, number_of + 1)]
    largest = most if full else min(most, max(-(-total // number_of), total * loads[0] // sum(loads)))
    least = 1 if total - largest >= number_of - 1 else 0
    holding, spare = [largest] + [least] * (number_of - 1), total - largest - least * (number_of - 1)
    while spare > 0:
        candidates = [i for i in range(1, number_of) if holding[i] < largest] or [i for i in range(1, number_of) if holding[i] < most]
        mass, left = sum([loads[i] for i in candidates]), spare
        for i in candidates:
            addition = min(most - holding[i], max(1, left * loads[i] // mass), spare)
            holding[i] = holding[i] + addition
            spare = spare - addition
    return np.array(holding)


def bell_draw(key, extent, deviation, limit, split=(), kind=jnp.bfloat16):
    level = shard_levels(key, extent, split, -0.22, 0.18) if split else 1.0
    values = jax.random.normal(key, extent, jnp.float32) * deviation * level
    return jnp.minimum(jnp.maximum(values, -limit), limit).astype(kind)


def setup_inputs(seed: int = 0) -> dict:
    key_list = jax.random.split(jax.random.key(seed), 18)
    tokens = bell_draw(key_list[0], (SEQS, LENGTH, D), 1.0, 6.0, ((0, 4), (1, 8)), jnp.float32)
    cotangent = bell_draw(key_list[1], (SEQS, LENGTH, D), 1.0, 6.0, ((0, 4), (1, 8)), jnp.float32)
    routes_keys = jax.random.split(jax.random.fold_in(key_list[2], 1), SEQS * LENGTH // TOK_DEV)
    routes_turns = jax.random.permutation(jax.random.fold_in(key_list[2], 3), SEQS * LENGTH // TOK_DEV)
    routes = jax.vmap(lambda own, number: assign_block(jax.random.fold_in(key_list[2], 2), own, number, TOK_DEV, EXPERTS, 1, CAP, 1))(routes_keys, routes_turns).reshape((SEQS, LENGTH, 1))
    mixer_gain = jnp.clip(1.0 + 0.1 * jax.random.normal(key_list[3], (D,), jnp.float32), 0.5, 1.5).astype(jnp.bfloat16)
    input_proj = bell_draw(key_list[4], (2, D, DI), D ** -0.5, 0.1875, ((2, 32),))
    conv_weight = bell_draw(key_list[5], (KERNEL, DI), KERNEL ** -0.5, 3.0, ((1, 32),))
    conv_bias = bell_draw(key_list[6], (DI,), 0.3, 1.5, ((0, 32),))
    select_proj = bell_draw(key_list[7], (RANK + 2 * STATE, DI), DI ** -0.5, 0.125, ((1, 32),))
    step_proj = bell_draw(key_list[8], (RANK, DI), RANK ** -0.5, 0.75, ((1, 32),))
    step_bias = jnp.clip(-5.0 + 3.0 * jax.random.uniform(key_list[9], (DI,), jnp.float32) ** shard_levels(key_list[9], (DI,), ((0, 32),), -0.2, 0.2), -5.0, -2.0).astype(jnp.bfloat16)
    decay_log = jnp.clip(-4.0 + 6.0 * jax.random.uniform(key_list[10], (STATE, DI), jnp.float32) ** shard_levels(key_list[10], (STATE, DI), ((1, 32),), -0.2, 0.2), -4.0, 2.0).astype(jnp.bfloat16)
    skip_gain = jnp.clip(0.5 + 1.0 * jax.random.uniform(key_list[11], (DI,), jnp.float32) ** shard_levels(key_list[11], (DI,), ((0, 32),), -0.2, 0.2), 0.5, 1.5).astype(jnp.bfloat16)
    output_proj = bell_draw(key_list[12], (DI, D), (DI // 4) ** -0.5, 0.25, ((0, 32),))
    expert_gain = jnp.clip(1.0 + 0.1 * jax.random.normal(key_list[13], (D,), jnp.float32), 0.5, 1.5).astype(jnp.bfloat16)
    router = bell_draw(key_list[14], (EXPERTS, D), (2 * D) ** -0.5, 0.125)
    expert_up = bell_draw(key_list[15], (D, EXPERTS * FF), D ** -0.5, 0.1875, ((0, 8), (1, 4)))
    expert_down = bell_draw(key_list[16], (EXPERTS * FF, D), (FF // 4) ** -0.5, 0.21875, ((0, 4), (1, 8)))
    return {"tokens": tokens, "cotangent": cotangent, "routes": routes, "mixer_gain": mixer_gain, "input_proj": input_proj, "conv_weight": conv_weight, "conv_bias": conv_bias, "select_proj": select_proj, "step_proj": step_proj, "step_bias": step_bias, "decay_log": decay_log, "skip_gain": skip_gain, "output_proj": output_proj, "expert_gain": expert_gain, "router": router, "expert_up": expert_up, "expert_down": expert_down}


@jax.custom_vjp
def low(v):
    return lax.optimization_barrier(v.astype(jnp.bfloat16)).astype(jnp.float32)

@jax.custom_vjp
def low_back(v):
    return v

def low_keep(v):
    return (low(v), None)

def low_pass(kept, grad):
    return (grad,)

def back_keep(v):
    return (v, None)

def back_low(kept, grad):
    return (low(grad),)
low.defvjp(low_keep, low_pass)
low_back.defvjp(back_keep, back_low)

def rms_norm(values, gain):
    return values * lax.rsqrt(lax.optimization_barrier(jnp.mean(values * values, axis=-1, keepdims=True)) + 1e-05) * gain

def gelu_exact(values):
    return jax.nn.gelu(values, approximate=False)

def combine_pairs(first, second):
    return (first[0] * second[0], second[0] * first[1] + second[1])

def selective_scan(delta, state_in, state_out, conv_act, rates):
    length = delta.shape[0]
    block = min(64, length)
    count = length // block

    def advance(start, pieces):
        block_delta, block_in, block_out, block_act = pieces
        decay = jnp.exp(block_delta[:, None, :] * rates[None])
        drive = (block_delta * block_act)[:, None, :] * block_in[:, :, None]
        acc_decay, acc_drive = lax.associative_scan(combine_pairs, (decay, drive), axis=0)
        states = acc_decay * start[None] + acc_drive
        return (states[-1], lax.optimization_barrier(jnp.sum(block_out[:, :, None] * states, axis=1)))
    pieces = tuple((v.reshape(count, block, v.shape[-1]) for v in (delta, state_in, state_out, conv_act)))
    begin = jnp.zeros(rates.shape, jnp.float32)
    final_state, outs = lax.scan(jax.checkpoint(advance), begin, pieces)
    return outs.reshape(length, delta.shape[1])

def place_tokens(route_seq):
    length = route_seq.shape[0]
    chosen = (route_seq[:, None] == jnp.arange(EXPERTS, dtype=jnp.int32)[None, :]).astype(jnp.int32)
    counted = jnp.cumsum(chosen.reshape(length // TOK_DEV, TOK_DEV, EXPERTS), axis=1).astype(jnp.int32)
    counted = counted.reshape(length, EXPERTS) - chosen
    position = lax.optimization_barrier(jnp.sum(counted * chosen, axis=1)).astype(jnp.int32)
    block_id = (jnp.arange(length, dtype=jnp.int32) // TOK_DEV).astype(jnp.int32)
    slots_seq = length // TOK_DEV * CAP
    slot = (route_seq * slots_seq + block_id * CAP + position).astype(jnp.int32)
    table = jnp.full((EXPERTS * slots_seq,), length, jnp.int32).at[slot].set(jnp.arange(length, dtype=jnp.int32))
    return (slot, table)

def layer(params, x_seq, route_seq, slot, table):
    mixer_gain, input_proj, conv_weight, conv_bias, select_proj, step_proj, step_bias, decay_log, skip_gain, output_proj, expert_gain, router, expert_up, expert_down = params
    length = x_seq.shape[0]
    width = x_seq.shape[1]
    inner = select_proj.shape[1]
    rank = step_proj.shape[0]
    state = decay_log.shape[0]
    kernel = conv_weight.shape[0]
    highest = lax.Precision.HIGHEST
    normed = low(rms_norm(x_seq, mixer_gain))
    conv_input = low_back(jnp.dot(normed, input_proj[0], precision=highest))
    gate_branch = low_back(jnp.dot(normed, input_proj[1], precision=highest))
    padded = jnp.concatenate([jnp.zeros((kernel - 1, inner), jnp.float32), conv_input], axis=0)
    conv_sum = conv_bias + sum((conv_weight[k] * padded[k:k + length] for k in range(kernel)))
    conv_act = jax.nn.silu(conv_sum)
    selected = low_back(jnp.dot(low(conv_act), select_proj.T, precision=highest))
    low_rank = selected[:, :rank]
    state_in = selected[:, rank:rank + state]
    state_out = selected[:, rank + state:]
    delta = jax.nn.softplus(jnp.dot(low_rank, step_proj, precision=highest) + step_bias)
    rates = -jnp.exp(decay_log)
    scanned = selective_scan(delta, state_in, state_out, conv_act, rates)
    mixed = (scanned + skip_gain * conv_act) * jax.nn.silu(gate_branch)
    middle = x_seq + low_back(jnp.dot(low(mixed), output_proj, precision=highest))
    normed_two = low(rms_norm(middle, expert_gain))
    probs = jax.nn.softmax(jnp.dot(normed_two, router.T, precision=highest), axis=-1)
    onehot = route_seq[:, None] == jnp.arange(EXPERTS, dtype=jnp.int32)[None, :]
    gate = lax.optimization_barrier(jnp.sum(jnp.where(onehot, probs, 0.0), axis=1))
    extended = jnp.concatenate([normed_two, jnp.zeros((1, width), jnp.float32)], axis=0)
    expert_rows = jnp.take(extended, table, axis=0).reshape(EXPERTS, -1, width)
    up_three = expert_up.reshape(width, EXPERTS, FF).transpose(1, 0, 2)
    down_three = expert_down.reshape(EXPERTS, FF, width)
    expert_pre = low_back(jnp.einsum('erd,edf->erf', expert_rows, up_three, precision=highest))
    expert_act = low(gelu_exact(expert_pre))
    expert_out = low_back(jnp.einsum('erf,efd->erd', expert_act, down_three, precision=highest))
    picked = jnp.take(expert_out.reshape(-1, width), slot, axis=0)
    return middle + gate[:, None] * picked

def reference(tokens, cotangent, routes, mixer_gain, input_proj, conv_weight, conv_bias, select_proj, step_proj, step_bias, decay_log, skip_gain, output_proj, expert_gain, router, expert_up, expert_down):
    params = tuple((p.astype(jnp.float32) for p in (mixer_gain, input_proj, conv_weight, conv_bias, select_proj, step_proj, step_bias, decay_log, skip_gain, output_proj, expert_gain, router, expert_up, expert_down)))

    def one_sequence(totals, pieces):
        x_seq, grad_seq, route_seq = pieces
        route_flat = route_seq[:, 0].astype(jnp.int32)
        slot, table = place_tokens(route_flat)

        def forward(weights, values):
            return layer(weights, values, route_flat, slot, table)
        result, pull = jax.vjp(forward, params, x_seq)
        grad_weights, grad_values = pull(grad_seq)
        totals = jax.tree.map(lambda a, b: a + b, totals, grad_weights)
        return (totals, (result, grad_values))
    start = jax.tree.map(jnp.zeros_like, params)
    totals, (outputs, grad_tokens) = lax.scan(one_sequence, start, (tokens, cotangent, routes))
    return (outputs, grad_tokens, totals[0], totals[1], totals[2], totals[3], totals[4], totals[5], totals[6], totals[7], totals[8], totals[9], totals[10], totals[11], totals[12], totals[13])
```

```python
import jax
import jax.numpy as jnp
from jax import lax
from jax.experimental import pallas as pl
from jax.sharding import PartitionSpec as P

CAP = 56


HIGHEST = lax.Precision.HIGHEST


def from_behind(value, axis, by):
    size = lax.axis_size(axis)
    pairs = [(i, i + by) for i in range(size) if 0 <= i + by < size]
    return lax.ppermute(value, axis, pairs)


def copy_kernel(from_ref, to_ref):
    to_ref[...] = from_ref[...]


def copied(values):
    return pl.pallas_call(
        copy_kernel, out_shape=jax.ShapeDtypeStruct(values.shape, values.dtype)
    )(values)


def rms_norm(values, gain):
    return values * lax.rsqrt(jnp.mean(values * values, axis=-1, keepdims=True) + 1e-05) * gain


def gelu_exact(values):
    return jax.nn.gelu(values, approximate=False)


def inner_rows(left, right, precision=None):
    return lax.dot_general(
        left,
        right,
        (((0,), (0,)), ((), ())),
        precision=precision,
        preferred_element_type=jnp.float32,
    )


def outer_cols(left, right, precision=None):
    return lax.dot_general(
        left,
        right,
        (((1,), (1,)), ((), ())),
        precision=precision,
        preferred_element_type=jnp.float32,
    )


def scan_block(length):
    return min(128, max(8, length // 16))


def split_by(values, block):
    return values.reshape(values.shape[0] // block, block, values.shape[-1])


def forward_chain(start, delta, state_in, state_out, conv_act, rates):
    length = delta.shape[0]
    inner = delta.shape[1]
    block = scan_block(length)

    def forward_turn(state_now, pieces):
        block_delta, block_in, block_out, block_act = pieces
        first = state_now
        outs = []
        for index in range(block):
            state_now = (
                jnp.exp(block_delta[index][None, :] * rates) * state_now
                + block_in[index][:, None] * (block_delta[index] * block_act[index])[None, :]
            )
            outs.append(jnp.sum(block_out[index][:, None] * state_now, axis=0))
        return (state_now, (jnp.stack(outs), first))

    final, (scanned, starts) = lax.scan(
        forward_turn,
        start,
        (
            split_by(delta, block),
            split_by(state_in, block),
            split_by(state_out, block),
            split_by(conv_act, block),
        ),
    )
    return (final, scanned.reshape(length, inner), starts)


def backward_chain(after, starts, delta, state_in, state_out, conv_act, grad_mixed, rates):
    length = delta.shape[0]
    inner = delta.shape[1]
    state = rates.shape[0]
    block = scan_block(length)

    def backward_turn(carry, pieces):
        incoming, rate_total = carry
        start, block_delta, block_in, block_out, block_act, block_grad = pieces
        decays = []
        priors = []
        posts = []
        state_now = start
        for index in range(block):
            decay = jnp.exp(block_delta[index][None, :] * rates)
            priors.append(state_now)
            state_now = (
                decay * state_now
                + block_in[index][:, None] * (block_delta[index] * block_act[index])[None, :]
            )
            decays.append(decay)
            posts.append(state_now)
        grad_delta_list = [None] * block
        grad_act_list = [None] * block
        grad_in_list = [None] * block
        grad_out_list = [None] * block
        for index in range(block - 1, -1, -1):
            grad_state = block_out[index][:, None] * block_grad[index][None, :] + incoming
            weighted = grad_state * priors[index] * decays[index]
            input_side = jnp.sum(grad_state * block_in[index][:, None], axis=0)
            grad_delta_list[index] = (
                jnp.sum(weighted * rates, axis=0) + block_act[index] * input_side
            )
            grad_act_list[index] = block_delta[index] * input_side
            grad_in_list[index] = jnp.sum(
                grad_state * (block_delta[index] * block_act[index])[None, :], axis=1
            )
            grad_out_list[index] = jnp.sum(posts[index] * block_grad[index][None, :], axis=1)
            rate_total = rate_total + weighted * block_delta[index][None, :]
            incoming = decays[index] * grad_state
        return (
            (incoming, rate_total),
            (
                jnp.stack(grad_delta_list),
                jnp.stack(grad_act_list),
                jnp.stack(grad_in_list),
                jnp.stack(grad_out_list),
            ),
        )

    begin = (after, jnp.zeros(rates.shape, jnp.float32))
    (unused_start, rate_total), (grad_delta, grad_act, grad_in, grad_out) = lax.scan(
        backward_turn,
        begin,
        (
            starts,
            split_by(delta, block),
            split_by(state_in, block),
            split_by(state_out, block),
            split_by(conv_act, block),
            split_by(grad_mixed, block),
        ),
        reverse=True,
    )
    return (
        grad_delta.reshape(length, inner),
        grad_act.reshape(length, inner),
        grad_in.reshape(length, state),
        grad_out.reshape(length, state),
        rate_total,
    )


def carry_states(through, local, backward):
    empty = jnp.zeros_like(local)
    direction = -1 if backward else 1

    def carry_turn(index, incoming):
        return from_behind(through * incoming + local, "seq", direction)

    return lax.fori_loop(0, lax.axis_size("seq") - 1, carry_turn, empty)


def keep_values(values):
    return values


def edge_forward(values):
    return from_behind(values, "seq", 1)


def edge_backward(values):
    return from_behind(values, "seq", -1)


def chained_start(delta, state_in, state_out, conv_act, rates):
    zero_state = jnp.zeros(rates.shape, jnp.float32)
    local_state, unused_out, unused_starts = forward_chain(
        zero_state, delta, state_in, state_out, conv_act, rates
    )
    through = jnp.exp(rates * jnp.sum(delta, axis=0)[None, :])
    return (carry_states(through, local_state, False), through)


def chained_back(delta, state_out, grad_mixed, rates, through):
    block = scan_block(delta.shape[0])

    def chained_turn(incoming, pieces):
        block_delta, block_out, block_grad = pieces
        for index in range(block - 1, -1, -1):
            grad_state = block_out[index][:, None] * block_grad[index][None, :] + incoming
            incoming = jnp.exp(block_delta[index][None, :] * rates) * grad_state
        return (incoming, None)

    local_grad, unused = lax.scan(
        chained_turn,
        jnp.zeros(rates.shape, jnp.float32),
        (split_by(delta, block), split_by(state_out, block), split_by(grad_mixed, block)),
        reverse=True,
    )
    return carry_states(through, local_grad, True)


def mixer_forward(normed_in, weights, edge_fn, select_fn, start_fn):
    w_input, w_conv, b_conv, w_select, w_step, b_step, w_decay, w_skip = weights
    length = normed_in.shape[0]
    rank = w_step.shape[0]
    state = w_decay.shape[0]
    kernel = w_conv.shape[0]
    conv_input = jnp.dot(normed_in, w_input[0], preferred_element_type=jnp.float32)
    gate_branch = jnp.dot(normed_in, w_input[1], preferred_element_type=jnp.float32)
    edge = edge_fn(conv_input[length - kernel + 1 :])
    extended = jnp.concatenate([edge, conv_input], axis=0)
    conv_taps = w_conv.astype(jnp.float32)
    conv_sum = b_conv.astype(jnp.float32) + sum(
        (conv_taps[k] * extended[k : k + length] for k in range(kernel))
    )
    conv_act, silu_pull_act = jax.vjp(jax.nn.silu, conv_sum)
    conv_low = conv_act.astype(jnp.bfloat16)
    selected = select_fn(outer_cols(conv_low, w_select))
    low_rank = selected[:, :rank]
    state_in = selected[:, rank : rank + state]
    state_out = selected[:, rank + state :]
    step_pre = jnp.dot(low_rank, w_step.astype(jnp.float32), precision=HIGHEST) + b_step.astype(
        jnp.float32
    )
    delta = jax.nn.softplus(step_pre)
    rates = -jnp.exp(w_decay.astype(jnp.float32))
    incoming, through = start_fn(delta, state_in, state_out, conv_act, rates)
    unused_end, scanned, starts = forward_chain(
        incoming, delta, state_in, state_out, conv_act, rates
    )
    mixed = scanned + w_skip.astype(jnp.float32) * conv_act
    silu_gate, silu_pull_gate = jax.vjp(jax.nn.silu, gate_branch)
    mixer_low = (mixed * silu_gate).astype(jnp.bfloat16)
    return (
        extended,
        conv_act,
        silu_pull_act,
        conv_low,
        low_rank,
        state_in,
        state_out,
        step_pre,
        delta,
        rates,
        starts,
        mixed,
        silu_gate,
        silu_pull_gate,
        through,
        mixer_low,
    )


def mixer_backward(grad_y, saved, weights, chain_back, select_back, edge_back):
    (
        extended,
        conv_act,
        silu_pull_act,
        conv_low,
        low_rank,
        state_in,
        state_out,
        step_pre,
        delta,
        rates,
        starts,
        mixed,
        silu_gate,
        silu_pull_gate,
        through,
        mixer_low,
    ) = saved
    w_input, w_conv, b_conv, w_select, w_step, b_step, w_decay, w_skip = weights
    length = grad_y.shape[0]
    kernel = w_conv.shape[0]
    conv_taps = w_conv.astype(jnp.float32)
    grad_mixed = grad_y * silu_gate
    grad_gate_branch = silu_pull_gate(grad_y * mixed)[0]
    grad_skip = jnp.sum(grad_mixed * conv_act, axis=0)
    after = chain_back(delta, state_out, grad_mixed, rates, through)
    grad_delta, grad_act_scan, grad_state_in, grad_state_out, grad_rates = backward_chain(
        after, starts, delta, state_in, state_out, conv_act, grad_mixed, rates
    )
    grad_decay = grad_rates * rates
    grad_conv_act = grad_mixed * w_skip.astype(jnp.float32) + grad_act_scan
    grad_step_pre = grad_delta * jax.nn.sigmoid(step_pre)
    grad_step_bias = jnp.sum(grad_step_pre, axis=0)
    grad_step_w = inner_rows(low_rank, grad_step_pre, HIGHEST)
    grad_low_rank = outer_cols(grad_step_pre, w_step.astype(jnp.float32), HIGHEST)
    summed = select_back((grad_low_rank, grad_state_in, grad_state_out))
    grad_selected = jnp.concatenate([summed[0], summed[1], summed[2]], axis=1).astype(jnp.bfloat16)
    grad_select_w = inner_rows(grad_selected, conv_low)
    grad_conv_act = grad_conv_act + jnp.dot(
        grad_selected, w_select, preferred_element_type=jnp.float32
    )
    grad_conv_sum = silu_pull_act(grad_conv_act)[0]
    edge_grad = edge_back(grad_conv_sum[: kernel - 1])
    later_back = jnp.concatenate([grad_conv_sum, edge_grad], axis=0)
    grad_conv_input = sum(
        (conv_taps[k] * later_back[kernel - 1 - k : kernel - 1 - k + length] for k in range(kernel))
    )
    grad_conv_w = jnp.stack(
        [jnp.sum(grad_conv_sum * extended[k : k + length], axis=0) for k in range(kernel)]
    )
    grad_conv_b = jnp.sum(grad_conv_sum, axis=0)
    return (
        grad_conv_input.astype(jnp.bfloat16),
        grad_gate_branch.astype(jnp.bfloat16),
        (
            grad_conv_w,
            grad_conv_b,
            grad_select_w,
            grad_step_w,
            grad_step_bias,
            grad_decay,
            grad_skip,
        ),
    )


def body(
    tokens,
    cotangent,
    routes,
    mixer_gain,
    input_proj,
    conv_weight,
    conv_bias,
    select_proj,
    step_proj,
    step_bias,
    decay_log,
    skip_gain,
    output_proj,
    expert_gain,
    router,
    expert_up,
    expert_down,
):
    rows = tokens.shape[1]
    width = tokens.shape[2]
    shards = (
        input_proj,
        conv_weight,
        conv_bias,
        select_proj,
        step_proj,
        step_bias,
        decay_log,
        skip_gain,
        output_proj,
    )
    w_up, w_down = (
        lax.all_gather(expert_up, "seq", axis=0, tiled=True),
        lax.all_gather(expert_down, "seq", axis=1, tiled=True),
    )
    experts = router.shape[0]
    copies = lax.axis_size("dp") // experts
    capacity = CAP
    x_in = copied(tokens.reshape(rows, width))
    gain_one = mixer_gain.astype(jnp.float32)
    normed = rms_norm(x_in, gain_one).astype(jnp.bfloat16)
    gathered = (
        lax.all_gather(shards[0], ("dp", "seq"), axis=2, tiled=True),
        lax.all_gather(shards[1], ("dp", "seq"), axis=1, tiled=True),
        lax.all_gather(shards[2], ("dp", "seq"), axis=0, tiled=True),
        lax.all_gather(shards[3], ("dp", "seq"), axis=1, tiled=True),
        lax.all_gather(shards[4], ("dp", "seq"), axis=1, tiled=True),
        lax.all_gather(shards[5], ("dp", "seq"), axis=0, tiled=True),
        lax.all_gather(shards[6], ("dp", "seq"), axis=1, tiled=True),
        lax.all_gather(shards[7], ("dp", "seq"), axis=0, tiled=True),
        lax.all_gather(shards[8], ("dp", "seq"), axis=0, tiled=True),
    )
    saved = mixer_forward(normed, gathered[:8], edge_forward, keep_values, chained_start)
    mixer_low = saved[-1]
    w_output = gathered[8]
    middle = x_in + jnp.dot(mixer_low, w_output, preferred_element_type=jnp.float32)
    gain_two = expert_gain.astype(jnp.float32)
    normed_two = rms_norm(middle, gain_two).astype(jnp.bfloat16)
    probs = jax.nn.softmax(outer_cols(normed_two, router), axis=-1)
    route = routes.reshape(rows)
    chosen = (route[:, None] == lax.broadcasted_iota(jnp.int32, (rows, experts), 1)).astype(
        jnp.float32
    )
    gate = jnp.sum(chosen * probs, axis=1)
    earlier = (
        lax.broadcasted_iota(jnp.int32, (rows, rows), 0)
        > lax.broadcasted_iota(jnp.int32, (rows, rows), 1)
    ).astype(jnp.float32)
    before = jnp.dot(earlier, chosen, precision=HIGHEST)
    position = jnp.sum(before * chosen, axis=1).astype(jnp.int32)
    slot = route * capacity + position
    dispatch_table = (
        slot[None, :] == lax.broadcasted_iota(jnp.int32, (experts * capacity, rows), 0)
    ).astype(jnp.bfloat16)
    buffer = jnp.dot(dispatch_table, normed_two, preferred_element_type=jnp.float32).astype(
        jnp.bfloat16
    )
    send = jnp.repeat(buffer.reshape(experts, capacity, width), copies, axis=0)
    received = lax.all_to_all(send, "dp", split_axis=0, concat_axis=0, tiled=True)
    sources = received.shape[0]
    expert_rows = received.reshape(-1, width)
    expert_pre = jnp.dot(expert_rows, w_up, preferred_element_type=jnp.float32)
    expert_act, gelu_pull = jax.vjp(gelu_exact, expert_pre)
    act_low = expert_act.astype(jnp.bfloat16)
    partial_out = jnp.dot(act_low, w_down, preferred_element_type=jnp.float32).reshape(
        sources, capacity, width
    )
    returned = lax.all_to_all(
        partial_out.astype(jnp.bfloat16), "dp", split_axis=0, concat_axis=0, tiled=True
    ).astype(partial_out.dtype)
    expert_out = jnp.sum(returned.reshape(experts, copies, capacity, width), axis=1).reshape(
        experts * capacity, width
    )
    picked = jnp.take(expert_out, slot, axis=0)
    output = middle + gate[:, None] * picked
    grad_out = cotangent.reshape(rows, width)
    grad_pick = (gate[:, None] * grad_out).astype(jnp.bfloat16)
    grad_gate = jnp.sum(grad_out * picked, axis=1)
    grad_buffer = jnp.dot(dispatch_table, grad_pick, preferred_element_type=jnp.float32).astype(
        jnp.bfloat16
    )
    grad_send = jnp.repeat(grad_buffer.reshape(experts, capacity, width), copies, axis=0)
    grad_rows = lax.all_to_all(grad_send, "dp", split_axis=0, concat_axis=0, tiled=True)
    grad_flat = grad_rows.reshape(-1, width)
    grad_down_w = inner_rows(act_low, grad_flat)
    grad_act = outer_cols(grad_flat, w_down)
    grad_pre = gelu_pull(grad_act)[0].astype(jnp.bfloat16)
    grad_up_w = inner_rows(expert_rows, grad_pre)
    grad_in_rows = outer_cols(grad_pre, w_up).reshape(sources, capacity, width)
    grad_back = lax.all_to_all(
        grad_in_rows.astype(jnp.bfloat16), "dp", split_axis=0, concat_axis=0, tiled=True
    ).astype(grad_in_rows.dtype)
    grad_slots = jnp.sum(grad_back.reshape(experts, copies, capacity, width), axis=1).reshape(
        experts * capacity, width
    )
    grad_logits = gate[:, None] * (chosen - probs) * grad_gate[:, None]
    router_full = router.astype(jnp.float32)
    grad_normed_two = jnp.take(grad_slots, slot, axis=0) + jnp.dot(
        grad_logits, router_full, precision=HIGHEST
    )
    grad_router = inner_rows(grad_logits, normed_two.astype(jnp.float32), HIGHEST)
    unused_two, pull_two = jax.vjp(rms_norm, middle, gain_two)
    grad_middle_norm, grad_gain_two = pull_two(grad_normed_two)
    grad_middle = grad_out + grad_middle_norm
    grad_middle_low = grad_middle.astype(jnp.bfloat16)
    w_input = gathered[0]
    grad_output_w = inner_rows(mixer_low, grad_middle_low)
    grad_y = outer_cols(grad_middle_low, w_output)
    grad_conv_input, grad_gate_branch, mixer_part = mixer_backward(
        grad_y, saved, gathered[:8], chained_back, keep_values, edge_backward
    )
    taps_grad, bias_grad, select_grad, step_grad, shift_grad, decay_grad, skip_grad = mixer_part
    grad_normed = outer_cols(grad_conv_input, w_input[0]) + outer_cols(grad_gate_branch, w_input[1])
    grad_input_w = jnp.stack(
        [inner_rows(normed, grad_conv_input), inner_rows(normed, grad_gate_branch)]
    )
    mixer_grads = (
        lax.psum_scatter(grad_input_w, ("dp", "seq"), scatter_dimension=2, tiled=True),
        lax.psum_scatter(taps_grad, ("dp", "seq"), scatter_dimension=1, tiled=True),
        lax.psum_scatter(bias_grad, ("dp", "seq"), scatter_dimension=0, tiled=True),
        lax.psum_scatter(select_grad, ("dp", "seq"), scatter_dimension=1, tiled=True),
        lax.psum_scatter(step_grad, ("dp", "seq"), scatter_dimension=1, tiled=True),
        lax.psum_scatter(shift_grad, ("dp", "seq"), scatter_dimension=0, tiled=True),
        lax.psum_scatter(decay_grad, ("dp", "seq"), scatter_dimension=1, tiled=True),
        lax.psum_scatter(skip_grad, ("dp", "seq"), scatter_dimension=0, tiled=True),
        lax.psum_scatter(grad_output_w, ("dp", "seq"), scatter_dimension=0, tiled=True),
    )
    unused_one, pull_one = jax.vjp(rms_norm, x_in, gain_one)
    grad_in_norm, grad_gain_one = pull_one(grad_normed)
    grad_tokens = grad_middle + grad_in_norm
    expert_grads = (
        lax.psum_scatter(
            grad_up_w.astype(jnp.bfloat16), "seq", scatter_dimension=0, tiled=True
        ).astype(jnp.float32),
        lax.psum_scatter(
            grad_down_w.astype(jnp.bfloat16), "seq", scatter_dimension=1, tiled=True
        ).astype(jnp.float32),
    )
    small_sums = lax.psum((grad_gain_one, grad_gain_two, grad_router), ("dp", "seq"))
    return (
        output.reshape(tokens.shape),
        grad_tokens.reshape(tokens.shape),
        small_sums[0],
        mixer_grads[0],
        mixer_grads[1],
        mixer_grads[2],
        mixer_grads[3],
        mixer_grads[4],
        mixer_grads[5],
        mixer_grads[6],
        mixer_grads[7],
        mixer_grads[8],
        small_sums[1],
        small_sums[2],
        expert_grads[0],
        expert_grads[1],
    )


def solution(mesh):
    placed = (
        P("dp", "seq", None),
        P("dp", "seq", None),
        P("dp", "seq", None),
        P(),
        P(None, None, ("dp", "seq")),
        P(None, ("dp", "seq")),
        P(("dp", "seq")),
        P(None, ("dp", "seq")),
        P(None, ("dp", "seq")),
        P(("dp", "seq")),
        P(None, ("dp", "seq")),
        P(("dp", "seq")),
        P(("dp", "seq"), None),
        P(),
        P(),
        P("seq", "dp"),
        P("dp", "seq"),
    )
    return jax.shard_map(
        body,
        mesh=mesh,
        in_specs=placed,
        out_specs=(
            P("dp", "seq", None),
            P("dp", "seq", None),
            P(),
            P(None, None, ("dp", "seq")),
            P(None, ("dp", "seq")),
            P(("dp", "seq")),
            P(None, ("dp", "seq")),
            P(None, ("dp", "seq")),
            P(("dp", "seq")),
            P(None, ("dp", "seq")),
            P(("dp", "seq")),
            P(("dp", "seq"), None),
            P(),
            P(),
            P("seq", "dp"),
            P("dp", "seq"),
        ),
        check_vma=False,
    )
```

```python
import functools
import math

import jax
import jax.numpy as jnp
from jax import lax
from jax.experimental import pallas as pl
from jax.experimental.pallas import tpu as pltpu
from jax.sharding import PartitionSpec as P

CAP = 56
LANES = 128
TIME_BLOCK = 128
LOG2E = math.log2(math.e)

HIGHEST = lax.Precision.HIGHEST


def rms_norm(values, gain):
    return values * lax.rsqrt(jnp.mean(values * values, axis=-1, keepdims=True) + 1e-05) * gain


def gelu_exact(values):
    return jax.nn.gelu(values, approximate=False)


def inner_rows(left, right, precision=None):
    return lax.dot_general(
        left,
        right,
        (((0,), (0,)), ((), ())),
        precision=precision,
        preferred_element_type=jnp.float32,
    )


def outer_cols(left, right, precision=None):
    return lax.dot_general(
        left,
        right,
        (((1,), (1,)), ((), ())),
        precision=precision,
        preferred_element_type=jnp.float32,
    )


def sublane_sums(parts):
    row = lax.broadcasted_iota(jnp.int32, parts[0].shape, 0)
    low4 = row < 4
    low2 = (row % 4) < 2
    low1 = (row % 2) < 1
    quads = []
    for k in range(4):
        a, b = parts[k], parts[k + 4]
        quads.append(jnp.where(low4, a, b) + pltpu.roll(jnp.where(low4, b, a), 4, 0))
    pairs = []
    for k in range(2):
        a, b = quads[k], quads[k + 2]
        pairs.append(
            jnp.where(low2, a, b) + jnp.where(low2, pltpu.roll(a, 6, 0), pltpu.roll(b, 2, 0))
        )
    a, b = pairs
    return jnp.where(low1, a, b) + jnp.where(low1, pltpu.roll(a, 7, 0), pltpu.roll(b, 1, 0))


def lane_column(block, k):
    return jnp.broadcast_to(block[:, k : k + 1], block.shape)


MESH = pl.DeviceIdType.MESH
VMEM_LIMIT = 56 * 1024 * 1024


def dot_nn(left, right, precision=None):
    return lax.dot_general(
        left, right, (((1,), (0,)), ((), ())), precision=precision,
        preferred_element_type=jnp.float32,
    )


def place():
    own, line = lax.axis_index("seq"), lax.axis_index("dp")
    return line, own, own // 2, lax.rem(own, 2)


def remote(source, target, send_sem, recv_sem, line, position):
    return pltpu.make_async_remote_copy(
        src_ref=source,
        dst_ref=target,
        send_sem=send_sem,
        recv_sem=recv_sem,
        device_id=(line, position),
        device_id_type=MESH,
    )


def greet(count, lines=1):
    line, own, _, _ = place()
    barrier = pltpu.get_barrier_semaphore()
    for k in range(1, count):
        pl.semaphore_signal(
            barrier, inc=1, device_id=(line, lax.rem(own + k, count)), device_id_type=MESH
        )
    for k in range(1, lines):
        pl.semaphore_signal(
            barrier, inc=1, device_id=(lax.rem(line + k, lines), own), device_id_type=MESH
        )
    pl.semaphore_wait(barrier, count - 1 + lines - 1)


def sigmoid(values):
    return 1.0 / (1.0 + jnp.exp(-values))


def softplus(values):
    return jnp.maximum(values, 0.0) + jnp.log1p(jnp.exp(-jnp.abs(values)))


class Cuts:
    def __init__(self, picks, rank, state, kernel):
        self.picks, self.rank, self.state, self.kernel = picks, rank, state, kernel
        self.step = picks
        self.decay = self.step + rank
        self.taps = self.decay + state
        self.conv_bias = self.taps + kernel
        self.step_bias = self.conv_bias + 1
        self.skip = self.step_bias + 1
        self.rows = self.skip + 1


def front_kernel(
    count, lines, cuts,
    normed_ref, packed_ref,
    all_ref, weights_ref, small_ref, ext_ref, sum_ref, act_ref, gate_ref, selected_ref,
    part_ref, partial_ref,
    send_w, recv_w, send_hi, recv_hi, send_x, recv_x, send_rs, recv_rs, send_ag, recv_ag,
):
    line, own, high, low = place()
    half = count // 2
    rows, width = normed_ref.shape
    shard = packed_ref.shape[0]
    inner = weights_ref.shape[0]
    kernel = cuts.kernel
    partner = 2 * high + 1 - low
    greet(count, lines)

    copies = []
    shard_rows = pl.ds(pl.multiple_of(line * shard, 16), shard)
    for k in range(1, half):
        copy = remote(
            normed_ref, all_ref.at[own], send_hi.at[k], recv_hi.at[k],
            line, 2 * lax.rem(high + k, half) + low,
        )
        copy.start()
        copies.append(copy)
    copy = remote(normed_ref, all_ref.at[own], send_x.at[0], recv_x.at[0], line, partner)
    copy.start()
    copies.append(copy)
    for k in range(1, lines):
        copy = remote(
            packed_ref, weights_ref.at[shard_rows], send_w.at[k], recv_w.at[k],
            lax.rem(line + k, lines), own,
        )
        copy.start()
        copies.append(copy)
    all_ref[own] = normed_ref[...]
    weights_ref[shard_rows, :] = packed_ref[...]
    if lines * shard < inner:
        weights_ref[lines * shard :, :] = jnp.zeros(
            (inner - lines * shard, weights_ref.shape[1]), weights_ref.dtype
        )
    ext_ref[0:8, :] = jnp.zeros((8, inner), jnp.float32)
    for k in range(1, half):
        block = 2 * lax.rem(high - k + half, half) + low
        remote(
            normed_ref, all_ref.at[block], send_hi.at[k], recv_hi.at[k], line, partner
        ).wait_recv()
        copy = remote(
            all_ref.at[block], all_ref.at[block], send_x.at[k], recv_x.at[k], line, partner
        )
        copy.start()
        copies.append(copy)
    for k in range(1, lines):
        from_line = lax.rem(line - k + lines, lines)
        there = pl.ds(pl.multiple_of(from_line * shard, 16), shard)
        remote(
            packed_ref, weights_ref.at[there], send_w.at[k], recv_w.at[k], from_line, own
        ).wait_recv()
    small_ref[...] = weights_ref[:, 3 * width :].astype(jnp.float32).T
    for k in range(half):
        block = 2 * lax.rem(high - k + half, half) + 1 - low
        remote(
            normed_ref, all_ref.at[block], send_x.at[k], recv_x.at[k], line, partner
        ).wait_recv()

    def project(b, carry):
        start = pl.multiple_of(b * rows, rows)
        block = all_ref[b]
        ext_ref[pl.ds(pl.multiple_of(start + 8, 8), rows), :] = outer_cols(
            block, weights_ref[:, :width]
        )
        gate_ref[pl.ds(start, rows), :] = outer_cols(block, weights_ref[:, width : 2 * width])
        return carry

    lax.fori_loop(0, count, project, 0)

    def convolve(b, carry):
        start = pl.multiple_of(b * rows, rows)
        window = ext_ref[pl.ds(start, rows + 8), :]
        total = small_ref[cuts.conv_bias : cuts.conv_bias + 1, :]
        for k in range(kernel):
            tap = small_ref[cuts.taps + k : cuts.taps + k + 1, :]
            total = total + tap * window[9 - kernel + k : 9 - kernel + k + rows]
        act = total * sigmoid(total)
        sum_ref[pl.ds(start, rows), :] = total
        act_ref[pl.ds(start, rows), :] = act
        part_ref[b] = outer_cols(
            small_ref[: cuts.picks, :].astype(jnp.bfloat16), act.astype(jnp.bfloat16)
        )
        return carry

    lax.fori_loop(0, count, convolve, 0)

    for k in range(1, count):
        there = lax.rem(own + k, count)
        copy = remote(
            part_ref.at[there], partial_ref.at[k], send_rs.at[k], recv_rs.at[k], line, there
        )
        copy.start()
        copies.append(copy)
    total = part_ref[own]
    for k in range(1, count):
        remote(
            part_ref.at[own], partial_ref.at[k], send_rs.at[k], recv_rs.at[k], line, partner
        ).wait_recv()
        total = total + partial_ref[k]
    selected_ref[own] = total
    for k in range(1, count):
        copy = remote(
            selected_ref.at[own], selected_ref.at[own], send_ag.at[k], recv_ag.at[k],
            line, lax.rem(own + k, count),
        )
        copy.start()
        copies.append(copy)
    for k in range(1, count):
        block = lax.rem(own - k + count, count)
        remote(
            selected_ref.at[block], selected_ref.at[block], send_ag.at[k], recv_ag.at[k],
            line, partner,
        ).wait_recv()
    for copy in copies:
        copy.wait_send()


def front(count, lines, cuts, normed, packed):
    rows, width = normed.shape
    shard, columns = packed.shape
    inner = -(-lines * shard // LANES) * LANES
    length = count * rows
    half = count // 2
    small = columns - 3 * width
    vmem = pl.BlockSpec(memory_space=pltpu.VMEM)

    def f32(*shape):
        return jax.ShapeDtypeStruct(shape, jnp.float32)

    dma = pltpu.SemaphoreType.DMA
    return pl.pallas_call(
        functools.partial(front_kernel, count, lines, cuts),
        in_specs=[vmem] * 2,
        out_specs=[vmem] * 8,
        out_shape=[
            jax.ShapeDtypeStruct((count, rows, width), jnp.bfloat16),
            jax.ShapeDtypeStruct((inner, columns), jnp.bfloat16),
            f32(small, inner),
            f32(length + 8, inner),
            f32(length, inner),
            f32(length, inner),
            f32(length, inner),
            f32(count, cuts.picks, rows),
        ],
        scratch_shapes=[
            pltpu.VMEM((count, cuts.picks, rows), jnp.float32),
            pltpu.VMEM((count, cuts.picks, rows), jnp.float32),
            dma((lines,)), dma((lines,)), dma((half,)), dma((half,)), dma((half,)), dma((half,)),
            dma((count,)), dma((count,)), dma((count,)), dma((count,)),
        ],
        compiler_params=pltpu.CompilerParams(
            collective_id=0, has_side_effects=True, vmem_limit_bytes=VMEM_LIMIT
        ),
        cost_estimate=pl.CostEstimate(
            flops=4 * length * width * inner,
            bytes_accessed=20 * length * inner,
            transcendentals=length * inner,
        ),
        name="front",
    )(normed, packed)


class Relay:
    def __init__(self, count, part, across, along, send_x, recv_x, send_hi, recv_hi):
        self.line, self.own, self.high, self.low = place()
        self.half = count // 2
        self.part, self.across, self.along = part, across, along
        self.send_x, self.recv_x, self.send_hi, self.recv_hi = send_x, recv_x, send_hi, recv_hi
        self.partner = 2 * self.high + 1 - self.low

    def over(self, block):
        i = block // 2
        return remote(
            self.part.at[block], self.across.at[i], self.send_x.at[i], self.recv_x.at[i],
            self.line, self.partner,
        )

    def on(self, block):
        i = block // 2
        k = lax.rem(i - self.high + self.half, self.half)
        return remote(
            self.part.at[block], self.along.at[k], self.send_hi.at[k], self.recv_hi.at[k],
            self.line, 2 * i + self.low,
        )

    def made(self, block):
        @pl.when(lax.rem(block, 2) != self.low)
        def _():
            self.over(block).start()

    def pass_on(self, block):
        @pl.when((lax.rem(block, 2) == self.low) & (block // 2 != self.high))
        def _():
            self.over(block).wait_recv()
            both = self.part[block].astype(jnp.float32) + self.across[block // 2].astype(
                jnp.float32
            )
            self.part[block] = both.astype(jnp.bfloat16)
            self.on(block).start()

    def finish(self):
        self.over(self.own).wait_recv()
        total = self.part[self.own].astype(jnp.float32) + self.across[self.high].astype(
            jnp.float32
        )
        for k in range(1, self.half):
            block = 2 * lax.rem(self.high + k, self.half) + self.low
            self.on(block).wait_recv()
            total = total + self.along[k].astype(jnp.float32)
        for i in range(self.half):
            self.over(2 * i + 1 - self.low).wait_send()
        for k in range(1, self.half):
            self.on(2 * lax.rem(self.high + k, self.half) + self.low).wait_send()
        return total

    @staticmethod
    def scratch(count, rows, width):
        half = count // 2
        dma = pltpu.SemaphoreType.DMA
        return [
            pltpu.VMEM((count, rows, width), jnp.bfloat16),
            pltpu.VMEM((half, rows, width), jnp.bfloat16),
            pltpu.VMEM((half, rows, width), jnp.bfloat16),
            dma((half,)), dma((half,)), dma((half,)), dma((half,)),
        ]


def scan_forward_kernel(
    count, cuts,
    act_ref, gate_ref, selected_ref, small_ref, output_ref,
    pre_ref, mixed_ref, mixer_low_ref, prior_ref, end_ref, summed_ref,
    state_ref, delta_ref, scanned_ref, *relay_refs,
):
    steps, inner = act_ref.shape
    tiles = inner // LANES
    state = cuts.state
    halves = state // 8
    step = pl.program_id(0)
    relay = Relay(count, *relay_refs)

    @pl.when(step == 0)
    def _():
        greet(count)
        state_ref[...] = jnp.zeros_like(state_ref)

    rates2 = -LOG2E * jnp.exp(small_ref[cuts.decay : cuts.decay + state, :])
    pre = inner_rows(
        selected_ref[0, : cuts.rank, :],
        small_ref[cuts.step : cuts.step + cuts.rank, :],
        HIGHEST,
    ) + small_ref[cuts.step_bias : cuts.step_bias + 1, :]
    pre_ref[...] = pre
    delta_ref[...] = softplus(pre)
    in_rows = cuts.rank
    out_rows = cuts.rank + state

    def group(g, states):
        states = [list(s) for s in states]
        base = pl.multiple_of(g * 8, 8)
        shift = lax.rem(steps - base, steps)
        b_cols = [
            pltpu.roll(selected_ref[0, in_rows + 8 * i : in_rows + 8 * i + 8, :], shift, 1)
            for i in range(halves)
        ]
        c_cols = [
            pltpu.roll(selected_ref[0, out_rows + 8 * i : out_rows + 8 * i + 8, :], shift, 1)
            for i in range(halves)
        ]
        d8 = delta_ref[pl.ds(base, 8), :]
        du8 = d8 * act_ref[pl.ds(base, 8), :]
        parts = [[None] * 8 for _ in range(tiles)]
        for k in range(8):
            b_now = [lane_column(b, k) for b in b_cols]
            c_now = [lane_column(c, k) for c in c_cols]
            for j in range(tiles):
                cols = slice(j * LANES, (j + 1) * LANES)
                d = jnp.broadcast_to(d8[k : k + 1, cols], (8, LANES))
                du = jnp.broadcast_to(du8[k : k + 1, cols], (8, LANES))
                total = None
                for i in range(halves):
                    old = states[j][i]
                    prior_ref[base + k, 8 * i : 8 * i + 8, cols] = old
                    new = jnp.exp2(d * rates2[8 * i : 8 * i + 8, cols]) * old + b_now[i] * du
                    states[j][i] = new
                    term = c_now[i] * new
                    total = term if total is None else total + term
                parts[j][k] = total
        for j in range(tiles):
            scanned_ref[pl.ds(base, 8), j * LANES : (j + 1) * LANES] = sublane_sums(parts[j])
        return tuple(tuple(s) for s in states)

    first = tuple(
        tuple(
            state_ref[8 * i : 8 * i + 8, j * LANES : (j + 1) * LANES] for i in range(halves)
        )
        for j in range(tiles)
    )
    last = lax.fori_loop(0, steps // 8, group, first)
    for j in range(tiles):
        for i in range(halves):
            state_ref[8 * i : 8 * i + 8, j * LANES : (j + 1) * LANES] = last[j][i]
    end_ref[...] = state_ref[...]

    mixed = scanned_ref[...] + small_ref[cuts.skip : cuts.skip + 1, :] * act_ref[...]
    gate = gate_ref[...]
    low = (mixed * (gate * sigmoid(gate))).astype(jnp.bfloat16)
    mixed_ref[...] = mixed
    mixer_low_ref[...] = low
    relay.part[step] = dot_nn(low, output_ref[...]).astype(jnp.bfloat16)
    relay.made(step)

    @pl.when(step >= 2)
    def _():
        relay.pass_on(step - 2)

    @pl.when(step == count - 1)
    def _():
        relay.pass_on(step - 1)
        relay.pass_on(step)
        summed_ref[...] = relay.finish()


def scan_forward(count, cuts, width, act, gate, selected, small, weights):
    length, inner = act.shape
    state = cuts.state
    block = length // count
    rows = pl.BlockSpec((block, inner), lambda t: (t, 0))
    whole = pl.BlockSpec((state, inner), lambda t: (0, 0))
    return pl.pallas_call(
        functools.partial(scan_forward_kernel, count, cuts),
        grid=(count,),
        in_specs=[
            rows,
            rows,
            pl.BlockSpec((1, cuts.picks, block), lambda t: (t, 0, 0)),
            pl.BlockSpec(small.shape, lambda t: (0, 0)),
            pl.BlockSpec((inner, width), lambda t: (0, 2)),
        ],
        out_specs=[
            rows,
            rows,
            rows,
            pl.BlockSpec((block, state, inner), lambda t: (t, 0, 0)),
            whole,
            pl.BlockSpec((block, width), lambda t: (0, 0)),
        ],
        out_shape=[
            jax.ShapeDtypeStruct((length, inner), jnp.float32),
            jax.ShapeDtypeStruct((length, inner), jnp.float32),
            jax.ShapeDtypeStruct((length, inner), jnp.bfloat16),
            jax.ShapeDtypeStruct((length, state, inner), jnp.float32),
            jax.ShapeDtypeStruct((state, inner), jnp.float32),
            jax.ShapeDtypeStruct((block, width), jnp.float32),
        ],
        scratch_shapes=[
            pltpu.VMEM((state, inner), jnp.float32),
            pltpu.VMEM((block, inner), jnp.float32),
            pltpu.VMEM((block, inner), jnp.float32),
            *Relay.scratch(count, block, width),
        ],
        compiler_params=pltpu.CompilerParams(
            collective_id=1, has_side_effects=True, vmem_limit_bytes=VMEM_LIMIT
        ),
        cost_estimate=pl.CostEstimate(
            flops=8 * length * state * inner,
            bytes_accessed=4 * length * inner * (state + 6),
            transcendentals=length * state * inner,
        ),
        name="scan_forward",
    )(act, gate, selected, small, weights)


def scan_backward_kernel(
    count, cuts,
    own_ref, act_ref, gate_ref, mixed_ref, pre_ref, selected_ref, small_ref, output_ref,
    prior_ref, end_ref,
    grad_gate_ref, grad_act_ref, grad_step_ref, rate_total_ref, rows_ref, grad_selected_ref,
    all_out_ref,
    incoming_ref, post_ref, delta_ref, grad_ref, grad_delta_ref, all_ref,
    part_ref, partial_ref, total_ref,
    send_hi, recv_hi, send_x, recv_x, send_rs, recv_rs, send_ag, recv_ag,
):
    steps, inner = act_ref.shape
    tiles = inner // LANES
    state = cuts.state
    halves = state // 8
    lane = lax.broadcasted_iota(jnp.int32, (8, steps), 1)
    line, own, high, low = place()
    half = count // 2
    partner = 2 * high + 1 - low
    index = pl.program_id(0)
    now = count - 1 - index

    def along(k):
        return remote(
            own_ref, all_ref.at[own], send_hi.at[k], recv_hi.at[high], line,
            2 * lax.rem(high + k, half) + low,
        )

    def across(block):
        i = block // 2
        return remote(
            all_ref.at[block], all_ref.at[block], send_x.at[i], recv_x.at[i], line, partner
        )

    def came_along(block):
        i = block // 2
        return remote(
            all_ref.at[block], all_ref.at[block], send_hi.at[0], recv_hi.at[i], line, partner
        )

    def hand_over(block):
        @pl.when((lax.rem(block, 2) == low) & (block // 2 != high))
        def _():
            came_along(block).wait_recv()
            across(block).start()

    @pl.when(index == 0)
    def _():
        greet(count)
        all_ref[own] = own_ref[...]
        incoming_ref[...] = jnp.zeros_like(incoming_ref)
        post_ref[...] = end_ref[...]
        rate_total_ref[...] = jnp.zeros_like(rate_total_ref)
        grad_step_ref[...] = jnp.zeros_like(grad_step_ref)
        rows_ref[...] = jnp.zeros_like(rows_ref)

    @pl.when(index == jnp.maximum(count - 3 - own, 0))
    def _():
        for k in range(1, half):
            along(k).start()
        across(own).start()

    @pl.when(index == 0)
    def _():
        hand_over(now)
        hand_over(now - 1)

    @pl.when(lax.rem(now, 2) != low)
    def _():
        across(now).wait_recv()

    gate = gate_ref[...]
    gate_sig = sigmoid(gate)
    grad_y = outer_cols(all_ref[now], output_ref[...])
    grad_gate_ref[...] = (
        grad_y * mixed_ref[...] * (gate_sig * (1.0 + gate * (1.0 - gate_sig)))
    ).astype(jnp.bfloat16)
    grad_mixed = grad_y * (gate * gate_sig)
    grad_ref[...] = grad_mixed
    delta_ref[...] = softplus(pre_ref[...])
    rows_ref[1:2, :] += jnp.sum(grad_mixed * act_ref[...], axis=0, keepdims=True)
    rates2 = -LOG2E * jnp.exp(small_ref[cuts.decay : cuts.decay + state, :])
    in_rows = cuts.rank
    out_rows = cuts.rank + state

    def tile_of(ref):
        return tuple(
            tuple(ref[8 * i : 8 * i + 8, j * LANES : (j + 1) * LANES] for i in range(halves))
            for j in range(tiles)
        )

    def group(turn, carry):
        incoming, posts, rate_total, in_acc, out_acc = carry
        incoming = [list(s) for s in incoming]
        posts = [list(s) for s in posts]
        rate_total = [list(s) for s in rate_total]
        in_acc, out_acc = list(in_acc), list(out_acc)
        base = pl.multiple_of((steps // 8 - 1 - turn) * 8, 8)
        shift = lax.rem(steps - base, steps)
        b_cols = [
            pltpu.roll(selected_ref[0, in_rows + 8 * i : in_rows + 8 * i + 8, :], shift, 1)
            for i in range(halves)
        ]
        c_cols = [
            pltpu.roll(selected_ref[0, out_rows + 8 * i : out_rows + 8 * i + 8, :], shift, 1)
            for i in range(halves)
        ]
        d8 = delta_ref[pl.ds(base, 8), :]
        u8 = act_ref[pl.ds(base, 8), :]
        du8 = d8 * u8
        g8 = grad_ref[pl.ds(base, 8), :]
        rate_parts = [[None] * 8 for _ in range(tiles)]
        side_parts = [[None] * 8 for _ in range(tiles)]
        for k in range(7, -1, -1):
            b_now = [lane_column(b, k) for b in b_cols]
            c_now = [lane_column(c, k) for c in c_cols]
            in_sum = [None] * halves
            out_sum = [None] * halves
            for j in range(tiles):
                cols = slice(j * LANES, (j + 1) * LANES)
                d = jnp.broadcast_to(d8[k : k + 1, cols], (8, LANES))
                du = jnp.broadcast_to(du8[k : k + 1, cols], (8, LANES))
                gm = jnp.broadcast_to(g8[k : k + 1, cols], (8, LANES))
                rate_part = None
                side_part = None
                for i in range(halves):
                    prior = prior_ref[base + k, 8 * i : 8 * i + 8, cols]
                    rates = rates2[8 * i : 8 * i + 8, cols]
                    grad_state = c_now[i] * gm + incoming[j][i]
                    passed = jnp.exp2(d * rates) * grad_state
                    incoming[j][i] = passed
                    weighted = passed * prior
                    term = weighted * rates
                    rate_part = term if rate_part is None else rate_part + term
                    term = grad_state * b_now[i]
                    side_part = term if side_part is None else side_part + term
                    term = grad_state * du
                    in_sum[i] = term if in_sum[i] is None else in_sum[i] + term
                    term = posts[j][i] * gm
                    out_sum[i] = term if out_sum[i] is None else out_sum[i] + term
                    rate_total[j][i] = rate_total[j][i] + weighted * d
                    posts[j][i] = prior
                rate_parts[j][k] = rate_part
                side_parts[j][k] = side_part
            here = lane == base + k
            for i in range(halves):
                in_acc[i] = jnp.where(here, jnp.sum(in_sum[i], axis=1, keepdims=True), in_acc[i])
                out_acc[i] = jnp.where(here, jnp.sum(out_sum[i], axis=1, keepdims=True), out_acc[i])
        for j in range(tiles):
            cols = slice(j * LANES, (j + 1) * LANES)
            side = sublane_sums(side_parts[j])
            grad_delta_ref[pl.ds(base, 8), cols] = (
                sublane_sums(rate_parts[j]) * (1.0 / LOG2E) + u8[:, cols] * side
            )
            grad_act_ref[pl.ds(base, 8), cols] = d8[:, cols] * side
        return (
            tuple(tuple(s) for s in incoming),
            tuple(tuple(s) for s in posts),
            tuple(tuple(s) for s in rate_total),
            tuple(in_acc),
            tuple(out_acc),
        )

    empty = tuple(jnp.zeros((8, steps), jnp.float32) for _ in range(halves))
    incoming, posts, rate_total, in_acc, out_acc = lax.fori_loop(
        0,
        steps // 8,
        group,
        (tile_of(incoming_ref), tile_of(post_ref), tile_of(rate_total_ref), empty, empty),
    )
    for i in range(halves):
        part_ref[now, in_rows + 8 * i : in_rows + 8 * i + 8, :] = in_acc[i]
        part_ref[now, out_rows + 8 * i : out_rows + 8 * i + 8, :] = out_acc[i]
        for j in range(tiles):
            cols = slice(j * LANES, (j + 1) * LANES)
            incoming_ref[8 * i : 8 * i + 8, cols] = incoming[j][i]
            post_ref[8 * i : 8 * i + 8, cols] = posts[j][i]
            rate_total_ref[8 * i : 8 * i + 8, cols] = rate_total[j][i]

    grad_act_ref[...] += grad_ref[...] * small_ref[cuts.skip : cuts.skip + 1, :]
    grad_pre = grad_delta_ref[...] * sigmoid(pre_ref[...])
    rows_ref[0:1, :] += jnp.sum(grad_pre, axis=0, keepdims=True)
    grad_step_ref[...] += dot_nn(selected_ref[0, : cuts.rank, :], grad_pre, HIGHEST)
    part_ref[now, : cuts.rank, :] = outer_cols(
        small_ref[cuts.step : cuts.step + cuts.rank, :], grad_pre, HIGHEST
    )

    def partial_to(block):
        return remote(
            part_ref.at[block], partial_ref.at[own], send_rs.at[block], recv_rs.at[own], line, block
        )

    @pl.when(now != own)
    def _():
        partial_to(now).start()

    def total_to(k):
        return remote(
            total_ref.at[own], total_ref.at[own], send_ag.at[k], recv_ag.at[own], line,
            lax.rem(own + k, count),
        )

    @pl.when(now >= 2)
    def _():
        hand_over(now - 2)

    @pl.when(index == jnp.minimum(count - 1 - own + 2, count - 1))
    def _():
        total = part_ref[own]
        for k in range(1, count):
            there = lax.rem(own + k, count)
            remote(
                part_ref.at[own], partial_ref.at[there], send_rs.at[own], recv_rs.at[there],
                line, there,
            ).wait_recv()
            total = total + partial_ref[there]
        total_ref[own] = total
        for k in range(1, count):
            total_to(k).start()

    @pl.when(index == count - 1)
    def _():
        for k in range(1, count):
            there = lax.rem(own + k, count)
            remote(
                total_ref.at[there], total_ref.at[there], send_ag.at[k], recv_ag.at[there],
                line, there,
            ).wait_recv()
        grad_selected_ref[...] = total_ref[...]
        all_out_ref[...] = all_ref[...]
        for k in range(1, half):
            along(k).wait_send()
        for i in range(half):
            across(2 * i + low).wait_send()
        for k in range(1, count):
            partial_to(lax.rem(own + k, count)).wait_send()
            total_to(k).wait_send()


def scan_backward(count, cuts, grad_low, act, gate, mixed, pre, selected, small, weights, priors, end):
    length, inner = act.shape
    state = cuts.state
    block = length // count
    width = grad_low.shape[1]
    half = count // 2

    def back(t):
        return count - 1 - t

    rows = pl.BlockSpec((block, inner), lambda t: (back(t), 0))
    whole = pl.BlockSpec((state, inner), lambda t: (0, 0))
    dma = pltpu.SemaphoreType.DMA
    picked = (count, cuts.picks, block)
    return pl.pallas_call(
        functools.partial(scan_backward_kernel, count, cuts),
        grid=(count,),
        in_specs=[
            pl.BlockSpec((block, width), lambda t: (0, 0)),
            rows,
            rows,
            rows,
            rows,
            pl.BlockSpec((1, cuts.picks, block), lambda t: (back(t), 0, 0)),
            pl.BlockSpec(small.shape, lambda t: (0, 0)),
            pl.BlockSpec((inner, width), lambda t: (0, 2)),
            pl.BlockSpec((block, state, inner), lambda t: (back(t), 0, 0)),
            whole,
        ],
        out_specs=[
            rows,
            rows,
            pl.BlockSpec((cuts.rank, inner), lambda t: (0, 0)),
            whole,
            pl.BlockSpec((8, inner), lambda t: (0, 0)),
            pl.BlockSpec(picked, lambda t: (0, 0, 0)),
            pl.BlockSpec((count, block, width), lambda t: (0, 0, 0)),
        ],
        out_shape=[
            jax.ShapeDtypeStruct((length, inner), jnp.bfloat16),
            jax.ShapeDtypeStruct((length, inner), jnp.float32),
            jax.ShapeDtypeStruct((cuts.rank, inner), jnp.float32),
            jax.ShapeDtypeStruct((state, inner), jnp.float32),
            jax.ShapeDtypeStruct((8, inner), jnp.float32),
            jax.ShapeDtypeStruct(picked, jnp.float32),
            jax.ShapeDtypeStruct((count, block, width), jnp.bfloat16),
        ],
        scratch_shapes=[
            pltpu.VMEM((state, inner), jnp.float32),
            pltpu.VMEM((state, inner), jnp.float32),
            pltpu.VMEM((block, inner), jnp.float32),
            pltpu.VMEM((block, inner), jnp.float32),
            pltpu.VMEM((block, inner), jnp.float32),
            pltpu.VMEM((count, block, width), jnp.bfloat16),
            pltpu.VMEM(picked, jnp.float32),
            pltpu.VMEM(picked, jnp.float32),
            pltpu.VMEM(picked, jnp.float32),
            dma((half,)), dma((half,)), dma((half,)), dma((half,)),
            dma((count,)), dma((count,)), dma((count,)), dma((count,)),
        ],
        compiler_params=pltpu.CompilerParams(
            collective_id=2, has_side_effects=True, vmem_limit_bytes=VMEM_LIMIT
        ),
        cost_estimate=pl.CostEstimate(
            flops=20 * length * state * inner,
            bytes_accessed=4 * length * inner * (state + 6),
            transcendentals=length * state * inner,
        ),
        name="scan_backward",
    )(grad_low, act, gate, mixed, pre, selected, small, weights, priors, end)


def back_kernel(
    count, cuts, width,
    grad_selected_ref, small_ref, conv_w_ref, gate_w_ref, ext_ref, sum_ref, grad_act_ref, grad_gate_ref,
    summed_ref, grad_conv_ref, grad_select_ref, rows_ref,
    grad_sum_ref, *relay_refs,
):
    relay = Relay(count, *relay_refs)
    length, inner = sum_ref.shape
    rows = length // count
    kernel = cuts.kernel
    greet(count)
    grad_select_ref[...] = jnp.zeros_like(grad_select_ref)
    rows_ref[...] = jnp.zeros_like(rows_ref)
    grad_sum_ref[length:, :] = jnp.zeros((8, inner), jnp.float32)
    select = small_ref[: cuts.picks, :].astype(jnp.bfloat16)

    def first(b, carry):
        start = pl.multiple_of(b * rows, rows)
        grad_selected = grad_selected_ref[b].astype(jnp.bfloat16)
        total = sum_ref[pl.ds(start, rows), :]
        sig = sigmoid(total)
        grad_act = grad_act_ref[pl.ds(start, rows), :] + inner_rows(grad_selected, select)
        grad_sum = grad_act * (sig * (1.0 + total * (1.0 - sig)))
        grad_sum_ref[pl.ds(start, rows), :] = grad_sum
        grad_select_ref[...] += dot_nn(grad_selected, (total * sig).astype(jnp.bfloat16))
        window = ext_ref[pl.ds(start, rows + 8), :]
        for k in range(kernel):
            rows_ref[k : k + 1, :] += jnp.sum(
                grad_sum * window[9 - kernel + k : 9 - kernel + k + rows], axis=0, keepdims=True
            )
        rows_ref[kernel : kernel + 1, :] += jnp.sum(grad_sum, axis=0, keepdims=True)
        return carry

    lax.fori_loop(0, count, first, 0)

    def order(j):
        return j // 2 + lax.rem(j, 2) * (count // 2)

    def second(j, carry):
        b = order(j)
        start = pl.multiple_of(b * rows, rows)
        window = grad_sum_ref[pl.ds(start, rows + 8), :]
        grad_conv = None
        for k in range(kernel):
            tap = small_ref[cuts.taps + k : cuts.taps + k + 1, :]
            term = tap * window[kernel - 1 - k : kernel - 1 - k + rows]
            grad_conv = term if grad_conv is None else grad_conv + term
        grad_conv = grad_conv.astype(jnp.bfloat16)
        grad_conv_ref[pl.ds(start, rows), :] = grad_conv
        relay.part[b] = (
            dot_nn(grad_conv, conv_w_ref[...])
            + dot_nn(grad_gate_ref[pl.ds(start, rows), :], gate_w_ref[...])
        ).astype(jnp.bfloat16)
        relay.made(b)
        return carry

    lax.fori_loop(0, count, second, 0)

    def third(j, carry):
        relay.pass_on(order(j))
        return carry

    lax.fori_loop(0, count, third, 0)
    summed_ref[...] = relay.finish()


def back(count, cuts, width, grad_selected, small, weights, ext, conv_sum, grad_act, grad_gate):
    length, inner = conv_sum.shape
    rows = length // count

    def full(shape):
        return pl.BlockSpec(shape, lambda i: (0,) * len(shape))

    return pl.pallas_call(
        functools.partial(back_kernel, count, cuts, width),
        grid=(1,),
        in_specs=[
            full(grad_selected.shape),
            full(small.shape),
            pl.BlockSpec((inner, width), lambda i: (0, 0)),
            pl.BlockSpec((inner, width), lambda i: (0, 1)),
            full(ext.shape),
            full(conv_sum.shape),
            full(grad_act.shape),
            full(grad_gate.shape),
        ],
        out_specs=[
            full((rows, width)),
            full((length, inner)),
            full((cuts.picks, inner)),
            full((8, inner)),
        ],
        out_shape=[
            jax.ShapeDtypeStruct((rows, width), jnp.float32),
            jax.ShapeDtypeStruct((length, inner), jnp.bfloat16),
            jax.ShapeDtypeStruct((cuts.picks, inner), jnp.float32),
            jax.ShapeDtypeStruct((8, inner), jnp.float32),
        ],
        scratch_shapes=[
            pltpu.VMEM((length + 8, inner), jnp.float32),
            *Relay.scratch(count, rows, width),
        ],
        compiler_params=pltpu.CompilerParams(
            collective_id=3, has_side_effects=True, vmem_limit_bytes=VMEM_LIMIT
        ),
        cost_estimate=pl.CostEstimate(
            flops=4 * length * width * inner,
            bytes_accessed=20 * length * inner,
            transcendentals=length * inner,
        ),
        name="back",
    )(grad_selected, small, weights, weights, ext, conv_sum, grad_act, grad_gate)


def body(
    tokens,
    cotangent,
    routes,
    mixer_gain,
    input_proj,
    conv_weight,
    conv_bias,
    select_proj,
    step_proj,
    step_bias,
    decay_log,
    skip_gain,
    output_proj,
    expert_gain,
    router,
    expert_up,
    expert_down,
):
    rows = tokens.shape[1]
    width = tokens.shape[2]
    shard = input_proj.shape[2]
    rank = step_proj.shape[0]
    state = decay_log.shape[0]
    kernel = conv_weight.shape[0]
    picks = select_proj.shape[0]
    count = lax.axis_size("seq")
    lines = lax.axis_size("dp")
    shard_rows = -(-shard // 16) * 16
    cuts = Cuts(picks, rank, state, kernel)

    x_in = tokens.reshape(rows, width)
    gain_one = mixer_gain.astype(jnp.float32)
    normed = rms_norm(x_in, gain_one).astype(jnp.bfloat16)

    small = jnp.concatenate(
        [
            select_proj,
            step_proj,
            decay_log,
            conv_weight,
            conv_bias[None, :],
            step_bias[None, :],
            skip_gain[None, :],
        ],
        axis=0,
    )
    small_pad = -(-cuts.rows // LANES) * LANES
    small = jnp.pad(small, ((0, small_pad - cuts.rows), (0, 0)))
    packed = jnp.concatenate(
        [input_proj.reshape(2 * width, shard).T, output_proj, small.T], axis=1
    )
    packed = jnp.pad(packed, ((0, shard_rows - shard), (0, 0)))
    w_up, w_down = (
        lax.all_gather(expert_up, "seq", axis=0, tiled=True),
        lax.all_gather(expert_down, "seq", axis=1, tiled=True),
    )
    (normed_all, weights, small_all, conv_ext, conv_sum, conv_act, gate_branch, selected) = front(
        count, lines, cuts, normed, packed
    )
    pre, mixed, mixer_low, priors, end, mixer_out = scan_forward(
        count, cuts, width, conv_act, gate_branch, selected, small_all, weights
    )
    middle = x_in + mixer_out

    experts = router.shape[0]
    copies = lax.axis_size("dp") // experts
    capacity = CAP
    gain_two = expert_gain.astype(jnp.float32)
    normed_two = rms_norm(middle, gain_two).astype(jnp.bfloat16)
    probs = jax.nn.softmax(outer_cols(normed_two, router), axis=-1)
    route = routes.reshape(rows)
    chosen = (route[:, None] == lax.broadcasted_iota(jnp.int32, (rows, experts), 1)).astype(
        jnp.float32
    )
    gate = jnp.sum(chosen * probs, axis=1)
    earlier = (
        lax.broadcasted_iota(jnp.int32, (rows, rows), 0)
        > lax.broadcasted_iota(jnp.int32, (rows, rows), 1)
    ).astype(jnp.float32)
    before = jnp.dot(earlier, chosen, precision=HIGHEST)
    position = jnp.sum(before * chosen, axis=1).astype(jnp.int32)
    slot = route * capacity + position
    dispatch_table = (
        slot[None, :] == lax.broadcasted_iota(jnp.int32, (experts * capacity, rows), 0)
    ).astype(jnp.bfloat16)
    buffer = jnp.dot(dispatch_table, normed_two, preferred_element_type=jnp.float32).astype(
        jnp.bfloat16
    )
    send = jnp.repeat(buffer.reshape(experts, capacity, width), copies, axis=0)
    received = lax.all_to_all(send, "dp", split_axis=0, concat_axis=0, tiled=True)
    sources = received.shape[0]
    expert_rows = received.reshape(-1, width)
    expert_pre = jnp.dot(expert_rows, w_up, preferred_element_type=jnp.float32)
    expert_act, gelu_pull = jax.vjp(gelu_exact, expert_pre)
    act_low = expert_act.astype(jnp.bfloat16)
    partial_out = jnp.dot(act_low, w_down, preferred_element_type=jnp.float32).reshape(
        sources, capacity, width
    )
    returned = lax.all_to_all(
        partial_out.astype(jnp.bfloat16), "dp", split_axis=0, concat_axis=0, tiled=True
    ).astype(partial_out.dtype)
    expert_out = jnp.sum(returned.reshape(experts, copies, capacity, width), axis=1).reshape(
        experts * capacity, width
    )
    picked = jnp.take(expert_out, slot, axis=0)
    output = middle + gate[:, None] * picked
    grad_out = cotangent.reshape(rows, width)
    grad_pick = (gate[:, None] * grad_out).astype(jnp.bfloat16)
    grad_gate = jnp.sum(grad_out * picked, axis=1)
    grad_buffer = jnp.dot(dispatch_table, grad_pick, preferred_element_type=jnp.float32).astype(
        jnp.bfloat16
    )
    grad_send = jnp.repeat(grad_buffer.reshape(experts, capacity, width), copies, axis=0)
    grad_rows = lax.all_to_all(grad_send, "dp", split_axis=0, concat_axis=0, tiled=True)
    grad_flat = grad_rows.reshape(-1, width)
    grad_down_w = inner_rows(act_low, grad_flat)
    grad_act = outer_cols(grad_flat, w_down)
    grad_pre = gelu_pull(grad_act)[0].astype(jnp.bfloat16)
    grad_up_w = inner_rows(expert_rows, grad_pre)
    grad_in_rows = outer_cols(grad_pre, w_up).reshape(sources, capacity, width)
    grad_back = lax.all_to_all(
        grad_in_rows.astype(jnp.bfloat16), "dp", split_axis=0, concat_axis=0, tiled=True
    ).astype(grad_in_rows.dtype)
    grad_slots = jnp.sum(grad_back.reshape(experts, copies, capacity, width), axis=1).reshape(
        experts * capacity, width
    )
    grad_logits = gate[:, None] * (chosen - probs) * grad_gate[:, None]
    router_full = router.astype(jnp.float32)
    grad_normed_two = jnp.take(grad_slots, slot, axis=0) + jnp.dot(
        grad_logits, router_full, precision=HIGHEST
    )
    grad_router = inner_rows(grad_logits, normed_two.astype(jnp.float32), HIGHEST)
    unused_two, pull_two = jax.vjp(rms_norm, middle, gain_two)
    grad_middle_norm, grad_gain_two = pull_two(grad_normed_two)
    grad_middle = grad_out + grad_middle_norm
    grad_middle_low = grad_middle.astype(jnp.bfloat16)

    (grad_gate_branch, grad_act, grad_step_w, rate_total, scan_rows, grad_selected, grad_middle_all) = (
        scan_backward(
            count, cuts, grad_middle_low, conv_act, gate_branch, mixed, pre, selected, small_all,
            weights, priors, end,
        )
    )
    grad_normed, grad_conv_input, grad_select_w, conv_rows = back(
        count, cuts, width, grad_selected, small_all, weights, conv_ext, conv_sum, grad_act,
        grad_gate_branch,
    )
    grad_decay = rate_total * -jnp.exp(small_all[cuts.decay : cuts.decay + state])
    normed_rows = normed_all.reshape(-1, width)
    grad_output_w = inner_rows(mixer_low, grad_middle_all.reshape(-1, width))
    grad_conv_w = inner_rows(grad_conv_input, normed_rows)
    grad_gate_w = inner_rows(grad_gate_branch, normed_rows)
    grad_small = jnp.concatenate(
        [
            grad_select_w,
            grad_step_w,
            grad_decay,
            conv_rows[: kernel + 1],
            scan_rows[:2],
            jnp.zeros((small_pad - cuts.rows, grad_decay.shape[1]), jnp.float32),
        ],
        axis=0,
    )
    grad_packed = jnp.concatenate(
        [part.astype(jnp.bfloat16) for part in (grad_conv_w, grad_gate_w, grad_output_w, grad_small.T)],
        axis=1,
    )
    grad_shard = lax.psum_scatter(
        grad_packed[: lines * shard_rows], "dp", scatter_dimension=0, tiled=True
    )[:shard].astype(jnp.float32)
    grad_input_w = grad_shard[:, : 2 * width].T.reshape(2, width, shard)
    small_shard = grad_shard[:, 3 * width :].T
    cut = 0
    small_grads = []
    for number in (picks, rank, state, kernel, 1, 1, 1):
        small_grads.append(small_shard[cut : cut + number])
        cut += number

    grad_gain_one = (
        jnp.sum(
            weights[:, :width].astype(jnp.float32) * grad_conv_w
            + weights[:, width : 2 * width].astype(jnp.float32) * grad_gate_w,
            axis=0,
        )
        / gain_one
    )
    unused_one, pull_one = jax.vjp(lambda v: rms_norm(v, gain_one), x_in)
    grad_tokens = grad_middle + pull_one(grad_normed)[0]
    expert_grads = (
        lax.psum_scatter(
            grad_up_w.astype(jnp.bfloat16), "seq", scatter_dimension=0, tiled=True
        ).astype(jnp.float32),
        lax.psum_scatter(
            grad_down_w.astype(jnp.bfloat16), "seq", scatter_dimension=1, tiled=True
        ).astype(jnp.float32),
    )
    small_sums = lax.psum(
        jnp.concatenate([grad_gain_one[None], grad_gain_two[None], grad_router], axis=0),
        ("dp", "seq"),
    )
    return (
        output.reshape(tokens.shape),
        grad_tokens.reshape(tokens.shape),
        small_sums[0],
        grad_input_w,
        small_grads[3],
        small_grads[4].reshape(shard),
        small_grads[0],
        small_grads[1],
        small_grads[5].reshape(shard),
        small_grads[2],
        small_grads[6].reshape(shard),
        grad_shard[:, 2 * width : 3 * width],
        small_sums[1],
        small_sums[2:],
        expert_grads[0],
        expert_grads[1],
    )


def solution(mesh):
    both = ("dp", "seq")
    placed = (
        P("dp", "seq", None),
        P("dp", "seq", None),
        P("dp", "seq", None),
        P(),
        P(None, None, both),
        P(None, both),
        P(both),
        P(None, both),
        P(None, both),
        P(both),
        P(None, both),
        P(both),
        P(both, None),
        P(),
        P(),
        P("seq", "dp"),
        P("dp", "seq"),
    )
    return jax.shard_map(
        body,
        mesh=mesh,
        in_specs=placed,
        out_specs=(
            P("dp", "seq", None),
            P("dp", "seq", None),
            P(),
            P(None, None, both),
            P(None, both),
            P(both),
            P(None, both),
            P(None, both),
            P(both),
            P(None, both),
            P(both),
            P(both, None),
            P(),
            P(),
            P("seq", "dp"),
            P("dp", "seq"),
        ),
        check_vma=False,
    )
```

```python
import functools
import math

import jax
import jax.numpy as jnp
from jax import lax
from jax.experimental import pallas as pl
from jax.experimental.pallas import tpu as pltpu
from jax.sharding import PartitionSpec as P

CAP = 56
LANES = 128
TIME_BLOCK = 128
LOG2E = math.log2(math.e)

HIGHEST = lax.Precision.HIGHEST


def rms_norm(values, gain):
    return values * lax.rsqrt(jnp.mean(values * values, axis=-1, keepdims=True) + 1e-05) * gain


def gelu_exact(values):
    return jax.nn.gelu(values, approximate=False)


def inner_rows(left, right, precision=None):
    return lax.dot_general(
        left,
        right,
        (((0,), (0,)), ((), ())),
        precision=precision,
        preferred_element_type=jnp.float32,
    )


def outer_cols(left, right, precision=None):
    return lax.dot_general(
        left,
        right,
        (((1,), (1,)), ((), ())),
        precision=precision,
        preferred_element_type=jnp.float32,
    )


def sublane_sums(parts):
    row = lax.broadcasted_iota(jnp.int32, parts[0].shape, 0)
    low4 = row < 4
    low2 = (row % 4) < 2
    low1 = (row % 2) < 1
    quads = []
    for k in range(4):
        a, b = parts[k], parts[k + 4]
        quads.append(jnp.where(low4, a, b) + pltpu.roll(jnp.where(low4, b, a), 4, 0))
    pairs = []
    for k in range(2):
        a, b = quads[k], quads[k + 2]
        pairs.append(
            jnp.where(low2, a, b) + jnp.where(low2, pltpu.roll(a, 6, 0), pltpu.roll(b, 2, 0))
        )
    a, b = pairs
    return jnp.where(low1, a, b) + jnp.where(low1, pltpu.roll(a, 7, 0), pltpu.roll(b, 1, 0))


def lane_column(block, k):
    return jnp.broadcast_to(block[:, k : k + 1], block.shape)


MESH = pl.DeviceIdType.MESH
VMEM_LIMIT = 56 * 1024 * 1024


def dot_nn(left, right, precision=None):
    return lax.dot_general(
        left, right, (((1,), (0,)), ((), ())), precision=precision,
        preferred_element_type=jnp.float32,
    )


def place():
    own, line = lax.axis_index("seq"), lax.axis_index("dp")
    return line, own, own // 2, lax.rem(own, 2)


def remote(source, target, send_sem, recv_sem, line, position):
    return pltpu.make_async_remote_copy(
        src_ref=source,
        dst_ref=target,
        send_sem=send_sem,
        recv_sem=recv_sem,
        device_id=(line, position),
        device_id_type=MESH,
    )


def greet(count, lines=1):
    line, own, _, _ = place()
    barrier = pltpu.get_barrier_semaphore()
    for k in range(1, count):
        pl.semaphore_signal(
            barrier, inc=1, device_id=(line, lax.rem(own + k, count)), device_id_type=MESH
        )
    for k in range(1, lines):
        pl.semaphore_signal(
            barrier, inc=1, device_id=(lax.rem(line + k, lines), own), device_id_type=MESH
        )
    pl.semaphore_wait(barrier, count - 1 + lines - 1)


def sigmoid(values):
    return 1.0 / (1.0 + jnp.exp(-values))


def softplus(values):
    return jnp.maximum(values, 0.0) + jnp.log1p(jnp.exp(-jnp.abs(values)))


class Cuts:
    def __init__(self, picks, rank, state, kernel):
        self.picks, self.rank, self.state, self.kernel = picks, rank, state, kernel
        self.step = picks
        self.decay = self.step + rank
        self.taps = self.decay + state
        self.conv_bias = self.taps + kernel
        self.step_bias = self.conv_bias + 1
        self.skip = self.step_bias + 1
        self.rows = self.skip + 1


def front_kernel(
    count, lines, cuts,
    normed_ref, packed_ref,
    all_ref, weights_ref, small_ref, ext_ref, sum_ref, act_ref, gate_ref, selected_ref,
    part_ref, partial_ref,
    send_w, recv_w, send_hi, recv_hi, send_x, recv_x, send_rs, recv_rs, send_ag, recv_ag,
):
    line, own, high, low = place()
    half = count // 2
    rows, width = normed_ref.shape
    shard = packed_ref.shape[0]
    inner = weights_ref.shape[0]
    kernel = cuts.kernel
    partner = 2 * high + 1 - low
    greet(count, lines)

    copies = []
    shard_rows = pl.ds(pl.multiple_of(line * shard, 16), shard)
    for k in range(1, half):
        copy = remote(
            normed_ref, all_ref.at[own], send_hi.at[k], recv_hi.at[k],
            line, 2 * lax.rem(high + k, half) + low,
        )
        copy.start()
        copies.append(copy)
    copy = remote(normed_ref, all_ref.at[own], send_x.at[0], recv_x.at[0], line, partner)
    copy.start()
    copies.append(copy)
    for k in range(1, lines):
        copy = remote(
            packed_ref, weights_ref.at[shard_rows], send_w.at[k], recv_w.at[k],
            lax.rem(line + k, lines), own,
        )
        copy.start()
        copies.append(copy)
    all_ref[own] = normed_ref[...]
    weights_ref[shard_rows, :] = packed_ref[...]
    if lines * shard < inner:
        weights_ref[lines * shard :, :] = jnp.zeros(
            (inner - lines * shard, weights_ref.shape[1]), weights_ref.dtype
        )
    ext_ref[0:8, :] = jnp.zeros((8, inner), jnp.float32)
    for k in range(1, half):
        block = 2 * lax.rem(high - k + half, half) + low
        remote(
            normed_ref, all_ref.at[block], send_hi.at[k], recv_hi.at[k], line, partner
        ).wait_recv()
        copy = remote(
            all_ref.at[block], all_ref.at[block], send_x.at[k], recv_x.at[k], line, partner
        )
        copy.start()
        copies.append(copy)
    for k in range(1, lines):
        from_line = lax.rem(line - k + lines, lines)
        there = pl.ds(pl.multiple_of(from_line * shard, 16), shard)
        remote(
            packed_ref, weights_ref.at[there], send_w.at[k], recv_w.at[k], from_line, own
        ).wait_recv()
    small_ref[...] = weights_ref[:, 3 * width :].astype(jnp.float32).T
    for k in range(half):
        block = 2 * lax.rem(high - k + half, half) + 1 - low
        remote(
            normed_ref, all_ref.at[block], send_x.at[k], recv_x.at[k], line, partner
        ).wait_recv()

    def project(b, carry):
        start = pl.multiple_of(b * rows, rows)
        block = all_ref[b]
        ext_ref[pl.ds(pl.multiple_of(start + 8, 8), rows), :] = outer_cols(
            block, weights_ref[:, :width]
        )
        gate_ref[pl.ds(start, rows), :] = outer_cols(block, weights_ref[:, width : 2 * width])
        return carry

    lax.fori_loop(0, count, project, 0)

    def convolve(b, carry):
        start = pl.multiple_of(b * rows, rows)
        window = ext_ref[pl.ds(start, rows + 8), :]
        total = small_ref[cuts.conv_bias : cuts.conv_bias + 1, :]
        for k in range(kernel):
            tap = small_ref[cuts.taps + k : cuts.taps + k + 1, :]
            total = total + tap * window[9 - kernel + k : 9 - kernel + k + rows]
        act = total * sigmoid(total)
        sum_ref[pl.ds(start, rows), :] = total
        act_ref[pl.ds(start, rows), :] = act
        part_ref[b] = outer_cols(
            small_ref[: cuts.picks, :].astype(jnp.bfloat16), act.astype(jnp.bfloat16)
        )
        return carry

    lax.fori_loop(0, count, convolve, 0)

    for k in range(1, count):
        there = lax.rem(own + k, count)
        copy = remote(
            part_ref.at[there], partial_ref.at[k], send_rs.at[k], recv_rs.at[k], line, there
        )
        copy.start()
        copies.append(copy)
    total = part_ref[own]
    for k in range(1, count):
        remote(
            part_ref.at[own], partial_ref.at[k], send_rs.at[k], recv_rs.at[k], line, partner
        ).wait_recv()
        total = total + partial_ref[k]
    selected_ref[own] = total
    for k in range(1, count):
        copy = remote(
            selected_ref.at[own], selected_ref.at[own], send_ag.at[k], recv_ag.at[k],
            line, lax.rem(own + k, count),
        )
        copy.start()
        copies.append(copy)
    for k in range(1, count):
        block = lax.rem(own - k + count, count)
        remote(
            selected_ref.at[block], selected_ref.at[block], send_ag.at[k], recv_ag.at[k],
            line, partner,
        ).wait_recv()
    for copy in copies:
        copy.wait_send()


def front(count, lines, cuts, normed, packed):
    rows, width = normed.shape
    shard, columns = packed.shape
    inner = -(-lines * shard // LANES) * LANES
    length = count * rows
    half = count // 2
    small = columns - 3 * width
    vmem = pl.BlockSpec(memory_space=pltpu.VMEM)

    def f32(*shape):
        return jax.ShapeDtypeStruct(shape, jnp.float32)

    dma = pltpu.SemaphoreType.DMA
    return pl.pallas_call(
        functools.partial(front_kernel, count, lines, cuts),
        in_specs=[vmem] * 2,
        out_specs=[vmem] * 8,
        out_shape=[
            jax.ShapeDtypeStruct((count, rows, width), jnp.bfloat16),
            jax.ShapeDtypeStruct((inner, columns), jnp.bfloat16),
            f32(small, inner),
            f32(length + 8, inner),
            f32(length, inner),
            f32(length, inner),
            f32(length, inner),
            f32(count, cuts.picks, rows),
        ],
        scratch_shapes=[
            pltpu.VMEM((count, cuts.picks, rows), jnp.float32),
            pltpu.VMEM((count, cuts.picks, rows), jnp.float32),
            dma((lines,)), dma((lines,)), dma((half,)), dma((half,)), dma((half,)), dma((half,)),
            dma((count,)), dma((count,)), dma((count,)), dma((count,)),
        ],
        compiler_params=pltpu.CompilerParams(
            collective_id=0, has_side_effects=True, vmem_limit_bytes=VMEM_LIMIT
        ),
        cost_estimate=pl.CostEstimate(
            flops=4 * length * width * inner,
            bytes_accessed=20 * length * inner,
            transcendentals=length * inner,
        ),
        name="front",
    )(normed, packed)


class Relay:
    def __init__(self, axis, count, part, across, along, send_x, recv_x, send_hi, recv_hi):
        self.axis = axis
        self.own = lax.axis_index(axis)
        self.other = lax.axis_index("dp" if axis == "seq" else "seq")
        self.high, self.low = self.own // 2, lax.rem(self.own, 2)
        self.half = count // 2
        self.part, self.across, self.along = part, across, along
        self.send_x, self.recv_x, self.send_hi, self.recv_hi = send_x, recv_x, send_hi, recv_hi
        self.partner = 2 * self.high + 1 - self.low

    def remote(self, source, target, send_sem, recv_sem, position):
        if self.axis == "seq":
            return remote(source, target, send_sem, recv_sem, self.other, position)
        return remote(source, target, send_sem, recv_sem, position, self.other)

    def over(self, block):
        i = block // 2
        return self.remote(
            self.part.at[block], self.across.at[i], self.send_x.at[i], self.recv_x.at[i],
            self.partner,
        )

    def on(self, block):
        i = block // 2
        k = lax.rem(i - self.high + self.half, self.half)
        return self.remote(
            self.part.at[block], self.along.at[k], self.send_hi.at[k], self.recv_hi.at[k],
            2 * i + self.low,
        )

    def made(self, block):
        @pl.when(lax.rem(block, 2) != self.low)
        def _():
            self.over(block).start()

    def pass_on(self, block):
        @pl.when((lax.rem(block, 2) == self.low) & (block // 2 != self.high))
        def _():
            self.over(block).wait_recv()
            both = self.part[block].astype(jnp.float32) + self.across[block // 2].astype(
                jnp.float32
            )
            self.part[block] = both.astype(jnp.bfloat16)
            self.on(block).start()

    def finish(self):
        self.over(self.own).wait_recv()
        total = self.part[self.own].astype(jnp.float32) + self.across[self.high].astype(
            jnp.float32
        )
        for k in range(1, self.half):
            block = 2 * lax.rem(self.high + k, self.half) + self.low
            self.on(block).wait_recv()
            total = total + self.along[k].astype(jnp.float32)
        for i in range(self.half):
            self.over(2 * i + 1 - self.low).wait_send()
        for k in range(1, self.half):
            self.on(2 * lax.rem(self.high + k, self.half) + self.low).wait_send()
        return total

    @staticmethod
    def scratch(count, rows, width):
        half = count // 2
        dma = pltpu.SemaphoreType.DMA
        return [
            pltpu.VMEM((count, rows, width), jnp.bfloat16),
            pltpu.VMEM((half, rows, width), jnp.bfloat16),
            pltpu.VMEM((half, rows, width), jnp.bfloat16),
            dma((half,)), dma((half,)), dma((half,)), dma((half,)),
        ]


def scan_forward_kernel(
    count, cuts,
    act_ref, gate_ref, selected_ref, small_ref, output_ref,
    pre_ref, mixed_ref, mixer_low_ref, prior_ref, end_ref, summed_ref,
    state_ref, delta_ref, scanned_ref, *relay_refs,
):
    steps, inner = act_ref.shape
    tiles = inner // LANES
    state = cuts.state
    halves = state // 8
    step = pl.program_id(0)
    relay = Relay("seq", count, *relay_refs)

    @pl.when(step == 0)
    def _():
        greet(count)
        state_ref[...] = jnp.zeros_like(state_ref)

    rates2 = -LOG2E * jnp.exp(small_ref[cuts.decay : cuts.decay + state, :])
    pre = inner_rows(
        selected_ref[0, : cuts.rank, :],
        small_ref[cuts.step : cuts.step + cuts.rank, :],
        HIGHEST,
    ) + small_ref[cuts.step_bias : cuts.step_bias + 1, :]
    pre_ref[...] = pre
    delta_ref[...] = softplus(pre)
    in_rows = cuts.rank
    out_rows = cuts.rank + state

    def group(g, states):
        states = [list(s) for s in states]
        base = pl.multiple_of(g * 8, 8)
        shift = lax.rem(steps - base, steps)
        b_cols = [
            pltpu.roll(selected_ref[0, in_rows + 8 * i : in_rows + 8 * i + 8, :], shift, 1)
            for i in range(halves)
        ]
        c_cols = [
            pltpu.roll(selected_ref[0, out_rows + 8 * i : out_rows + 8 * i + 8, :], shift, 1)
            for i in range(halves)
        ]
        d8 = delta_ref[pl.ds(base, 8), :]
        du8 = d8 * act_ref[pl.ds(base, 8), :]
        parts = [[None] * 8 for _ in range(tiles)]
        for k in range(8):
            b_now = [lane_column(b, k) for b in b_cols]
            c_now = [lane_column(c, k) for c in c_cols]
            for j in range(tiles):
                cols = slice(j * LANES, (j + 1) * LANES)
                d = jnp.broadcast_to(d8[k : k + 1, cols], (8, LANES))
                du = jnp.broadcast_to(du8[k : k + 1, cols], (8, LANES))
                total = None
                for i in range(halves):
                    old = states[j][i]
                    prior_ref[base + k, 8 * i : 8 * i + 8, cols] = old
                    new = jnp.exp2(d * rates2[8 * i : 8 * i + 8, cols]) * old + b_now[i] * du
                    states[j][i] = new
                    term = c_now[i] * new
                    total = term if total is None else total + term
                parts[j][k] = total
        for j in range(tiles):
            scanned_ref[pl.ds(base, 8), j * LANES : (j + 1) * LANES] = sublane_sums(parts[j])
        return tuple(tuple(s) for s in states)

    first = tuple(
        tuple(
            state_ref[8 * i : 8 * i + 8, j * LANES : (j + 1) * LANES] for i in range(halves)
        )
        for j in range(tiles)
    )
    last = lax.fori_loop(0, steps // 8, group, first)
    for j in range(tiles):
        for i in range(halves):
            state_ref[8 * i : 8 * i + 8, j * LANES : (j + 1) * LANES] = last[j][i]
    end_ref[...] = state_ref[...]

    mixed = scanned_ref[...] + small_ref[cuts.skip : cuts.skip + 1, :] * act_ref[...]
    gate = gate_ref[...]
    low = (mixed * (gate * sigmoid(gate))).astype(jnp.bfloat16)
    mixed_ref[...] = mixed
    mixer_low_ref[...] = low
    relay.part[step] = dot_nn(low, output_ref[...]).astype(jnp.bfloat16)
    relay.made(step)

    @pl.when(step >= 2)
    def _():
        relay.pass_on(step - 2)

    @pl.when(step == count - 1)
    def _():
        relay.pass_on(step - 1)
        relay.pass_on(step)
        summed_ref[...] = relay.finish()


def scan_forward(count, cuts, width, act, gate, selected, small, weights):
    length, inner = act.shape
    state = cuts.state
    block = length // count
    rows = pl.BlockSpec((block, inner), lambda t: (t, 0))
    whole = pl.BlockSpec((state, inner), lambda t: (0, 0))
    return pl.pallas_call(
        functools.partial(scan_forward_kernel, count, cuts),
        grid=(count,),
        in_specs=[
            rows,
            rows,
            pl.BlockSpec((1, cuts.picks, block), lambda t: (t, 0, 0)),
            pl.BlockSpec(small.shape, lambda t: (0, 0)),
            pl.BlockSpec((inner, width), lambda t: (0, 2)),
        ],
        out_specs=[
            rows,
            rows,
            rows,
            pl.BlockSpec((block, state, inner), lambda t: (t, 0, 0)),
            whole,
            pl.BlockSpec((block, width), lambda t: (0, 0)),
        ],
        out_shape=[
            jax.ShapeDtypeStruct((length, inner), jnp.float32),
            jax.ShapeDtypeStruct((length, inner), jnp.float32),
            jax.ShapeDtypeStruct((length, inner), jnp.bfloat16),
            jax.ShapeDtypeStruct((length, state, inner), jnp.float32),
            jax.ShapeDtypeStruct((state, inner), jnp.float32),
            jax.ShapeDtypeStruct((block, width), jnp.float32),
        ],
        scratch_shapes=[
            pltpu.VMEM((state, inner), jnp.float32),
            pltpu.VMEM((block, inner), jnp.float32),
            pltpu.VMEM((block, inner), jnp.float32),
            *Relay.scratch(count, block, width),
        ],
        compiler_params=pltpu.CompilerParams(
            collective_id=1, has_side_effects=True, vmem_limit_bytes=VMEM_LIMIT
        ),
        cost_estimate=pl.CostEstimate(
            flops=8 * length * state * inner,
            bytes_accessed=4 * length * inner * (state + 6),
            transcendentals=length * state * inner,
        ),
        name="scan_forward",
    )(act, gate, selected, small, weights)


def scan_backward_kernel(
    count, cuts,
    own_ref, act_ref, gate_ref, mixed_ref, pre_ref, selected_ref, small_ref, output_ref,
    prior_ref, end_ref,
    grad_gate_ref, grad_act_ref, grad_step_ref, rate_total_ref, rows_ref, grad_selected_ref,
    all_out_ref,
    incoming_ref, post_ref, delta_ref, grad_ref, grad_delta_ref, all_ref,
    part_ref, partial_ref, total_ref,
    send_hi, recv_hi, send_x, recv_x, send_rs, recv_rs, send_ag, recv_ag,
):
    steps, inner = act_ref.shape
    tiles = inner // LANES
    state = cuts.state
    halves = state // 8
    lane = lax.broadcasted_iota(jnp.int32, (8, steps), 1)
    line, own, high, low = place()
    half = count // 2
    partner = 2 * high + 1 - low
    index = pl.program_id(0)
    now = count - 1 - index

    def along(k):
        return remote(
            own_ref, all_ref.at[own], send_hi.at[k], recv_hi.at[high], line,
            2 * lax.rem(high + k, half) + low,
        )

    def across(block):
        i = block // 2
        return remote(
            all_ref.at[block], all_ref.at[block], send_x.at[i], recv_x.at[i], line, partner
        )

    def came_along(block):
        i = block // 2
        return remote(
            all_ref.at[block], all_ref.at[block], send_hi.at[0], recv_hi.at[i], line, partner
        )

    def hand_over(block):
        @pl.when((lax.rem(block, 2) == low) & (block // 2 != high))
        def _():
            came_along(block).wait_recv()
            across(block).start()

    @pl.when(index == 0)
    def _():
        greet(count)
        all_ref[own] = own_ref[...]
        incoming_ref[...] = jnp.zeros_like(incoming_ref)
        post_ref[...] = end_ref[...]
        rate_total_ref[...] = jnp.zeros_like(rate_total_ref)
        grad_step_ref[...] = jnp.zeros_like(grad_step_ref)
        rows_ref[...] = jnp.zeros_like(rows_ref)

    @pl.when(index == jnp.maximum(count - 3 - own, 0))
    def _():
        for k in range(1, half):
            along(k).start()
        across(own).start()

    @pl.when(index == 0)
    def _():
        hand_over(now)
        hand_over(now - 1)

    @pl.when(lax.rem(now, 2) != low)
    def _():
        across(now).wait_recv()

    gate = gate_ref[...]
    gate_sig = sigmoid(gate)
    grad_y = outer_cols(all_ref[now], output_ref[...])
    grad_gate_ref[...] = (
        grad_y * mixed_ref[...] * (gate_sig * (1.0 + gate * (1.0 - gate_sig)))
    ).astype(jnp.bfloat16)
    grad_mixed = grad_y * (gate * gate_sig)
    grad_ref[...] = grad_mixed
    delta_ref[...] = softplus(pre_ref[...])
    rows_ref[1:2, :] += jnp.sum(grad_mixed * act_ref[...], axis=0, keepdims=True)
    rates2 = -LOG2E * jnp.exp(small_ref[cuts.decay : cuts.decay + state, :])
    in_rows = cuts.rank
    out_rows = cuts.rank + state

    def tile_of(ref):
        return tuple(
            tuple(ref[8 * i : 8 * i + 8, j * LANES : (j + 1) * LANES] for i in range(halves))
            for j in range(tiles)
        )

    def group(turn, carry):
        incoming, posts, rate_total, in_acc, out_acc = carry
        incoming = [list(s) for s in incoming]
        posts = [list(s) for s in posts]
        rate_total = [list(s) for s in rate_total]
        in_acc, out_acc = list(in_acc), list(out_acc)
        base = pl.multiple_of((steps // 8 - 1 - turn) * 8, 8)
        shift = lax.rem(steps - base, steps)
        b_cols = [
            pltpu.roll(selected_ref[0, in_rows + 8 * i : in_rows + 8 * i + 8, :], shift, 1)
            for i in range(halves)
        ]
        c_cols = [
            pltpu.roll(selected_ref[0, out_rows + 8 * i : out_rows + 8 * i + 8, :], shift, 1)
            for i in range(halves)
        ]
        d8 = delta_ref[pl.ds(base, 8), :]
        u8 = act_ref[pl.ds(base, 8), :]
        du8 = d8 * u8
        g8 = grad_ref[pl.ds(base, 8), :]
        rate_parts = [[None] * 8 for _ in range(tiles)]
        side_parts = [[None] * 8 for _ in range(tiles)]
        for k in range(7, -1, -1):
            b_now = [lane_column(b, k) for b in b_cols]
            c_now = [lane_column(c, k) for c in c_cols]
            in_sum = [None] * halves
            out_sum = [None] * halves
            for j in range(tiles):
                cols = slice(j * LANES, (j + 1) * LANES)
                d = jnp.broadcast_to(d8[k : k + 1, cols], (8, LANES))
                du = jnp.broadcast_to(du8[k : k + 1, cols], (8, LANES))
                gm = jnp.broadcast_to(g8[k : k + 1, cols], (8, LANES))
                rate_part = None
                side_part = None
                for i in range(halves):
                    prior = prior_ref[base + k, 8 * i : 8 * i + 8, cols]
                    rates = rates2[8 * i : 8 * i + 8, cols]
                    grad_state = c_now[i] * gm + incoming[j][i]
                    passed = jnp.exp2(d * rates) * grad_state
                    incoming[j][i] = passed
                    weighted = passed * prior
                    term = weighted * rates
                    rate_part = term if rate_part is None else rate_part + term
                    term = grad_state * b_now[i]
                    side_part = term if side_part is None else side_part + term
                    term = grad_state * du
                    in_sum[i] = term if in_sum[i] is None else in_sum[i] + term
                    term = posts[j][i] * gm
                    out_sum[i] = term if out_sum[i] is None else out_sum[i] + term
                    rate_total[j][i] = rate_total[j][i] + weighted * d
                    posts[j][i] = prior
                rate_parts[j][k] = rate_part
                side_parts[j][k] = side_part
            here = lane == base + k
            for i in range(halves):
                in_acc[i] = jnp.where(here, jnp.sum(in_sum[i], axis=1, keepdims=True), in_acc[i])
                out_acc[i] = jnp.where(here, jnp.sum(out_sum[i], axis=1, keepdims=True), out_acc[i])
        for j in range(tiles):
            cols = slice(j * LANES, (j + 1) * LANES)
            side = sublane_sums(side_parts[j])
            grad_delta_ref[pl.ds(base, 8), cols] = (
                sublane_sums(rate_parts[j]) * (1.0 / LOG2E) + u8[:, cols] * side
            )
            grad_act_ref[pl.ds(base, 8), cols] = d8[:, cols] * side
        return (
            tuple(tuple(s) for s in incoming),
            tuple(tuple(s) for s in posts),
            tuple(tuple(s) for s in rate_total),
            tuple(in_acc),
            tuple(out_acc),
        )

    empty = tuple(jnp.zeros((8, steps), jnp.float32) for _ in range(halves))
    incoming, posts, rate_total, in_acc, out_acc = lax.fori_loop(
        0,
        steps // 8,
        group,
        (tile_of(incoming_ref), tile_of(post_ref), tile_of(rate_total_ref), empty, empty),
    )
    for i in range(halves):
        part_ref[now, in_rows + 8 * i : in_rows + 8 * i + 8, :] = in_acc[i]
        part_ref[now, out_rows + 8 * i : out_rows + 8 * i + 8, :] = out_acc[i]
        for j in range(tiles):
            cols = slice(j * LANES, (j + 1) * LANES)
            incoming_ref[8 * i : 8 * i + 8, cols] = incoming[j][i]
            post_ref[8 * i : 8 * i + 8, cols] = posts[j][i]
            rate_total_ref[8 * i : 8 * i + 8, cols] = rate_total[j][i]

    grad_act_ref[...] += grad_ref[...] * small_ref[cuts.skip : cuts.skip + 1, :]
    grad_pre = grad_delta_ref[...] * sigmoid(pre_ref[...])
    rows_ref[0:1, :] += jnp.sum(grad_pre, axis=0, keepdims=True)
    grad_step_ref[...] += dot_nn(selected_ref[0, : cuts.rank, :], grad_pre, HIGHEST)
    part_ref[now, : cuts.rank, :] = outer_cols(
        small_ref[cuts.step : cuts.step + cuts.rank, :], grad_pre, HIGHEST
    )

    def partial_to(block):
        return remote(
            part_ref.at[block], partial_ref.at[own], send_rs.at[block], recv_rs.at[own], line, block
        )

    @pl.when(now != own)
    def _():
        partial_to(now).start()

    def total_to(k):
        return remote(
            total_ref.at[own], total_ref.at[own], send_ag.at[k], recv_ag.at[own], line,
            lax.rem(own + k, count),
        )

    @pl.when(now >= 2)
    def _():
        hand_over(now - 2)

    @pl.when(index == jnp.minimum(count - 1 - own + 2, count - 1))
    def _():
        total = part_ref[own]
        for k in range(1, count):
            there = lax.rem(own + k, count)
            remote(
                part_ref.at[own], partial_ref.at[there], send_rs.at[own], recv_rs.at[there],
                line, there,
            ).wait_recv()
            total = total + partial_ref[there]
        total_ref[own] = total
        for k in range(1, count):
            total_to(k).start()

    @pl.when(index == count - 1)
    def _():
        for k in range(1, count):
            there = lax.rem(own + k, count)
            remote(
                total_ref.at[there], total_ref.at[there], send_ag.at[k], recv_ag.at[there],
                line, there,
            ).wait_recv()
        grad_selected_ref[...] = total_ref[...]
        all_out_ref[...] = all_ref[...]
        for k in range(1, half):
            along(k).wait_send()
        for i in range(half):
            across(2 * i + low).wait_send()
        for k in range(1, count):
            partial_to(lax.rem(own + k, count)).wait_send()
            total_to(k).wait_send()


def scan_backward(count, cuts, grad_low, act, gate, mixed, pre, selected, small, weights, priors, end):
    length, inner = act.shape
    state = cuts.state
    block = length // count
    width = grad_low.shape[1]
    half = count // 2

    def back(t):
        return count - 1 - t

    rows = pl.BlockSpec((block, inner), lambda t: (back(t), 0))
    whole = pl.BlockSpec((state, inner), lambda t: (0, 0))
    dma = pltpu.SemaphoreType.DMA
    picked = (count, cuts.picks, block)
    return pl.pallas_call(
        functools.partial(scan_backward_kernel, count, cuts),
        grid=(count,),
        in_specs=[
            pl.BlockSpec((block, width), lambda t: (0, 0)),
            rows,
            rows,
            rows,
            rows,
            pl.BlockSpec((1, cuts.picks, block), lambda t: (back(t), 0, 0)),
            pl.BlockSpec(small.shape, lambda t: (0, 0)),
            pl.BlockSpec((inner, width), lambda t: (0, 2)),
            pl.BlockSpec((block, state, inner), lambda t: (back(t), 0, 0)),
            whole,
        ],
        out_specs=[
            rows,
            rows,
            pl.BlockSpec((cuts.rank, inner), lambda t: (0, 0)),
            whole,
            pl.BlockSpec((8, inner), lambda t: (0, 0)),
            pl.BlockSpec(picked, lambda t: (0, 0, 0)),
            pl.BlockSpec((count, block, width), lambda t: (0, 0, 0)),
        ],
        out_shape=[
            jax.ShapeDtypeStruct((length, inner), jnp.bfloat16),
            jax.ShapeDtypeStruct((length, inner), jnp.float32),
            jax.ShapeDtypeStruct((cuts.rank, inner), jnp.float32),
            jax.ShapeDtypeStruct((state, inner), jnp.float32),
            jax.ShapeDtypeStruct((8, inner), jnp.float32),
            jax.ShapeDtypeStruct(picked, jnp.float32),
            jax.ShapeDtypeStruct((count, block, width), jnp.bfloat16),
        ],
        scratch_shapes=[
            pltpu.VMEM((state, inner), jnp.float32),
            pltpu.VMEM((state, inner), jnp.float32),
            pltpu.VMEM((block, inner), jnp.float32),
            pltpu.VMEM((block, inner), jnp.float32),
            pltpu.VMEM((block, inner), jnp.float32),
            pltpu.VMEM((count, block, width), jnp.bfloat16),
            pltpu.VMEM(picked, jnp.float32),
            pltpu.VMEM(picked, jnp.float32),
            pltpu.VMEM(picked, jnp.float32),
            dma((half,)), dma((half,)), dma((half,)), dma((half,)),
            dma((count,)), dma((count,)), dma((count,)), dma((count,)),
        ],
        compiler_params=pltpu.CompilerParams(
            collective_id=2, has_side_effects=True, vmem_limit_bytes=VMEM_LIMIT
        ),
        cost_estimate=pl.CostEstimate(
            flops=20 * length * state * inner,
            bytes_accessed=4 * length * inner * (state + 6),
            transcendentals=length * state * inner,
        ),
        name="scan_backward",
    )(grad_low, act, gate, mixed, pre, selected, small, weights, priors, end)


def back_kernel(
    count, lines, cuts,
    grad_selected_ref, small_ref, weights_ref, ext_ref, sum_ref, grad_act_ref, grad_gate_ref,
    mixer_low_ref, normed_ref, grad_middle_ref, grad_step_ref, rate_total_ref, scan_rows_ref,
    vectors_ref,
    summed_ref, shard_ref, totals_ref,
    grad_sum_ref, grad_conv_ref, grad_small_ref, ours_ref, theirs_ref,
    send_v, recv_v, send_u, recv_u, *relay_refs,
):
    relay = Relay("seq", count, *relay_refs[:7])
    spread = Relay("dp", lines, *relay_refs[7:])
    line, own, _, _ = place()
    length, inner = sum_ref.shape
    width = normed_ref.shape[1]
    rows = length // count
    kernel = cuts.kernel
    shard = shard_ref.shape[0]
    greet(count, lines)
    grad_small_ref[...] = jnp.zeros_like(grad_small_ref)
    grad_sum_ref[length:, :] = jnp.zeros((8, inner), jnp.float32)
    select = small_ref[: cuts.picks, :].astype(jnp.bfloat16)

    def first(b, carry):
        start = pl.multiple_of(b * rows, rows)
        grad_selected = grad_selected_ref[b].astype(jnp.bfloat16)
        total = sum_ref[pl.ds(start, rows), :]
        sig = sigmoid(total)
        grad_act = grad_act_ref[pl.ds(start, rows), :] + inner_rows(grad_selected, select)
        grad_sum = grad_act * (sig * (1.0 + total * (1.0 - sig)))
        grad_sum_ref[pl.ds(start, rows), :] = grad_sum
        grad_small_ref[: cuts.picks, :] += dot_nn(
            grad_selected, (total * sig).astype(jnp.bfloat16)
        )
        window = ext_ref[pl.ds(start, rows + 8), :]
        for k in range(kernel):
            row = slice(cuts.taps + k, cuts.taps + k + 1)
            grad_small_ref[row, :] += jnp.sum(
                grad_sum * window[9 - kernel + k : 9 - kernel + k + rows], axis=0, keepdims=True
            )
        row = slice(cuts.conv_bias, cuts.conv_bias + 1)
        grad_small_ref[row, :] += jnp.sum(grad_sum, axis=0, keepdims=True)
        return carry

    lax.fori_loop(0, count, first, 0)

    def order(j):
        return j // 2 + lax.rem(j, 2) * (count // 2)

    def second(j, carry):
        b = order(j)
        start = pl.multiple_of(b * rows, rows)
        window = grad_sum_ref[pl.ds(start, rows + 8), :]
        grad_conv = None
        for k in range(kernel):
            tap = small_ref[cuts.taps + k : cuts.taps + k + 1, :]
            term = tap * window[kernel - 1 - k : kernel - 1 - k + rows]
            grad_conv = term if grad_conv is None else grad_conv + term
        grad_conv = grad_conv.astype(jnp.bfloat16)
        grad_conv_ref[pl.ds(start, rows), :] = grad_conv
        relay.part[b] = (
            dot_nn(grad_conv, weights_ref[:, :width])
            + dot_nn(grad_gate_ref[pl.ds(start, rows), :], weights_ref[:, width : 2 * width])
        ).astype(jnp.bfloat16)
        relay.made(b)
        return carry

    lax.fori_loop(0, count, second, 0)

    decay = slice(cuts.decay, cuts.decay + cuts.state)
    grad_small_ref[cuts.step : cuts.step + cuts.rank, :] = grad_step_ref[...]
    grad_small_ref[decay, :] = -rate_total_ref[...] * jnp.exp(small_ref[decay, :])
    grad_small_ref[cuts.step_bias : cuts.step_bias + 2, :] = scan_rows_ref[0:2, :]
    small_t = grad_small_ref[...].T
    for d in range(lines):
        spread.part[d, :, 3 * width :] = small_t[d * shard : (d + 1) * shard].astype(jnp.bfloat16)
    chunk = width // 3
    ours_ref[...] = vectors_ref[...]
    for left_ref, right_ref, place_at in (
        (mixer_low_ref, grad_middle_ref, 2 * width),
        (grad_conv_ref, normed_ref, 0),
        (grad_gate_ref, normed_ref, width),
    ):

        def columns(c, carry, left_ref=left_ref, right_ref=right_ref, place_at=place_at):
            here = pl.ds(pl.multiple_of(c * chunk, chunk), chunk)
            there = pl.ds(pl.multiple_of(place_at + c * chunk, chunk), chunk)
            grad = inner_rows(left_ref[...], right_ref[:, here])
            if place_at < 2 * width:
                ours_ref[0:1, here] += jnp.sum(
                    weights_ref[:, there].astype(jnp.float32) * grad, axis=0, keepdims=True
                )
            low = grad.astype(jnp.bfloat16)
            for d in range(lines):
                spread.part[d, :, there] = low[d * shard : (d + 1) * shard]
            return carry

        lax.fori_loop(0, 3, columns, 0)
        if place_at == 2 * width:
            lax.fori_loop(0, count, lambda j, carry: (relay.pass_on(order(j)), carry)[1], 0)
    for d in range(lines):
        spread.made(d)

    def sum_over(size, axis, send, recv):
        here = own if axis == "seq" else line

        def copy(k, slot):
            there = lax.rem(here + k, size)
            target = (line, there) if axis == "seq" else (there, own)
            return remote(ours_ref, theirs_ref.at[slot], send.at[k], recv.at[k], *target)

        base = 0 if axis == "seq" else count
        for k in range(1, size):
            copy(k, base + k).start()
        total = ours_ref[...]
        for k in range(1, size):
            copy(k, base + k).wait_recv()
            total = total + theirs_ref[base + k]
        for k in range(1, size):
            copy(k, base + k).wait_send()
        return total

    ours_ref[...] = sum_over(count, "seq", send_v, recv_v)
    for d in range(lines):
        spread.pass_on(d)
    totals_ref[...] = sum_over(lines, "dp", send_u, recv_u)
    summed_ref[...] = relay.finish()
    shard_ref[...] = spread.finish()


def back(
    count, lines, shard, cuts, grad_selected, small, weights, ext, conv_sum, grad_act, grad_gate,
    mixer_low, normed, grad_middle, grad_step, rate_total, scan_rows, vectors,
):
    length, inner = conv_sum.shape
    width = normed.shape[1]
    columns = weights.shape[1]
    rows = length // count
    vmem = pl.BlockSpec(memory_space=pltpu.VMEM)
    dma = pltpu.SemaphoreType.DMA
    args = (
        grad_selected, small, weights, ext, conv_sum, grad_act, grad_gate, mixer_low, normed,
        grad_middle, grad_step, rate_total, scan_rows, vectors,
    )
    return pl.pallas_call(
        functools.partial(back_kernel, count, lines, cuts),
        in_specs=[vmem] * len(args),
        out_specs=[vmem] * 3,
        out_shape=[
            jax.ShapeDtypeStruct((rows, width), jnp.float32),
            jax.ShapeDtypeStruct((shard, columns), jnp.float32),
            jax.ShapeDtypeStruct(vectors.shape, jnp.float32),
        ],
        scratch_shapes=[
            pltpu.VMEM((length + 8, inner), jnp.float32),
            pltpu.VMEM((length, inner), jnp.bfloat16),
            pltpu.VMEM(small.shape, jnp.float32),
            pltpu.VMEM(vectors.shape, jnp.float32),
            pltpu.VMEM((count + lines, *vectors.shape), jnp.float32),
            dma((count,)), dma((count,)), dma((lines,)), dma((lines,)),
            *Relay.scratch(count, rows, width),
            *Relay.scratch(lines, shard, columns),
        ],
        compiler_params=pltpu.CompilerParams(
            collective_id=3, has_side_effects=True, vmem_limit_bytes=VMEM_LIMIT
        ),
        cost_estimate=pl.CostEstimate(
            flops=10 * length * width * inner,
            bytes_accessed=30 * length * inner,
            transcendentals=length * inner,
        ),
        name="back",
    )(*args)


def body(
    tokens,
    cotangent,
    routes,
    mixer_gain,
    input_proj,
    conv_weight,
    conv_bias,
    select_proj,
    step_proj,
    step_bias,
    decay_log,
    skip_gain,
    output_proj,
    expert_gain,
    router,
    expert_up,
    expert_down,
):
    rows = tokens.shape[1]
    width = tokens.shape[2]
    shard = input_proj.shape[2]
    rank = step_proj.shape[0]
    state = decay_log.shape[0]
    kernel = conv_weight.shape[0]
    picks = select_proj.shape[0]
    count = lax.axis_size("seq")
    lines = lax.axis_size("dp")
    shard_rows = -(-shard // 16) * 16
    cuts = Cuts(picks, rank, state, kernel)

    x_in = tokens.reshape(rows, width)
    gain_one = mixer_gain.astype(jnp.float32)
    normed = rms_norm(x_in, gain_one).astype(jnp.bfloat16)

    small = jnp.concatenate(
        [
            select_proj,
            step_proj,
            decay_log,
            conv_weight,
            conv_bias[None, :],
            step_bias[None, :],
            skip_gain[None, :],
        ],
        axis=0,
    )
    small_pad = -(-cuts.rows // LANES) * LANES
    small = jnp.pad(small, ((0, small_pad - cuts.rows), (0, 0)))
    packed = jnp.concatenate(
        [input_proj.reshape(2 * width, shard).T, output_proj, small.T], axis=1
    )
    packed = jnp.pad(packed, ((0, shard_rows - shard), (0, 0)))
    w_up, w_down = (
        lax.all_gather(expert_up, "seq", axis=0, tiled=True),
        lax.all_gather(expert_down, "seq", axis=1, tiled=True),
    )
    (normed_all, weights, small_all, conv_ext, conv_sum, conv_act, gate_branch, selected) = front(
        count, lines, cuts, normed, packed
    )
    pre, mixed, mixer_low, priors, end, mixer_out = scan_forward(
        count, cuts, width, conv_act, gate_branch, selected, small_all, weights
    )
    middle = x_in + mixer_out

    experts = router.shape[0]
    copies = lax.axis_size("dp") // experts
    capacity = CAP
    gain_two = expert_gain.astype(jnp.float32)
    normed_two = rms_norm(middle, gain_two).astype(jnp.bfloat16)
    probs = jax.nn.softmax(outer_cols(normed_two, router), axis=-1)
    route = routes.reshape(rows)
    chosen = (route[:, None] == lax.broadcasted_iota(jnp.int32, (rows, experts), 1)).astype(
        jnp.float32
    )
    gate = jnp.sum(chosen * probs, axis=1)
    earlier = (
        lax.broadcasted_iota(jnp.int32, (rows, rows), 0)
        > lax.broadcasted_iota(jnp.int32, (rows, rows), 1)
    ).astype(jnp.float32)
    before = jnp.dot(earlier, chosen, precision=HIGHEST)
    position = jnp.sum(before * chosen, axis=1).astype(jnp.int32)
    slot = route * capacity + position
    dispatch_table = (
        slot[None, :] == lax.broadcasted_iota(jnp.int32, (experts * capacity, rows), 0)
    ).astype(jnp.bfloat16)
    buffer = jnp.dot(dispatch_table, normed_two, preferred_element_type=jnp.float32).astype(
        jnp.bfloat16
    )
    send = jnp.repeat(buffer.reshape(experts, capacity, width), copies, axis=0)
    received = lax.all_to_all(send, "dp", split_axis=0, concat_axis=0, tiled=True)
    sources = received.shape[0]
    expert_rows = received.reshape(-1, width)
    expert_pre = jnp.dot(expert_rows, w_up, preferred_element_type=jnp.float32)
    expert_act, gelu_pull = jax.vjp(gelu_exact, expert_pre)
    act_low = expert_act.astype(jnp.bfloat16)
    partial_out = jnp.dot(act_low, w_down, preferred_element_type=jnp.float32).reshape(
        sources, capacity, width
    )
    returned = lax.all_to_all(
        partial_out.astype(jnp.bfloat16), "dp", split_axis=0, concat_axis=0, tiled=True
    ).astype(partial_out.dtype)
    expert_out = jnp.sum(returned.reshape(experts, copies, capacity, width), axis=1).reshape(
        experts * capacity, width
    )
    picked = jnp.take(expert_out, slot, axis=0)
    output = middle + gate[:, None] * picked
    grad_out = cotangent.reshape(rows, width)
    grad_pick = (gate[:, None] * grad_out).astype(jnp.bfloat16)
    grad_gate = jnp.sum(grad_out * picked, axis=1)
    grad_buffer = jnp.dot(dispatch_table, grad_pick, preferred_element_type=jnp.float32).astype(
        jnp.bfloat16
    )
    grad_send = jnp.repeat(grad_buffer.reshape(experts, capacity, width), copies, axis=0)
    grad_rows = lax.all_to_all(grad_send, "dp", split_axis=0, concat_axis=0, tiled=True)
    grad_flat = grad_rows.reshape(-1, width)
    grad_down_w = inner_rows(act_low, grad_flat)
    grad_act = outer_cols(grad_flat, w_down)
    grad_pre = gelu_pull(grad_act)[0].astype(jnp.bfloat16)
    grad_up_w = inner_rows(expert_rows, grad_pre)
    grad_in_rows = outer_cols(grad_pre, w_up).reshape(sources, capacity, width)
    grad_back = lax.all_to_all(
        grad_in_rows.astype(jnp.bfloat16), "dp", split_axis=0, concat_axis=0, tiled=True
    ).astype(grad_in_rows.dtype)
    grad_slots = jnp.sum(grad_back.reshape(experts, copies, capacity, width), axis=1).reshape(
        experts * capacity, width
    )
    grad_logits = gate[:, None] * (chosen - probs) * grad_gate[:, None]
    router_full = router.astype(jnp.float32)
    grad_normed_two = jnp.take(grad_slots, slot, axis=0) + jnp.dot(
        grad_logits, router_full, precision=HIGHEST
    )
    grad_router = inner_rows(grad_logits, normed_two.astype(jnp.float32), HIGHEST)
    unused_two, pull_two = jax.vjp(rms_norm, middle, gain_two)
    grad_middle_norm, grad_gain_two = pull_two(grad_normed_two)
    grad_middle = grad_out + grad_middle_norm
    grad_middle_low = grad_middle.astype(jnp.bfloat16)

    grad_middle_low, grad_up_low, grad_down_low = lax.optimization_barrier(
        (grad_middle_low, grad_up_w.astype(jnp.bfloat16), grad_down_w.astype(jnp.bfloat16))
    )
    expert_grads = (
        lax.psum_scatter(grad_up_low, "seq", scatter_dimension=0, tiled=True).astype(jnp.float32),
        lax.psum_scatter(grad_down_low, "seq", scatter_dimension=1, tiled=True).astype(
            jnp.float32
        ),
    )

    (grad_gate_branch, grad_act, grad_step_w, rate_total, scan_rows, grad_selected, grad_middle_all) = (
        scan_backward(
            count, cuts, grad_middle_low, conv_act, gate_branch, mixed, pre, selected, small_all,
            weights, priors, end,
        )
    )
    vectors = jnp.concatenate(
        [
            jnp.zeros((1, width), jnp.float32),
            grad_gain_two[None],
            grad_router,
            jnp.zeros((6 - experts, width), jnp.float32),
        ],
        axis=0,
    )
    grad_normed, grad_shard, totals = back(
        count, lines, shard_rows, cuts, grad_selected, small_all, weights, conv_ext, conv_sum,
        grad_act, grad_gate_branch, mixer_low, normed_all.reshape(-1, width),
        grad_middle_all.reshape(-1, width), grad_step_w, rate_total, scan_rows, vectors,
    )
    grad_shard = grad_shard[:shard]
    grad_input_w = grad_shard[:, : 2 * width].T.reshape(2, width, shard)
    small_shard = grad_shard[:, 3 * width :].T
    cut = 0
    small_grads = []
    for number in (picks, rank, state, kernel, 1, 1, 1):
        small_grads.append(small_shard[cut : cut + number])
        cut += number
    unused_one, pull_one = jax.vjp(lambda v: rms_norm(v, gain_one), x_in)
    grad_tokens = grad_middle + pull_one(grad_normed)[0]
    return (
        output.reshape(tokens.shape),
        grad_tokens.reshape(tokens.shape),
        totals[0] / gain_one,
        grad_input_w,
        small_grads[3],
        small_grads[4].reshape(shard),
        small_grads[0],
        small_grads[1],
        small_grads[5].reshape(shard),
        small_grads[2],
        small_grads[6].reshape(shard),
        grad_shard[:, 2 * width : 3 * width],
        totals[1],
        totals[2 : 2 + experts],
        expert_grads[0],
        expert_grads[1],
    )


def solution(mesh):
    both = ("dp", "seq")
    placed = (
        P("dp", "seq", None),
        P("dp", "seq", None),
        P("dp", "seq", None),
        P(),
        P(None, None, both),
        P(None, both),
        P(both),
        P(None, both),
        P(None, both),
        P(both),
        P(None, both),
        P(both),
        P(both, None),
        P(),
        P(),
        P("seq", "dp"),
        P("dp", "seq"),
    )
    return jax.shard_map(
        body,
        mesh=mesh,
        in_specs=placed,
        out_specs=(
            P("dp", "seq", None),
            P("dp", "seq", None),
            P(),
            P(None, None, both),
            P(None, both),
            P(both),
            P(None, both),
            P(None, both),
            P(both),
            P(None, both),
            P(both),
            P(both, None),
            P(),
            P(),
            P("seq", "dp"),
            P("dp", "seq"),
        ),
        check_vma=False,
    )
```

```python
import functools
import math

import jax
import jax.numpy as jnp
from jax import lax
from jax.experimental import pallas as pl
from jax.experimental.pallas import tpu as pltpu
from jax.sharding import PartitionSpec as P

CAP = 56
LANES = 128
TIME_BLOCK = 128
LOG2E = math.log2(math.e)

HIGHEST = lax.Precision.HIGHEST


def rms_norm(values, gain):
    return values * lax.rsqrt(jnp.mean(values * values, axis=-1, keepdims=True) + 1e-05) * gain


def inner_rows(left, right, precision=None):
    return lax.dot_general(
        left,
        right,
        (((0,), (0,)), ((), ())),
        precision=precision,
        preferred_element_type=jnp.float32,
    )


def outer_cols(left, right, precision=None):
    return lax.dot_general(
        left,
        right,
        (((1,), (1,)), ((), ())),
        precision=precision,
        preferred_element_type=jnp.float32,
    )


def sublane_sums(parts):
    row = lax.broadcasted_iota(jnp.int32, parts[0].shape, 0)
    low4 = row < 4
    low2 = (row % 4) < 2
    low1 = (row % 2) < 1
    quads = []
    for k in range(4):
        a, b = parts[k], parts[k + 4]
        quads.append(jnp.where(low4, a, b) + pltpu.roll(jnp.where(low4, b, a), 4, 0))
    pairs = []
    for k in range(2):
        a, b = quads[k], quads[k + 2]
        pairs.append(
            jnp.where(low2, a, b) + jnp.where(low2, pltpu.roll(a, 6, 0), pltpu.roll(b, 2, 0))
        )
    a, b = pairs
    return jnp.where(low1, a, b) + jnp.where(low1, pltpu.roll(a, 7, 0), pltpu.roll(b, 1, 0))


def lane_column(block, k):
    return jnp.broadcast_to(block[:, k : k + 1], block.shape)


MESH = pl.DeviceIdType.MESH
VMEM_LIMIT = 60 * 1024 * 1024


def dot_nn(left, right, precision=None):
    return lax.dot_general(
        left, right, (((1,), (0,)), ((), ())), precision=precision,
        preferred_element_type=jnp.float32,
    )


def place():
    own, line = lax.axis_index("seq"), lax.axis_index("dp")
    return line, own, own // 2, lax.rem(own, 2)


def remote(source, target, send_sem, recv_sem, line, position):
    return pltpu.make_async_remote_copy(
        src_ref=source,
        dst_ref=target,
        send_sem=send_sem,
        recv_sem=recv_sem,
        device_id=(line, position),
        device_id_type=MESH,
    )


def greet(count, lines=1):
    line, own, _, _ = place()
    barrier = pltpu.get_barrier_semaphore()
    for k in range(1, count):
        pl.semaphore_signal(
            barrier, inc=1, device_id=(line, lax.rem(own + k, count)), device_id_type=MESH
        )
    for k in range(1, lines):
        pl.semaphore_signal(
            barrier, inc=1, device_id=(lax.rem(line + k, lines), own), device_id_type=MESH
        )
    pl.semaphore_wait(barrier, count - 1 + lines - 1)


def sigmoid(values):
    return 1.0 / (1.0 + jnp.exp(-values))


def softplus(values):
    return jnp.maximum(values, 0.0) + jnp.log1p(jnp.exp(-jnp.abs(values)))


class Cuts:
    def __init__(self, picks, rank, state, kernel):
        self.picks, self.rank, self.state, self.kernel = picks, rank, state, kernel
        self.step = picks
        self.decay = self.step + rank
        self.taps = self.decay + state
        self.conv_bias = self.taps + kernel
        self.step_bias = self.conv_bias + 1
        self.skip = self.step_bias + 1
        self.rows = self.skip + 1


class Relay:
    def __init__(self, axis, half, high, low, seat, block, refs):
        self.axis, self.half, self.high, self.low = axis, half, high, low
        self.seat, self.block = seat, block
        self.other = lax.axis_index("dp" if axis == "seq" else "seq")
        self.part, self.across, self.along = refs[:3]
        self.send_x, self.recv_x, self.send_hi, self.recv_hi = refs[3:]

    def remote(self, source, target, send_sem, recv_sem, position):
        if self.axis == "seq":
            return remote(source, target, send_sem, recv_sem, self.other, position)
        return remote(source, target, send_sem, recv_sem, position, self.other)

    def over(self, i, low):
        return self.remote(
            self.part.at[self.block(i, low)], self.across.at[i], self.send_x.at[i],
            self.recv_x.at[i], self.seat(self.high, 1 - self.low),
        )

    def on(self, i):
        k = lax.rem(i - self.high + self.half, self.half)
        return self.remote(
            self.across.at[i], self.along.at[k], self.send_hi.at[k], self.recv_hi.at[k],
            self.seat(i, self.low),
        )

    def made(self, i, low):
        @pl.when(low != self.low)
        def _():
            self.over(i, low).start()

    def summed(self, i):
        self.over(i, self.low).wait_recv()
        return self.part[self.block(i, self.low)].astype(jnp.float32) + self.across[i].astype(
            jnp.float32
        )

    def pass_on(self, i, low):
        @pl.when((low == self.low) & (i != self.high))
        def _():
            self.across[i] = self.summed(i).astype(jnp.bfloat16)
            self.on(i).start()

    def finish(self):
        total = self.summed(self.high)
        for k in range(1, self.half):
            self.on(lax.rem(self.high + k, self.half)).wait_recv()
            total = total + self.along[k].astype(jnp.float32)
        for i in range(self.half):
            self.over(i, 1 - self.low).wait_send()
        for k in range(1, self.half):
            self.on(lax.rem(self.high + k, self.half)).wait_send()
        return total


def whole_relay(axis, count, refs):
    own = lax.axis_index(axis)

    def seat(i, low):
        return 2 * i + low

    return Relay(axis, count // 2, own // 2, lax.rem(own, 2), seat, seat, refs)


def relay_scratch(count, rows, width, part=True):
    half = count // 2
    dma = pltpu.SemaphoreType.DMA
    own = [pltpu.VMEM((count, rows, width), jnp.bfloat16)] if part else []
    return own + [
        pltpu.VMEM((half, rows, width), jnp.bfloat16),
        pltpu.VMEM((half, rows, width), jnp.bfloat16),
        dma((half,)), dma((half,)), dma((half,)), dma((half,)),
    ]


def square():
    own = lax.axis_index("seq")
    return own // 4, lax.rem(own // 2, 2), lax.rem(own, 2)


def seat_of(q, f, low):
    return 4 * q + 2 * f + low


class Gather:
    def __init__(self, count, shard_ref, land_ref, swap_s, swap_r, line_s, line_r, pair_s, pair_r):
        self.line = lax.axis_index("dp")
        self.q, self.f, self.low = square()
        self.quarter = count // 4
        self.shard, self.land = shard_ref, land_ref
        self.swap_s, self.swap_r = swap_s, swap_r
        self.line_s, self.line_r, self.pair_s, self.pair_r = line_s, line_r, pair_s, pair_r
        self.cut = land_ref.shape[2]

    def columns(self, f):
        return pl.ds(pl.multiple_of(f * self.cut, LANES), self.cut)

    def piece(self, j, k, low):
        q = lax.rem(self.q - k + self.quarter, self.quarter)
        return seat_of(q, lax.rem(self.f + j, 2), low)

    def swap(self):
        own = self.piece(0, 0, self.low)
        return remote(
            self.shard.at[:, self.columns(1 - self.f)], self.land.at[own], self.swap_s, self.swap_r,
            self.line, self.piece(1, 0, self.low),
        )

    def along(self, j, k):
        piece = self.piece(j, 0, self.low)
        there = seat_of(lax.rem(self.q + k, self.quarter), self.f, self.low)
        return remote(
            self.land.at[piece], self.land.at[piece], self.line_s.at[j, k], self.line_r.at[j, k],
            self.line, there,
        )

    def pair(self, j, k, low):
        piece = self.piece(j, k, low)
        return remote(
            self.land.at[piece], self.land.at[piece], self.pair_s.at[j, k], self.pair_r.at[j, k],
            self.line, seat_of(self.q, self.f, 1 - self.low),
        )

    def start(self):
        self.swap().start()
        self.land[self.piece(0, 0, self.low)] = self.shard[:, self.columns(self.f)]

    def spread(self, j):
        if j == 1:
            mate = self.piece(1, 0, self.low)
            remote(
                self.land.at[mate], self.land.at[mate], self.swap_s, self.swap_r, self.line, mate
            ).wait_recv()
        for k in range(1, self.quarter):
            self.along(j, k).start()
        self.pair(j, 0, self.low).start()

    def forward(self):
        for j in range(2):
            for k in range(1, self.quarter):
                piece = self.piece(j, k, self.low)
                remote(
                    self.land.at[piece], self.land.at[piece], self.line_s.at[j, k],
                    self.line_r.at[j, k], self.line, piece,
                ).wait_recv()
                self.pair(j, k, self.low).start()

    def finish(self):
        for j in range(2):
            for k in range(self.quarter):
                self.pair(j, k, 1 - self.low).wait_recv()
        self.swap().wait_send()
        for j in range(2):
            for k in range(1, self.quarter):
                self.along(j, k).wait_send()
            for k in range(self.quarter):
                self.pair(j, k, self.low).wait_send()


def gather_scratch(count):
    dma = pltpu.SemaphoreType.DMA
    quarter = count // 4
    return [dma, dma] + [dma((2, quarter)) for _ in range(4)]


class Scatter:
    def __init__(self, count, part_ref, other_ref, held_ref, swap_s, swap_r, refs):
        self.line = lax.axis_index("dp")
        self.q, self.f, self.low = square()
        self.quarter = count // 4
        self.other, self.held = other_ref, held_ref
        self.swap_s, self.swap_r = swap_s, swap_r
        self.relays = []
        for j in range(2):
            cut = lax.rem(self.f + j, 2)

            def seat(i, low):
                return seat_of(i, self.f, low)

            def block(i, low, cut=cut):
                return seat_of(i, cut, low)

            mine = tuple(ref.at[j] for ref in refs)
            self.relays.append(
                Relay("seq", self.quarter, self.q, self.low, seat, block, (part_ref, *mine))
            )

    def swap(self):
        return remote(
            self.held, self.other, self.swap_s, self.swap_r, self.line,
            seat_of(self.q, 1 - self.f, self.low),
        )

    def start(self):
        for j in (1, 0):
            for i in range(self.quarter):
                self.relays[j].over(i, 1 - self.low).start()

    def pass_on(self):
        for j in (1, 0):
            for k in range(1, self.quarter):
                self.relays[j].pass_on(lax.rem(self.q + k, self.quarter), self.low)

    def hand_over(self):
        self.held[...] = self.relays[1].finish().astype(jnp.bfloat16)
        self.swap().start()

    def finish(self, out_ref):
        cut = self.held.shape[1]
        out_ref[:, pl.ds(pl.multiple_of(self.f * cut, LANES), cut)] = self.relays[0].finish()
        self.swap().wait_recv()
        out_ref[:, pl.ds(pl.multiple_of((1 - self.f) * cut, LANES), cut)] = self.other[...].astype(
            jnp.float32
        )
        self.swap().wait_send()


def scatter_scratch(count, rows, cut):
    dma = pltpu.SemaphoreType.DMA
    quarter = count // 4
    return [
        pltpu.VMEM((rows, cut), jnp.bfloat16),
        pltpu.VMEM((rows, cut), jnp.bfloat16),
        dma, dma,
        pltpu.VMEM((2, quarter, rows, cut), jnp.bfloat16),
        pltpu.VMEM((2, quarter, rows, cut), jnp.bfloat16),
        *[dma((2, quarter)) for _ in range(4)],
    ]


def front_kernel(
    count, lines, cuts,
    normed_ref, packed_ref, expert_ref,
    all_ref, weights_ref, small_ref, ext_ref, sum_ref, act_ref, gate_ref, selected_ref, land_ref,
    part_ref, partial_ref,
    send_w, recv_w, send_hi, recv_hi, send_x, recv_x, send_rs, recv_rs, send_ag, recv_ag,
    *gather_refs,
):
    line, own, high, low = place()
    half = count // 2
    gather = Gather(count, expert_ref, land_ref, *gather_refs)
    rows, width = normed_ref.shape
    shard = packed_ref.shape[0]
    inner = weights_ref.shape[0]
    kernel = cuts.kernel
    partner = 2 * high + 1 - low
    greet(count, lines)

    copies = []
    shard_rows = pl.ds(pl.multiple_of(line * shard, 16), shard)
    for k in range(1, half):
        copy = remote(
            normed_ref, all_ref.at[own], send_hi.at[k], recv_hi.at[k],
            line, 2 * lax.rem(high + k, half) + low,
        )
        copy.start()
        copies.append(copy)
    copy = remote(normed_ref, all_ref.at[own], send_x.at[0], recv_x.at[0], line, partner)
    copy.start()
    copies.append(copy)
    for k in range(1, lines):
        copy = remote(
            packed_ref, weights_ref.at[shard_rows], send_w.at[k], recv_w.at[k],
            lax.rem(line + k, lines), own,
        )
        copy.start()
        copies.append(copy)
    gather.start()
    all_ref[own] = normed_ref[...]
    weights_ref[shard_rows, :] = packed_ref[...]
    if lines * shard < inner:
        weights_ref[lines * shard :, :] = jnp.zeros(
            (inner - lines * shard, weights_ref.shape[1]), weights_ref.dtype
        )
    ext_ref[0:8, :] = jnp.zeros((8, inner), jnp.float32)
    for k in range(1, half):
        block = 2 * lax.rem(high - k + half, half) + low
        remote(
            normed_ref, all_ref.at[block], send_hi.at[k], recv_hi.at[k], line, partner
        ).wait_recv()
        copy = remote(
            all_ref.at[block], all_ref.at[block], send_x.at[k], recv_x.at[k], line, partner
        )
        copy.start()
        copies.append(copy)
    gather.spread(0)
    gather.spread(1)
    for k in range(1, lines):
        from_line = lax.rem(line - k + lines, lines)
        there = pl.ds(pl.multiple_of(from_line * shard, 16), shard)
        remote(
            packed_ref, weights_ref.at[there], send_w.at[k], recv_w.at[k], from_line, own
        ).wait_recv()
    small_ref[...] = weights_ref[:, 3 * width :].astype(jnp.float32).T
    for k in range(half):
        block = 2 * lax.rem(high - k + half, half) + 1 - low
        remote(
            normed_ref, all_ref.at[block], send_x.at[k], recv_x.at[k], line, partner
        ).wait_recv()

    def project(b, carry):
        start = pl.multiple_of(b * rows, rows)
        block = all_ref[b]
        ext_ref[pl.ds(pl.multiple_of(start + 8, 8), rows), :] = outer_cols(
            block, weights_ref[:, :width]
        )
        gate_ref[pl.ds(start, rows), :] = outer_cols(block, weights_ref[:, width : 2 * width])
        return carry

    lax.fori_loop(0, count, project, 0)

    def convolve(b, carry):
        start = pl.multiple_of(b * rows, rows)
        window = ext_ref[pl.ds(start, rows + 8), :]
        total = small_ref[cuts.conv_bias : cuts.conv_bias + 1, :]
        for k in range(kernel):
            tap = small_ref[cuts.taps + k : cuts.taps + k + 1, :]
            total = total + tap * window[9 - kernel + k : 9 - kernel + k + rows]
        act = total * sigmoid(total)
        sum_ref[pl.ds(start, rows), :] = total
        act_ref[pl.ds(start, rows), :] = act
        part_ref[b] = outer_cols(
            small_ref[: cuts.picks, :].astype(jnp.bfloat16), act.astype(jnp.bfloat16)
        )
        return carry

    lax.fori_loop(0, count, convolve, 0)

    gather.forward()
    for k in range(1, count):
        there = lax.rem(own + k, count)
        copy = remote(
            part_ref.at[there], partial_ref.at[k], send_rs.at[k], recv_rs.at[k], line, there
        )
        copy.start()
        copies.append(copy)
    total = part_ref[own]
    for k in range(1, count):
        remote(
            part_ref.at[own], partial_ref.at[k], send_rs.at[k], recv_rs.at[k], line, partner
        ).wait_recv()
        total = total + partial_ref[k]
    selected_ref[own] = total
    for k in range(1, count):
        copy = remote(
            selected_ref.at[own], selected_ref.at[own], send_ag.at[k], recv_ag.at[k],
            line, lax.rem(own + k, count),
        )
        copy.start()
        copies.append(copy)
    for k in range(1, count):
        block = lax.rem(own - k + count, count)
        remote(
            selected_ref.at[block], selected_ref.at[block], send_ag.at[k], recv_ag.at[k],
            line, partner,
        ).wait_recv()
    for copy in copies:
        copy.wait_send()
    gather.finish()


def front(count, lines, cuts, normed, packed, expert):
    rows, width = normed.shape
    shard, columns = packed.shape
    inner = -(-lines * shard // LANES) * LANES
    length = count * rows
    half = count // 2
    small = columns - 3 * width
    vmem = pl.BlockSpec(memory_space=pltpu.VMEM)

    def f32(*shape):
        return jax.ShapeDtypeStruct(shape, jnp.float32)

    dma = pltpu.SemaphoreType.DMA
    return pl.pallas_call(
        functools.partial(front_kernel, count, lines, cuts),
        in_specs=[vmem] * 3,
        out_specs=[vmem] * 9,
        out_shape=[
            jax.ShapeDtypeStruct((count, rows, width), jnp.bfloat16),
            jax.ShapeDtypeStruct((inner, columns), jnp.bfloat16),
            f32(small, inner),
            f32(length + 8, inner),
            f32(length, inner),
            f32(length, inner),
            f32(length, inner),
            f32(count, cuts.picks, rows),
            jax.ShapeDtypeStruct((count, expert.shape[0], expert.shape[1] // 2), jnp.bfloat16),
        ],
        scratch_shapes=[
            pltpu.VMEM((count, cuts.picks, rows), jnp.float32),
            pltpu.VMEM((count, cuts.picks, rows), jnp.float32),
            dma((lines,)), dma((lines,)), dma((half,)), dma((half,)), dma((half,)), dma((half,)),
            dma((count,)), dma((count,)), dma((count,)), dma((count,)),
            *gather_scratch(count),
        ],
        compiler_params=pltpu.CompilerParams(
            collective_id=0, has_side_effects=True, vmem_limit_bytes=VMEM_LIMIT
        ),
        cost_estimate=pl.CostEstimate(
            flops=4 * length * width * inner,
            bytes_accessed=20 * length * inner,
            transcendentals=length * inner,
        ),
        name="front",
    )(normed, packed, expert)


def scan_forward_kernel(
    count, cuts,
    act_ref, gate_ref, selected_ref, small_ref, output_ref, expert_ref,
    pre_ref, mixed_ref, mixer_low_ref, prior_ref, end_ref, summed_ref, expert_out_ref,
    state_ref, delta_ref, scanned_ref, land_ref, *refs,
):
    steps, inner = act_ref.shape
    tiles = inner // LANES
    state = cuts.state
    halves = state // 8
    step = pl.program_id(0)
    relay = whole_relay("seq", count, refs[:7])
    gather = Gather(count, expert_ref, land_ref, *refs[7:])

    @pl.when(step == 0)
    def _():
        greet(count)
        gather.start()
        state_ref[...] = jnp.zeros_like(state_ref)

    @pl.when(step == 1)
    def _():
        gather.spread(0)
        gather.spread(1)

    @pl.when(step == count // 2)
    def _():
        gather.forward()

    rates2 = -LOG2E * jnp.exp(small_ref[cuts.decay : cuts.decay + state, :])
    pre = inner_rows(
        selected_ref[0, : cuts.rank, :],
        small_ref[cuts.step : cuts.step + cuts.rank, :],
        HIGHEST,
    ) + small_ref[cuts.step_bias : cuts.step_bias + 1, :]
    pre_ref[...] = pre
    delta_ref[...] = softplus(pre)
    in_rows = cuts.rank
    out_rows = cuts.rank + state

    def group(g, states):
        states = [list(s) for s in states]
        base = pl.multiple_of(g * 8, 8)
        shift = lax.rem(steps - base, steps)
        b_cols = [
            pltpu.roll(selected_ref[0, in_rows + 8 * i : in_rows + 8 * i + 8, :], shift, 1)
            for i in range(halves)
        ]
        c_cols = [
            pltpu.roll(selected_ref[0, out_rows + 8 * i : out_rows + 8 * i + 8, :], shift, 1)
            for i in range(halves)
        ]
        d8 = delta_ref[pl.ds(base, 8), :]
        du8 = d8 * act_ref[pl.ds(base, 8), :]
        parts = [[None] * 8 for _ in range(tiles)]
        for k in range(8):
            b_now = [lane_column(b, k) for b in b_cols]
            c_now = [lane_column(c, k) for c in c_cols]
            for j in range(tiles):
                cols = slice(j * LANES, (j + 1) * LANES)
                d = jnp.broadcast_to(d8[k : k + 1, cols], (8, LANES))
                du = jnp.broadcast_to(du8[k : k + 1, cols], (8, LANES))
                total = None
                for i in range(halves):
                    old = states[j][i]
                    prior_ref[base + k, 8 * i : 8 * i + 8, cols] = old
                    new = jnp.exp2(d * rates2[8 * i : 8 * i + 8, cols]) * old + b_now[i] * du
                    states[j][i] = new
                    term = c_now[i] * new
                    total = term if total is None else total + term
                parts[j][k] = total
        for j in range(tiles):
            scanned_ref[pl.ds(base, 8), j * LANES : (j + 1) * LANES] = sublane_sums(parts[j])
        return tuple(tuple(s) for s in states)

    first = tuple(
        tuple(
            state_ref[8 * i : 8 * i + 8, j * LANES : (j + 1) * LANES] for i in range(halves)
        )
        for j in range(tiles)
    )
    last = lax.fori_loop(0, steps // 8, group, first)
    for j in range(tiles):
        for i in range(halves):
            state_ref[8 * i : 8 * i + 8, j * LANES : (j + 1) * LANES] = last[j][i]
    end_ref[...] = state_ref[...]

    mixed = scanned_ref[...] + small_ref[cuts.skip : cuts.skip + 1, :] * act_ref[...]
    gate = gate_ref[...]
    low = (mixed * (gate * sigmoid(gate))).astype(jnp.bfloat16)
    mixed_ref[...] = mixed
    mixer_low_ref[...] = low
    relay.part[step] = dot_nn(low, output_ref[...]).astype(jnp.bfloat16)
    relay.made(step // 2, lax.rem(step, 2))

    def pass_on(block):
        relay.pass_on(block // 2, lax.rem(block, 2))

    @pl.when(step >= 2)
    def _():
        pass_on(step - 2)

    @pl.when(step == count - 1)
    def _():
        pass_on(step - 1)
        pass_on(step)
        summed_ref[...] = relay.finish()
        gather.finish()
        expert_out_ref[...] = land_ref[...]


def scan_forward(count, cuts, width, act, gate, selected, small, weights, expert):
    length, inner = act.shape
    state = cuts.state
    block = length // count
    rows = pl.BlockSpec((block, inner), lambda t: (t, 0))
    whole = pl.BlockSpec((state, inner), lambda t: (0, 0))
    pieces = (count, expert.shape[0], expert.shape[1] // 2)
    return pl.pallas_call(
        functools.partial(scan_forward_kernel, count, cuts),
        grid=(count,),
        in_specs=[
            rows,
            rows,
            pl.BlockSpec((1, cuts.picks, block), lambda t: (t, 0, 0)),
            pl.BlockSpec(small.shape, lambda t: (0, 0)),
            pl.BlockSpec((inner, width), lambda t: (0, 2)),
            pl.BlockSpec(expert.shape, lambda t: (0, 0)),
        ],
        out_specs=[
            rows,
            rows,
            rows,
            pl.BlockSpec((block, state, inner), lambda t: (t, 0, 0)),
            whole,
            pl.BlockSpec((block, width), lambda t: (0, 0)),
            pl.BlockSpec(pieces, lambda t: (0, 0, 0)),
        ],
        out_shape=[
            jax.ShapeDtypeStruct((length, inner), jnp.float32),
            jax.ShapeDtypeStruct((length, inner), jnp.float32),
            jax.ShapeDtypeStruct((length, inner), jnp.bfloat16),
            jax.ShapeDtypeStruct((length, state, inner), jnp.float32),
            jax.ShapeDtypeStruct((state, inner), jnp.float32),
            jax.ShapeDtypeStruct((block, width), jnp.float32),
            jax.ShapeDtypeStruct(pieces, jnp.bfloat16),
        ],
        scratch_shapes=[
            pltpu.VMEM((state, inner), jnp.float32),
            pltpu.VMEM((block, inner), jnp.float32),
            pltpu.VMEM((block, inner), jnp.float32),
            pltpu.VMEM(pieces, jnp.bfloat16),
            *relay_scratch(count, block, width),
            *gather_scratch(count),
        ],
        compiler_params=pltpu.CompilerParams(
            collective_id=1, has_side_effects=True, vmem_limit_bytes=VMEM_LIMIT
        ),
        cost_estimate=pl.CostEstimate(
            flops=8 * length * state * inner,
            bytes_accessed=4 * length * inner * (state + 6),
            transcendentals=length * state * inner,
        ),
        name="scan_forward",
    )(act, gate, selected, small, weights, expert)


def scan_backward_kernel(
    count, cuts,
    own_ref, act_ref, gate_ref, mixed_ref, pre_ref, selected_ref, small_ref, output_ref,
    prior_ref, end_ref, expert_ref,
    grad_gate_ref, grad_act_ref, grad_step_ref, rate_total_ref, rows_ref, grad_selected_ref,
    all_out_ref, expert_out_ref,
    incoming_ref, post_ref, delta_ref, grad_ref, grad_delta_ref, all_ref,
    part_ref, partial_ref, total_ref,
    send_hi, recv_hi, send_x, recv_x, send_rs, recv_rs, send_ag, recv_ag,
    other_ref, held_ref, swap_s, swap_r, *scatter_refs,
):
    steps, inner = act_ref.shape
    tiles = inner // LANES
    state = cuts.state
    halves = state // 8
    lane = lax.broadcasted_iota(jnp.int32, (8, steps), 1)
    line, own, high, low = place()
    half = count // 2
    partner = 2 * high + 1 - low
    index = pl.program_id(0)
    now = count - 1 - index
    scatter = Scatter(count, expert_ref, other_ref, held_ref, swap_s, swap_r, scatter_refs)

    def along(k):
        return remote(
            own_ref, all_ref.at[own], send_hi.at[k], recv_hi.at[high], line,
            2 * lax.rem(high + k, half) + low,
        )

    def across(block):
        i = block // 2
        return remote(
            all_ref.at[block], all_ref.at[block], send_x.at[i], recv_x.at[i], line, partner
        )

    def came_along(block):
        i = block // 2
        return remote(
            all_ref.at[block], all_ref.at[block], send_hi.at[0], recv_hi.at[i], line, partner
        )

    def hand_over(block):
        @pl.when((lax.rem(block, 2) == low) & (block // 2 != high))
        def _():
            came_along(block).wait_recv()
            across(block).start()

    @pl.when(index == 0)
    def _():
        greet(count)
        all_ref[own] = own_ref[...]
        incoming_ref[...] = jnp.zeros_like(incoming_ref)
        post_ref[...] = end_ref[...]
        rate_total_ref[...] = jnp.zeros_like(rate_total_ref)
        grad_step_ref[...] = jnp.zeros_like(grad_step_ref)
        rows_ref[...] = jnp.zeros_like(rows_ref)

    @pl.when(index == jnp.maximum(count - 3 - own, 0))
    def _():
        for k in range(1, half):
            along(k).start()
        across(own).start()

    @pl.when(index == 0)
    def _():
        hand_over(now)
        hand_over(now - 1)

    @pl.when(lax.rem(now, 2) != low)
    def _():
        across(now).wait_recv()

    gate = gate_ref[...]
    gate_sig = sigmoid(gate)
    grad_y = outer_cols(all_ref[now], output_ref[...])
    grad_gate_ref[...] = (
        grad_y * mixed_ref[...] * (gate_sig * (1.0 + gate * (1.0 - gate_sig)))
    ).astype(jnp.bfloat16)
    grad_mixed = grad_y * (gate * gate_sig)
    grad_ref[...] = grad_mixed
    delta_ref[...] = softplus(pre_ref[...])
    rows_ref[1:2, :] += jnp.sum(grad_mixed * act_ref[...], axis=0, keepdims=True)
    rates2 = -LOG2E * jnp.exp(small_ref[cuts.decay : cuts.decay + state, :])
    in_rows = cuts.rank
    out_rows = cuts.rank + state

    def tile_of(ref):
        return tuple(
            tuple(ref[8 * i : 8 * i + 8, j * LANES : (j + 1) * LANES] for i in range(halves))
            for j in range(tiles)
        )

    def group(turn, carry):
        incoming, posts, rate_total, in_acc, out_acc = carry
        incoming = [list(s) for s in incoming]
        posts = [list(s) for s in posts]
        rate_total = [list(s) for s in rate_total]
        in_acc, out_acc = list(in_acc), list(out_acc)
        base = pl.multiple_of((steps // 8 - 1 - turn) * 8, 8)
        shift = lax.rem(steps - base, steps)
        b_cols = [
            pltpu.roll(selected_ref[0, in_rows + 8 * i : in_rows + 8 * i + 8, :], shift, 1)
            for i in range(halves)
        ]
        c_cols = [
            pltpu.roll(selected_ref[0, out_rows + 8 * i : out_rows + 8 * i + 8, :], shift, 1)
            for i in range(halves)
        ]
        d8 = delta_ref[pl.ds(base, 8), :]
        u8 = act_ref[pl.ds(base, 8), :]
        du8 = d8 * u8
        g8 = grad_ref[pl.ds(base, 8), :]
        rate_parts = [[None] * 8 for _ in range(tiles)]
        side_parts = [[None] * 8 for _ in range(tiles)]
        for k in range(7, -1, -1):
            b_now = [lane_column(b, k) for b in b_cols]
            c_now = [lane_column(c, k) for c in c_cols]
            in_sum = [None] * halves
            out_sum = [None] * halves
            for j in range(tiles):
                cols = slice(j * LANES, (j + 1) * LANES)
                d = jnp.broadcast_to(d8[k : k + 1, cols], (8, LANES))
                du = jnp.broadcast_to(du8[k : k + 1, cols], (8, LANES))
                gm = jnp.broadcast_to(g8[k : k + 1, cols], (8, LANES))
                rate_part = None
                side_part = None
                for i in range(halves):
                    prior = prior_ref[base + k, 8 * i : 8 * i + 8, cols]
                    rates = rates2[8 * i : 8 * i + 8, cols]
                    grad_state = c_now[i] * gm + incoming[j][i]
                    passed = jnp.exp2(d * rates) * grad_state
                    incoming[j][i] = passed
                    weighted = passed * prior
                    term = weighted * rates
                    rate_part = term if rate_part is None else rate_part + term
                    term = grad_state * b_now[i]
                    side_part = term if side_part is None else side_part + term
                    term = grad_state * du
                    in_sum[i] = term if in_sum[i] is None else in_sum[i] + term
                    term = posts[j][i] * gm
                    out_sum[i] = term if out_sum[i] is None else out_sum[i] + term
                    rate_total[j][i] = rate_total[j][i] + weighted * d
                    posts[j][i] = prior
                rate_parts[j][k] = rate_part
                side_parts[j][k] = side_part
            here = lane == base + k
            for i in range(halves):
                in_acc[i] = jnp.where(here, jnp.sum(in_sum[i], axis=1, keepdims=True), in_acc[i])
                out_acc[i] = jnp.where(here, jnp.sum(out_sum[i], axis=1, keepdims=True), out_acc[i])
        for j in range(tiles):
            cols = slice(j * LANES, (j + 1) * LANES)
            side = sublane_sums(side_parts[j])
            grad_delta_ref[pl.ds(base, 8), cols] = (
                sublane_sums(rate_parts[j]) * (1.0 / LOG2E) + u8[:, cols] * side
            )
            grad_act_ref[pl.ds(base, 8), cols] = d8[:, cols] * side
        return (
            tuple(tuple(s) for s in incoming),
            tuple(tuple(s) for s in posts),
            tuple(tuple(s) for s in rate_total),
            tuple(in_acc),
            tuple(out_acc),
        )

    empty = tuple(jnp.zeros((8, steps), jnp.float32) for _ in range(halves))
    incoming, posts, rate_total, in_acc, out_acc = lax.fori_loop(
        0,
        steps // 8,
        group,
        (tile_of(incoming_ref), tile_of(post_ref), tile_of(rate_total_ref), empty, empty),
    )
    for i in range(halves):
        part_ref[now, in_rows + 8 * i : in_rows + 8 * i + 8, :] = in_acc[i]
        part_ref[now, out_rows + 8 * i : out_rows + 8 * i + 8, :] = out_acc[i]
        for j in range(tiles):
            cols = slice(j * LANES, (j + 1) * LANES)
            incoming_ref[8 * i : 8 * i + 8, cols] = incoming[j][i]
            post_ref[8 * i : 8 * i + 8, cols] = posts[j][i]
            rate_total_ref[8 * i : 8 * i + 8, cols] = rate_total[j][i]

    grad_act_ref[...] += grad_ref[...] * small_ref[cuts.skip : cuts.skip + 1, :]
    grad_pre = grad_delta_ref[...] * sigmoid(pre_ref[...])
    rows_ref[0:1, :] += jnp.sum(grad_pre, axis=0, keepdims=True)
    grad_step_ref[...] += dot_nn(selected_ref[0, : cuts.rank, :], grad_pre, HIGHEST)
    part_ref[now, : cuts.rank, :] = outer_cols(
        small_ref[cuts.step : cuts.step + cuts.rank, :], grad_pre, HIGHEST
    )

    def partial_to(block):
        return remote(
            part_ref.at[block], partial_ref.at[own], send_rs.at[block], recv_rs.at[own], line, block
        )

    @pl.when(now != own)
    def _():
        partial_to(now).start()

    def total_to(k):
        return remote(
            total_ref.at[own], total_ref.at[own], send_ag.at[k], recv_ag.at[own], line,
            lax.rem(own + k, count),
        )

    @pl.when(now >= 2)
    def _():
        hand_over(now - 2)

    @pl.when(index == 1)
    def _():
        scatter.start()

    @pl.when(index == count // 2)
    def _():
        scatter.pass_on()

    @pl.when(index == count - 2)
    def _():
        scatter.hand_over()

    @pl.when(index == jnp.minimum(count - 1 - own + 2, count - 1))
    def _():
        total = part_ref[own]
        for k in range(1, count):
            there = lax.rem(own + k, count)
            remote(
                part_ref.at[own], partial_ref.at[there], send_rs.at[own], recv_rs.at[there],
                line, there,
            ).wait_recv()
            total = total + partial_ref[there]
        total_ref[own] = total
        for k in range(1, count):
            total_to(k).start()

    @pl.when(index == count - 1)
    def _():
        for k in range(1, count):
            there = lax.rem(own + k, count)
            remote(
                total_ref.at[there], total_ref.at[there], send_ag.at[k], recv_ag.at[there],
                line, there,
            ).wait_recv()
        grad_selected_ref[...] = total_ref[...]
        all_out_ref[...] = all_ref[...]
        for k in range(1, half):
            along(k).wait_send()
        for i in range(half):
            across(2 * i + low).wait_send()
        for k in range(1, count):
            partial_to(lax.rem(own + k, count)).wait_send()
            total_to(k).wait_send()
        scatter.finish(expert_out_ref)


def scan_backward(
    count, cuts, grad_low, act, gate, mixed, pre, selected, small, weights, priors, end, expert
):
    length, inner = act.shape
    state = cuts.state
    block = length // count
    width = grad_low.shape[1]
    half = count // 2

    def back(t):
        return count - 1 - t

    rows = pl.BlockSpec((block, inner), lambda t: (back(t), 0))
    whole = pl.BlockSpec((state, inner), lambda t: (0, 0))
    dma = pltpu.SemaphoreType.DMA
    picked = (count, cuts.picks, block)
    return pl.pallas_call(
        functools.partial(scan_backward_kernel, count, cuts),
        grid=(count,),
        in_specs=[
            pl.BlockSpec((block, width), lambda t: (0, 0)),
            rows,
            rows,
            rows,
            rows,
            pl.BlockSpec((1, cuts.picks, block), lambda t: (back(t), 0, 0)),
            pl.BlockSpec(small.shape, lambda t: (0, 0)),
            pl.BlockSpec((inner, width), lambda t: (0, 2)),
            pl.BlockSpec((block, state, inner), lambda t: (back(t), 0, 0)),
            whole,
            pl.BlockSpec(expert.shape, lambda t: (0, 0, 0)),
        ],
        out_specs=[
            rows,
            rows,
            pl.BlockSpec((cuts.rank, inner), lambda t: (0, 0)),
            whole,
            pl.BlockSpec((8, inner), lambda t: (0, 0)),
            pl.BlockSpec(picked, lambda t: (0, 0, 0)),
            pl.BlockSpec((count, block, width), lambda t: (0, 0, 0)),
            pl.BlockSpec((expert.shape[1], 2 * expert.shape[2]), lambda t: (0, 0)),
        ],
        out_shape=[
            jax.ShapeDtypeStruct((length, inner), jnp.bfloat16),
            jax.ShapeDtypeStruct((length, inner), jnp.float32),
            jax.ShapeDtypeStruct((cuts.rank, inner), jnp.float32),
            jax.ShapeDtypeStruct((state, inner), jnp.float32),
            jax.ShapeDtypeStruct((8, inner), jnp.float32),
            jax.ShapeDtypeStruct(picked, jnp.float32),
            jax.ShapeDtypeStruct((count, block, width), jnp.bfloat16),
            jax.ShapeDtypeStruct((expert.shape[1], 2 * expert.shape[2]), jnp.float32),
        ],
        scratch_shapes=[
            pltpu.VMEM((state, inner), jnp.float32),
            pltpu.VMEM((state, inner), jnp.float32),
            pltpu.VMEM((block, inner), jnp.float32),
            pltpu.VMEM((block, inner), jnp.float32),
            pltpu.VMEM((block, inner), jnp.float32),
            pltpu.VMEM((count, block, width), jnp.bfloat16),
            pltpu.VMEM(picked, jnp.float32),
            pltpu.VMEM(picked, jnp.float32),
            pltpu.VMEM(picked, jnp.float32),
            dma((half,)), dma((half,)), dma((half,)), dma((half,)),
            dma((count,)), dma((count,)), dma((count,)), dma((count,)),
            *scatter_scratch(count, expert.shape[1], expert.shape[2]),
        ],
        compiler_params=pltpu.CompilerParams(
            collective_id=2, has_side_effects=True, vmem_limit_bytes=VMEM_LIMIT
        ),
        cost_estimate=pl.CostEstimate(
            flops=20 * length * state * inner,
            bytes_accessed=4 * length * inner * (state + 6),
            transcendentals=length * state * inner,
        ),
        name="scan_backward",
    )(grad_low, act, gate, mixed, pre, selected, small, weights, priors, end, expert)


def back_kernel(
    count, lines, cuts,
    grad_selected_ref, small_ref, weights_ref, ext_ref, sum_ref, grad_act_ref, grad_gate_ref,
    mixer_low_ref, normed_ref, grad_middle_ref, grad_step_ref, rate_total_ref, scan_rows_ref,
    vectors_ref, expert_ref,
    summed_ref, shard_ref, totals_ref, expert_out_ref,
    grad_sum_ref, grad_conv_ref, grad_small_ref, ours_ref, theirs_ref,
    send_v, recv_v, send_u, recv_u, other_ref, held_ref, swap_s, swap_r, *refs,
):
    scatter = Scatter(count, expert_ref, other_ref, held_ref, swap_s, swap_r, refs[:6])
    relay = whole_relay("seq", count, refs[6:13])
    spread = whole_relay("dp", lines, refs[13:])
    line, own, _, _ = place()
    length, inner = sum_ref.shape
    width = normed_ref.shape[1]
    rows = length // count
    kernel = cuts.kernel
    shard = shard_ref.shape[0]
    greet(count, lines)
    scatter.start()
    grad_small_ref[...] = jnp.zeros_like(grad_small_ref)
    grad_sum_ref[length:, :] = jnp.zeros((8, inner), jnp.float32)
    select = small_ref[: cuts.picks, :].astype(jnp.bfloat16)

    def first(b, carry):
        start = pl.multiple_of(b * rows, rows)
        grad_selected = grad_selected_ref[b].astype(jnp.bfloat16)
        total = sum_ref[pl.ds(start, rows), :]
        sig = sigmoid(total)
        grad_act = grad_act_ref[pl.ds(start, rows), :] + inner_rows(grad_selected, select)
        grad_sum = grad_act * (sig * (1.0 + total * (1.0 - sig)))
        grad_sum_ref[pl.ds(start, rows), :] = grad_sum
        grad_small_ref[: cuts.picks, :] += dot_nn(
            grad_selected, (total * sig).astype(jnp.bfloat16)
        )
        window = ext_ref[pl.ds(start, rows + 8), :]
        for k in range(kernel):
            row = slice(cuts.taps + k, cuts.taps + k + 1)
            grad_small_ref[row, :] += jnp.sum(
                grad_sum * window[9 - kernel + k : 9 - kernel + k + rows], axis=0, keepdims=True
            )
        row = slice(cuts.conv_bias, cuts.conv_bias + 1)
        grad_small_ref[row, :] += jnp.sum(grad_sum, axis=0, keepdims=True)
        return carry

    lax.fori_loop(0, count, first, 0)

    def order(j):
        return j // 2 + lax.rem(j, 2) * (count // 2)

    def second(j, carry):
        b = order(j)
        start = pl.multiple_of(b * rows, rows)
        window = grad_sum_ref[pl.ds(start, rows + 8), :]
        grad_conv = None
        for k in range(kernel):
            tap = small_ref[cuts.taps + k : cuts.taps + k + 1, :]
            term = tap * window[kernel - 1 - k : kernel - 1 - k + rows]
            grad_conv = term if grad_conv is None else grad_conv + term
        grad_conv = grad_conv.astype(jnp.bfloat16)
        grad_conv_ref[pl.ds(start, rows), :] = grad_conv
        relay.part[b] = (
            dot_nn(grad_conv, weights_ref[:, :width])
            + dot_nn(grad_gate_ref[pl.ds(start, rows), :], weights_ref[:, width : 2 * width])
        ).astype(jnp.bfloat16)
        relay.made(b // 2, lax.rem(b, 2))
        return carry

    lax.fori_loop(0, count, second, 0)
    scatter.pass_on()

    decay = slice(cuts.decay, cuts.decay + cuts.state)
    grad_small_ref[cuts.step : cuts.step + cuts.rank, :] = grad_step_ref[...]
    grad_small_ref[decay, :] = -rate_total_ref[...] * jnp.exp(small_ref[decay, :])
    grad_small_ref[cuts.step_bias : cuts.step_bias + 2, :] = scan_rows_ref[0:2, :]
    small_t = grad_small_ref[...].T
    for d in range(lines):
        spread.part[d, :, 3 * width :] = small_t[d * shard : (d + 1) * shard].astype(jnp.bfloat16)
    chunk = width // 3

    def pass_on(j, carry):
        b = order(j)
        relay.pass_on(b // 2, lax.rem(b, 2))
        return carry

    ours_ref[...] = vectors_ref[...]
    for left_ref, right_ref, place_at in (
        (mixer_low_ref, grad_middle_ref, 2 * width),
        (grad_conv_ref, normed_ref, 0),
        (grad_gate_ref, normed_ref, width),
    ):

        def columns(c, carry, left_ref=left_ref, right_ref=right_ref, place_at=place_at):
            here = pl.ds(pl.multiple_of(c * chunk, chunk), chunk)
            there = pl.ds(pl.multiple_of(place_at + c * chunk, chunk), chunk)
            grad = inner_rows(left_ref[...], right_ref[:, here])
            if place_at < 2 * width:
                ours_ref[0:1, here] += jnp.sum(
                    weights_ref[:, there].astype(jnp.float32) * grad, axis=0, keepdims=True
                )
            low = grad.astype(jnp.bfloat16)
            for d in range(lines):
                spread.part[d, :, there] = low[d * shard : (d + 1) * shard]
            return carry

        lax.fori_loop(0, 3, columns, 0)
        if place_at == 2 * width:
            lax.fori_loop(0, count, pass_on, 0)
    for d in range(lines):
        spread.made(d // 2, d % 2)
    scatter.hand_over()

    def sum_over(size, axis, send, recv):
        here = own if axis == "seq" else line

        def copy(k, slot):
            there = lax.rem(here + k, size)
            target = (line, there) if axis == "seq" else (there, own)
            return remote(ours_ref, theirs_ref.at[slot], send.at[k], recv.at[k], *target)

        base = 0 if axis == "seq" else count
        for k in range(1, size):
            copy(k, base + k).start()
        total = ours_ref[...]
        for k in range(1, size):
            copy(k, base + k).wait_recv()
            total = total + theirs_ref[base + k]
        for k in range(1, size):
            copy(k, base + k).wait_send()
        return total

    ours_ref[...] = sum_over(count, "seq", send_v, recv_v)
    for d in range(lines):
        spread.pass_on(d // 2, d % 2)
    totals_ref[...] = sum_over(lines, "dp", send_u, recv_u)
    summed_ref[...] = relay.finish()
    shard_ref[...] = spread.finish()
    scatter.finish(expert_out_ref)


def back(
    count, lines, shard, cuts, grad_selected, small, weights, ext, conv_sum, grad_act, grad_gate,
    mixer_low, normed, grad_middle, grad_step, rate_total, scan_rows, vectors, expert,
):
    length, inner = conv_sum.shape
    width = normed.shape[1]
    columns = weights.shape[1]
    rows = length // count
    vmem = pl.BlockSpec(memory_space=pltpu.VMEM)
    dma = pltpu.SemaphoreType.DMA
    args = (
        grad_selected, small, weights, ext, conv_sum, grad_act, grad_gate, mixer_low, normed,
        grad_middle, grad_step, rate_total, scan_rows, vectors, expert,
    )
    return pl.pallas_call(
        functools.partial(back_kernel, count, lines, cuts),
        in_specs=[vmem] * len(args),
        out_specs=[vmem] * 4,
        out_shape=[
            jax.ShapeDtypeStruct((rows, width), jnp.float32),
            jax.ShapeDtypeStruct((shard, columns), jnp.float32),
            jax.ShapeDtypeStruct(vectors.shape, jnp.float32),
            jax.ShapeDtypeStruct((expert.shape[1], 2 * expert.shape[2]), jnp.float32),
        ],
        scratch_shapes=[
            pltpu.VMEM((length + 8, inner), jnp.float32),
            pltpu.VMEM((length, inner), jnp.bfloat16),
            pltpu.VMEM(small.shape, jnp.float32),
            pltpu.VMEM(vectors.shape, jnp.float32),
            pltpu.VMEM((count + lines, *vectors.shape), jnp.float32),
            dma((count,)), dma((count,)), dma((lines,)), dma((lines,)),
            *scatter_scratch(count, expert.shape[1], expert.shape[2]),
            *relay_scratch(count, rows, width),
            *relay_scratch(lines, shard, columns),
        ],
        compiler_params=pltpu.CompilerParams(
            collective_id=3, has_side_effects=True, vmem_limit_bytes=VMEM_LIMIT
        ),
        cost_estimate=pl.CostEstimate(
            flops=10 * length * width * inner,
            bytes_accessed=30 * length * inner,
            transcendentals=length * inner,
        ),
        name="back",
    )(*args)


SLOTS = 64


def gauss(values):
    return 0.5 * (1.0 + lax.erf(values * math.sqrt(0.5)))


def split_low(values):
    high = values.astype(jnp.bfloat16)
    return high, (values - high.astype(jnp.float32)).astype(jnp.bfloat16)


def experts_kernel(
    count, lines, experts,
    x_ref, mixer_ref, grad_ref, chosen_ref, table_ref, back_table_ref, gain_ref, router_ref,
    up_ref, down_ref,
    output_ref, grad_middle_ref, grad_low_ref, vectors_ref, grad_up_ref, grad_down_ref,
    middle_ref, normed_ref, send_ref, rows_ref, made_ref, got_ref, act_ref, slope_ref, pre_ref,
    send_sem, recv_sem, home_s, home_r,
):
    line, own, _, _ = place()
    q, f, low = square()
    mate = seat_of(q, 1 - f, low)
    copies = lines // experts
    barrier = pltpu.get_barrier_semaphore()
    for d in range(1, lines):
        for where in (own, mate):
            pl.semaphore_signal(
                barrier, inc=1, device_id=(lax.rem(line + d, lines), where), device_id_type=MESH
            )
    pl.semaphore_signal(barrier, inc=1, device_id=(line, mate), device_id_type=MESH)
    pl.semaphore_wait(barrier, 2 * lines - 1)

    peers = [(j, d) for d in range(lines) for j in (1, 0) if (j, d) != (0, 0)]

    def out_copy(what, j, d):
        there = lax.rem(line + d, lines)
        return remote(
            send_ref.at[what, there // copies], rows_ref.at[what, j, line],
            send_sem.at[what, j, d], recv_sem.at[what, j, line],
            there, mate if j else own,
        )

    def arrived(what, j, d):
        from_line = lax.rem(line + d, lines)
        return remote(
            send_ref.at[what, 0], rows_ref.at[what, j, from_line],
            send_sem.at[what, j, d], recv_sem.at[what, j, from_line],
            from_line, mate if j else own,
        )

    def home_copy(what, j, d):
        there = lax.rem(line + d, lines)
        return remote(
            made_ref.at[what, j, there], got_ref.at[what, j, line],
            home_s.at[what, j, d], home_r.at[what, j, line],
            there, mate if j else own,
        )

    def came_home(what, j, d):
        from_line = lax.rem(line + d, lines)
        return remote(
            made_ref.at[what, j, 0], got_ref.at[what, j, from_line],
            home_s.at[what, j, d], home_r.at[what, j, from_line],
            from_line, mate if j else own,
        )

    middle = x_ref[...] + mixer_ref[...]
    middle_ref[...] = middle
    gain = gain_ref[...]
    scale = lax.rsqrt(jnp.mean(middle * middle, axis=1, keepdims=True) + 1e-05)
    normed = (middle * scale * gain).astype(jnp.bfloat16)
    normed_ref[...] = normed
    rows, width = middle.shape
    slots = table_ref.shape[0] // experts

    def dispatch(what, values):
        sent = dot_nn(table_ref[...], values).astype(jnp.bfloat16)
        for e in range(experts):
            send_ref[what, e] = sent[e * slots : (e + 1) * slots]
        for j, d in peers:
            out_copy(what, j, d).start()
        rows_ref[what, 0, line] = send_ref[what, line // copies]

    dispatch(0, normed)
    lane = lax.broadcasted_iota(jnp.int32, (rows, LANES), 1)
    logits = jnp.where(lane < experts, outer_cols(normed, router_ref[...]), -jnp.inf)
    grown = jnp.exp(logits - jnp.max(logits, axis=1, keepdims=True))
    probs = grown / jnp.sum(grown, axis=1, keepdims=True)
    chosen = chosen_ref[...]
    gate = jnp.sum(chosen * probs, axis=1, keepdims=True)
    dispatch(1, (gate * grad_ref[...]).astype(jnp.bfloat16))

    total = 2 * lines * slots
    hidden = up_ref.shape[1]
    chunk = hidden // 3 if hidden % (3 * LANES) == 0 else hidden
    parts = hidden // chunk

    def rows_of(ref, what):
        return ref[what].reshape(total, width)

    def columns(c):
        return pl.ds(pl.multiple_of(c * chunk, LANES), chunk)

    for j, d in peers:
        arrived(0, j, d).wait_recv()

    def rise(c, carry):
        pre_ref[:, columns(c)] = dot_nn(rows_of(rows_ref, 0), up_ref[:, columns(c)])
        pre = pre_ref[:, columns(c)]
        half = gauss(pre)
        act_ref[:, columns(c)] = (pre * half).astype(jnp.bfloat16)
        pre_ref[:, columns(c)] = half + pre * (
            jnp.exp(-0.5 * pre * pre) * (1.0 / math.sqrt(2.0 * math.pi))
        )
        return carry

    lax.fori_loop(0, parts, rise, 0)

    wide = width // 3

    def send_home(what, left_ref, right_ref):
        def make(c, carry):
            here = pl.ds(pl.multiple_of(c * wide, LANES), wide)
            there = pl.ds(pl.multiple_of(c * wide, LANES), wide)
            made = outer_cols(left_ref[...], right_ref[there, :]).astype(jnp.bfloat16)
            made_ref[what, :, :, :, here] = made.reshape(2, lines, slots, wide)
            return carry

        lax.fori_loop(0, 3, make, 0)
        for j, d in peers:
            home_copy(what, j, d).start()
        got_ref[what, 0, line] = made_ref[what, 0, line]

    for j, d in peers:
        arrived(1, j, d).wait_recv()

    def fall(c, carry):
        slope_ref[:, columns(c)] = (
            dot_nn(rows_of(rows_ref, 1), down_ref[:, columns(c)]) * pre_ref[:, columns(c)]
        ).astype(jnp.bfloat16)
        return carry

    lax.fori_loop(0, parts, fall, 0)
    send_home(1, slope_ref, up_ref)
    send_home(0, act_ref, down_ref)

    pieces = grad_up_ref.shape[1]

    def weigh(c, carry):
        up = inner_rows(rows_of(rows_ref, 0), slope_ref[:, columns(c)]).astype(jnp.bfloat16)
        down = inner_rows(rows_of(rows_ref, 1), act_ref[:, columns(c)]).astype(jnp.bfloat16)
        grad_up_ref[:, :, columns(c)] = up.reshape(count, pieces, chunk)
        grad_down_ref[:, :, columns(c)] = down.reshape(count, pieces, chunk)
        return carry

    lax.fori_loop(0, parts, weigh, 0)

    def home(what):
        for j, d in peers:
            came_home(what, j, d).wait_recv()
        both = None
        for e in range(experts):
            own_rows = None
            for c in range(copies):
                for j in range(2):
                    term = got_ref[what, j, e * copies + c].astype(jnp.float32)
                    own_rows = term if own_rows is None else own_rows + term
            high, rest = split_low(own_rows)
            here = back_table_ref[e]
            term = dot_nn(here, high) + dot_nn(here, rest)
            both = term if both is None else both + term
        return both

    grad = grad_ref[...]
    middle = middle_ref[...]
    picked = home(0)
    output_ref[...] = middle + gate * picked
    grad_gate = jnp.sum(grad * picked, axis=1, keepdims=True)
    grad_logits = gate * (chosen - probs) * grad_gate
    grad_normed = home(1) + dot_nn(grad_logits, router_ref[...].astype(jnp.float32), HIGHEST)
    scaled = gain * grad_normed
    grad_middle = (
        grad
        + scale * scaled
        - middle * (scale * scale * scale) * jnp.mean(scaled * middle, axis=1, keepdims=True)
    )
    grad_middle_ref[...] = grad_middle
    grad_low_ref[...] = grad_middle.astype(jnp.bfloat16)
    vectors_ref[...] = jnp.zeros_like(vectors_ref)
    vectors_ref[1:2, :] = jnp.sum(grad_normed * middle * scale, axis=0, keepdims=True)
    vectors_ref[2 : 2 + experts, :] = inner_rows(
        grad_logits, normed_ref[...].astype(jnp.float32), HIGHEST
    )[:experts]
    for what in range(2):
        for j, d in peers:
            out_copy(what, j, d).wait_send()
            home_copy(what, j, d).wait_send()


def run_experts(
    count, lines, experts, x, mixer, grad, chosen, table, back_table, gain, router, up, down
):
    rows, width = x.shape
    slots = table.shape[0] // experts
    total = 2 * lines * slots
    hidden = up.shape[1]
    pieces = (count, up.shape[0] // count, hidden)
    vmem = pl.BlockSpec(memory_space=pltpu.VMEM)
    dma = pltpu.SemaphoreType.DMA
    args = (x, mixer, grad, chosen, table, back_table, gain, router, up, down)
    low = jnp.bfloat16
    return pl.pallas_call(
        functools.partial(experts_kernel, count, lines, experts),
        in_specs=[vmem] * len(args),
        out_specs=[vmem] * 6,
        out_shape=[
            jax.ShapeDtypeStruct((rows, width), jnp.float32),
            jax.ShapeDtypeStruct((rows, width), jnp.float32),
            jax.ShapeDtypeStruct((rows, width), low),
            jax.ShapeDtypeStruct((8, width), jnp.float32),
            jax.ShapeDtypeStruct(pieces, low),
            jax.ShapeDtypeStruct(pieces, low),
        ],
        scratch_shapes=[
            pltpu.VMEM((rows, width), jnp.float32),
            pltpu.VMEM((rows, width), low),
            pltpu.VMEM((2, experts, slots, width), low),
            pltpu.VMEM((2, 2, lines, slots, width), low),
            pltpu.VMEM((2, 2, lines, slots, width), low),
            pltpu.VMEM((2, 2, lines, slots, width), low),
            pltpu.VMEM((total, hidden), low),
            pltpu.VMEM((total, hidden), low),
            pltpu.VMEM((total, hidden), jnp.float32),
            dma((2, 2, lines)), dma((2, 2, lines)), dma((2, 2, lines)), dma((2, 2, lines)),
        ],
        compiler_params=pltpu.CompilerParams(
            collective_id=4, has_side_effects=True, vmem_limit_bytes=VMEM_LIMIT
        ),
        cost_estimate=pl.CostEstimate(
            flops=12 * total * width * hidden,
            bytes_accessed=8 * width * hidden,
            transcendentals=2 * total * hidden,
        ),
        name="experts",
    )(*args)


def body(
    tokens,
    cotangent,
    routes,
    mixer_gain,
    input_proj,
    conv_weight,
    conv_bias,
    select_proj,
    step_proj,
    step_bias,
    decay_log,
    skip_gain,
    output_proj,
    expert_gain,
    router,
    expert_up,
    expert_down,
):
    rows = tokens.shape[1]
    width = tokens.shape[2]
    shard = input_proj.shape[2]
    rank = step_proj.shape[0]
    state = decay_log.shape[0]
    kernel = conv_weight.shape[0]
    picks = select_proj.shape[0]
    count = lax.axis_size("seq")
    lines = lax.axis_size("dp")
    shard_rows = -(-shard // 16) * 16
    cuts = Cuts(picks, rank, state, kernel)

    x_in = tokens.reshape(rows, width)
    gain_one = mixer_gain.astype(jnp.float32)
    normed = rms_norm(x_in, gain_one).astype(jnp.bfloat16)

    small = jnp.concatenate(
        [
            select_proj,
            step_proj,
            decay_log,
            conv_weight,
            conv_bias[None, :],
            step_bias[None, :],
            skip_gain[None, :],
        ],
        axis=0,
    )
    small_pad = -(-cuts.rows // LANES) * LANES
    small = jnp.pad(small, ((0, small_pad - cuts.rows), (0, 0)))
    packed = jnp.concatenate(
        [input_proj.reshape(2 * width, shard).T, output_proj, small.T], axis=1
    )
    packed = jnp.pad(packed, ((0, shard_rows - shard), (0, 0)))
    (normed_all, weights, small_all, conv_ext, conv_sum, conv_act, gate_branch, selected, up_cut) = (
        front(count, lines, cuts, normed, packed, expert_up)
    )
    pre, mixed, mixer_low, priors, end, mixer_out, down_cut = scan_forward(
        count, cuts, width, conv_act, gate_branch, selected, small_all, weights, expert_down.T
    )

    experts = router.shape[0]
    route = routes.reshape(rows)
    chosen = (route[:, None] == lax.broadcasted_iota(jnp.int32, (rows, LANES), 1)).astype(
        jnp.float32
    )
    earlier = (
        lax.broadcasted_iota(jnp.int32, (rows, rows), 0)
        > lax.broadcasted_iota(jnp.int32, (rows, rows), 1)
    ).astype(jnp.float32)
    before = jnp.dot(earlier, chosen, precision=HIGHEST)
    position = jnp.sum(before * chosen, axis=1).astype(jnp.int32)
    slot = route * SLOTS + position
    table = (
        slot[None, :] == lax.broadcasted_iota(jnp.int32, (experts * SLOTS, rows), 0)
    ).astype(jnp.bfloat16)
    back_table = (
        slot[None, :, None]
        == lax.broadcasted_iota(jnp.int32, (experts, rows, SLOTS), 2)
        + SLOTS * lax.broadcasted_iota(jnp.int32, (experts, rows, SLOTS), 0)
    ).astype(jnp.bfloat16)
    output, grad_middle, grad_middle_low, vectors, grad_up_low, grad_down_low = run_experts(
        count,
        lines,
        experts,
        x_in,
        mixer_out,
        cotangent.reshape(rows, width),
        chosen,
        table,
        back_table,
        expert_gain.astype(jnp.float32)[None],
        jnp.pad(router, ((0, LANES - experts), (0, 0))),
        up_cut.reshape(-1, up_cut.shape[2]),
        down_cut.reshape(-1, down_cut.shape[2]),
    )

    (grad_gate_branch, grad_act, grad_step_w, rate_total, scan_rows, grad_selected, grad_middle_all,
     grad_down_t) = (
        scan_backward(
            count, cuts, grad_middle_low, conv_act, gate_branch, mixed, pre, selected, small_all,
            weights, priors, end, grad_down_low,
        )
    )
    grad_normed, grad_shard, totals, grad_up = back(
        count, lines, shard_rows, cuts, grad_selected, small_all, weights, conv_ext, conv_sum,
        grad_act, grad_gate_branch, mixer_low, normed_all.reshape(-1, width),
        grad_middle_all.reshape(-1, width), grad_step_w, rate_total, scan_rows, vectors,
        grad_up_low,
    )
    grad_shard = grad_shard[:shard]
    grad_input_w = grad_shard[:, : 2 * width].T.reshape(2, width, shard)
    small_shard = grad_shard[:, 3 * width :].T
    cut = 0
    small_grads = []
    for number in (picks, rank, state, kernel, 1, 1, 1):
        small_grads.append(small_shard[cut : cut + number])
        cut += number
    unused_one, pull_one = jax.vjp(lambda v: rms_norm(v, gain_one), x_in)
    grad_tokens = grad_middle + pull_one(grad_normed)[0]
    return (
        output.reshape(tokens.shape),
        grad_tokens.reshape(tokens.shape),
        totals[0] / gain_one,
        grad_input_w,
        small_grads[3],
        small_grads[4].reshape(shard),
        small_grads[0],
        small_grads[1],
        small_grads[5].reshape(shard),
        small_grads[2],
        small_grads[6].reshape(shard),
        grad_shard[:, 2 * width : 3 * width],
        totals[1],
        totals[2 : 2 + experts],
        grad_up,
        grad_down_t.T,
    )


def solution(mesh):
    both = ("dp", "seq")
    placed = (
        P("dp", "seq", None),
        P("dp", "seq", None),
        P("dp", "seq", None),
        P(),
        P(None, None, both),
        P(None, both),
        P(both),
        P(None, both),
        P(None, both),
        P(both),
        P(None, both),
        P(both),
        P(both, None),
        P(),
        P(),
        P("seq", "dp"),
        P("dp", "seq"),
    )
    return jax.shard_map(
        body,
        mesh=mesh,
        in_specs=placed,
        out_specs=(
            P("dp", "seq", None),
            P("dp", "seq", None),
            P(),
            P(None, None, both),
            P(None, both),
            P(both),
            P(None, both),
            P(None, both),
            P(both),
            P(None, both),
            P(both),
            P(both, None),
            P(),
            P(),
            P("seq", "dp"),
            P("dp", "seq"),
        ),
        check_vma=False,
    )
```

```python
import functools
import math

import jax
import jax.numpy as jnp
from jax import lax
from jax.experimental import pallas as pl
from jax.experimental.pallas import tpu as pltpu
from jax.sharding import PartitionSpec as P

CAP = 56
LANES = 128
TIME_BLOCK = 128
LOG2E = math.log2(math.e)

HIGHEST = lax.Precision.HIGHEST


def rms_norm(values, gain):
    return values * lax.rsqrt(jnp.mean(values * values, axis=-1, keepdims=True) + 1e-05) * gain


def inner_rows(left, right, precision=None):
    return lax.dot_general(
        left,
        right,
        (((0,), (0,)), ((), ())),
        precision=precision,
        preferred_element_type=jnp.float32,
    )


def outer_cols(left, right, precision=None):
    return lax.dot_general(
        left,
        right,
        (((1,), (1,)), ((), ())),
        precision=precision,
        preferred_element_type=jnp.float32,
    )


def sublane_sums(parts):
    row = lax.broadcasted_iota(jnp.int32, parts[0].shape, 0)
    low4 = row < 4
    low2 = (row % 4) < 2
    low1 = (row % 2) < 1
    quads = []
    for k in range(4):
        a, b = parts[k], parts[k + 4]
        quads.append(jnp.where(low4, a, b) + pltpu.roll(jnp.where(low4, b, a), 4, 0))
    pairs = []
    for k in range(2):
        a, b = quads[k], quads[k + 2]
        pairs.append(
            jnp.where(low2, a, b) + jnp.where(low2, pltpu.roll(a, 6, 0), pltpu.roll(b, 2, 0))
        )
    a, b = pairs
    return jnp.where(low1, a, b) + jnp.where(low1, pltpu.roll(a, 7, 0), pltpu.roll(b, 1, 0))


MESH = pl.DeviceIdType.MESH
VMEM_LIMIT = 60 * 1024 * 1024


def dot_nn(left, right, precision=None):
    return lax.dot_general(
        left, right, (((1,), (0,)), ((), ())), precision=precision,
        preferred_element_type=jnp.float32,
    )


def place():
    own, line = lax.axis_index("seq"), lax.axis_index("dp")
    return line, own, own // 2, lax.rem(own, 2)


def remote(source, target, send_sem, recv_sem, line, position):
    return pltpu.make_async_remote_copy(
        src_ref=source,
        dst_ref=target,
        send_sem=send_sem,
        recv_sem=recv_sem,
        device_id=(line, position),
        device_id_type=MESH,
    )


def greet(count, lines=1):
    line, own, _, _ = place()
    barrier = pltpu.get_barrier_semaphore()
    for k in range(1, count):
        pl.semaphore_signal(
            barrier, inc=1, device_id=(line, lax.rem(own + k, count)), device_id_type=MESH
        )
    for k in range(1, lines):
        pl.semaphore_signal(
            barrier, inc=1, device_id=(lax.rem(line + k, lines), own), device_id_type=MESH
        )
    pl.semaphore_wait(barrier, count - 1 + lines - 1)


def sigmoid(values):
    return 1.0 / (1.0 + jnp.exp(-values))


def softplus(values):
    return jnp.maximum(values, 0.0) + jnp.log1p(jnp.exp(-jnp.abs(values)))


class Cuts:
    def __init__(self, picks, rank, state, kernel):
        self.picks, self.rank, self.state, self.kernel = picks, rank, state, kernel
        self.step = picks
        self.decay = self.step + rank
        self.taps = self.decay + state
        self.conv_bias = self.taps + kernel
        self.step_bias = self.conv_bias + 1
        self.skip = self.step_bias + 1
        self.rows = self.skip + 1
        self.sent = -(-picks // 16) * 16


class Relay:
    def __init__(self, axis, half, high, low, seat, block, refs):
        self.axis, self.half, self.high, self.low = axis, half, high, low
        self.seat, self.block = seat, block
        self.other = lax.axis_index("dp" if axis == "seq" else "seq")
        self.part, self.across, self.along = refs[:3]
        self.send_x, self.recv_x, self.send_hi, self.recv_hi = refs[3:]

    def remote(self, source, target, send_sem, recv_sem, position):
        if self.axis == "seq":
            return remote(source, target, send_sem, recv_sem, self.other, position)
        return remote(source, target, send_sem, recv_sem, position, self.other)

    def over(self, i, low):
        return self.remote(
            self.part.at[self.block(i, low)], self.across.at[i], self.send_x.at[i],
            self.recv_x.at[i], self.seat(self.high, 1 - self.low),
        )

    def on(self, i):
        k = lax.rem(i - self.high + self.half, self.half)
        return self.remote(
            self.across.at[i], self.along.at[k], self.send_hi.at[k], self.recv_hi.at[k],
            self.seat(i, self.low),
        )

    def made(self, i, low):
        @pl.when(low != self.low)
        def _():
            self.over(i, low).start()

    def summed(self, i):
        self.over(i, self.low).wait_recv()
        return self.part[self.block(i, self.low)].astype(jnp.float32) + self.across[i].astype(
            jnp.float32
        )

    def pass_on(self, i, low):
        @pl.when((low == self.low) & (i != self.high))
        def _():
            self.across[i] = self.summed(i).astype(jnp.bfloat16)
            self.on(i).start()

    def finish(self):
        total = self.summed(self.high)
        for k in range(1, self.half):
            self.on(lax.rem(self.high + k, self.half)).wait_recv()
            total = total + self.along[k].astype(jnp.float32)
        for i in range(self.half):
            self.over(i, 1 - self.low).wait_send()
        for k in range(1, self.half):
            self.on(lax.rem(self.high + k, self.half)).wait_send()
        return total


def whole_relay(axis, count, refs):
    own = lax.axis_index(axis)

    def seat(i, low):
        return 2 * i + low

    return Relay(axis, count // 2, own // 2, lax.rem(own, 2), seat, seat, refs)


def relay_scratch(count, rows, width, part=True):
    half = count // 2
    dma = pltpu.SemaphoreType.DMA
    own = [pltpu.VMEM((count, rows, width), jnp.bfloat16)] if part else []
    return own + [
        pltpu.VMEM((half, rows, width), jnp.bfloat16),
        pltpu.VMEM((half, rows, width), jnp.bfloat16),
        dma((half,)), dma((half,)), dma((half,)), dma((half,)),
    ]


def square():
    own = lax.axis_index("seq")
    return own // 4, lax.rem(own // 2, 2), lax.rem(own, 2)


def seat_of(q, f, low):
    return 4 * q + 2 * f + low


class Gather:
    def __init__(self, count, shard_ref, land_ref, swap_s, swap_r, line_s, line_r, pair_s, pair_r):
        self.line = lax.axis_index("dp")
        self.q, self.f, self.low = square()
        self.quarter = count // 4
        self.shard, self.land = shard_ref, land_ref
        self.swap_s, self.swap_r = swap_s, swap_r
        self.line_s, self.line_r, self.pair_s, self.pair_r = line_s, line_r, pair_s, pair_r
        self.cut = land_ref.shape[2]

    def columns(self, f):
        return pl.ds(pl.multiple_of(f * self.cut, LANES), self.cut)

    def piece(self, j, k, low):
        q = lax.rem(self.q - k + self.quarter, self.quarter)
        return seat_of(q, lax.rem(self.f + j, 2), low)

    def swap(self):
        own = self.piece(0, 0, self.low)
        return remote(
            self.shard.at[:, self.columns(1 - self.f)], self.land.at[own], self.swap_s, self.swap_r,
            self.line, self.piece(1, 0, self.low),
        )

    def along(self, j, k):
        piece = self.piece(j, 0, self.low)
        there = seat_of(lax.rem(self.q + k, self.quarter), self.f, self.low)
        return remote(
            self.land.at[piece], self.land.at[piece], self.line_s.at[j, k], self.line_r.at[j, k],
            self.line, there,
        )

    def pair(self, j, k, low):
        piece = self.piece(j, k, low)
        return remote(
            self.land.at[piece], self.land.at[piece], self.pair_s.at[j, k], self.pair_r.at[j, k],
            self.line, seat_of(self.q, self.f, 1 - self.low),
        )

    def start(self):
        self.swap().start()
        self.land[self.piece(0, 0, self.low)] = self.shard[:, self.columns(self.f)]

    def spread(self, j):
        if j == 1:
            mate = self.piece(1, 0, self.low)
            remote(
                self.land.at[mate], self.land.at[mate], self.swap_s, self.swap_r, self.line, mate
            ).wait_recv()
        for k in range(1, self.quarter):
            self.along(j, k).start()
        self.pair(j, 0, self.low).start()

    def forward(self, j):
        for k in range(1, self.quarter):
            piece = self.piece(j, k, self.low)
            remote(
                self.land.at[piece], self.land.at[piece], self.line_s.at[j, k],
                self.line_r.at[j, k], self.line, piece,
            ).wait_recv()
            self.pair(j, k, self.low).start()

    def finish(self):
        for j in range(2):
            for k in range(self.quarter):
                self.pair(j, k, 1 - self.low).wait_recv()
        self.swap().wait_send()
        for j in range(2):
            for k in range(1, self.quarter):
                self.along(j, k).wait_send()
            for k in range(self.quarter):
                self.pair(j, k, self.low).wait_send()


def gather_scratch(count):
    dma = pltpu.SemaphoreType.DMA
    quarter = count // 4
    return [dma, dma] + [dma((2, quarter)) for _ in range(4)]


class Scatter:
    def __init__(self, count, part_ref, other_ref, held_ref, swap_s, swap_r, refs):
        self.line = lax.axis_index("dp")
        self.q, self.f, self.low = square()
        self.quarter = count // 4
        self.other, self.held = other_ref, held_ref
        self.swap_s, self.swap_r = swap_s, swap_r
        self.relays = []
        for j in range(2):
            cut = lax.rem(self.f + j, 2)

            def seat(i, low):
                return seat_of(i, self.f, low)

            def block(i, low, cut=cut):
                return seat_of(i, cut, low)

            mine = tuple(ref.at[j] for ref in refs)
            self.relays.append(
                Relay("seq", self.quarter, self.q, self.low, seat, block, (part_ref, *mine))
            )

    def swap(self):
        return remote(
            self.held, self.other, self.swap_s, self.swap_r, self.line,
            seat_of(self.q, 1 - self.f, self.low),
        )

    def turns(self):
        far = [(j, lax.rem(self.q + k, self.quarter)) for k in range(1, self.quarter) for j in (1, 0)]
        return far + [(1, self.q), (0, self.q)]

    def send(self, turn):
        j, i = self.turns()[turn]
        self.relays[j].over(i, 1 - self.low).start()

    def pass_on(self, turn):
        j, i = self.turns()[turn]
        self.relays[j].pass_on(i, self.low)

    def send_far(self):
        for turn in range(2 * self.quarter - 2):
            self.send(turn)

    def pass_far(self):
        for turn in range(2 * self.quarter - 2):
            self.pass_on(turn)

    def send_near(self):
        self.send(2 * self.quarter - 2)
        self.send(2 * self.quarter - 1)

    def hand_over(self):
        self.held[...] = self.relays[1].finish().astype(jnp.bfloat16)
        self.swap().start()

    def finish(self, out_ref):
        cut = self.held.shape[1]
        out_ref[:, pl.ds(pl.multiple_of(self.f * cut, LANES), cut)] = self.relays[0].finish()
        self.swap().wait_recv()
        out_ref[:, pl.ds(pl.multiple_of((1 - self.f) * cut, LANES), cut)] = self.other[...].astype(
            jnp.float32
        )
        self.swap().wait_send()


def scatter_scratch(count, rows, cut):
    dma = pltpu.SemaphoreType.DMA
    quarter = count // 4
    return [
        pltpu.VMEM((rows, cut), jnp.bfloat16),
        pltpu.VMEM((rows, cut), jnp.bfloat16),
        dma, dma,
        pltpu.VMEM((2, quarter, rows, cut), jnp.bfloat16),
        pltpu.VMEM((2, quarter, rows, cut), jnp.bfloat16),
        *[dma((2, quarter)) for _ in range(4)],
    ]


def front_kernel(
    count, lines, cuts,
    normed_ref, packed_ref, expert_ref,
    all_ref, weights_ref, small_ref, ext_ref, sum_ref, act_ref, gate_ref, selected_ref, land_ref,
    part_ref, partial_ref, total_ref,
    send_w, recv_w, send_up, send_down, recv_hi, send_x, recv_x, send_rs, recv_rs, send_ag, recv_ag,
    *gather_refs,
):
    line, own, high, low = place()
    half = count // 2
    gather = Gather(count, expert_ref, land_ref, *gather_refs)
    rows, width = normed_ref.shape
    shard = packed_ref.shape[0]
    inner = weights_ref.shape[0]
    kernel = cuts.kernel
    partner = 2 * high + 1 - low
    greet(count, lines)

    copies = []
    shard_rows = pl.ds(pl.multiple_of(line * shard, 16), shard)
    def step_on(i, up):
        block = 2 * i + low
        return remote(
            all_ref.at[block], all_ref.at[block], (send_up if up else send_down).at[i],
            recv_hi.at[i], line, 2 * (high + (1 if up else -1)) + low,
        )

    def can_go(up):
        return high < half - 1 if up else high > 0

    all_ref[own] = normed_ref[...]
    for up in (True, False):

        @pl.when(can_go(up))
        def _(up=up):
            step_on(high, up).start()

    remote(all_ref.at[own], all_ref.at[own], send_x.at[high], recv_x.at[high], line, partner).start()
    for k in range(1, lines):
        copy = remote(
            packed_ref, weights_ref.at[shard_rows], send_w.at[k], recv_w.at[k],
            lax.rem(line + k, lines), own,
        )
        copy.start()
        copies.append(copy)
    gather.start()
    weights_ref[shard_rows, :] = packed_ref[...]
    if lines * shard < inner:
        weights_ref[lines * shard :, :] = jnp.zeros(
            (inner - lines * shard, weights_ref.shape[1]), weights_ref.dtype
        )
    ext_ref[0:8, :] = jnp.zeros((8, inner), jnp.float32)
    def cross(i):
        block = 2 * i + low
        return remote(
            all_ref.at[block], all_ref.at[block], send_x.at[i], recv_x.at[i], line, partner
        )

    for k in range(1, half):
        for up in (True, False):
            i = high - k if up else high + k

            @pl.when(i >= 0 if up else i < half)
            def _(i=i, up=up):
                step_on(i, up).wait_recv()

                @pl.when(can_go(up))
                def _():
                    step_on(i, up).start()

                cross(i).start()

    gather.spread(0)
    gather.spread(1)
    for k in range(1, lines):
        from_line = lax.rem(line - k + lines, lines)
        there = pl.ds(pl.multiple_of(from_line * shard, 16), shard)
        remote(
            packed_ref, weights_ref.at[there], send_w.at[k], recv_w.at[k], from_line, own
        ).wait_recv()
    small_ref[...] = weights_ref[:, 3 * width :].astype(jnp.float32).T
    for i in range(half):
        block = 2 * i + 1 - low
        remote(
            all_ref.at[block], all_ref.at[block], send_x.at[i], recv_x.at[i], line, partner
        ).wait_recv()

    def project(b, carry):
        start = pl.multiple_of(b * rows, rows)
        block = all_ref[b]
        ext_ref[pl.ds(pl.multiple_of(start + 8, 8), rows), :] = outer_cols(
            block, weights_ref[:, :width]
        )
        gate_ref[pl.ds(start, rows), :] = outer_cols(block, weights_ref[:, width : 2 * width])
        return carry

    lax.fori_loop(0, count, project, 0)

    def convolve(b, carry):
        start = pl.multiple_of(b * rows, rows)
        window = ext_ref[pl.ds(start, rows + 8), :]
        total = small_ref[cuts.conv_bias : cuts.conv_bias + 1, :]
        for k in range(kernel):
            tap = small_ref[cuts.taps + k : cuts.taps + k + 1, :]
            total = total + tap * window[9 - kernel + k : 9 - kernel + k + rows]
        act = total * sigmoid(total)
        sum_ref[pl.ds(start, rows), :] = total
        act_ref[pl.ds(start, rows), :] = act
        part_ref[b] = outer_cols(
            small_ref[: cuts.sent, :].astype(jnp.bfloat16), act.astype(jnp.bfloat16)
        ).astype(jnp.bfloat16)
        return carry

    lax.fori_loop(0, count, convolve, 0)

    for k in range(1, count):
        there = lax.rem(own + k, count)
        copy = remote(
            part_ref.at[there], partial_ref.at[k], send_rs.at[k], recv_rs.at[k], line, there
        )
        copy.start()
        copies.append(copy)
    total = part_ref[own].astype(jnp.float32)
    for k in range(1, count):
        remote(
            part_ref.at[own], partial_ref.at[k], send_rs.at[k], recv_rs.at[k], line, partner
        ).wait_recv()
        total = total + partial_ref[k].astype(jnp.float32)
    total_ref[own] = total.astype(jnp.bfloat16)
    for k in range(1, count):
        copy = remote(
            total_ref.at[own], total_ref.at[own], send_ag.at[k], recv_ag.at[k],
            line, lax.rem(own + k, count),
        )
        copy.start()
        copies.append(copy)
    gather.forward(0)
    gather.forward(1)
    for k in range(1, count):
        block = lax.rem(own - k + count, count)
        remote(
            total_ref.at[block], total_ref.at[block], send_ag.at[k], recv_ag.at[k],
            line, partner,
        ).wait_recv()
    selected_ref[...] = total_ref[...].astype(jnp.float32)[:, : cuts.picks]
    for copy in copies:
        copy.wait_send()
    for i in range(half):
        cross(i).wait_send()
        for up in (True, False):

            @pl.when(can_go(up) & (i <= high if up else i >= high))
            def _(i=i, up=up):
                step_on(i, up).wait_send()

    gather.finish()


def front(count, lines, cuts, normed, packed, expert):
    rows, width = normed.shape
    shard, columns = packed.shape
    inner = -(-lines * shard // LANES) * LANES
    length = count * rows
    half = count // 2
    small = columns - 3 * width
    vmem = pl.BlockSpec(memory_space=pltpu.VMEM)

    def f32(*shape):
        return jax.ShapeDtypeStruct(shape, jnp.float32)

    dma = pltpu.SemaphoreType.DMA
    return pl.pallas_call(
        functools.partial(front_kernel, count, lines, cuts),
        in_specs=[vmem] * 3,
        out_specs=[vmem] * 9,
        out_shape=[
            jax.ShapeDtypeStruct((count, rows, width), jnp.bfloat16),
            jax.ShapeDtypeStruct((inner, columns), jnp.bfloat16),
            f32(small, inner),
            f32(length + 8, inner),
            f32(length, inner),
            f32(length, inner),
            f32(length, inner),
            f32(count, cuts.picks, rows),
            jax.ShapeDtypeStruct((count, expert.shape[0], expert.shape[1] // 2), jnp.bfloat16),
        ],
        scratch_shapes=[
            *[pltpu.VMEM((count, cuts.sent, rows), jnp.bfloat16)] * 3,
            dma((lines,)), dma((lines,)), dma((half,)), dma((half,)), dma((half,)), dma((half,)),
            dma((half,)), dma((count,)), dma((count,)), dma((count,)), dma((count,)),
            *gather_scratch(count),
        ],
        compiler_params=pltpu.CompilerParams(
            collective_id=0, has_side_effects=True, vmem_limit_bytes=VMEM_LIMIT
        ),
        cost_estimate=pl.CostEstimate(
            flops=4 * length * width * inner,
            bytes_accessed=20 * length * inner,
            transcendentals=length * inner,
        ),
        name="front",
    )(normed, packed, expert)


def spread_lanes(values, wide_ref, out_ref):
    state, steps = values.shape
    high = values.astype(jnp.bfloat16).astype(jnp.float32)
    rest = values - high
    lane = lax.broadcasted_iota(jnp.int32, (state, steps), 1)

    def fill(g, carry):
        for k in range(8):
            t = g * 8 + k
            here = pl.ds(pl.multiple_of(t * state, state), state)
            mask = lane == t
            wide_ref[here, :steps] = jnp.where(mask, high, 0.0).astype(jnp.bfloat16)
            wide_ref[here, steps:] = jnp.where(mask, rest, 0.0).astype(jnp.bfloat16)
        return carry

    lax.fori_loop(0, steps // 8, fill, 0)
    ones = jnp.ones((2 * steps, LANES), jnp.bfloat16)
    out_ref[...] = dot_nn(wide_ref[...], ones)


def scan_forward_kernel(
    count, cuts,
    act_ref, gate_ref, selected_ref, small_ref, output_ref, expert_ref,
    pre_ref, mixed_ref, mixer_low_ref, prior_ref, end_ref, summed_ref, expert_out_ref,
    state_ref, delta_ref, scanned_ref, wide_ref, wide_in_ref, wide_out_ref, land_ref, *refs,
):
    steps, inner = act_ref.shape
    tiles = inner // LANES
    state = cuts.state
    halves = state // 8
    step = pl.program_id(0)
    relay = whole_relay("seq", count, refs[:7])
    gather = Gather(count, expert_ref, land_ref, *refs[7:])

    @pl.when(step == 0)
    def _():
        greet(count)
        gather.start()
        state_ref[...] = jnp.zeros_like(state_ref)

    @pl.when(step == 0)
    def _():
        gather.spread(0)

    @pl.when(step == 3)
    def _():
        gather.spread(1)

    rates2 = -LOG2E * jnp.exp(small_ref[cuts.decay : cuts.decay + state, :])
    pre = inner_rows(
        selected_ref[0, : cuts.rank, :],
        small_ref[cuts.step : cuts.step + cuts.rank, :],
        HIGHEST,
    ) + small_ref[cuts.step_bias : cuts.step_bias + 1, :]
    pre_ref[...] = pre
    delta_ref[...] = softplus(pre)
    in_rows = cuts.rank
    out_rows = cuts.rank + state
    spread_lanes(selected_ref[0, in_rows : in_rows + state, :], wide_ref, wide_in_ref)
    spread_lanes(selected_ref[0, out_rows : out_rows + state, :], wide_ref, wide_out_ref)

    def group(g, states):
        states = [list(s) for s in states]
        base = pl.multiple_of(g * 8, 8)
        d8 = delta_ref[pl.ds(base, 8), :]
        du8 = d8 * act_ref[pl.ds(base, 8), :]
        parts = [[None] * 8 for _ in range(tiles)]
        for k in range(8):
            rows_now = [pl.ds((base + k) * state + 8 * i, 8) for i in range(halves)]
            b_now = [wide_in_ref[here, :] for here in rows_now]
            c_now = [wide_out_ref[here, :] for here in rows_now]
            for j in range(tiles):
                cols = slice(j * LANES, (j + 1) * LANES)
                d = jnp.broadcast_to(d8[k : k + 1, cols], (8, LANES))
                du = jnp.broadcast_to(du8[k : k + 1, cols], (8, LANES))
                total = None
                for i in range(halves):
                    old = states[j][i]
                    prior_ref[base + k, 8 * i : 8 * i + 8, cols] = old
                    new = jnp.exp2(d * rates2[8 * i : 8 * i + 8, cols]) * old + b_now[i] * du
                    states[j][i] = new
                    term = c_now[i] * new
                    total = term if total is None else total + term
                parts[j][k] = total
        for j in range(tiles):
            scanned_ref[pl.ds(base, 8), j * LANES : (j + 1) * LANES] = sublane_sums(parts[j])
        return tuple(tuple(s) for s in states)

    first = tuple(
        tuple(
            state_ref[8 * i : 8 * i + 8, j * LANES : (j + 1) * LANES] for i in range(halves)
        )
        for j in range(tiles)
    )
    last = lax.fori_loop(0, steps // 8, group, first)
    for j in range(tiles):
        for i in range(halves):
            state_ref[8 * i : 8 * i + 8, j * LANES : (j + 1) * LANES] = last[j][i]
    end_ref[...] = state_ref[...]

    mixed = scanned_ref[...] + small_ref[cuts.skip : cuts.skip + 1, :] * act_ref[...]
    gate = gate_ref[...]
    low = (mixed * (gate * sigmoid(gate))).astype(jnp.bfloat16)
    mixed_ref[...] = mixed
    mixer_low_ref[...] = low
    relay.part[step] = dot_nn(low, output_ref[...]).astype(jnp.bfloat16)
    relay.made(step // 2, lax.rem(step, 2))

    def pass_on(block):
        relay.pass_on(block // 2, lax.rem(block, 2))

    @pl.when(step >= LAG)
    def _():
        pass_on(step - LAG)

    @pl.when(step == count - 1)
    def _():
        for late in range(LAG - 1, -1, -1):
            pass_on(step - late)
        gather.forward(0)
        gather.forward(1)
        summed_ref[...] = relay.finish()
        gather.finish()
        expert_out_ref[...] = land_ref[...]


def scan_forward(count, cuts, width, act, gate, selected, small, weights, expert):
    length, inner = act.shape
    state = cuts.state
    block = length // count
    rows = pl.BlockSpec((block, inner), lambda t: (t, 0))
    whole = pl.BlockSpec((state, inner), lambda t: (0, 0))
    pieces = (count, expert.shape[0], expert.shape[1] // 2)
    return pl.pallas_call(
        functools.partial(scan_forward_kernel, count, cuts),
        grid=(count,),
        in_specs=[
            rows,
            rows,
            pl.BlockSpec((1, cuts.picks, block), lambda t: (t, 0, 0)),
            pl.BlockSpec(small.shape, lambda t: (0, 0)),
            pl.BlockSpec((inner, width), lambda t: (0, 2)),
            pl.BlockSpec(expert.shape, lambda t: (0, 0)),
        ],
        out_specs=[
            rows,
            rows,
            rows,
            pl.BlockSpec((block, state, inner), lambda t: (t, 0, 0)),
            whole,
            pl.BlockSpec((block, width), lambda t: (0, 0)),
            pl.BlockSpec(pieces, lambda t: (0, 0, 0)),
        ],
        out_shape=[
            jax.ShapeDtypeStruct((length, inner), jnp.float32),
            jax.ShapeDtypeStruct((length, inner), jnp.float32),
            jax.ShapeDtypeStruct((length, inner), jnp.bfloat16),
            jax.ShapeDtypeStruct((length, state, inner), jnp.float32),
            jax.ShapeDtypeStruct((state, inner), jnp.float32),
            jax.ShapeDtypeStruct((block, width), jnp.float32),
            jax.ShapeDtypeStruct(pieces, jnp.bfloat16),
        ],
        scratch_shapes=[
            pltpu.VMEM((state, inner), jnp.float32),
            pltpu.VMEM((block, inner), jnp.float32),
            pltpu.VMEM((block, inner), jnp.float32),
            pltpu.VMEM((block * state, 2 * block), jnp.bfloat16),
            pltpu.VMEM((block * state, LANES), jnp.float32),
            pltpu.VMEM((block * state, LANES), jnp.float32),
            pltpu.VMEM(pieces, jnp.bfloat16),
            *relay_scratch(count, block, width),
            *gather_scratch(count),
        ],
        compiler_params=pltpu.CompilerParams(
            collective_id=1, has_side_effects=True, vmem_limit_bytes=VMEM_LIMIT
        ),
        cost_estimate=pl.CostEstimate(
            flops=8 * length * state * inner,
            bytes_accessed=4 * length * inner * (state + 6),
            transcendentals=length * state * inner,
        ),
        name="scan_forward",
    )(act, gate, selected, small, weights, expert)


def scan_backward_kernel(
    count, cuts,
    own_ref, act_ref, gate_ref, mixed_ref, pre_ref, selected_ref, small_ref, output_ref,
    prior_ref, end_ref, expert_ref,
    grad_gate_ref, grad_act_ref, grad_step_ref, rate_total_ref, rows_ref, grad_selected_ref,
    all_out_ref, expert_out_ref,
    incoming_ref, post_ref, delta_ref, grad_ref, grad_delta_ref, wide_ref, wide_in_ref,
    wide_out_ref, all_ref,
    stage_ref, part_ref, partial_ref, total_ref,
    send_hi, recv_hi, send_x, recv_x, send_rs, recv_rs, send_ag, recv_ag,
    other_ref, held_ref, swap_s, swap_r, *scatter_refs,
):
    steps, inner = act_ref.shape
    tiles = inner // LANES
    state = cuts.state
    halves = state // 8
    lane = lax.broadcasted_iota(jnp.int32, (8, steps), 1)
    line, own, high, low = place()
    half = count // 2
    partner = 2 * high + 1 - low
    index = pl.program_id(0)
    now = count - 1 - index
    scatter = Scatter(count, expert_ref, other_ref, held_ref, swap_s, swap_r, scatter_refs)

    def along(k):
        return remote(
            own_ref, all_ref.at[own], send_hi.at[k], recv_hi.at[high], line,
            2 * lax.rem(high + k, half) + low,
        )

    def across(block):
        i = block // 2
        return remote(
            all_ref.at[block], all_ref.at[block], send_x.at[i], recv_x.at[i], line, partner
        )

    def came_along(block):
        i = block // 2
        return remote(
            all_ref.at[block], all_ref.at[block], send_hi.at[0], recv_hi.at[i], line, partner
        )

    def hand_over(block):
        @pl.when((lax.rem(block, 2) == low) & (block // 2 != high))
        def _():
            came_along(block).wait_recv()
            across(block).start()

    @pl.when(index == 0)
    def _():
        greet(count)
        all_ref[own] = own_ref[...]
        incoming_ref[...] = jnp.zeros_like(incoming_ref)
        post_ref[...] = end_ref[...]
        rate_total_ref[...] = jnp.zeros_like(rate_total_ref)
        grad_step_ref[...] = jnp.zeros_like(grad_step_ref)
        rows_ref[...] = jnp.zeros_like(rows_ref)
        stage_ref[...] = jnp.zeros_like(stage_ref)

    @pl.when(index == jnp.maximum(count - 3 - own, 0))
    def _():
        for k in range(1, half):
            along(k).start()
        across(own).start()

    @pl.when(index == 0)
    def _():
        hand_over(now)
        hand_over(now - 1)

    @pl.when(lax.rem(now, 2) != low)
    def _():
        across(now).wait_recv()

    gate = gate_ref[...]
    gate_sig = sigmoid(gate)
    grad_y = outer_cols(all_ref[now], output_ref[...])
    grad_gate_ref[...] = (
        grad_y * mixed_ref[...] * (gate_sig * (1.0 + gate * (1.0 - gate_sig)))
    ).astype(jnp.bfloat16)
    grad_mixed = grad_y * (gate * gate_sig)
    grad_ref[...] = grad_mixed
    delta_ref[...] = softplus(pre_ref[...])
    rows_ref[1:2, :] += jnp.sum(grad_mixed * act_ref[...], axis=0, keepdims=True)
    rates2 = -LOG2E * jnp.exp(small_ref[cuts.decay : cuts.decay + state, :])
    in_rows = cuts.rank
    out_rows = cuts.rank + state
    spread_lanes(selected_ref[0, in_rows : in_rows + state, :], wide_ref, wide_in_ref)
    spread_lanes(selected_ref[0, out_rows : out_rows + state, :], wide_ref, wide_out_ref)

    def tile_of(ref):
        return tuple(
            tuple(ref[8 * i : 8 * i + 8, j * LANES : (j + 1) * LANES] for i in range(halves))
            for j in range(tiles)
        )

    def group(turn, carry):
        incoming, posts, rate_total, in_acc, out_acc = carry
        incoming = [list(s) for s in incoming]
        posts = [list(s) for s in posts]
        rate_total = [list(s) for s in rate_total]
        in_acc, out_acc = list(in_acc), list(out_acc)
        base = pl.multiple_of((steps // 8 - 1 - turn) * 8, 8)
        d8 = delta_ref[pl.ds(base, 8), :]
        u8 = act_ref[pl.ds(base, 8), :]
        du8 = d8 * u8
        g8 = grad_ref[pl.ds(base, 8), :]
        rate_parts = [[None] * 8 for _ in range(tiles)]
        side_parts = [[None] * 8 for _ in range(tiles)]
        for k in range(7, -1, -1):
            rows_now = [pl.ds((base + k) * state + 8 * i, 8) for i in range(halves)]
            b_now = [wide_in_ref[here, :] for here in rows_now]
            c_now = [wide_out_ref[here, :] for here in rows_now]
            in_sum = [None] * halves
            out_sum = [None] * halves
            for j in range(tiles):
                cols = slice(j * LANES, (j + 1) * LANES)
                d = jnp.broadcast_to(d8[k : k + 1, cols], (8, LANES))
                du = jnp.broadcast_to(du8[k : k + 1, cols], (8, LANES))
                gm = jnp.broadcast_to(g8[k : k + 1, cols], (8, LANES))
                rate_part = None
                side_part = None
                for i in range(halves):
                    prior = prior_ref[base + k, 8 * i : 8 * i + 8, cols]
                    rates = rates2[8 * i : 8 * i + 8, cols]
                    grad_state = c_now[i] * gm + incoming[j][i]
                    passed = jnp.exp2(d * rates) * grad_state
                    incoming[j][i] = passed
                    weighted = passed * prior
                    term = weighted * rates
                    rate_part = term if rate_part is None else rate_part + term
                    term = grad_state * b_now[i]
                    side_part = term if side_part is None else side_part + term
                    term = grad_state * du
                    in_sum[i] = term if in_sum[i] is None else in_sum[i] + term
                    term = posts[j][i] * gm
                    out_sum[i] = term if out_sum[i] is None else out_sum[i] + term
                    rate_total[j][i] = rate_total[j][i] + weighted * d
                    posts[j][i] = prior
                rate_parts[j][k] = rate_part
                side_parts[j][k] = side_part
            here = lane == base + k
            for i in range(halves):
                in_acc[i] = jnp.where(here, jnp.sum(in_sum[i], axis=1, keepdims=True), in_acc[i])
                out_acc[i] = jnp.where(here, jnp.sum(out_sum[i], axis=1, keepdims=True), out_acc[i])
        for j in range(tiles):
            cols = slice(j * LANES, (j + 1) * LANES)
            side = sublane_sums(side_parts[j])
            grad_delta_ref[pl.ds(base, 8), cols] = (
                sublane_sums(rate_parts[j]) * (1.0 / LOG2E) + u8[:, cols] * side
            )
            grad_act_ref[pl.ds(base, 8), cols] = d8[:, cols] * side
        return (
            tuple(tuple(s) for s in incoming),
            tuple(tuple(s) for s in posts),
            tuple(tuple(s) for s in rate_total),
            tuple(in_acc),
            tuple(out_acc),
        )

    empty = tuple(jnp.zeros((8, steps), jnp.float32) for _ in range(halves))
    incoming, posts, rate_total, in_acc, out_acc = lax.fori_loop(
        0,
        steps // 8,
        group,
        (tile_of(incoming_ref), tile_of(post_ref), tile_of(rate_total_ref), empty, empty),
    )
    for i in range(halves):
        stage_ref[in_rows + 8 * i : in_rows + 8 * i + 8, :] = in_acc[i]
        stage_ref[out_rows + 8 * i : out_rows + 8 * i + 8, :] = out_acc[i]
        for j in range(tiles):
            cols = slice(j * LANES, (j + 1) * LANES)
            incoming_ref[8 * i : 8 * i + 8, cols] = incoming[j][i]
            post_ref[8 * i : 8 * i + 8, cols] = posts[j][i]
            rate_total_ref[8 * i : 8 * i + 8, cols] = rate_total[j][i]

    grad_act_ref[...] += grad_ref[...] * small_ref[cuts.skip : cuts.skip + 1, :]
    grad_pre = grad_delta_ref[...] * sigmoid(pre_ref[...])
    rows_ref[0:1, :] += jnp.sum(grad_pre, axis=0, keepdims=True)
    grad_step_ref[...] += dot_nn(selected_ref[0, : cuts.rank, :], grad_pre, HIGHEST)
    stage_ref[: cuts.rank, :] = outer_cols(
        small_ref[cuts.step : cuts.step + cuts.rank, :], grad_pre, HIGHEST
    )
    part_ref[now] = stage_ref[...].astype(jnp.bfloat16)

    def partial_to(block):
        return remote(
            part_ref.at[block], partial_ref.at[own], send_rs.at[block], recv_rs.at[own], line, block
        )

    @pl.when(now != own)
    def _():
        partial_to(now).start()

    def total_to(k):
        return remote(
            total_ref.at[own], total_ref.at[own], send_ag.at[k], recv_ag.at[own], line,
            lax.rem(own + k, count),
        )

    @pl.when(now >= 2)
    def _():
        hand_over(now - 2)

    @pl.when(index == FAR_AT)
    def _():
        scatter.send_far()

    @pl.when(index == NEAR_AT)
    def _():
        scatter.send_near()

    @pl.when(index == count // 2 + PASS_AFTER)
    def _():
        scatter.pass_far()

    @pl.when(index == count - 1)
    def _():
        scatter.hand_over()

    @pl.when(index == jnp.minimum(count - 1 - own + 2, count - 1))
    def _():
        total = part_ref[own].astype(jnp.float32)
        for k in range(1, count):
            there = lax.rem(own + k, count)
            remote(
                part_ref.at[own], partial_ref.at[there], send_rs.at[own], recv_rs.at[there],
                line, there,
            ).wait_recv()
            total = total + partial_ref[there].astype(jnp.float32)
        total_ref[own] = total.astype(jnp.bfloat16)
        for k in range(1, count):
            total_to(k).start()

    @pl.when(index == count - 1)
    def _():
        for k in range(1, count):
            there = lax.rem(own + k, count)
            remote(
                total_ref.at[there], total_ref.at[there], send_ag.at[k], recv_ag.at[there],
                line, there,
            ).wait_recv()
        grad_selected_ref[...] = total_ref[...]
        all_out_ref[...] = all_ref[...]
        for k in range(1, half):
            along(k).wait_send()
        for i in range(half):
            across(2 * i + low).wait_send()
        for k in range(1, count):
            partial_to(lax.rem(own + k, count)).wait_send()
            total_to(k).wait_send()
        scatter.finish(expert_out_ref)


def scan_backward(
    count, cuts, grad_low, act, gate, mixed, pre, selected, small, weights, priors, end, expert
):
    length, inner = act.shape
    state = cuts.state
    block = length // count
    width = grad_low.shape[1]
    half = count // 2

    def back(t):
        return count - 1 - t

    rows = pl.BlockSpec((block, inner), lambda t: (back(t), 0))
    whole = pl.BlockSpec((state, inner), lambda t: (0, 0))
    dma = pltpu.SemaphoreType.DMA
    picked = (count, cuts.sent, block)
    return pl.pallas_call(
        functools.partial(scan_backward_kernel, count, cuts),
        grid=(count,),
        in_specs=[
            pl.BlockSpec((block, width), lambda t: (0, 0)),
            rows,
            rows,
            rows,
            rows,
            pl.BlockSpec((1, cuts.picks, block), lambda t: (back(t), 0, 0)),
            pl.BlockSpec(small.shape, lambda t: (0, 0)),
            pl.BlockSpec((inner, width), lambda t: (0, 2)),
            pl.BlockSpec((block, state, inner), lambda t: (back(t), 0, 0)),
            whole,
            pl.BlockSpec(expert.shape, lambda t: (0, 0, 0)),
        ],
        out_specs=[
            rows,
            rows,
            pl.BlockSpec((cuts.rank, inner), lambda t: (0, 0)),
            whole,
            pl.BlockSpec((8, inner), lambda t: (0, 0)),
            pl.BlockSpec(picked, lambda t: (0, 0, 0)),
            pl.BlockSpec((count, block, width), lambda t: (0, 0, 0)),
            pl.BlockSpec((expert.shape[1], 2 * expert.shape[2]), lambda t: (0, 0)),
        ],
        out_shape=[
            jax.ShapeDtypeStruct((length, inner), jnp.bfloat16),
            jax.ShapeDtypeStruct((length, inner), jnp.float32),
            jax.ShapeDtypeStruct((cuts.rank, inner), jnp.float32),
            jax.ShapeDtypeStruct((state, inner), jnp.float32),
            jax.ShapeDtypeStruct((8, inner), jnp.float32),
            jax.ShapeDtypeStruct(picked, jnp.bfloat16),
            jax.ShapeDtypeStruct((count, block, width), jnp.bfloat16),
            jax.ShapeDtypeStruct((expert.shape[1], 2 * expert.shape[2]), jnp.float32),
        ],
        scratch_shapes=[
            pltpu.VMEM((state, inner), jnp.float32),
            pltpu.VMEM((state, inner), jnp.float32),
            pltpu.VMEM((block, inner), jnp.float32),
            pltpu.VMEM((block, inner), jnp.float32),
            pltpu.VMEM((block, inner), jnp.float32),
            pltpu.VMEM((block * state, 2 * block), jnp.bfloat16),
            pltpu.VMEM((block * state, LANES), jnp.float32),
            pltpu.VMEM((block * state, LANES), jnp.float32),
            pltpu.VMEM((count, block, width), jnp.bfloat16),
            pltpu.VMEM(picked[1:], jnp.float32),
            *[pltpu.VMEM(picked, jnp.bfloat16)] * 3,
            dma((half,)), dma((half,)), dma((half,)), dma((half,)),
            dma((count,)), dma((count,)), dma((count,)), dma((count,)),
            *scatter_scratch(count, expert.shape[1], expert.shape[2]),
        ],
        compiler_params=pltpu.CompilerParams(
            collective_id=2, has_side_effects=True, vmem_limit_bytes=VMEM_LIMIT
        ),
        cost_estimate=pl.CostEstimate(
            flops=20 * length * state * inner,
            bytes_accessed=4 * length * inner * (state + 6),
            transcendentals=length * state * inner,
        ),
        name="scan_backward",
    )(grad_low, act, gate, mixed, pre, selected, small, weights, priors, end, expert)


def back_kernel(
    count, lines, cuts,
    grad_selected_ref, small_ref, weights_ref, ext_ref, sum_ref, grad_act_ref, grad_gate_ref,
    mixer_low_ref, normed_ref, grad_middle_ref, grad_step_ref, rate_total_ref, scan_rows_ref,
    vectors_ref, expert_ref,
    summed_ref, shard_ref, totals_ref, expert_out_ref,
    grad_sum_ref, grad_conv_ref, grad_small_ref, ours_ref, theirs_ref,
    send_v, recv_v, send_u, recv_u, other_ref, held_ref, swap_s, swap_r, *refs,
):
    scatter = Scatter(count, expert_ref, other_ref, held_ref, swap_s, swap_r, refs[:6])
    relay = whole_relay("seq", count, refs[6:13])
    spread = whole_relay("dp", lines, refs[13:])
    line, own, _, _ = place()
    length, inner = sum_ref.shape
    width = normed_ref.shape[1]
    rows = length // count
    kernel = cuts.kernel
    shard = shard_ref.shape[0]
    greet(count, lines)
    scatter.send_far()
    grad_small_ref[...] = jnp.zeros_like(grad_small_ref)
    grad_sum_ref[length:, :] = jnp.zeros((8, inner), jnp.float32)
    select = small_ref[: cuts.sent, :].astype(jnp.bfloat16)

    def first(b, carry):
        start = pl.multiple_of(b * rows, rows)
        grad_selected = grad_selected_ref[b]
        total = sum_ref[pl.ds(start, rows), :]
        sig = sigmoid(total)
        grad_act = grad_act_ref[pl.ds(start, rows), :] + inner_rows(grad_selected, select)
        grad_sum = grad_act * (sig * (1.0 + total * (1.0 - sig)))
        grad_sum_ref[pl.ds(start, rows), :] = grad_sum
        grad_small_ref[: cuts.sent, :] += dot_nn(
            grad_selected, (total * sig).astype(jnp.bfloat16)
        )
        window = ext_ref[pl.ds(start, rows + 8), :]
        for k in range(kernel):
            row = slice(cuts.taps + k, cuts.taps + k + 1)
            grad_small_ref[row, :] += jnp.sum(
                grad_sum * window[9 - kernel + k : 9 - kernel + k + rows], axis=0, keepdims=True
            )
        row = slice(cuts.conv_bias, cuts.conv_bias + 1)
        grad_small_ref[row, :] += jnp.sum(grad_sum, axis=0, keepdims=True)
        return carry

    lax.fori_loop(0, count, first, 0)

    def order(j):
        return j // 2 + lax.rem(j, 2) * (count // 2)

    def second(j, carry):
        b = order(j)
        start = pl.multiple_of(b * rows, rows)
        window = grad_sum_ref[pl.ds(start, rows + 8), :]
        grad_conv = None
        for k in range(kernel):
            tap = small_ref[cuts.taps + k : cuts.taps + k + 1, :]
            term = tap * window[kernel - 1 - k : kernel - 1 - k + rows]
            grad_conv = term if grad_conv is None else grad_conv + term
        grad_conv = grad_conv.astype(jnp.bfloat16)
        grad_conv_ref[pl.ds(start, rows), :] = grad_conv
        relay.part[b] = (
            dot_nn(grad_conv, weights_ref[:, :width])
            + dot_nn(grad_gate_ref[pl.ds(start, rows), :], weights_ref[:, width : 2 * width])
        ).astype(jnp.bfloat16)
        relay.made(b // 2, lax.rem(b, 2))
        return carry

    lax.fori_loop(0, count, second, 0)
    scatter.send_near()
    scatter.pass_far()

    decay = slice(cuts.decay, cuts.decay + cuts.state)
    grad_small_ref[cuts.step : cuts.step + cuts.rank, :] = grad_step_ref[...]
    grad_small_ref[decay, :] = -rate_total_ref[...] * jnp.exp(small_ref[decay, :])
    grad_small_ref[cuts.step_bias : cuts.step_bias + 2, :] = scan_rows_ref[0:2, :]
    small_t = grad_small_ref[...].T
    for d in range(lines):
        spread.part[d, :, 3 * width :] = small_t[d * shard : (d + 1) * shard].astype(jnp.bfloat16)
    chunk = width // 3

    def pass_on(j, carry):
        b = order(j)
        relay.pass_on(b // 2, lax.rem(b, 2))
        return carry

    ours_ref[...] = vectors_ref[...]
    for left_ref, right_ref, place_at in (
        (mixer_low_ref, grad_middle_ref, 2 * width),
        (grad_conv_ref, normed_ref, 0),
        (grad_gate_ref, normed_ref, width),
    ):

        def columns(c, carry, left_ref=left_ref, right_ref=right_ref, place_at=place_at):
            here = pl.ds(pl.multiple_of(c * chunk, chunk), chunk)
            there = pl.ds(pl.multiple_of(place_at + c * chunk, chunk), chunk)
            grad = inner_rows(left_ref[...], right_ref[:, here])
            if place_at < 2 * width:
                ours_ref[0:1, here] += jnp.sum(
                    weights_ref[:, there].astype(jnp.float32) * grad, axis=0, keepdims=True
                )
            low = grad.astype(jnp.bfloat16)
            for d in range(lines):
                spread.part[d, :, there] = low[d * shard : (d + 1) * shard]
            return carry

        lax.fori_loop(0, 3, columns, 0)
        if place_at == 2 * width:
            lax.fori_loop(0, count, pass_on, 0)
    for d in range(lines):
        spread.made(d // 2, d % 2)
    scatter.hand_over()

    def sum_over(size, axis, send, recv):
        here = own if axis == "seq" else line

        def copy(k, slot):
            there = lax.rem(here + k, size)
            target = (line, there) if axis == "seq" else (there, own)
            return remote(ours_ref, theirs_ref.at[slot], send.at[k], recv.at[k], *target)

        base = 0 if axis == "seq" else count
        for k in range(1, size):
            copy(k, base + k).start()
        total = ours_ref[...]
        for k in range(1, size):
            copy(k, base + k).wait_recv()
            total = total + theirs_ref[base + k]
        for k in range(1, size):
            copy(k, base + k).wait_send()
        return total

    ours_ref[...] = sum_over(count, "seq", send_v, recv_v)
    for d in range(lines):
        spread.pass_on(d // 2, d % 2)
    totals_ref[...] = sum_over(lines, "dp", send_u, recv_u)
    summed_ref[...] = relay.finish()
    shard_ref[...] = spread.finish()
    scatter.finish(expert_out_ref)


def back(
    count, lines, shard, cuts, grad_selected, small, weights, ext, conv_sum, grad_act, grad_gate,
    mixer_low, normed, grad_middle, grad_step, rate_total, scan_rows, vectors, expert,
):
    length, inner = conv_sum.shape
    width = normed.shape[1]
    columns = weights.shape[1]
    rows = length // count
    vmem = pl.BlockSpec(memory_space=pltpu.VMEM)
    dma = pltpu.SemaphoreType.DMA
    args = (
        grad_selected, small, weights, ext, conv_sum, grad_act, grad_gate, mixer_low, normed,
        grad_middle, grad_step, rate_total, scan_rows, vectors, expert,
    )
    return pl.pallas_call(
        functools.partial(back_kernel, count, lines, cuts),
        in_specs=[vmem] * len(args),
        out_specs=[vmem] * 4,
        out_shape=[
            jax.ShapeDtypeStruct((rows, width), jnp.float32),
            jax.ShapeDtypeStruct((shard, columns), jnp.float32),
            jax.ShapeDtypeStruct(vectors.shape, jnp.float32),
            jax.ShapeDtypeStruct((expert.shape[1], 2 * expert.shape[2]), jnp.float32),
        ],
        scratch_shapes=[
            pltpu.VMEM((length + 8, inner), jnp.float32),
            pltpu.VMEM((length, inner), jnp.bfloat16),
            pltpu.VMEM(small.shape, jnp.float32),
            pltpu.VMEM(vectors.shape, jnp.float32),
            pltpu.VMEM((count + lines, *vectors.shape), jnp.float32),
            dma((count,)), dma((count,)), dma((lines,)), dma((lines,)),
            *scatter_scratch(count, expert.shape[1], expert.shape[2]),
            *relay_scratch(count, rows, width),
            *relay_scratch(lines, shard, columns),
        ],
        compiler_params=pltpu.CompilerParams(
            collective_id=3, has_side_effects=True, vmem_limit_bytes=VMEM_LIMIT
        ),
        cost_estimate=pl.CostEstimate(
            flops=10 * length * width * inner,
            bytes_accessed=30 * length * inner,
            transcendentals=length * inner,
        ),
        name="back",
    )(*args)


LAG = 3
FAR_AT = 0
NEAR_AT = 2
PASS_AFTER = 0
SLOTS = 64


def gauss(values):
    return 0.5 * (1.0 + lax.erf(values * math.sqrt(0.5)))


def split_low(values):
    high = values.astype(jnp.bfloat16)
    return high, (values - high.astype(jnp.float32)).astype(jnp.bfloat16)


def experts_kernel(
    count, lines, experts,
    x_ref, mixer_ref, grad_ref, chosen_ref, table_ref, back_table_ref, gain_ref, router_ref,
    up_ref, down_ref,
    output_ref, grad_middle_ref, grad_low_ref, vectors_ref, grad_up_ref, grad_down_ref,
    middle_ref, normed_ref, send_ref, rows_ref, made_ref, got_ref, act_ref, slope_ref, pre_ref,
    send_sem, recv_sem, home_s, home_r,
):
    line, own, _, _ = place()
    q, f, low = square()
    mate = seat_of(q, 1 - f, low)
    copies = lines // experts
    barrier = pltpu.get_barrier_semaphore()
    for d in range(1, lines):
        for where in (own, mate):
            pl.semaphore_signal(
                barrier, inc=1, device_id=(lax.rem(line + d, lines), where), device_id_type=MESH
            )
    pl.semaphore_signal(barrier, inc=1, device_id=(line, mate), device_id_type=MESH)
    pl.semaphore_wait(barrier, 2 * lines - 1)

    peers = [(j, d) for d in range(lines) for j in (1, 0) if (j, d) != (0, 0)]

    def out_copy(what, j, d):
        there = lax.rem(line + d, lines)
        return remote(
            send_ref.at[what, there // copies], rows_ref.at[what, j, line],
            send_sem.at[what, j, d], recv_sem.at[what, j, line],
            there, mate if j else own,
        )

    def arrived(what, j, d):
        from_line = lax.rem(line + d, lines)
        return remote(
            send_ref.at[what, 0], rows_ref.at[what, j, from_line],
            send_sem.at[what, j, d], recv_sem.at[what, j, from_line],
            from_line, mate if j else own,
        )

    def home_copy(what, j, d):
        there = lax.rem(line + d, lines)
        return remote(
            made_ref.at[what, j, there], got_ref.at[what, j, line],
            home_s.at[what, j, d], home_r.at[what, j, line],
            there, mate if j else own,
        )

    def came_home(what, j, d):
        from_line = lax.rem(line + d, lines)
        return remote(
            made_ref.at[what, j, 0], got_ref.at[what, j, from_line],
            home_s.at[what, j, d], home_r.at[what, j, from_line],
            from_line, mate if j else own,
        )

    middle = x_ref[...] + mixer_ref[...]
    middle_ref[...] = middle
    gain = gain_ref[...]
    scale = lax.rsqrt(jnp.mean(middle * middle, axis=1, keepdims=True) + 1e-05)
    normed = (middle * scale * gain).astype(jnp.bfloat16)
    normed_ref[...] = normed
    rows, width = middle.shape
    slots = table_ref.shape[0] // experts

    def dispatch(what, values):
        sent = dot_nn(table_ref[...], values).astype(jnp.bfloat16)
        for e in range(experts):
            send_ref[what, e] = sent[e * slots : (e + 1) * slots]
        for j, d in peers:
            out_copy(what, j, d).start()
        rows_ref[what, 0, line] = send_ref[what, line // copies]

    dispatch(0, normed)
    lane = lax.broadcasted_iota(jnp.int32, (rows, LANES), 1)
    logits = jnp.where(lane < experts, outer_cols(normed, router_ref[...]), -jnp.inf)
    grown = jnp.exp(logits - jnp.max(logits, axis=1, keepdims=True))
    probs = grown / jnp.sum(grown, axis=1, keepdims=True)
    chosen = chosen_ref[...]
    gate = jnp.sum(chosen * probs, axis=1, keepdims=True)
    dispatch(1, (gate * grad_ref[...]).astype(jnp.bfloat16))

    total = 2 * lines * slots
    hidden = up_ref.shape[1]
    chunk = hidden // 3 if hidden % (3 * LANES) == 0 else hidden
    parts = hidden // chunk

    def rows_of(ref, what):
        return ref[what].reshape(total, width)

    def columns(c):
        return pl.ds(pl.multiple_of(c * chunk, LANES), chunk)

    for j, d in peers:
        arrived(0, j, d).wait_recv()

    def rise(c, carry):
        pre_ref[:, columns(c)] = dot_nn(rows_of(rows_ref, 0), up_ref[:, columns(c)])
        pre = pre_ref[:, columns(c)]
        half = gauss(pre)
        act_ref[:, columns(c)] = (pre * half).astype(jnp.bfloat16)
        pre_ref[:, columns(c)] = half + pre * (
            jnp.exp(-0.5 * pre * pre) * (1.0 / math.sqrt(2.0 * math.pi))
        )
        return carry

    lax.fori_loop(0, parts, rise, 0)

    wide = width // 3

    def send_home(what, left_ref, right_ref):
        def make(c, carry):
            here = pl.ds(pl.multiple_of(c * wide, LANES), wide)
            there = pl.ds(pl.multiple_of(c * wide, LANES), wide)
            made = outer_cols(left_ref[...], right_ref[there, :]).astype(jnp.bfloat16)
            made_ref[what, :, :, :, here] = made.reshape(2, lines, slots, wide)
            return carry

        lax.fori_loop(0, 3, make, 0)
        for j, d in peers:
            home_copy(what, j, d).start()
        got_ref[what, 0, line] = made_ref[what, 0, line]

    for j, d in peers:
        arrived(1, j, d).wait_recv()

    def fall(c, carry):
        slope_ref[:, columns(c)] = (
            dot_nn(rows_of(rows_ref, 1), down_ref[:, columns(c)]) * pre_ref[:, columns(c)]
        ).astype(jnp.bfloat16)
        return carry

    lax.fori_loop(0, parts, fall, 0)
    send_home(1, slope_ref, up_ref)
    send_home(0, act_ref, down_ref)

    pieces = grad_up_ref.shape[1]

    def weigh(c, carry):
        up = inner_rows(rows_of(rows_ref, 0), slope_ref[:, columns(c)]).astype(jnp.bfloat16)
        down = inner_rows(rows_of(rows_ref, 1), act_ref[:, columns(c)]).astype(jnp.bfloat16)
        grad_up_ref[:, :, columns(c)] = up.reshape(count, pieces, chunk)
        grad_down_ref[:, :, columns(c)] = down.reshape(count, pieces, chunk)
        return carry

    lax.fori_loop(0, parts, weigh, 0)

    def home(what):
        for j, d in peers:
            came_home(what, j, d).wait_recv()
        both = None
        for e in range(experts):
            own_rows = None
            for c in range(copies):
                for j in range(2):
                    term = got_ref[what, j, e * copies + c].astype(jnp.float32)
                    own_rows = term if own_rows is None else own_rows + term
            high, rest = split_low(own_rows)
            here = back_table_ref[e]
            term = dot_nn(here, high) + dot_nn(here, rest)
            both = term if both is None else both + term
        return both

    grad = grad_ref[...]
    middle = middle_ref[...]
    picked = home(0)
    output_ref[...] = middle + gate * picked
    grad_gate = jnp.sum(grad * picked, axis=1, keepdims=True)
    grad_logits = gate * (chosen - probs) * grad_gate
    grad_normed = home(1) + dot_nn(grad_logits, router_ref[...].astype(jnp.float32), HIGHEST)
    scaled = gain * grad_normed
    grad_middle = (
        grad
        + scale * scaled
        - middle * (scale * scale * scale) * jnp.mean(scaled * middle, axis=1, keepdims=True)
    )
    grad_middle_ref[...] = grad_middle
    grad_low_ref[...] = grad_middle.astype(jnp.bfloat16)
    vectors_ref[...] = jnp.zeros_like(vectors_ref)
    vectors_ref[1:2, :] = jnp.sum(grad_normed * middle * scale, axis=0, keepdims=True)
    vectors_ref[2 : 2 + experts, :] = inner_rows(
        grad_logits, normed_ref[...].astype(jnp.float32), HIGHEST
    )[:experts]
    for what in range(2):
        for j, d in peers:
            out_copy(what, j, d).wait_send()
            home_copy(what, j, d).wait_send()


def run_experts(
    count, lines, experts, x, mixer, grad, chosen, table, back_table, gain, router, up, down
):
    rows, width = x.shape
    slots = table.shape[0] // experts
    total = 2 * lines * slots
    hidden = up.shape[1]
    pieces = (count, up.shape[0] // count, hidden)
    vmem = pl.BlockSpec(memory_space=pltpu.VMEM)
    dma = pltpu.SemaphoreType.DMA
    args = (x, mixer, grad, chosen, table, back_table, gain, router, up, down)
    low = jnp.bfloat16
    return pl.pallas_call(
        functools.partial(experts_kernel, count, lines, experts),
        in_specs=[vmem] * len(args),
        out_specs=[vmem] * 6,
        out_shape=[
            jax.ShapeDtypeStruct((rows, width), jnp.float32),
            jax.ShapeDtypeStruct((rows, width), jnp.float32),
            jax.ShapeDtypeStruct((rows, width), low),
            jax.ShapeDtypeStruct((8, width), jnp.float32),
            jax.ShapeDtypeStruct(pieces, low),
            jax.ShapeDtypeStruct(pieces, low),
        ],
        scratch_shapes=[
            pltpu.VMEM((rows, width), jnp.float32),
            pltpu.VMEM((rows, width), low),
            pltpu.VMEM((2, experts, slots, width), low),
            pltpu.VMEM((2, 2, lines, slots, width), low),
            pltpu.VMEM((2, 2, lines, slots, width), low),
            pltpu.VMEM((2, 2, lines, slots, width), low),
            pltpu.VMEM((total, hidden), low),
            pltpu.VMEM((total, hidden), low),
            pltpu.VMEM((total, hidden), jnp.float32),
            dma((2, 2, lines)), dma((2, 2, lines)), dma((2, 2, lines)), dma((2, 2, lines)),
        ],
        compiler_params=pltpu.CompilerParams(
            collective_id=4, has_side_effects=True, vmem_limit_bytes=VMEM_LIMIT
        ),
        cost_estimate=pl.CostEstimate(
            flops=12 * total * width * hidden,
            bytes_accessed=8 * width * hidden,
            transcendentals=2 * total * hidden,
        ),
        name="experts",
    )(*args)


def body(
    tokens,
    cotangent,
    routes,
    mixer_gain,
    input_proj,
    conv_weight,
    conv_bias,
    select_proj,
    step_proj,
    step_bias,
    decay_log,
    skip_gain,
    output_proj,
    expert_gain,
    router,
    expert_up,
    expert_down,
):
    rows = tokens.shape[1]
    width = tokens.shape[2]
    shard = input_proj.shape[2]
    rank = step_proj.shape[0]
    state = decay_log.shape[0]
    kernel = conv_weight.shape[0]
    picks = select_proj.shape[0]
    count = lax.axis_size("seq")
    lines = lax.axis_size("dp")
    shard_rows = -(-shard // 16) * 16
    cuts = Cuts(picks, rank, state, kernel)

    x_in = tokens.reshape(rows, width)
    gain_one = mixer_gain.astype(jnp.float32)
    normed = rms_norm(x_in, gain_one).astype(jnp.bfloat16)

    small = jnp.concatenate(
        [
            select_proj,
            step_proj,
            decay_log,
            conv_weight,
            conv_bias[None, :],
            step_bias[None, :],
            skip_gain[None, :],
        ],
        axis=0,
    )
    small_pad = -(-cuts.rows // LANES) * LANES
    small = jnp.pad(small, ((0, small_pad - cuts.rows), (0, 0)))
    packed = jnp.concatenate(
        [input_proj.reshape(2 * width, shard).T, output_proj, small.T], axis=1
    )
    packed = jnp.pad(packed, ((0, shard_rows - shard), (0, 0)))
    (normed_all, weights, small_all, conv_ext, conv_sum, conv_act, gate_branch, selected, up_cut) = (
        front(count, lines, cuts, normed, packed, expert_up)
    )
    pre, mixed, mixer_low, priors, end, mixer_out, down_cut = scan_forward(
        count, cuts, width, conv_act, gate_branch, selected, small_all, weights, expert_down.T
    )

    experts = router.shape[0]
    route = routes.reshape(rows)
    chosen = (route[:, None] == lax.broadcasted_iota(jnp.int32, (rows, LANES), 1)).astype(
        jnp.float32
    )
    earlier = (
        lax.broadcasted_iota(jnp.int32, (rows, rows), 0)
        > lax.broadcasted_iota(jnp.int32, (rows, rows), 1)
    ).astype(jnp.float32)
    before = jnp.dot(earlier, chosen, precision=HIGHEST)
    position = jnp.sum(before * chosen, axis=1).astype(jnp.int32)
    slot = route * SLOTS + position
    table = (
        slot[None, :] == lax.broadcasted_iota(jnp.int32, (experts * SLOTS, rows), 0)
    ).astype(jnp.bfloat16)
    back_table = (
        slot[None, :, None]
        == lax.broadcasted_iota(jnp.int32, (experts, rows, SLOTS), 2)
        + SLOTS * lax.broadcasted_iota(jnp.int32, (experts, rows, SLOTS), 0)
    ).astype(jnp.bfloat16)
    output, grad_middle, grad_middle_low, vectors, grad_up_low, grad_down_low = run_experts(
        count,
        lines,
        experts,
        x_in,
        mixer_out,
        cotangent.reshape(rows, width),
        chosen,
        table,
        back_table,
        expert_gain.astype(jnp.float32)[None],
        jnp.pad(router, ((0, LANES - experts), (0, 0))),
        up_cut.reshape(-1, up_cut.shape[2]),
        down_cut.reshape(-1, down_cut.shape[2]),
    )

    (grad_gate_branch, grad_act, grad_step_w, rate_total, scan_rows, grad_selected, grad_middle_all,
     grad_down_t) = (
        scan_backward(
            count, cuts, grad_middle_low, conv_act, gate_branch, mixed, pre, selected, small_all,
            weights, priors, end, grad_down_low,
        )
    )
    grad_normed, grad_shard, totals, grad_up = back(
        count, lines, shard_rows, cuts, grad_selected, small_all, weights, conv_ext, conv_sum,
        grad_act, grad_gate_branch, mixer_low, normed_all.reshape(-1, width),
        grad_middle_all.reshape(-1, width), grad_step_w, rate_total, scan_rows, vectors,
        grad_up_low,
    )
    grad_shard = grad_shard[:shard]
    grad_input_w = grad_shard[:, : 2 * width].T.reshape(2, width, shard)
    small_shard = grad_shard[:, 3 * width :].T
    cut = 0
    small_grads = []
    for number in (picks, rank, state, kernel, 1, 1, 1):
        small_grads.append(small_shard[cut : cut + number])
        cut += number
    unused_one, pull_one = jax.vjp(lambda v: rms_norm(v, gain_one), x_in)
    grad_tokens = grad_middle + pull_one(grad_normed)[0]
    return (
        output.reshape(tokens.shape),
        grad_tokens.reshape(tokens.shape),
        totals[0] / gain_one,
        grad_input_w,
        small_grads[3],
        small_grads[4].reshape(shard),
        small_grads[0],
        small_grads[1],
        small_grads[5].reshape(shard),
        small_grads[2],
        small_grads[6].reshape(shard),
        grad_shard[:, 2 * width : 3 * width],
        totals[1],
        totals[2 : 2 + experts],
        grad_up,
        grad_down_t.T,
    )


def solution(mesh):
    both = ("dp", "seq")
    placed = (
        P("dp", "seq", None),
        P("dp", "seq", None),
        P("dp", "seq", None),
        P(),
        P(None, None, both),
        P(None, both),
        P(both),
        P(None, both),
        P(None, both),
        P(both),
        P(None, both),
        P(both),
        P(both, None),
        P(),
        P(),
        P("seq", "dp"),
        P("dp", "seq"),
    )
    return jax.shard_map(
        body,
        mesh=mesh,
        in_specs=placed,
        out_specs=(
            P("dp", "seq", None),
            P("dp", "seq", None),
            P(),
            P(None, None, both),
            P(None, both),
            P(both),
            P(None, both),
            P(None, both),
            P(both),
            P(None, both),
            P(both),
            P(both, None),
            P(),
            P(),
            P("seq", "dp"),
            P("dp", "seq"),
        ),
        check_vma=False,
    )
```

```python
import functools
import math

import jax
import jax.numpy as jnp
from jax import lax
from jax.experimental import pallas as pl
from jax.experimental.pallas import tpu as pltpu
from jax.sharding import PartitionSpec as P

CAP = 56
LANES = 128
TIME_BLOCK = 128
LOG2E = math.log2(math.e)

HIGHEST = lax.Precision.HIGHEST


def inner_rows(left, right, precision=None):
    return lax.dot_general(
        left,
        right,
        (((0,), (0,)), ((), ())),
        precision=precision,
        preferred_element_type=jnp.float32,
    )


def outer_cols(left, right, precision=None):
    return lax.dot_general(
        left,
        right,
        (((1,), (1,)), ((), ())),
        precision=precision,
        preferred_element_type=jnp.float32,
    )


def sublane_sums(parts):
    row = lax.broadcasted_iota(jnp.int32, parts[0].shape, 0)
    low4 = row < 4
    low2 = (row % 4) < 2
    low1 = (row % 2) < 1
    quads = []
    for k in range(4):
        a, b = parts[k], parts[k + 4]
        quads.append(jnp.where(low4, a, b) + pltpu.roll(jnp.where(low4, b, a), 4, 0))
    pairs = []
    for k in range(2):
        a, b = quads[k], quads[k + 2]
        pairs.append(
            jnp.where(low2, a, b) + jnp.where(low2, pltpu.roll(a, 6, 0), pltpu.roll(b, 2, 0))
        )
    a, b = pairs
    return jnp.where(low1, a, b) + jnp.where(low1, pltpu.roll(a, 7, 0), pltpu.roll(b, 1, 0))


MESH = pl.DeviceIdType.MESH
VMEM_LIMIT = 60 * 1024 * 1024


def dot_nn(left, right, precision=None):
    return lax.dot_general(
        left, right, (((1,), (0,)), ((), ())), precision=precision,
        preferred_element_type=jnp.float32,
    )


def place():
    own, line = lax.axis_index("seq"), lax.axis_index("dp")
    return line, own, own // 2, lax.rem(own, 2)


def remote(source, target, send_sem, recv_sem, line, position):
    return pltpu.make_async_remote_copy(
        src_ref=source,
        dst_ref=target,
        send_sem=send_sem,
        recv_sem=recv_sem,
        device_id=(line, position),
        device_id_type=MESH,
    )


def greet(count, lines=1):
    line, own, _, _ = place()
    barrier = pltpu.get_barrier_semaphore()
    for k in range(1, count):
        pl.semaphore_signal(
            barrier, inc=1, device_id=(line, lax.rem(own + k, count)), device_id_type=MESH
        )
    for k in range(1, lines):
        pl.semaphore_signal(
            barrier, inc=1, device_id=(lax.rem(line + k, lines), own), device_id_type=MESH
        )
    pl.semaphore_wait(barrier, count - 1 + lines - 1)


def sigmoid(values):
    return 1.0 / (1.0 + jnp.exp(-values))


def softplus(values):
    return jnp.maximum(values, 0.0) + jnp.log1p(jnp.exp(-jnp.abs(values)))


class Cuts:
    def __init__(self, picks, rank, state, kernel):
        self.picks, self.rank, self.state, self.kernel = picks, rank, state, kernel
        self.step = picks
        self.decay = self.step + rank
        self.taps = self.decay + state
        self.conv_bias = self.taps + kernel
        self.step_bias = self.conv_bias + 1
        self.skip = self.step_bias + 1
        self.rows = self.skip + 1
        self.sent = -(-picks // 16) * 16


class Relay:
    def __init__(self, axis, half, high, low, seat, block, refs):
        self.axis, self.half, self.high, self.low = axis, half, high, low
        self.seat, self.block = seat, block
        self.other = lax.axis_index("dp" if axis == "seq" else "seq")
        self.part, self.across, self.along = refs[:3]
        self.send_x, self.recv_x, self.send_hi, self.recv_hi = refs[3:]

    def remote(self, source, target, send_sem, recv_sem, position):
        if self.axis == "seq":
            return remote(source, target, send_sem, recv_sem, self.other, position)
        return remote(source, target, send_sem, recv_sem, position, self.other)

    def over(self, i, low):
        return self.remote(
            self.part.at[self.block(i, low)], self.across.at[i], self.send_x.at[i],
            self.recv_x.at[i], self.seat(self.high, 1 - self.low),
        )

    def on(self, i):
        k = lax.rem(i - self.high + self.half, self.half)
        return self.remote(
            self.across.at[i], self.along.at[k], self.send_hi.at[k], self.recv_hi.at[k],
            self.seat(i, self.low),
        )

    def made(self, i, low):
        @pl.when(low != self.low)
        def _():
            self.over(i, low).start()

    def summed(self, i):
        self.over(i, self.low).wait_recv()
        return self.part[self.block(i, self.low)].astype(jnp.float32) + self.across[i].astype(
            jnp.float32
        )

    def pass_on(self, i, low):
        @pl.when((low == self.low) & (i != self.high))
        def _():
            self.across[i] = self.summed(i).astype(jnp.bfloat16)
            self.on(i).start()

    def finish(self, sent=None):
        total = self.summed(self.high)
        for k in range(1, self.half):
            self.on(lax.rem(self.high + k, self.half)).wait_recv()
            total = total + self.along[k].astype(jnp.float32)
        for i in range(self.half) if sent is None else sent:
            self.over(i, 1 - self.low).wait_send()
        for k in range(1, self.half):
            self.on(lax.rem(self.high + k, self.half)).wait_send()
        return total


def whole_relay(axis, count, refs):
    own = lax.axis_index(axis)

    def seat(i, low):
        return 2 * i + low

    return Relay(axis, count // 2, own // 2, lax.rem(own, 2), seat, seat, refs)


def relay_scratch(count, rows, width, part=True):
    half = count // 2
    dma = pltpu.SemaphoreType.DMA
    own = [pltpu.VMEM((count, rows, width), jnp.bfloat16)] if part else []
    return own + [
        pltpu.VMEM((half, rows, width), jnp.bfloat16),
        pltpu.VMEM((half, rows, width), jnp.bfloat16),
        dma((half,)), dma((half,)), dma((half,)), dma((half,)),
    ]


def square():
    own = lax.axis_index("seq")
    return own // 4, lax.rem(own // 2, 2), lax.rem(own, 2)


def seat_of(q, f, low):
    return 4 * q + 2 * f + low


class Gather:
    def __init__(self, count, shard_ref, land_ref, swap_s, swap_r, line_s, line_r, pair_s, pair_r):
        self.line = lax.axis_index("dp")
        self.q, self.f, self.low = square()
        self.quarter = count // 4
        self.shard, self.land = shard_ref, land_ref
        self.swap_s, self.swap_r = swap_s, swap_r
        self.line_s, self.line_r, self.pair_s, self.pair_r = line_s, line_r, pair_s, pair_r
        self.cut = land_ref.shape[2]

    def columns(self, f):
        return pl.ds(pl.multiple_of(f * self.cut, LANES), self.cut)

    def piece(self, j, k, low):
        q = lax.rem(self.q - k + self.quarter, self.quarter)
        return seat_of(q, lax.rem(self.f + j, 2), low)

    def swap(self):
        own = self.piece(0, 0, self.low)
        return remote(
            self.shard.at[:, self.columns(1 - self.f)], self.land.at[own], self.swap_s, self.swap_r,
            self.line, self.piece(1, 0, self.low),
        )

    def along(self, j, k):
        piece = self.piece(j, 0, self.low)
        there = seat_of(lax.rem(self.q + k, self.quarter), self.f, self.low)
        return remote(
            self.land.at[piece], self.land.at[piece], self.line_s.at[j, k], self.line_r.at[j, k],
            self.line, there,
        )

    def pair(self, j, k, low):
        piece = self.piece(j, k, low)
        return remote(
            self.land.at[piece], self.land.at[piece], self.pair_s.at[j, k], self.pair_r.at[j, k],
            self.line, seat_of(self.q, self.f, 1 - self.low),
        )

    def start(self):
        self.swap().start()
        self.land[self.piece(0, 0, self.low)] = self.shard[:, self.columns(self.f)]

    def spread(self, j):
        if j == 1:
            mate = self.piece(1, 0, self.low)
            remote(
                self.land.at[mate], self.land.at[mate], self.swap_s, self.swap_r, self.line, mate
            ).wait_recv()
        for k in range(1, self.quarter):
            self.along(j, k).start()
        self.pair(j, 0, self.low).start()

    def forward(self, j):
        for k in range(1, self.quarter):
            piece = self.piece(j, k, self.low)
            remote(
                self.land.at[piece], self.land.at[piece], self.line_s.at[j, k],
                self.line_r.at[j, k], self.line, piece,
            ).wait_recv()
            self.pair(j, k, self.low).start()

    def finish(self):
        for j in range(2):
            for k in range(self.quarter):
                self.pair(j, k, 1 - self.low).wait_recv()
        self.swap().wait_send()
        for j in range(2):
            for k in range(1, self.quarter):
                self.along(j, k).wait_send()
            for k in range(self.quarter):
                self.pair(j, k, self.low).wait_send()


def gather_scratch(count):
    dma = pltpu.SemaphoreType.DMA
    quarter = count // 4
    return [dma, dma] + [dma((2, quarter)) for _ in range(4)]


class Scatter:
    def __init__(self, count, part_ref, far_ref, other_ref, held_ref, swap_s, swap_r, refs):
        self.line = lax.axis_index("dp")
        self.q, self.f, self.low = square()
        self.quarter = count // 4
        self.far, self.other, self.held = far_ref, other_ref, held_ref
        self.swap_s, self.swap_r = swap_s, swap_r
        self.relays = []
        for j in range(2):
            cut = lax.rem(self.f + j, 2)

            def seat(i, low):
                return seat_of(i, self.f, low)

            def block(i, low, cut=cut):
                return seat_of(i, cut, low)

            mine = tuple(ref.at[j] for ref in refs)
            self.relays.append(
                Relay("seq", self.quarter, self.q, self.low, seat, block, (part_ref, *mine))
            )

    def swap(self):
        return remote(
            self.held, self.other, self.swap_s, self.swap_r, self.line,
            seat_of(self.q, 1 - self.f, self.low),
        )

    def far_places(self):
        return [
            (j, lax.rem(self.q + k, self.quarter)) for k in range(1, self.quarter) for j in (1, 0)
        ]

    def send_far(self):
        for j, i in self.far_places():
            self.relays[j].over(i, 1 - self.low).start()

    def pass_far(self):
        for j, i in self.far_places():
            relay = self.relays[j]
            if self.far is None:
                relay.pass_on(i, self.low)
            else:
                both = relay.part[relay.block(i, self.low)].astype(jnp.float32) + self.far[
                    j, i
                ].astype(jnp.float32)
                relay.across[i] = both.astype(jnp.bfloat16)
                relay.on(i).start()

    def total(self, j):
        return self.relays[j].finish(None if self.far is None else [self.q])

    def send_near(self):
        for j in (1, 0):
            self.relays[j].over(self.q, 1 - self.low).start()

    def hand_over(self):
        self.held[...] = self.total(1).astype(jnp.bfloat16)
        self.swap().start()

    def finish(self, out_ref):
        cut = self.held.shape[1]
        out_ref[:, pl.ds(pl.multiple_of(self.f * cut, LANES), cut)] = self.total(0)
        self.swap().wait_recv()
        out_ref[:, pl.ds(pl.multiple_of((1 - self.f) * cut, LANES), cut)] = self.other[...].astype(
            jnp.float32
        )
        self.swap().wait_send()


def scatter_scratch(count, rows, cut):
    dma = pltpu.SemaphoreType.DMA
    quarter = count // 4
    return [
        pltpu.VMEM((rows, cut), jnp.bfloat16),
        pltpu.VMEM((rows, cut), jnp.bfloat16),
        dma, dma,
        pltpu.VMEM((2, quarter, rows, cut), jnp.bfloat16),
        pltpu.VMEM((2, quarter, rows, cut), jnp.bfloat16),
        *[dma((2, quarter)) for _ in range(4)],
    ]


def front_kernel(
    count, lines, cuts,
    x_ref, gain_ref, input_ref, output_ref, select_ref, step_ref, decay_ref, taps_ref, conv_bias_ref,
    step_bias_ref, skip_ref, expert_ref,
    all_ref, weights_ref, small_ref, ext_ref, sum_ref, act_ref, gate_ref, selected_ref, land_ref,
    normed_ref, packed_ref, table_ref, part_ref, partial_ref, total_ref,
    send_w, recv_w, send_up, send_down, recv_hi, send_x, recv_x, send_rs, recv_rs, send_ag, recv_ag,
    *gather_refs,
):
    line, own, high, low = place()
    half = count // 2
    gather = Gather(count, expert_ref, land_ref, *gather_refs)
    rows, width = x_ref.shape
    shard = packed_ref.shape[0]
    inner = weights_ref.shape[0]
    kernel = cuts.kernel
    partner = 2 * high + 1 - low

    own_shard = output_ref.shape[0]
    extra = jnp.zeros((shard - own_shard, width), jnp.float32)

    def padded(values):
        return jnp.concatenate([values.astype(jnp.float32), extra], axis=0).astype(jnp.bfloat16)

    packed_ref[:, :width] = padded(input_ref[0])
    packed_ref[:, width : 2 * width] = padded(input_ref[1])
    packed_ref[:, 2 * width : 3 * width] = padded(output_ref[...])
    table_ref[...] = jnp.zeros_like(table_ref)
    table_ref[:own_shard, : cuts.picks] = select_ref[...].astype(jnp.float32)
    picked = table_ref[:LANES, :].T
    table_ref[...] = jnp.zeros_like(table_ref)
    table_ref[:LANES, :] = picked
    for at, ref in (
        (cuts.step, step_ref),
        (cuts.decay, decay_ref),
        (cuts.taps, taps_ref),
        (cuts.conv_bias, conv_bias_ref),
        (cuts.step_bias, step_bias_ref),
        (cuts.skip, skip_ref),
    ):
        table_ref[at : at + ref.shape[0], :own_shard] = ref[...].astype(jnp.float32)
    packed_ref[:, 3 * width :] = table_ref[...].T[:shard].astype(jnp.bfloat16)
    x = x_ref[...]
    scale = lax.rsqrt(jnp.mean(x * x, axis=1, keepdims=True) + 1e-05)
    normed_ref[...] = (x * scale * gain_ref[...]).astype(jnp.bfloat16)
    greet(count, lines)

    copies = []
    shard_rows = pl.ds(pl.multiple_of(line * shard, 16), shard)
    def step_on(i, up):
        block = 2 * i + low
        return remote(
            all_ref.at[block], all_ref.at[block], (send_up if up else send_down).at[i],
            recv_hi.at[i], line, 2 * (high + (1 if up else -1)) + low,
        )

    def can_go(up):
        return high < half - 1 if up else high > 0

    all_ref[own] = normed_ref[...]
    for up in (True, False):

        @pl.when(can_go(up))
        def _(up=up):
            step_on(high, up).start()

    remote(all_ref.at[own], all_ref.at[own], send_x.at[high], recv_x.at[high], line, partner).start()
    for k in range(1, lines):
        copy = remote(
            packed_ref, weights_ref.at[shard_rows], send_w.at[k], recv_w.at[k],
            lax.rem(line + k, lines), own,
        )
        copy.start()
        copies.append(copy)
    gather.start()
    weights_ref[shard_rows, :] = packed_ref[...]
    if lines * shard < inner:
        weights_ref[lines * shard :, :] = jnp.zeros(
            (inner - lines * shard, weights_ref.shape[1]), weights_ref.dtype
        )
    ext_ref[0:8, :] = jnp.zeros((8, inner), jnp.float32)
    def cross(i):
        block = 2 * i + low
        return remote(
            all_ref.at[block], all_ref.at[block], send_x.at[i], recv_x.at[i], line, partner
        )

    for k in range(1, half):
        for up in (True, False):
            i = high - k if up else high + k

            @pl.when(i >= 0 if up else i < half)
            def _(i=i, up=up):
                step_on(i, up).wait_recv()

                @pl.when(can_go(up))
                def _():
                    step_on(i, up).start()

                cross(i).start()

    gather.spread(0)
    gather.spread(1)
    for k in range(1, lines):
        from_line = lax.rem(line - k + lines, lines)
        there = pl.ds(pl.multiple_of(from_line * shard, 16), shard)
        remote(
            packed_ref, weights_ref.at[there], send_w.at[k], recv_w.at[k], from_line, own
        ).wait_recv()
    small_ref[...] = weights_ref[:, 3 * width :].astype(jnp.float32).T
    for i in range(half):
        block = 2 * i + 1 - low
        remote(
            all_ref.at[block], all_ref.at[block], send_x.at[i], recv_x.at[i], line, partner
        ).wait_recv()

    def project(b, carry):
        start = pl.multiple_of(b * rows, rows)
        block = all_ref[b]
        ext_ref[pl.ds(pl.multiple_of(start + 8, 8), rows), :] = outer_cols(
            block, weights_ref[:, :width]
        )
        gate_ref[pl.ds(start, rows), :] = outer_cols(block, weights_ref[:, width : 2 * width])
        return carry

    lax.fori_loop(0, count, project, 0)

    def convolve(b, carry):
        start = pl.multiple_of(b * rows, rows)
        window = ext_ref[pl.ds(start, rows + 8), :]
        total = small_ref[cuts.conv_bias : cuts.conv_bias + 1, :]
        for k in range(kernel):
            tap = small_ref[cuts.taps + k : cuts.taps + k + 1, :]
            total = total + tap * window[9 - kernel + k : 9 - kernel + k + rows]
        act = total * sigmoid(total)
        sum_ref[pl.ds(start, rows), :] = total
        act_ref[pl.ds(start, rows), :] = act
        part_ref[b] = outer_cols(
            small_ref[: cuts.sent, :].astype(jnp.bfloat16), act.astype(jnp.bfloat16)
        ).astype(jnp.bfloat16)
        return carry

    lax.fori_loop(0, count, convolve, 0)

    for k in range(1, count):
        there = lax.rem(own + k, count)
        copy = remote(
            part_ref.at[there], partial_ref.at[k], send_rs.at[k], recv_rs.at[k], line, there
        )
        copy.start()
        copies.append(copy)
    total = part_ref[own].astype(jnp.float32)
    for k in range(1, count):
        remote(
            part_ref.at[own], partial_ref.at[k], send_rs.at[k], recv_rs.at[k], line, partner
        ).wait_recv()
        total = total + partial_ref[k].astype(jnp.float32)
    total_ref[own] = total.astype(jnp.bfloat16)
    for k in range(1, count):
        copy = remote(
            total_ref.at[own], total_ref.at[own], send_ag.at[k], recv_ag.at[k],
            line, lax.rem(own + k, count),
        )
        copy.start()
        copies.append(copy)
    gather.forward(0)
    gather.forward(1)
    for k in range(1, count):
        block = lax.rem(own - k + count, count)
        remote(
            total_ref.at[block], total_ref.at[block], send_ag.at[k], recv_ag.at[k],
            line, partner,
        ).wait_recv()
    selected_ref[...] = total_ref[...].astype(jnp.float32)[:, : cuts.picks]
    for copy in copies:
        copy.wait_send()
    for i in range(half):
        cross(i).wait_send()
        for up in (True, False):

            @pl.when(can_go(up) & (i <= high if up else i >= high))
            def _(i=i, up=up):
                step_on(i, up).wait_send()

    gather.finish()


def front(count, lines, cuts, shard, small, *args):
    rows, width = args[0].shape
    expert = args[-1]
    columns = 3 * width + small
    inner = -(-lines * shard // LANES) * LANES
    length = count * rows
    half = count // 2
    vmem = pl.BlockSpec(memory_space=pltpu.VMEM)

    def f32(*shape):
        return jax.ShapeDtypeStruct(shape, jnp.float32)

    dma = pltpu.SemaphoreType.DMA
    return pl.pallas_call(
        functools.partial(front_kernel, count, lines, cuts),
        in_specs=[vmem] * len(args),
        out_specs=[vmem] * 9,
        out_shape=[
            jax.ShapeDtypeStruct((count, rows, width), jnp.bfloat16),
            jax.ShapeDtypeStruct((inner, columns), jnp.bfloat16),
            f32(small, inner),
            f32(length + 8, inner),
            f32(length, inner),
            f32(length, inner),
            f32(length, inner),
            f32(count, cuts.picks, rows),
            jax.ShapeDtypeStruct((count, expert.shape[0], expert.shape[1] // 2), jnp.bfloat16),
        ],
        scratch_shapes=[
            pltpu.VMEM((rows, width), jnp.bfloat16),
            pltpu.VMEM((shard, columns), jnp.bfloat16),
            pltpu.VMEM((small, LANES), jnp.float32),
            *[pltpu.VMEM((count, cuts.sent, rows), jnp.bfloat16)] * 3,
            dma((lines,)), dma((lines,)), dma((half,)), dma((half,)), dma((half,)), dma((half,)),
            dma((half,)), dma((count,)), dma((count,)), dma((count,)), dma((count,)),
            *gather_scratch(count),
        ],
        compiler_params=pltpu.CompilerParams(
            collective_id=0, has_side_effects=True, vmem_limit_bytes=VMEM_LIMIT
        ),
        cost_estimate=pl.CostEstimate(
            flops=4 * length * width * inner,
            bytes_accessed=20 * length * inner,
            transcendentals=length * inner,
        ),
        name="front",
    )(*args)


def spread_lanes(values, wide_ref, out_ref):
    state, steps = values.shape
    high = values.astype(jnp.bfloat16).astype(jnp.float32)
    rest = values - high
    lane = lax.broadcasted_iota(jnp.int32, (state, steps), 1)

    def fill(g, carry):
        for k in range(8):
            t = g * 8 + k
            here = pl.ds(pl.multiple_of(t * state, state), state)
            mask = lane == t
            wide_ref[here, :steps] = jnp.where(mask, high, 0.0).astype(jnp.bfloat16)
            wide_ref[here, steps:] = jnp.where(mask, rest, 0.0).astype(jnp.bfloat16)
        return carry

    lax.fori_loop(0, steps // 8, fill, 0)
    ones = jnp.ones((2 * steps, LANES), jnp.bfloat16)
    out_ref[...] = dot_nn(wide_ref[...], ones)


def scan_forward_kernel(
    count, cuts,
    act_ref, gate_ref, selected_ref, small_ref, output_ref, expert_ref,
    pre_ref, mixed_ref, mixer_low_ref, prior_ref, end_ref, summed_ref, expert_out_ref,
    state_ref, delta_ref, scanned_ref, wide_ref, wide_in_ref, wide_out_ref, land_ref, *refs,
):
    steps, inner = act_ref.shape
    tiles = inner // LANES
    state = cuts.state
    halves = state // 8
    step = pl.program_id(0)
    relay = whole_relay("seq", count, refs[:7])
    gather = Gather(count, expert_ref, land_ref, *refs[7:])

    @pl.when(step == 0)
    def _():
        greet(count)
        gather.start()
        state_ref[...] = jnp.zeros_like(state_ref)

    @pl.when(step == 0)
    def _():
        gather.spread(0)

    @pl.when(step == 3)
    def _():
        gather.spread(1)

    rates2 = -LOG2E * jnp.exp(small_ref[cuts.decay : cuts.decay + state, :])
    pre = inner_rows(
        selected_ref[0, : cuts.rank, :],
        small_ref[cuts.step : cuts.step + cuts.rank, :],
        HIGHEST,
    ) + small_ref[cuts.step_bias : cuts.step_bias + 1, :]
    pre_ref[...] = pre
    delta_ref[...] = softplus(pre)
    in_rows = cuts.rank
    out_rows = cuts.rank + state
    spread_lanes(selected_ref[0, in_rows : in_rows + state, :], wide_ref, wide_in_ref)
    spread_lanes(selected_ref[0, out_rows : out_rows + state, :], wide_ref, wide_out_ref)

    def group(g, states):
        states = [list(s) for s in states]
        base = pl.multiple_of(g * 8, 8)
        d8 = delta_ref[pl.ds(base, 8), :]
        du8 = d8 * act_ref[pl.ds(base, 8), :]
        parts = [[None] * 8 for _ in range(tiles)]
        for k in range(8):
            rows_now = [pl.ds((base + k) * state + 8 * i, 8) for i in range(halves)]
            b_now = [wide_in_ref[here, :] for here in rows_now]
            c_now = [wide_out_ref[here, :] for here in rows_now]
            for j in range(tiles):
                cols = slice(j * LANES, (j + 1) * LANES)
                d = jnp.broadcast_to(d8[k : k + 1, cols], (8, LANES))
                du = jnp.broadcast_to(du8[k : k + 1, cols], (8, LANES))
                total = None
                for i in range(halves):
                    old = states[j][i]
                    prior_ref[base + k, 8 * i : 8 * i + 8, cols] = old
                    new = jnp.exp2(d * rates2[8 * i : 8 * i + 8, cols]) * old + b_now[i] * du
                    states[j][i] = new
                    term = c_now[i] * new
                    total = term if total is None else total + term
                parts[j][k] = total
        for j in range(tiles):
            scanned_ref[pl.ds(base, 8), j * LANES : (j + 1) * LANES] = sublane_sums(parts[j])
        return tuple(tuple(s) for s in states)

    first = tuple(
        tuple(
            state_ref[8 * i : 8 * i + 8, j * LANES : (j + 1) * LANES] for i in range(halves)
        )
        for j in range(tiles)
    )
    last = lax.fori_loop(0, steps // 8, group, first)
    for j in range(tiles):
        for i in range(halves):
            state_ref[8 * i : 8 * i + 8, j * LANES : (j + 1) * LANES] = last[j][i]
    end_ref[...] = state_ref[...]

    mixed = scanned_ref[...] + small_ref[cuts.skip : cuts.skip + 1, :] * act_ref[...]
    gate = gate_ref[...]
    low = (mixed * (gate * sigmoid(gate))).astype(jnp.bfloat16)
    mixed_ref[...] = mixed
    mixer_low_ref[...] = low
    relay.part[step] = dot_nn(low, output_ref[...]).astype(jnp.bfloat16)
    relay.made(step // 2, lax.rem(step, 2))

    def pass_on(block):
        relay.pass_on(block // 2, lax.rem(block, 2))

    @pl.when(step >= LAG)
    def _():
        pass_on(step - LAG)

    @pl.when(step == count - 1)
    def _():
        for late in range(LAG - 1, -1, -1):
            pass_on(step - late)
        gather.forward(0)
        gather.forward(1)
        summed_ref[...] = relay.finish()
        gather.finish()
        expert_out_ref[...] = land_ref[...]


def scan_forward(count, cuts, width, act, gate, selected, small, weights, expert):
    length, inner = act.shape
    state = cuts.state
    block = length // count
    rows = pl.BlockSpec((block, inner), lambda t: (t, 0))
    whole = pl.BlockSpec((state, inner), lambda t: (0, 0))
    pieces = (count, expert.shape[0], expert.shape[1] // 2)
    return pl.pallas_call(
        functools.partial(scan_forward_kernel, count, cuts),
        grid=(count,),
        in_specs=[
            rows,
            rows,
            pl.BlockSpec((1, cuts.picks, block), lambda t: (t, 0, 0)),
            pl.BlockSpec(small.shape, lambda t: (0, 0)),
            pl.BlockSpec((inner, width), lambda t: (0, 2)),
            pl.BlockSpec(expert.shape, lambda t: (0, 0)),
        ],
        out_specs=[
            rows,
            rows,
            rows,
            pl.BlockSpec((block, state, inner), lambda t: (t, 0, 0)),
            whole,
            pl.BlockSpec((block, width), lambda t: (0, 0)),
            pl.BlockSpec(pieces, lambda t: (0, 0, 0)),
        ],
        out_shape=[
            jax.ShapeDtypeStruct((length, inner), jnp.float32),
            jax.ShapeDtypeStruct((length, inner), jnp.float32),
            jax.ShapeDtypeStruct((length, inner), jnp.bfloat16),
            jax.ShapeDtypeStruct((length, state, inner), jnp.float32),
            jax.ShapeDtypeStruct((state, inner), jnp.float32),
            jax.ShapeDtypeStruct((block, width), jnp.float32),
            jax.ShapeDtypeStruct(pieces, jnp.bfloat16),
        ],
        scratch_shapes=[
            pltpu.VMEM((state, inner), jnp.float32),
            pltpu.VMEM((block, inner), jnp.float32),
            pltpu.VMEM((block, inner), jnp.float32),
            pltpu.VMEM((block * state, 2 * block), jnp.bfloat16),
            pltpu.VMEM((block * state, LANES), jnp.float32),
            pltpu.VMEM((block * state, LANES), jnp.float32),
            pltpu.VMEM(pieces, jnp.bfloat16),
            *relay_scratch(count, block, width),
            *gather_scratch(count),
        ],
        compiler_params=pltpu.CompilerParams(
            collective_id=1, has_side_effects=True, vmem_limit_bytes=VMEM_LIMIT
        ),
        cost_estimate=pl.CostEstimate(
            flops=8 * length * state * inner,
            bytes_accessed=4 * length * inner * (state + 6),
            transcendentals=length * state * inner,
        ),
        name="scan_forward",
    )(act, gate, selected, small, weights, expert)


def scan_backward_kernel(
    count, cuts,
    own_ref, act_ref, gate_ref, mixed_ref, pre_ref, selected_ref, small_ref, output_ref,
    prior_ref, end_ref, expert_ref,
    grad_gate_ref, grad_act_ref, grad_step_ref, rate_total_ref, rows_ref, grad_selected_ref,
    all_out_ref, expert_out_ref,
    incoming_ref, post_ref, delta_ref, grad_ref, grad_delta_ref, wide_ref, wide_in_ref,
    wide_out_ref, all_ref,
    stage_ref, part_ref, partial_ref, total_ref,
    send_hi, recv_hi, send_x, recv_x, send_rs, recv_rs, send_ag, recv_ag,
    other_ref, held_ref, swap_s, swap_r, *scatter_refs,
):
    steps, inner = act_ref.shape
    tiles = inner // LANES
    state = cuts.state
    halves = state // 8
    lane = lax.broadcasted_iota(jnp.int32, (8, steps), 1)
    line, own, high, low = place()
    half = count // 2
    partner = 2 * high + 1 - low
    index = pl.program_id(0)
    now = count - 1 - index
    scatter = Scatter(
        count, expert_ref, None, other_ref, held_ref, swap_s, swap_r, scatter_refs
    )

    def along(k):
        return remote(
            own_ref, all_ref.at[own], send_hi.at[k], recv_hi.at[high], line,
            2 * lax.rem(high + k, half) + low,
        )

    def across(block):
        i = block // 2
        return remote(
            all_ref.at[block], all_ref.at[block], send_x.at[i], recv_x.at[i], line, partner
        )

    def came_along(block):
        i = block // 2
        return remote(
            all_ref.at[block], all_ref.at[block], send_hi.at[0], recv_hi.at[i], line, partner
        )

    def hand_over(block):
        @pl.when((lax.rem(block, 2) == low) & (block // 2 != high))
        def _():
            came_along(block).wait_recv()
            across(block).start()

    @pl.when(index == 0)
    def _():
        greet(count)
        all_ref[own] = own_ref[...]
        incoming_ref[...] = jnp.zeros_like(incoming_ref)
        post_ref[...] = end_ref[...]
        rate_total_ref[...] = jnp.zeros_like(rate_total_ref)
        grad_step_ref[...] = jnp.zeros_like(grad_step_ref)
        rows_ref[...] = jnp.zeros_like(rows_ref)
        stage_ref[...] = jnp.zeros_like(stage_ref)

    @pl.when(index == jnp.maximum(count - 3 - own, 0))
    def _():
        for k in range(1, half):
            along(k).start()
        across(own).start()

    @pl.when(index == 0)
    def _():
        hand_over(now)
        hand_over(now - 1)

    @pl.when(lax.rem(now, 2) != low)
    def _():
        across(now).wait_recv()

    gate = gate_ref[...]
    gate_sig = sigmoid(gate)
    grad_y = outer_cols(all_ref[now], output_ref[...])
    grad_gate_ref[...] = (
        grad_y * mixed_ref[...] * (gate_sig * (1.0 + gate * (1.0 - gate_sig)))
    ).astype(jnp.bfloat16)
    grad_mixed = grad_y * (gate * gate_sig)
    grad_ref[...] = grad_mixed
    delta_ref[...] = softplus(pre_ref[...])
    rows_ref[1:2, :] += jnp.sum(grad_mixed * act_ref[...], axis=0, keepdims=True)
    rates2 = -LOG2E * jnp.exp(small_ref[cuts.decay : cuts.decay + state, :])
    in_rows = cuts.rank
    out_rows = cuts.rank + state
    spread_lanes(selected_ref[0, in_rows : in_rows + state, :], wide_ref, wide_in_ref)
    spread_lanes(selected_ref[0, out_rows : out_rows + state, :], wide_ref, wide_out_ref)

    def tile_of(ref):
        return tuple(
            tuple(ref[8 * i : 8 * i + 8, j * LANES : (j + 1) * LANES] for i in range(halves))
            for j in range(tiles)
        )

    def group(turn, carry):
        incoming, posts, rate_total, in_acc, out_acc = carry
        incoming = [list(s) for s in incoming]
        posts = [list(s) for s in posts]
        rate_total = [list(s) for s in rate_total]
        in_acc, out_acc = list(in_acc), list(out_acc)
        base = pl.multiple_of((steps // 8 - 1 - turn) * 8, 8)
        d8 = delta_ref[pl.ds(base, 8), :]
        u8 = act_ref[pl.ds(base, 8), :]
        du8 = d8 * u8
        g8 = grad_ref[pl.ds(base, 8), :]
        rate_parts = [[None] * 8 for _ in range(tiles)]
        side_parts = [[None] * 8 for _ in range(tiles)]
        for k in range(7, -1, -1):
            rows_now = [pl.ds((base + k) * state + 8 * i, 8) for i in range(halves)]
            b_now = [wide_in_ref[here, :] for here in rows_now]
            c_now = [wide_out_ref[here, :] for here in rows_now]
            in_sum = [None] * halves
            out_sum = [None] * halves
            for j in range(tiles):
                cols = slice(j * LANES, (j + 1) * LANES)
                d = jnp.broadcast_to(d8[k : k + 1, cols], (8, LANES))
                du = jnp.broadcast_to(du8[k : k + 1, cols], (8, LANES))
                gm = jnp.broadcast_to(g8[k : k + 1, cols], (8, LANES))
                rate_part = None
                side_part = None
                for i in range(halves):
                    prior = prior_ref[base + k, 8 * i : 8 * i + 8, cols]
                    rates = rates2[8 * i : 8 * i + 8, cols]
                    grad_state = c_now[i] * gm + incoming[j][i]
                    passed = jnp.exp2(d * rates) * grad_state
                    incoming[j][i] = passed
                    weighted = passed * prior
                    term = weighted * rates
                    rate_part = term if rate_part is None else rate_part + term
                    term = grad_state * b_now[i]
                    side_part = term if side_part is None else side_part + term
                    term = grad_state * du
                    in_sum[i] = term if in_sum[i] is None else in_sum[i] + term
                    term = posts[j][i] * gm
                    out_sum[i] = term if out_sum[i] is None else out_sum[i] + term
                    rate_total[j][i] = rate_total[j][i] + weighted * d
                    posts[j][i] = prior
                rate_parts[j][k] = rate_part
                side_parts[j][k] = side_part
            here = lane == base + k
            for i in range(halves):
                in_acc[i] = jnp.where(here, jnp.sum(in_sum[i], axis=1, keepdims=True), in_acc[i])
                out_acc[i] = jnp.where(here, jnp.sum(out_sum[i], axis=1, keepdims=True), out_acc[i])
        for j in range(tiles):
            cols = slice(j * LANES, (j + 1) * LANES)
            side = sublane_sums(side_parts[j])
            grad_delta_ref[pl.ds(base, 8), cols] = (
                sublane_sums(rate_parts[j]) * (1.0 / LOG2E) + u8[:, cols] * side
            )
            grad_act_ref[pl.ds(base, 8), cols] = d8[:, cols] * side
        return (
            tuple(tuple(s) for s in incoming),
            tuple(tuple(s) for s in posts),
            tuple(tuple(s) for s in rate_total),
            tuple(in_acc),
            tuple(out_acc),
        )

    empty = tuple(jnp.zeros((8, steps), jnp.float32) for _ in range(halves))
    incoming, posts, rate_total, in_acc, out_acc = lax.fori_loop(
        0,
        steps // 8,
        group,
        (tile_of(incoming_ref), tile_of(post_ref), tile_of(rate_total_ref), empty, empty),
    )
    for i in range(halves):
        stage_ref[in_rows + 8 * i : in_rows + 8 * i + 8, :] = in_acc[i]
        stage_ref[out_rows + 8 * i : out_rows + 8 * i + 8, :] = out_acc[i]
        for j in range(tiles):
            cols = slice(j * LANES, (j + 1) * LANES)
            incoming_ref[8 * i : 8 * i + 8, cols] = incoming[j][i]
            post_ref[8 * i : 8 * i + 8, cols] = posts[j][i]
            rate_total_ref[8 * i : 8 * i + 8, cols] = rate_total[j][i]

    grad_act_ref[...] += grad_ref[...] * small_ref[cuts.skip : cuts.skip + 1, :]
    grad_pre = grad_delta_ref[...] * sigmoid(pre_ref[...])
    rows_ref[0:1, :] += jnp.sum(grad_pre, axis=0, keepdims=True)
    grad_step_ref[...] += dot_nn(selected_ref[0, : cuts.rank, :], grad_pre, HIGHEST)
    stage_ref[: cuts.rank, :] = outer_cols(
        small_ref[cuts.step : cuts.step + cuts.rank, :], grad_pre, HIGHEST
    )
    part_ref[now] = stage_ref[...].astype(jnp.bfloat16)

    def partial_to(block):
        return remote(
            part_ref.at[block], partial_ref.at[own], send_rs.at[block], recv_rs.at[own], line, block
        )

    @pl.when(now != own)
    def _():
        partial_to(now).start()

    def total_to(k):
        return remote(
            total_ref.at[own], total_ref.at[own], send_ag.at[k], recv_ag.at[own], line,
            lax.rem(own + k, count),
        )

    @pl.when(now >= 2)
    def _():
        hand_over(now - 2)

    @pl.when(index == NEAR_AT)
    def _():
        scatter.send_near()

    @pl.when(index == FAR_AT)
    def _():
        scatter.send_far()

    @pl.when(index == PASS_AT)
    def _():
        scatter.pass_far()

    @pl.when(index == count - 1)
    def _():
        scatter.hand_over()

    @pl.when(index == jnp.minimum(count - 1 - own + 2, count - 1))
    def _():
        total = part_ref[own].astype(jnp.float32)
        for k in range(1, count):
            there = lax.rem(own + k, count)
            remote(
                part_ref.at[own], partial_ref.at[there], send_rs.at[own], recv_rs.at[there],
                line, there,
            ).wait_recv()
            total = total + partial_ref[there].astype(jnp.float32)
        total_ref[own] = total.astype(jnp.bfloat16)
        for k in range(1, count):
            total_to(k).start()

    @pl.when(index == count - 1)
    def _():
        for k in range(1, count):
            there = lax.rem(own + k, count)
            remote(
                total_ref.at[there], total_ref.at[there], send_ag.at[k], recv_ag.at[there],
                line, there,
            ).wait_recv()
        grad_selected_ref[...] = total_ref[...]
        all_out_ref[...] = all_ref[...]
        for k in range(1, half):
            along(k).wait_send()
        for i in range(half):
            across(2 * i + low).wait_send()
        for k in range(1, count):
            partial_to(lax.rem(own + k, count)).wait_send()
            total_to(k).wait_send()
        scatter.finish(expert_out_ref)


def scan_backward(
    count, cuts, grad_low, act, gate, mixed, pre, selected, small, weights, priors, end, expert
):
    length, inner = act.shape
    state = cuts.state
    block = length // count
    width = grad_low.shape[1]
    half = count // 2

    def back(t):
        return count - 1 - t

    rows = pl.BlockSpec((block, inner), lambda t: (back(t), 0))
    whole = pl.BlockSpec((state, inner), lambda t: (0, 0))
    dma = pltpu.SemaphoreType.DMA
    picked = (count, cuts.sent, block)
    return pl.pallas_call(
        functools.partial(scan_backward_kernel, count, cuts),
        grid=(count,),
        in_specs=[
            pl.BlockSpec((block, width), lambda t: (0, 0)),
            rows,
            rows,
            rows,
            rows,
            pl.BlockSpec((1, cuts.picks, block), lambda t: (back(t), 0, 0)),
            pl.BlockSpec(small.shape, lambda t: (0, 0)),
            pl.BlockSpec((inner, width), lambda t: (0, 2)),
            pl.BlockSpec((block, state, inner), lambda t: (back(t), 0, 0)),
            whole,
            pl.BlockSpec(expert.shape, lambda t: (0, 0, 0)),
        ],
        out_specs=[
            rows,
            rows,
            pl.BlockSpec((cuts.rank, inner), lambda t: (0, 0)),
            whole,
            pl.BlockSpec((8, inner), lambda t: (0, 0)),
            pl.BlockSpec(picked, lambda t: (0, 0, 0)),
            pl.BlockSpec((count, block, width), lambda t: (0, 0, 0)),
            pl.BlockSpec((expert.shape[1], 2 * expert.shape[2]), lambda t: (0, 0)),
        ],
        out_shape=[
            jax.ShapeDtypeStruct((length, inner), jnp.bfloat16),
            jax.ShapeDtypeStruct((length, inner), jnp.float32),
            jax.ShapeDtypeStruct((cuts.rank, inner), jnp.float32),
            jax.ShapeDtypeStruct((state, inner), jnp.float32),
            jax.ShapeDtypeStruct((8, inner), jnp.float32),
            jax.ShapeDtypeStruct(picked, jnp.bfloat16),
            jax.ShapeDtypeStruct((count, block, width), jnp.bfloat16),
            jax.ShapeDtypeStruct((expert.shape[1], 2 * expert.shape[2]), jnp.float32),
        ],
        scratch_shapes=[
            pltpu.VMEM((state, inner), jnp.float32),
            pltpu.VMEM((state, inner), jnp.float32),
            pltpu.VMEM((block, inner), jnp.float32),
            pltpu.VMEM((block, inner), jnp.float32),
            pltpu.VMEM((block, inner), jnp.float32),
            pltpu.VMEM((block * state, 2 * block), jnp.bfloat16),
            pltpu.VMEM((block * state, LANES), jnp.float32),
            pltpu.VMEM((block * state, LANES), jnp.float32),
            pltpu.VMEM((count, block, width), jnp.bfloat16),
            pltpu.VMEM(picked[1:], jnp.float32),
            *[pltpu.VMEM(picked, jnp.bfloat16)] * 3,
            dma((half,)), dma((half,)), dma((half,)), dma((half,)),
            dma((count,)), dma((count,)), dma((count,)), dma((count,)),
            *scatter_scratch(count, expert.shape[1], expert.shape[2]),
        ],
        compiler_params=pltpu.CompilerParams(
            collective_id=2, has_side_effects=True, vmem_limit_bytes=VMEM_LIMIT
        ),
        cost_estimate=pl.CostEstimate(
            flops=20 * length * state * inner,
            bytes_accessed=4 * length * inner * (state + 6),
            transcendentals=length * state * inner,
        ),
        name="scan_backward",
    )(grad_low, act, gate, mixed, pre, selected, small, weights, priors, end, expert)


def back_kernel(
    count, lines, cuts,
    grad_selected_ref, small_ref, weights_ref, ext_ref, sum_ref, grad_act_ref, grad_gate_ref,
    mixer_low_ref, normed_ref, grad_middle_ref, grad_step_ref, rate_total_ref, scan_rows_ref,
    vectors_ref, expert_ref, far_ref, x_ref, gain_ref, kept_ref,
    tokens_ref, input_ref, output_ref, select_ref, step_ref, decay_ref, taps_ref, conv_bias_ref,
    step_bias_ref, skip_ref, totals_ref, expert_out_ref,
    grad_sum_ref, grad_conv_ref, grad_small_ref, ours_ref, theirs_ref,
    send_v, recv_v, send_u, recv_u, other_ref, held_ref, swap_s, swap_r, *refs,
):
    scatter = Scatter(count, expert_ref, far_ref, other_ref, held_ref, swap_s, swap_r, refs[:6])
    relay = whole_relay("seq", count, refs[6:13])
    spread = whole_relay("dp", lines, refs[13:])
    line, own, _, _ = place()
    length, inner = sum_ref.shape
    width = normed_ref.shape[1]
    rows = length // count
    kernel = cuts.kernel
    shard = spread.part.shape[1]
    own_shard = output_ref.shape[0]
    greet(count, lines)
    scatter.pass_far()
    scatter.send_near()
    grad_small_ref[...] = jnp.zeros_like(grad_small_ref)
    grad_sum_ref[length:, :] = jnp.zeros((8, inner), jnp.float32)
    select = small_ref[: cuts.sent, :].astype(jnp.bfloat16)

    def first(b, carry):
        start = pl.multiple_of(b * rows, rows)
        grad_selected = grad_selected_ref[b]
        total = sum_ref[pl.ds(start, rows), :]
        sig = sigmoid(total)
        grad_act = grad_act_ref[pl.ds(start, rows), :] + inner_rows(grad_selected, select)
        grad_sum = grad_act * (sig * (1.0 + total * (1.0 - sig)))
        grad_sum_ref[pl.ds(start, rows), :] = grad_sum
        grad_small_ref[: cuts.sent, :] += dot_nn(
            grad_selected, (total * sig).astype(jnp.bfloat16)
        )
        window = ext_ref[pl.ds(start, rows + 8), :]
        for k in range(kernel):
            row = slice(cuts.taps + k, cuts.taps + k + 1)
            grad_small_ref[row, :] += jnp.sum(
                grad_sum * window[9 - kernel + k : 9 - kernel + k + rows], axis=0, keepdims=True
            )
        row = slice(cuts.conv_bias, cuts.conv_bias + 1)
        grad_small_ref[row, :] += jnp.sum(grad_sum, axis=0, keepdims=True)
        return carry

    lax.fori_loop(0, count, first, 0)

    def order(j):
        return j // 2 + lax.rem(j, 2) * (count // 2)

    def second(j, carry):
        b = order(j)
        start = pl.multiple_of(b * rows, rows)
        window = grad_sum_ref[pl.ds(start, rows + 8), :]
        grad_conv = None
        for k in range(kernel):
            tap = small_ref[cuts.taps + k : cuts.taps + k + 1, :]
            term = tap * window[kernel - 1 - k : kernel - 1 - k + rows]
            grad_conv = term if grad_conv is None else grad_conv + term
        grad_conv = grad_conv.astype(jnp.bfloat16)
        grad_conv_ref[pl.ds(start, rows), :] = grad_conv
        relay.part[b] = (
            dot_nn(grad_conv, weights_ref[:, :width])
            + dot_nn(grad_gate_ref[pl.ds(start, rows), :], weights_ref[:, width : 2 * width])
        ).astype(jnp.bfloat16)
        relay.made(b // 2, lax.rem(b, 2))
        return carry

    lax.fori_loop(0, count, second, 0)

    decay = slice(cuts.decay, cuts.decay + cuts.state)
    grad_small_ref[cuts.step : cuts.step + cuts.rank, :] = grad_step_ref[...]
    grad_small_ref[decay, :] = -rate_total_ref[...] * jnp.exp(small_ref[decay, :])
    grad_small_ref[cuts.step_bias : cuts.step_bias + 2, :] = scan_rows_ref[0:2, :]
    small_t = grad_small_ref[...].T
    for d in range(lines):
        spread.part[d, :, 3 * width :] = small_t[d * shard : (d + 1) * shard].astype(jnp.bfloat16)
    chunk = width // 3

    def pass_on(j, carry):
        b = order(j)
        relay.pass_on(b // 2, lax.rem(b, 2))
        return carry

    ours_ref[...] = vectors_ref[...]
    for left_ref, right_ref, place_at in (
        (mixer_low_ref, grad_middle_ref, 2 * width),
        (grad_conv_ref, normed_ref, 0),
        (grad_gate_ref, normed_ref, width),
    ):

        def columns(c, carry, left_ref=left_ref, right_ref=right_ref, place_at=place_at):
            here = pl.ds(pl.multiple_of(c * chunk, chunk), chunk)
            there = pl.ds(pl.multiple_of(place_at + c * chunk, chunk), chunk)
            grad = inner_rows(left_ref[...], right_ref[:, here])
            if place_at < 2 * width:
                ours_ref[0:1, here] += jnp.sum(
                    weights_ref[:, there].astype(jnp.float32) * grad, axis=0, keepdims=True
                )
            low = grad.astype(jnp.bfloat16)
            for d in range(lines):
                spread.part[d, :, there] = low[d * shard : (d + 1) * shard]
            return carry

        lax.fori_loop(0, 3, columns, 0)
        if place_at == 2 * width:
            lax.fori_loop(0, count, pass_on, 0)
    for d in range(lines):
        spread.made(d // 2, d % 2)
    scatter.hand_over()

    def sum_over(size, axis, send, recv):
        here = own if axis == "seq" else line

        def copy(k, slot):
            there = lax.rem(here + k, size)
            target = (line, there) if axis == "seq" else (there, own)
            return remote(ours_ref, theirs_ref.at[slot], send.at[k], recv.at[k], *target)

        base = 0 if axis == "seq" else count
        for k in range(1, size):
            copy(k, base + k).start()
        total = ours_ref[...]
        for k in range(1, size):
            copy(k, base + k).wait_recv()
            total = total + theirs_ref[base + k]
        for k in range(1, size):
            copy(k, base + k).wait_send()
        return total

    ours_ref[...] = sum_over(count, "seq", send_v, recv_v)
    for d in range(lines):
        spread.pass_on(d // 2, d % 2)
    totals_ref[...] = sum_over(lines, "dp", send_u, recv_u)
    x = x_ref[...]
    scale = lax.rsqrt(jnp.mean(x * x, axis=1, keepdims=True) + 1e-05)
    scaled = gain_ref[...] * relay.finish()
    tokens_ref[...] = (
        kept_ref[...]
        + scale * scaled
        - x * (scale * scale * scale) * jnp.mean(scaled * x, axis=1, keepdims=True)
    )
    total = spread.finish()
    input_ref[0] = total[:own_shard, :width]
    input_ref[1] = total[:own_shard, width : 2 * width]
    output_ref[...] = total[:own_shard, 2 * width : 3 * width]
    small = total[:, 3 * width :]
    select_ref[...] = small[:own_shard, : cuts.picks]
    small = jnp.concatenate(
        [small, jnp.zeros((LANES - shard, small.shape[1]), jnp.float32)], axis=0
    ).T
    for at, ref in (
        (cuts.step, step_ref),
        (cuts.decay, decay_ref),
        (cuts.taps, taps_ref),
        (cuts.conv_bias, conv_bias_ref),
        (cuts.step_bias, step_bias_ref),
        (cuts.skip, skip_ref),
    ):
        ref[...] = small[at : at + ref.shape[0], :own_shard]
    scatter.finish(expert_out_ref)


def back(
    count, lines, shard, own_shard, cuts, grad_selected, small, weights, ext, conv_sum, grad_act, grad_gate,
    mixer_low, normed, grad_middle, grad_step, rate_total, scan_rows, vectors, expert, far,
    x, gain, kept,
):
    length, inner = conv_sum.shape
    width = normed.shape[1]
    columns = weights.shape[1]
    rows = length // count
    vmem = pl.BlockSpec(memory_space=pltpu.VMEM)
    dma = pltpu.SemaphoreType.DMA
    args = (
        grad_selected, small, weights, ext, conv_sum, grad_act, grad_gate, mixer_low, normed,
        grad_middle, grad_step, rate_total, scan_rows, vectors, expert, far, x, gain, kept,
    )
    return pl.pallas_call(
        functools.partial(back_kernel, count, lines, cuts),
        in_specs=[vmem] * len(args),
        out_specs=[vmem] * 12,
        out_shape=[
            *[
                jax.ShapeDtypeStruct(shape, jnp.float32)
                for shape in (
                    (rows, width),
                    (2, own_shard, width),
                    (own_shard, width),
                    (own_shard, cuts.picks),
                    (cuts.rank, own_shard),
                    (cuts.state, own_shard),
                    (cuts.kernel, own_shard),
                    (1, own_shard),
                    (1, own_shard),
                    (1, own_shard),
                    vectors.shape,
                )
            ],
            jax.ShapeDtypeStruct((expert.shape[1], 2 * expert.shape[2]), jnp.float32),
        ],
        scratch_shapes=[
            pltpu.VMEM((length + 8, inner), jnp.float32),
            pltpu.VMEM((length, inner), jnp.bfloat16),
            pltpu.VMEM(small.shape, jnp.float32),
            pltpu.VMEM(vectors.shape, jnp.float32),
            pltpu.VMEM((count + lines, *vectors.shape), jnp.float32),
            dma((count,)), dma((count,)), dma((lines,)), dma((lines,)),
            *scatter_scratch(count, expert.shape[1], expert.shape[2]),
            *relay_scratch(count, rows, width),
            *relay_scratch(lines, shard, columns),
        ],
        compiler_params=pltpu.CompilerParams(
            collective_id=3, has_side_effects=True, vmem_limit_bytes=VMEM_LIMIT
        ),
        cost_estimate=pl.CostEstimate(
            flops=10 * length * width * inner,
            bytes_accessed=30 * length * inner,
            transcendentals=length * inner,
        ),
        name="back",
    )(*args)


LAG = 3
FAR_AT = 0
NEAR_AT = 2
PASS_AT = 4
SLOTS = 64


def gauss(values):
    return 0.5 * (1.0 + lax.erf(values * math.sqrt(0.5)))


def split_low(values):
    high = values.astype(jnp.bfloat16)
    return high, (values - high.astype(jnp.float32)).astype(jnp.bfloat16)


def experts_kernel(
    count, lines, experts,
    x_ref, mixer_ref, grad_ref, route_ref, gain_ref, router_ref,
    up_ref, down_ref,
    output_ref, grad_middle_ref, grad_low_ref, vectors_ref, grad_up_ref, grad_down_ref, far_up_ref,
    table_ref, back_table_ref, middle_ref, normed_ref, send_ref, rows_ref, made_ref, got_ref, act_ref, slope_ref, pre_ref,
    send_sem, recv_sem, home_s, home_r, far_s, far_r,
):
    line, own, _, _ = place()
    q, f, low = square()
    mate = seat_of(q, 1 - f, low)
    copies = lines // experts
    barrier = pltpu.get_barrier_semaphore()
    for d in range(1, lines):
        for where in (own, mate):
            pl.semaphore_signal(
                barrier, inc=1, device_id=(lax.rem(line + d, lines), where), device_id_type=MESH
            )
    partner = seat_of(q, f, 1 - low)
    for where in (mate, partner):
        pl.semaphore_signal(barrier, inc=1, device_id=(line, where), device_id_type=MESH)
    pl.semaphore_wait(barrier, 2 * lines)

    peers = [(j, d) for d in range(lines) for j in (1, 0) if (j, d) != (0, 0)]

    def out_copy(what, j, d):
        there = lax.rem(line + d, lines)
        return remote(
            send_ref.at[what, there // copies], rows_ref.at[what, j, line],
            send_sem.at[what, j, d], recv_sem.at[what, j, line],
            there, mate if j else own,
        )

    def arrived(what, j, d):
        from_line = lax.rem(line + d, lines)
        return remote(
            send_ref.at[what, 0], rows_ref.at[what, j, from_line],
            send_sem.at[what, j, d], recv_sem.at[what, j, from_line],
            from_line, mate if j else own,
        )

    def home_copy(what, j, d):
        there = lax.rem(line + d, lines)
        return remote(
            made_ref.at[what, j, there], got_ref.at[what, j, line],
            home_s.at[what, j, d], home_r.at[what, j, line],
            there, mate if j else own,
        )

    def came_home(what, j, d):
        from_line = lax.rem(line + d, lines)
        return remote(
            made_ref.at[what, j, 0], got_ref.at[what, j, from_line],
            home_s.at[what, j, d], home_r.at[what, j, from_line],
            from_line, mate if j else own,
        )

    middle = x_ref[...] + mixer_ref[...]
    middle_ref[...] = middle
    gain = gain_ref[...]
    scale = lax.rsqrt(jnp.mean(middle * middle, axis=1, keepdims=True) + 1e-05)
    normed = (middle * scale * gain).astype(jnp.bfloat16)
    normed_ref[...] = normed
    rows, width = middle.shape
    slots = SLOTS
    lane = lax.broadcasted_iota(jnp.int32, (rows, LANES), 1)
    route_along = jnp.broadcast_to(route_ref[...].astype(jnp.float32), (rows, rows))
    route_down = route_along.T[:, :LANES]
    chosen = (route_down == lane.astype(jnp.float32)).astype(jnp.float32)
    earlier = (
        lax.broadcasted_iota(jnp.int32, (rows, rows), 0)
        > lax.broadcasted_iota(jnp.int32, (rows, rows), 1)
    ).astype(jnp.bfloat16)
    before = dot_nn(earlier, chosen.astype(jnp.bfloat16))
    slot_down = route_down[:, :1] * slots + jnp.sum(before * chosen, axis=1, keepdims=True)
    slot_along = jnp.broadcast_to(slot_down, (rows, rows)).T[:1, :]
    table_ref[...] = (
        jnp.broadcast_to(slot_along, table_ref.shape)
        == lax.broadcasted_iota(jnp.int32, table_ref.shape, 0).astype(jnp.float32)
    ).astype(jnp.bfloat16)
    for e in range(experts):
        places = lax.broadcasted_iota(jnp.int32, (rows, slots), 1) + e * slots
        back_table_ref[e] = (
            jnp.broadcast_to(slot_down, (rows, slots)) == places.astype(jnp.float32)
        ).astype(jnp.bfloat16)

    def dispatch(what, values):
        sent = dot_nn(table_ref[...], values).astype(jnp.bfloat16)
        for e in range(experts):
            send_ref[what, e] = sent[e * slots : (e + 1) * slots]
        for j, d in peers:
            out_copy(what, j, d).start()
        rows_ref[what, 0, line] = send_ref[what, line // copies]

    dispatch(0, normed)
    router_f = jnp.concatenate(
        [
            router_ref[...].astype(jnp.float32),
            jnp.zeros((LANES - experts, width), jnp.float32),
        ],
        axis=0,
    )
    router = router_f.astype(jnp.bfloat16)
    logits = jnp.where(lane < experts, outer_cols(normed, router), -jnp.inf)
    grown = jnp.exp(logits - jnp.max(logits, axis=1, keepdims=True))
    probs = grown / jnp.sum(grown, axis=1, keepdims=True)
    gate = jnp.sum(chosen * probs, axis=1, keepdims=True)
    dispatch(1, (gate * grad_ref[...]).astype(jnp.bfloat16))

    total = 2 * lines * slots
    hidden = up_ref.shape[1]
    chunk = hidden // 3 if hidden % (3 * LANES) == 0 else hidden
    parts = hidden // chunk

    def rows_of(ref, what):
        return ref[what].reshape(total, width)

    def columns(c):
        return pl.ds(pl.multiple_of(c * chunk, LANES), chunk)

    for j, d in peers:
        arrived(0, j, d).wait_recv()

    def rise(c, carry):
        pre_ref[:, columns(c)] = dot_nn(rows_of(rows_ref, 0), up_ref[:, columns(c)])
        pre = pre_ref[:, columns(c)]
        half = gauss(pre)
        act_ref[:, columns(c)] = (pre * half).astype(jnp.bfloat16)
        pre_ref[:, columns(c)] = half + pre * (
            jnp.exp(-0.5 * pre * pre) * (1.0 / math.sqrt(2.0 * math.pi))
        )
        return carry

    lax.fori_loop(0, parts, rise, 0)

    wide = width // 3

    def send_home(what, left_ref, right_ref):
        def make(c, carry):
            here = pl.ds(pl.multiple_of(c * wide, LANES), wide)
            there = pl.ds(pl.multiple_of(c * wide, LANES), wide)
            made = outer_cols(left_ref[...], right_ref[there, :]).astype(jnp.bfloat16)
            made_ref[what, :, :, :, here] = made.reshape(2, lines, slots, wide)
            return carry

        lax.fori_loop(0, 3, make, 0)
        for j, d in peers:
            home_copy(what, j, d).start()
        got_ref[what, 0, line] = made_ref[what, 0, line]

    for j, d in peers:
        arrived(1, j, d).wait_recv()

    def fall(c, carry):
        slope_ref[:, columns(c)] = (
            dot_nn(rows_of(rows_ref, 1), down_ref[:, columns(c)]) * pre_ref[:, columns(c)]
        ).astype(jnp.bfloat16)
        return carry

    lax.fori_loop(0, parts, fall, 0)
    send_home(1, slope_ref, up_ref)
    send_home(0, act_ref, down_ref)

    pieces = grad_up_ref.shape[1]

    def weigh(c, carry):
        up = inner_rows(rows_of(rows_ref, 0), slope_ref[:, columns(c)]).astype(jnp.bfloat16)
        down = inner_rows(rows_of(rows_ref, 1), act_ref[:, columns(c)]).astype(jnp.bfloat16)
        grad_up_ref[:, :, columns(c)] = up.reshape(count, pieces, chunk)
        grad_down_ref[:, :, columns(c)] = down.reshape(count, pieces, chunk)
        return carry

    lax.fori_loop(0, parts, weigh, 0)

    far_copies = []
    for k in range(1, count // 4):
        i = lax.rem(q + k, count // 4)
        for j in (1, 0):
            far_copies.append(
                remote(
                    grad_up_ref.at[seat_of(i, lax.rem(f + j, 2), 1 - low)], far_up_ref.at[j, i],
                    far_s.at[j, i], far_r.at[j, i], line, partner,
                )
            )
            far_copies[-1].start()

    def home(what):
        for j, d in peers:
            came_home(what, j, d).wait_recv()
        both = None
        for e in range(experts):
            own_rows = None
            for c in range(copies):
                for j in range(2):
                    term = got_ref[what, j, e * copies + c].astype(jnp.float32)
                    own_rows = term if own_rows is None else own_rows + term
            high, rest = split_low(own_rows)
            here = back_table_ref[e]
            term = dot_nn(here, high) + dot_nn(here, rest)
            both = term if both is None else both + term
        return both

    grad = grad_ref[...]
    middle = middle_ref[...]
    picked = home(0)
    output_ref[...] = middle + gate * picked
    grad_gate = jnp.sum(grad * picked, axis=1, keepdims=True)
    grad_logits = gate * (chosen - probs) * grad_gate
    grad_normed = home(1) + dot_nn(grad_logits, router_f, HIGHEST)
    scaled = gain * grad_normed
    grad_middle = (
        grad
        + scale * scaled
        - middle * (scale * scale * scale) * jnp.mean(scaled * middle, axis=1, keepdims=True)
    )
    grad_middle_ref[...] = grad_middle
    grad_low_ref[...] = grad_middle.astype(jnp.bfloat16)
    vectors_ref[...] = jnp.zeros_like(vectors_ref)
    vectors_ref[1:2, :] = jnp.sum(grad_normed * middle * scale, axis=0, keepdims=True)
    vectors_ref[2 : 2 + experts, :] = inner_rows(
        grad_logits, normed_ref[...].astype(jnp.float32), HIGHEST
    )[:experts]
    for what in range(2):
        for j, d in peers:
            out_copy(what, j, d).wait_send()
            home_copy(what, j, d).wait_send()
    for copy in far_copies:
        copy.wait()


def run_experts(
    count, lines, experts, x, mixer, grad, route, gain, router, up, down
):
    rows, width = x.shape
    slots = SLOTS
    total = 2 * lines * slots
    hidden = up.shape[1]
    pieces = (count, up.shape[0] // count, hidden)
    vmem = pl.BlockSpec(memory_space=pltpu.VMEM)
    dma = pltpu.SemaphoreType.DMA
    args = (x, mixer, grad, route, gain, router, up, down)
    low = jnp.bfloat16
    return pl.pallas_call(
        functools.partial(experts_kernel, count, lines, experts),
        in_specs=[vmem] * len(args),
        out_specs=[vmem] * 7,
        out_shape=[
            jax.ShapeDtypeStruct((rows, width), jnp.float32),
            jax.ShapeDtypeStruct((rows, width), jnp.float32),
            jax.ShapeDtypeStruct((rows, width), low),
            jax.ShapeDtypeStruct((8, width), jnp.float32),
            jax.ShapeDtypeStruct(pieces, low),
            jax.ShapeDtypeStruct(pieces, low),
            jax.ShapeDtypeStruct((2, count // 4, *pieces[1:]), low),
        ],
        scratch_shapes=[
            pltpu.VMEM((experts * slots, rows), low),
            pltpu.VMEM((experts, rows, slots), low),
            pltpu.VMEM((rows, width), jnp.float32),
            pltpu.VMEM((rows, width), low),
            pltpu.VMEM((2, experts, slots, width), low),
            pltpu.VMEM((2, 2, lines, slots, width), low),
            pltpu.VMEM((2, 2, lines, slots, width), low),
            pltpu.VMEM((2, 2, lines, slots, width), low),
            pltpu.VMEM((total, hidden), low),
            pltpu.VMEM((total, hidden), low),
            pltpu.VMEM((total, hidden), jnp.float32),
            dma((2, 2, lines)), dma((2, 2, lines)), dma((2, 2, lines)), dma((2, 2, lines)),
            dma((2, count // 4)), dma((2, count // 4)),
        ],
        compiler_params=pltpu.CompilerParams(
            collective_id=4, has_side_effects=True, vmem_limit_bytes=VMEM_LIMIT
        ),
        cost_estimate=pl.CostEstimate(
            flops=12 * total * width * hidden,
            bytes_accessed=8 * width * hidden,
            transcendentals=2 * total * hidden,
        ),
        name="experts",
    )(*args)


def body(
    tokens,
    cotangent,
    routes,
    mixer_gain,
    input_proj,
    conv_weight,
    conv_bias,
    select_proj,
    step_proj,
    step_bias,
    decay_log,
    skip_gain,
    output_proj,
    expert_gain,
    router,
    expert_up,
    expert_down,
):
    rows = tokens.shape[1]
    width = tokens.shape[2]
    shard = input_proj.shape[2]
    rank = step_proj.shape[0]
    state = decay_log.shape[0]
    kernel = conv_weight.shape[0]
    picks = select_proj.shape[0]
    count = lax.axis_size("seq")
    lines = lax.axis_size("dp")
    shard_rows = -(-shard // 16) * 16
    cuts = Cuts(picks, rank, state, kernel)

    x_in = tokens.reshape(rows, width)
    gain_one = mixer_gain.astype(jnp.float32)
    small_pad = -(-cuts.rows // LANES) * LANES
    (normed_all, weights, small_all, conv_ext, conv_sum, conv_act, gate_branch, selected, up_cut) = (
        front(
            count, lines, cuts, shard_rows, small_pad,
            x_in, gain_one[None], input_proj.transpose(0, 2, 1), output_proj, select_proj.T,
            step_proj, decay_log, conv_weight, conv_bias[None], step_bias[None], skip_gain[None],
            expert_up,
        )
    )
    pre, mixed, mixer_low, priors, end, mixer_out, down_cut = scan_forward(
        count, cuts, width, conv_act, gate_branch, selected, small_all, weights, expert_down.T
    )

    experts = router.shape[0]
    (output, grad_middle, grad_middle_low, vectors, grad_up_low, grad_down_low, far_up) = run_experts(
        count,
        lines,
        experts,
        x_in,
        mixer_out,
        cotangent.reshape(rows, width),
        routes.reshape(1, rows),
        expert_gain.astype(jnp.float32)[None],
        router,
        up_cut.reshape(-1, up_cut.shape[2]),
        down_cut.reshape(-1, down_cut.shape[2]),
    )

    (grad_gate_branch, grad_act, grad_step_w, rate_total, scan_rows, grad_selected, grad_middle_all,
     grad_down_t) = (
        scan_backward(
            count, cuts, grad_middle_low, conv_act, gate_branch, mixed, pre, selected, small_all,
            weights, priors, end, grad_down_low,
        )
    )
    (grad_tokens, grad_input, grad_output, grad_select, grad_step, grad_decay, grad_taps,
     grad_conv_bias, grad_step_bias, grad_skip, totals, grad_up) = back(
        count, lines, shard_rows, shard, cuts, grad_selected, small_all, weights, conv_ext, conv_sum,
        grad_act, grad_gate_branch, mixer_low, normed_all.reshape(-1, width),
        grad_middle_all.reshape(-1, width), grad_step_w, rate_total, scan_rows, vectors,
        grad_up_low, far_up, x_in, gain_one[None], grad_middle,
    )
    return (
        output.reshape(tokens.shape),
        grad_tokens.reshape(tokens.shape),
        totals[0] / gain_one,
        grad_input.transpose(0, 2, 1),
        grad_taps,
        grad_conv_bias.reshape(shard),
        grad_select.T,
        grad_step,
        grad_step_bias.reshape(shard),
        grad_decay,
        grad_skip.reshape(shard),
        grad_output,
        totals[1],
        totals[2 : 2 + experts],
        grad_up,
        grad_down_t.T,
    )


def solution(mesh):
    both = ("dp", "seq")
    placed = (
        P("dp", "seq", None),
        P("dp", "seq", None),
        P("dp", "seq", None),
        P(),
        P(None, None, both),
        P(None, both),
        P(both),
        P(None, both),
        P(None, both),
        P(both),
        P(None, both),
        P(both),
        P(both, None),
        P(),
        P(),
        P("seq", "dp"),
        P("dp", "seq"),
    )
    return jax.shard_map(
        body,
        mesh=mesh,
        in_specs=placed,
        out_specs=(
            P("dp", "seq", None),
            P("dp", "seq", None),
            P(),
            P(None, None, both),
            P(None, both),
            P(both),
            P(None, both),
            P(None, both),
            P(both),
            P(None, both),
            P(both),
            P(both, None),
            P(),
            P(),
            P("seq", "dp"),
            P("dp", "seq"),
        ),
        check_vma=False,
    )
```

```python
import functools
import math

import jax
import jax.numpy as jnp
from jax import lax
from jax.experimental import pallas as pl
from jax.experimental.pallas import tpu as pltpu
from jax.sharding import PartitionSpec as P

CAP = 56
LANES = 128
TIME_BLOCK = 128
LOG2E = math.log2(math.e)

HIGHEST = lax.Precision.HIGHEST


def inner_rows(left, right, precision=None):
    return lax.dot_general(
        left,
        right,
        (((0,), (0,)), ((), ())),
        precision=precision,
        preferred_element_type=jnp.float32,
    )


def outer_cols(left, right, precision=None):
    return lax.dot_general(
        left,
        right,
        (((1,), (1,)), ((), ())),
        precision=precision,
        preferred_element_type=jnp.float32,
    )


def sublane_sums(parts):
    row = lax.broadcasted_iota(jnp.int32, parts[0].shape, 0)
    low4 = row < 4
    low2 = (row % 4) < 2
    low1 = (row % 2) < 1
    quads = []
    for k in range(4):
        a, b = parts[k], parts[k + 4]
        quads.append(jnp.where(low4, a, b) + pltpu.roll(jnp.where(low4, b, a), 4, 0))
    pairs = []
    for k in range(2):
        a, b = quads[k], quads[k + 2]
        pairs.append(
            jnp.where(low2, a, b) + jnp.where(low2, pltpu.roll(a, 6, 0), pltpu.roll(b, 2, 0))
        )
    a, b = pairs
    return jnp.where(low1, a, b) + jnp.where(low1, pltpu.roll(a, 7, 0), pltpu.roll(b, 1, 0))


MESH = pl.DeviceIdType.MESH
VMEM_LIMIT = 60 * 1024 * 1024


def dot_nn(left, right, precision=None):
    return lax.dot_general(
        left, right, (((1,), (0,)), ((), ())), precision=precision,
        preferred_element_type=jnp.float32,
    )


def place():
    own, line = lax.axis_index("seq"), lax.axis_index("dp")
    return line, own, own // 2, lax.rem(own, 2)


def remote(source, target, send_sem, recv_sem, line, position):
    return pltpu.make_async_remote_copy(
        src_ref=source,
        dst_ref=target,
        send_sem=send_sem,
        recv_sem=recv_sem,
        device_id=(line, position),
        device_id_type=MESH,
    )


def greet(count, lines=1):
    line, own, _, _ = place()
    barrier = pltpu.get_barrier_semaphore()
    for k in range(1, count):
        pl.semaphore_signal(
            barrier, inc=1, device_id=(line, lax.rem(own + k, count)), device_id_type=MESH
        )
    for k in range(1, lines):
        pl.semaphore_signal(
            barrier, inc=1, device_id=(lax.rem(line + k, lines), own), device_id_type=MESH
        )
    pl.semaphore_wait(barrier, count - 1 + lines - 1)


def sigmoid(values):
    return 1.0 / (1.0 + jnp.exp(-values))


def softplus(values):
    return jnp.maximum(values, 0.0) + jnp.log1p(jnp.exp(-jnp.abs(values)))


class Cuts:
    def __init__(self, picks, rank, state, kernel):
        self.picks, self.rank, self.state, self.kernel = picks, rank, state, kernel
        self.step = picks
        self.decay = self.step + rank
        self.taps = self.decay + state
        self.conv_bias = self.taps + kernel
        self.step_bias = self.conv_bias + 1
        self.skip = self.step_bias + 1
        self.rows = self.skip + 1
        self.sent = -(-picks // 16) * 16


class Relay:
    def __init__(self, axis, half, high, low, seat, block, refs):
        self.axis, self.half, self.high, self.low = axis, half, high, low
        self.seat, self.block = seat, block
        self.other = lax.axis_index("dp" if axis == "seq" else "seq")
        self.part, self.across, self.along = refs[:3]
        self.send_x, self.recv_x, self.send_hi, self.recv_hi = refs[3:]

    def remote(self, source, target, send_sem, recv_sem, position):
        if self.axis == "seq":
            return remote(source, target, send_sem, recv_sem, self.other, position)
        return remote(source, target, send_sem, recv_sem, position, self.other)

    def over(self, i, low):
        return self.remote(
            self.part.at[self.block(i, low)], self.across.at[i], self.send_x.at[i],
            self.recv_x.at[i], self.seat(self.high, 1 - self.low),
        )

    def on(self, i):
        k = lax.rem(i - self.high + self.half, self.half)
        return self.remote(
            self.across.at[i], self.along.at[k], self.send_hi.at[k], self.recv_hi.at[k],
            self.seat(i, self.low),
        )

    def made(self, i, low):
        @pl.when(low != self.low)
        def _():
            self.over(i, low).start()

    def summed(self, i):
        self.over(i, self.low).wait_recv()
        return self.part[self.block(i, self.low)].astype(jnp.float32) + self.across[i].astype(
            jnp.float32
        )

    def pass_on(self, i, low):
        @pl.when((low == self.low) & (i != self.high))
        def _():
            self.across[i] = self.summed(i).astype(jnp.bfloat16)
            self.on(i).start()

    def finish(self, sent=None):
        total = self.summed(self.high)
        for k in range(1, self.half):
            self.on(lax.rem(self.high + k, self.half)).wait_recv()
            total = total + self.along[k].astype(jnp.float32)
        for i in range(self.half) if sent is None else sent:
            self.over(i, 1 - self.low).wait_send()
        for k in range(1, self.half):
            self.on(lax.rem(self.high + k, self.half)).wait_send()
        return total


def whole_relay(axis, count, refs):
    own = lax.axis_index(axis)

    def seat(i, low):
        return 2 * i + low

    return Relay(axis, count // 2, own // 2, lax.rem(own, 2), seat, seat, refs)


def relay_scratch(count, rows, width, part=True):
    half = count // 2
    dma = pltpu.SemaphoreType.DMA
    own = [pltpu.VMEM((count, rows, width), jnp.bfloat16)] if part else []
    return own + [
        pltpu.VMEM((half, rows, width), jnp.bfloat16),
        pltpu.VMEM((half, rows, width), jnp.bfloat16),
        dma((half,)), dma((half,)), dma((half,)), dma((half,)),
    ]


def square():
    own = lax.axis_index("seq")
    return own // 4, lax.rem(own // 2, 2), lax.rem(own, 2)


def seat_of(q, f, low):
    return 4 * q + 2 * f + low


class Gather:
    def __init__(self, count, shard_ref, land_ref, swap_s, swap_r, line_s, line_r, pair_s, pair_r):
        self.line = lax.axis_index("dp")
        self.q, self.f, self.low = square()
        self.quarter = count // 4
        self.shard, self.land = shard_ref, land_ref
        self.swap_s, self.swap_r = swap_s, swap_r
        self.line_s, self.line_r, self.pair_s, self.pair_r = line_s, line_r, pair_s, pair_r
        self.cut = land_ref.shape[2]

    def columns(self, f):
        return pl.ds(pl.multiple_of(f * self.cut, LANES), self.cut)

    def piece(self, j, k, low):
        q = lax.rem(self.q - k + self.quarter, self.quarter)
        return seat_of(q, lax.rem(self.f + j, 2), low)

    def swap(self):
        own = self.piece(0, 0, self.low)
        return remote(
            self.shard.at[:, self.columns(1 - self.f)], self.land.at[own], self.swap_s, self.swap_r,
            self.line, self.piece(1, 0, self.low),
        )

    def along(self, j, k):
        piece = self.piece(j, 0, self.low)
        there = seat_of(lax.rem(self.q + k, self.quarter), self.f, self.low)
        return remote(
            self.land.at[piece], self.land.at[piece], self.line_s.at[j, k], self.line_r.at[j, k],
            self.line, there,
        )

    def pair(self, j, k, low):
        piece = self.piece(j, k, low)
        return remote(
            self.land.at[piece], self.land.at[piece], self.pair_s.at[j, k], self.pair_r.at[j, k],
            self.line, seat_of(self.q, self.f, 1 - self.low),
        )

    def start(self):
        self.swap().start()
        self.land[self.piece(0, 0, self.low)] = self.shard[:, self.columns(self.f)]

    def spread(self, j):
        if j == 1:
            mate = self.piece(1, 0, self.low)
            remote(
                self.land.at[mate], self.land.at[mate], self.swap_s, self.swap_r, self.line, mate
            ).wait_recv()
        for k in range(1, self.quarter):
            self.along(j, k).start()
        self.pair(j, 0, self.low).start()

    def forward(self, j):
        for k in range(1, self.quarter):
            piece = self.piece(j, k, self.low)
            remote(
                self.land.at[piece], self.land.at[piece], self.line_s.at[j, k],
                self.line_r.at[j, k], self.line, piece,
            ).wait_recv()
            self.pair(j, k, self.low).start()

    def finish(self):
        for j in range(2):
            for k in range(self.quarter):
                self.pair(j, k, 1 - self.low).wait_recv()
        self.swap().wait_send()
        for j in range(2):
            for k in range(1, self.quarter):
                self.along(j, k).wait_send()
            for k in range(self.quarter):
                self.pair(j, k, self.low).wait_send()


def gather_scratch(count):
    dma = pltpu.SemaphoreType.DMA
    quarter = count // 4
    return [dma, dma] + [dma((2, quarter)) for _ in range(4)]


class Scatter:
    def __init__(self, count, part_ref, far_ref, other_ref, held_ref, swap_s, swap_r, refs):
        self.line = lax.axis_index("dp")
        self.q, self.f, self.low = square()
        self.quarter = count // 4
        self.far, self.other, self.held = far_ref, other_ref, held_ref
        self.swap_s, self.swap_r = swap_s, swap_r
        self.relays = []
        for j in range(2):
            cut = lax.rem(self.f + j, 2)

            def seat(i, low):
                return seat_of(i, self.f, low)

            def block(i, low, cut=cut):
                return seat_of(i, cut, low)

            mine = tuple(ref.at[j] for ref in refs)
            self.relays.append(
                Relay("seq", self.quarter, self.q, self.low, seat, block, (part_ref, *mine))
            )

    def swap(self):
        return remote(
            self.held, self.other, self.swap_s, self.swap_r, self.line,
            seat_of(self.q, 1 - self.f, self.low),
        )

    def far_places(self):
        return [
            (j, lax.rem(self.q + k, self.quarter)) for k in range(1, self.quarter) for j in (1, 0)
        ]

    def send_far(self):
        for j, i in self.far_places():
            self.relays[j].over(i, 1 - self.low).start()

    def pass_far(self):
        for j, i in self.far_places():
            relay = self.relays[j]
            if self.far is None:
                relay.pass_on(i, self.low)
            else:
                both = relay.part[relay.block(i, self.low)].astype(jnp.float32) + self.far[
                    j, i
                ].astype(jnp.float32)
                relay.across[i] = both.astype(jnp.bfloat16)
                relay.on(i).start()

    def total(self, j):
        return self.relays[j].finish(None if self.far is None else [self.q])

    def send_near(self):
        for j in (1, 0):
            self.relays[j].over(self.q, 1 - self.low).start()

    def hand_over(self):
        self.held[...] = self.total(1).astype(jnp.bfloat16)
        self.swap().start()

    def finish(self, out_ref):
        cut = self.held.shape[1]
        out_ref[:, pl.ds(pl.multiple_of(self.f * cut, LANES), cut)] = self.total(0)
        self.swap().wait_recv()
        out_ref[:, pl.ds(pl.multiple_of((1 - self.f) * cut, LANES), cut)] = self.other[...].astype(
            jnp.float32
        )
        self.swap().wait_send()


def scatter_scratch(count, rows, cut):
    dma = pltpu.SemaphoreType.DMA
    quarter = count // 4
    return [
        pltpu.VMEM((rows, cut), jnp.bfloat16),
        pltpu.VMEM((rows, cut), jnp.bfloat16),
        dma, dma,
        pltpu.VMEM((2, quarter, rows, cut), jnp.bfloat16),
        pltpu.VMEM((2, quarter, rows, cut), jnp.bfloat16),
        *[dma((2, quarter)) for _ in range(4)],
    ]


def front_kernel(
    count, lines, cuts,
    x_ref, gain_ref, input_ref, output_ref, select_ref, step_ref, decay_ref, taps_ref, conv_bias_ref,
    step_bias_ref, skip_ref, expert_ref,
    all_ref, weights_ref, small_ref, ext_ref, sum_ref, act_ref, gate_ref, selected_ref, land_ref,
    normed_ref, packed_ref, table_ref, part_ref, partial_ref, total_ref,
    send_w, recv_w, send_up, send_down, recv_hi, send_x, recv_x, send_rs, recv_rs, send_ag, recv_ag,
    *gather_refs,
):
    line, own, high, low = place()
    half = count // 2
    gather = Gather(count, expert_ref, land_ref, *gather_refs)
    rows, width = x_ref.shape
    shard = packed_ref.shape[0]
    inner = weights_ref.shape[0]
    kernel = cuts.kernel
    partner = 2 * high + 1 - low

    own_shard = output_ref.shape[0]
    extra = jnp.zeros((shard - own_shard, width), jnp.float32)

    def padded(values):
        return jnp.concatenate([values.astype(jnp.float32), extra], axis=0).astype(jnp.bfloat16)

    packed_ref[:, :width] = padded(input_ref[0])
    packed_ref[:, width : 2 * width] = padded(input_ref[1])
    packed_ref[:, 2 * width : 3 * width] = padded(output_ref[...])
    table_ref[...] = jnp.zeros_like(table_ref)
    table_ref[:own_shard, : cuts.picks] = select_ref[...].astype(jnp.float32)
    picked = table_ref[:LANES, :].T
    table_ref[...] = jnp.zeros_like(table_ref)
    table_ref[:LANES, :] = picked
    for at, ref in (
        (cuts.step, step_ref),
        (cuts.decay, decay_ref),
        (cuts.taps, taps_ref),
        (cuts.conv_bias, conv_bias_ref),
        (cuts.step_bias, step_bias_ref),
        (cuts.skip, skip_ref),
    ):
        table_ref[at : at + ref.shape[0], :own_shard] = ref[...].astype(jnp.float32)
    packed_ref[:, 3 * width :] = table_ref[...].T[:shard].astype(jnp.bfloat16)
    x = x_ref[...]
    scale = lax.rsqrt(jnp.mean(x * x, axis=1, keepdims=True) + 1e-05)
    normed_ref[...] = (x * scale * gain_ref[...]).astype(jnp.bfloat16)
    greet(count, lines)

    copies = []
    shard_rows = pl.ds(pl.multiple_of(line * shard, 16), shard)
    def step_on(i, up):
        block = 2 * i + low
        return remote(
            all_ref.at[block], all_ref.at[block], (send_up if up else send_down).at[i],
            recv_hi.at[i], line, 2 * (high + (1 if up else -1)) + low,
        )

    def can_go(up):
        return high < half - 1 if up else high > 0

    all_ref[own] = normed_ref[...]
    for up in (True, False):

        @pl.when(can_go(up))
        def _(up=up):
            step_on(high, up).start()

    remote(all_ref.at[own], all_ref.at[own], send_x.at[high], recv_x.at[high], line, partner).start()
    for k in range(1, lines):
        copy = remote(
            packed_ref, weights_ref.at[shard_rows], send_w.at[k], recv_w.at[k],
            lax.rem(line + k, lines), own,
        )
        copy.start()
        copies.append(copy)
    gather.start()
    weights_ref[shard_rows, :] = packed_ref[...]
    if lines * shard < inner:
        weights_ref[lines * shard :, :] = jnp.zeros(
            (inner - lines * shard, weights_ref.shape[1]), weights_ref.dtype
        )
    ext_ref[0:8, :] = jnp.zeros((8, inner), jnp.float32)
    def cross(i):
        block = 2 * i + low
        return remote(
            all_ref.at[block], all_ref.at[block], send_x.at[i], recv_x.at[i], line, partner
        )

    for k in range(1, half):
        for up in (True, False):
            i = high - k if up else high + k

            @pl.when(i >= 0 if up else i < half)
            def _(i=i, up=up):
                step_on(i, up).wait_recv()

                @pl.when(can_go(up))
                def _():
                    step_on(i, up).start()

                cross(i).start()

    gather.spread(0)
    gather.spread(1)
    for k in range(1, lines):
        from_line = lax.rem(line - k + lines, lines)
        there = pl.ds(pl.multiple_of(from_line * shard, 16), shard)
        remote(
            packed_ref, weights_ref.at[there], send_w.at[k], recv_w.at[k], from_line, own
        ).wait_recv()
    small_ref[...] = weights_ref[:, 3 * width :].astype(jnp.float32).T
    for i in range(half):
        block = 2 * i + 1 - low
        remote(
            all_ref.at[block], all_ref.at[block], send_x.at[i], recv_x.at[i], line, partner
        ).wait_recv()

    def project(b, carry):
        start = pl.multiple_of(b * rows, rows)
        block = all_ref[b]
        ext_ref[pl.ds(pl.multiple_of(start + 8, 8), rows), :] = outer_cols(
            block, weights_ref[:, :width]
        )
        gate_ref[pl.ds(start, rows), :] = outer_cols(block, weights_ref[:, width : 2 * width])
        return carry

    lax.fori_loop(0, count, project, 0)

    def convolve(b, carry):
        start = pl.multiple_of(b * rows, rows)
        window = ext_ref[pl.ds(start, rows + 8), :]
        total = small_ref[cuts.conv_bias : cuts.conv_bias + 1, :]
        for k in range(kernel):
            tap = small_ref[cuts.taps + k : cuts.taps + k + 1, :]
            total = total + tap * window[9 - kernel + k : 9 - kernel + k + rows]
        act = total * sigmoid(total)
        sum_ref[pl.ds(start, rows), :] = total
        act_ref[pl.ds(start, rows), :] = act
        part_ref[b] = outer_cols(
            small_ref[: cuts.sent, :].astype(jnp.bfloat16), act.astype(jnp.bfloat16)
        ).astype(jnp.bfloat16)
        return carry

    lax.fori_loop(0, count, convolve, 0)

    for k in range(1, count):
        there = lax.rem(own + k, count)
        copy = remote(
            part_ref.at[there], partial_ref.at[k], send_rs.at[k], recv_rs.at[k], line, there
        )
        copy.start()
        copies.append(copy)
    total = part_ref[own].astype(jnp.float32)
    for k in range(1, count):
        remote(
            part_ref.at[own], partial_ref.at[k], send_rs.at[k], recv_rs.at[k], line, partner
        ).wait_recv()
        total = total + partial_ref[k].astype(jnp.float32)
    total_ref[own] = total.astype(jnp.bfloat16)
    for k in range(1, count):
        copy = remote(
            total_ref.at[own], total_ref.at[own], send_ag.at[k], recv_ag.at[k],
            line, lax.rem(own + k, count),
        )
        copy.start()
        copies.append(copy)
    gather.forward(0)
    gather.forward(1)
    for k in range(1, count):
        block = lax.rem(own - k + count, count)
        remote(
            total_ref.at[block], total_ref.at[block], send_ag.at[k], recv_ag.at[k],
            line, partner,
        ).wait_recv()
    selected_ref[...] = total_ref[...].astype(jnp.float32)[:, : cuts.picks]
    for copy in copies:
        copy.wait_send()
    for i in range(half):
        cross(i).wait_send()
        for up in (True, False):

            @pl.when(can_go(up) & (i <= high if up else i >= high))
            def _(i=i, up=up):
                step_on(i, up).wait_send()

    gather.finish()


def front(count, lines, cuts, shard, small, *args):
    rows, width = args[0].shape
    expert = args[-1]
    columns = 3 * width + small
    inner = -(-lines * shard // LANES) * LANES
    length = count * rows
    half = count // 2
    vmem = pl.BlockSpec(memory_space=pltpu.VMEM)

    def f32(*shape):
        return jax.ShapeDtypeStruct(shape, jnp.float32)

    dma = pltpu.SemaphoreType.DMA
    return pl.pallas_call(
        functools.partial(front_kernel, count, lines, cuts),
        in_specs=[vmem] * len(args),
        out_specs=[vmem] * 9,
        out_shape=[
            jax.ShapeDtypeStruct((count, rows, width), jnp.bfloat16),
            jax.ShapeDtypeStruct((inner, columns), jnp.bfloat16),
            f32(small, inner),
            f32(length + 8, inner),
            f32(length, inner),
            f32(length, inner),
            f32(length, inner),
            f32(count, cuts.picks, rows),
            jax.ShapeDtypeStruct((count, expert.shape[0], expert.shape[1] // 2), jnp.bfloat16),
        ],
        scratch_shapes=[
            pltpu.VMEM((rows, width), jnp.bfloat16),
            pltpu.VMEM((shard, columns), jnp.bfloat16),
            pltpu.VMEM((small, LANES), jnp.float32),
            *[pltpu.VMEM((count, cuts.sent, rows), jnp.bfloat16)] * 3,
            dma((lines,)), dma((lines,)), dma((half,)), dma((half,)), dma((half,)), dma((half,)),
            dma((half,)), dma((count,)), dma((count,)), dma((count,)), dma((count,)),
            *gather_scratch(count),
        ],
        compiler_params=pltpu.CompilerParams(
            collective_id=0, has_side_effects=True, vmem_limit_bytes=VMEM_LIMIT
        ),
        cost_estimate=pl.CostEstimate(
            flops=4 * length * width * inner,
            bytes_accessed=20 * length * inner,
            transcendentals=length * inner,
        ),
        name="front",
    )(*args)


def spread_lanes(values, wide_ref, out_ref):
    state, steps = values.shape
    high = values.astype(jnp.bfloat16).astype(jnp.float32)
    rest = values - high
    lane = lax.broadcasted_iota(jnp.int32, (state, steps), 1)

    def fill(g, carry):
        for k in range(8):
            t = g * 8 + k
            here = pl.ds(pl.multiple_of(t * state, state), state)
            mask = lane == t
            wide_ref[here, :steps] = jnp.where(mask, high, 0.0).astype(jnp.bfloat16)
            wide_ref[here, steps:] = jnp.where(mask, rest, 0.0).astype(jnp.bfloat16)
        return carry

    lax.fori_loop(0, steps // 8, fill, 0)
    ones = jnp.ones((2 * steps, LANES), jnp.bfloat16)
    out_ref[...] = dot_nn(wide_ref[...], ones)


def scan_forward_kernel(
    count, cuts,
    act_ref, gate_ref, selected_ref, small_ref, output_ref, expert_ref,
    pre_ref, mixed_ref, mixer_low_ref, prior_ref, end_ref, summed_ref, expert_out_ref,
    state_ref, delta_ref, scanned_ref, wide_ref, wide_in_ref, wide_out_ref, land_ref, *refs,
):
    steps, inner = act_ref.shape
    tiles = inner // LANES
    state = cuts.state
    halves = state // 8
    step = pl.program_id(0)
    relay = whole_relay("seq", count, refs[:7])
    gather = Gather(count, expert_ref, land_ref, *refs[7:])

    @pl.when(step == 0)
    def _():
        greet(count)
        gather.start()
        state_ref[...] = jnp.zeros_like(state_ref)

    @pl.when(step == 0)
    def _():
        gather.spread(0)

    @pl.when(step == 3)
    def _():
        gather.spread(1)

    rates2 = -LOG2E * jnp.exp(small_ref[cuts.decay : cuts.decay + state, :])
    pre = inner_rows(
        selected_ref[0, : cuts.rank, :],
        small_ref[cuts.step : cuts.step + cuts.rank, :],
        HIGHEST,
    ) + small_ref[cuts.step_bias : cuts.step_bias + 1, :]
    pre_ref[...] = pre
    delta_ref[...] = softplus(pre)
    in_rows = cuts.rank
    out_rows = cuts.rank + state
    spread_lanes(selected_ref[0, in_rows : in_rows + state, :], wide_ref, wide_in_ref)
    spread_lanes(selected_ref[0, out_rows : out_rows + state, :], wide_ref, wide_out_ref)

    def group(g, states):
        states = [list(s) for s in states]
        base = pl.multiple_of(g * 8, 8)
        d8 = delta_ref[pl.ds(base, 8), :]
        du8 = d8 * act_ref[pl.ds(base, 8), :]
        parts = [[None] * 8 for _ in range(tiles)]
        for k in range(8):
            rows_now = [pl.ds((base + k) * state + 8 * i, 8) for i in range(halves)]
            b_now = [wide_in_ref[here, :] for here in rows_now]
            c_now = [wide_out_ref[here, :] for here in rows_now]
            for j in range(tiles):
                cols = slice(j * LANES, (j + 1) * LANES)
                d = jnp.broadcast_to(d8[k : k + 1, cols], (8, LANES))
                du = jnp.broadcast_to(du8[k : k + 1, cols], (8, LANES))
                total = None
                for i in range(halves):
                    old = states[j][i]
                    prior_ref[base + k, 8 * i : 8 * i + 8, cols] = old
                    new = jnp.exp2(d * rates2[8 * i : 8 * i + 8, cols]) * old + b_now[i] * du
                    states[j][i] = new
                    term = c_now[i] * new
                    total = term if total is None else total + term
                parts[j][k] = total
        for j in range(tiles):
            scanned_ref[pl.ds(base, 8), j * LANES : (j + 1) * LANES] = sublane_sums(parts[j])
        return tuple(tuple(s) for s in states)

    first = tuple(
        tuple(
            state_ref[8 * i : 8 * i + 8, j * LANES : (j + 1) * LANES] for i in range(halves)
        )
        for j in range(tiles)
    )
    last = lax.fori_loop(0, steps // 8, group, first)
    for j in range(tiles):
        for i in range(halves):
            state_ref[8 * i : 8 * i + 8, j * LANES : (j + 1) * LANES] = last[j][i]
    end_ref[...] = state_ref[...]

    mixed = scanned_ref[...] + small_ref[cuts.skip : cuts.skip + 1, :] * act_ref[...]
    gate = gate_ref[...]
    low = (mixed * (gate * sigmoid(gate))).astype(jnp.bfloat16)
    mixed_ref[...] = mixed
    mixer_low_ref[...] = low
    relay.part[step] = dot_nn(low, output_ref[...]).astype(jnp.bfloat16)
    relay.made(step // 2, lax.rem(step, 2))

    def pass_on(block):
        relay.pass_on(block // 2, lax.rem(block, 2))

    @pl.when(step >= LAG)
    def _():
        pass_on(step - LAG)

    @pl.when(step == count - 1)
    def _():
        for late in range(LAG - 1, -1, -1):
            pass_on(step - late)
        gather.forward(0)
        gather.forward(1)
        summed_ref[...] = relay.finish()
        gather.finish()
        expert_out_ref[...] = land_ref[...]


def scan_forward(count, cuts, width, act, gate, selected, small, weights, expert):
    length, inner = act.shape
    state = cuts.state
    block = length // count
    rows = pl.BlockSpec((block, inner), lambda t: (t, 0))
    whole = pl.BlockSpec((state, inner), lambda t: (0, 0))
    pieces = (count, expert.shape[0], expert.shape[1] // 2)
    return pl.pallas_call(
        functools.partial(scan_forward_kernel, count, cuts),
        grid=(count,),
        in_specs=[
            rows,
            rows,
            pl.BlockSpec((1, cuts.picks, block), lambda t: (t, 0, 0)),
            pl.BlockSpec(small.shape, lambda t: (0, 0)),
            pl.BlockSpec((inner, width), lambda t: (0, 2)),
            pl.BlockSpec(expert.shape, lambda t: (0, 0)),
        ],
        out_specs=[
            rows,
            rows,
            rows,
            pl.BlockSpec((block, state, inner), lambda t: (t, 0, 0)),
            whole,
            pl.BlockSpec((block, width), lambda t: (0, 0)),
            pl.BlockSpec(pieces, lambda t: (0, 0, 0)),
        ],
        out_shape=[
            jax.ShapeDtypeStruct((length, inner), jnp.float32),
            jax.ShapeDtypeStruct((length, inner), jnp.float32),
            jax.ShapeDtypeStruct((length, inner), jnp.bfloat16),
            jax.ShapeDtypeStruct((length, state, inner), jnp.float32),
            jax.ShapeDtypeStruct((state, inner), jnp.float32),
            jax.ShapeDtypeStruct((block, width), jnp.float32),
            jax.ShapeDtypeStruct(pieces, jnp.bfloat16),
        ],
        scratch_shapes=[
            pltpu.VMEM((state, inner), jnp.float32),
            pltpu.VMEM((block, inner), jnp.float32),
            pltpu.VMEM((block, inner), jnp.float32),
            pltpu.VMEM((block * state, 2 * block), jnp.bfloat16),
            pltpu.VMEM((block * state, LANES), jnp.float32),
            pltpu.VMEM((block * state, LANES), jnp.float32),
            pltpu.VMEM(pieces, jnp.bfloat16),
            *relay_scratch(count, block, width),
            *gather_scratch(count),
        ],
        compiler_params=pltpu.CompilerParams(
            collective_id=1, has_side_effects=True, vmem_limit_bytes=VMEM_LIMIT
        ),
        cost_estimate=pl.CostEstimate(
            flops=8 * length * state * inner,
            bytes_accessed=4 * length * inner * (state + 6),
            transcendentals=length * state * inner,
        ),
        name="scan_forward",
    )(act, gate, selected, small, weights, expert)


def scan_backward_kernel(
    count, cuts,
    own_ref, act_ref, gate_ref, mixed_ref, pre_ref, selected_ref, small_ref, output_ref,
    prior_ref, end_ref, expert_ref,
    grad_gate_ref, grad_act_ref, grad_step_ref, rate_total_ref, rows_ref, grad_selected_ref,
    all_out_ref, expert_out_ref,
    incoming_ref, post_ref, delta_ref, grad_ref, grad_delta_ref, wide_ref, wide_in_ref,
    wide_out_ref, all_ref,
    stage_ref, part_ref, partial_ref, total_ref,
    send_hi, recv_hi, send_x, recv_x, send_rs, recv_rs, send_ag, recv_ag,
    other_ref, held_ref, swap_s, swap_r, *scatter_refs,
):
    steps, inner = act_ref.shape
    tiles = inner // LANES
    state = cuts.state
    halves = state // 8
    lane = lax.broadcasted_iota(jnp.int32, (8, steps), 1)
    line, own, high, low = place()
    half = count // 2
    partner = 2 * high + 1 - low
    index = pl.program_id(0)
    now = count - 1 - index
    scatter = Scatter(
        count, expert_ref, None, other_ref, held_ref, swap_s, swap_r, scatter_refs
    )

    def along(k):
        return remote(
            own_ref, all_ref.at[own], send_hi.at[k], recv_hi.at[high], line,
            2 * lax.rem(high + k, half) + low,
        )

    def across(block):
        i = block // 2
        return remote(
            all_ref.at[block], all_ref.at[block], send_x.at[i], recv_x.at[i], line, partner
        )

    def came_along(block):
        i = block // 2
        return remote(
            all_ref.at[block], all_ref.at[block], send_hi.at[0], recv_hi.at[i], line, partner
        )

    def hand_over(block):
        @pl.when((lax.rem(block, 2) == low) & (block // 2 != high))
        def _():
            came_along(block).wait_recv()
            across(block).start()

    @pl.when(index == 0)
    def _():
        greet(count)
        all_ref[own] = own_ref[...]
        incoming_ref[...] = jnp.zeros_like(incoming_ref)
        post_ref[...] = end_ref[...]
        rate_total_ref[...] = jnp.zeros_like(rate_total_ref)
        grad_step_ref[...] = jnp.zeros_like(grad_step_ref)
        rows_ref[...] = jnp.zeros_like(rows_ref)
        stage_ref[...] = jnp.zeros_like(stage_ref)

    @pl.when(index == 0)
    def _():
        for k in range(1, half):
            along(k).start()
        across(own).start()

    @pl.when(index == 0)
    def _():
        hand_over(now - 0)
        hand_over(now - 1)

    @pl.when(lax.rem(now, 2) != low)
    def _():
        across(now).wait_recv()

    gate = gate_ref[...]
    gate_sig = sigmoid(gate)
    grad_y = outer_cols(all_ref[now], output_ref[...])
    grad_gate_ref[...] = (
        grad_y * mixed_ref[...] * (gate_sig * (1.0 + gate * (1.0 - gate_sig)))
    ).astype(jnp.bfloat16)
    grad_mixed = grad_y * (gate * gate_sig)
    grad_ref[...] = grad_mixed
    delta_ref[...] = softplus(pre_ref[...])
    rows_ref[1:2, :] += jnp.sum(grad_mixed * act_ref[...], axis=0, keepdims=True)
    rates2 = -LOG2E * jnp.exp(small_ref[cuts.decay : cuts.decay + state, :])
    in_rows = cuts.rank
    out_rows = cuts.rank + state
    spread_lanes(selected_ref[0, in_rows : in_rows + state, :], wide_ref, wide_in_ref)
    spread_lanes(selected_ref[0, out_rows : out_rows + state, :], wide_ref, wide_out_ref)

    def tile_of(ref):
        return tuple(
            tuple(ref[8 * i : 8 * i + 8, j * LANES : (j + 1) * LANES] for i in range(halves))
            for j in range(tiles)
        )

    def group(turn, carry):
        incoming, posts, rate_total, in_acc, out_acc = carry
        incoming = [list(s) for s in incoming]
        posts = [list(s) for s in posts]
        rate_total = [list(s) for s in rate_total]
        in_acc, out_acc = list(in_acc), list(out_acc)
        base = pl.multiple_of((steps // 8 - 1 - turn) * 8, 8)
        d8 = delta_ref[pl.ds(base, 8), :]
        u8 = act_ref[pl.ds(base, 8), :]
        du8 = d8 * u8
        g8 = grad_ref[pl.ds(base, 8), :]
        rate_parts = [[None] * 8 for _ in range(tiles)]
        side_parts = [[None] * 8 for _ in range(tiles)]
        for k in range(7, -1, -1):
            rows_now = [pl.ds((base + k) * state + 8 * i, 8) for i in range(halves)]
            b_now = [wide_in_ref[here, :] for here in rows_now]
            c_now = [wide_out_ref[here, :] for here in rows_now]
            in_sum = [None] * halves
            out_sum = [None] * halves
            for j in range(tiles):
                cols = slice(j * LANES, (j + 1) * LANES)
                d = jnp.broadcast_to(d8[k : k + 1, cols], (8, LANES))
                du = jnp.broadcast_to(du8[k : k + 1, cols], (8, LANES))
                gm = jnp.broadcast_to(g8[k : k + 1, cols], (8, LANES))
                rate_part = None
                side_part = None
                for i in range(halves):
                    prior = prior_ref[base + k, 8 * i : 8 * i + 8, cols]
                    rates = rates2[8 * i : 8 * i + 8, cols]
                    grad_state = c_now[i] * gm + incoming[j][i]
                    passed = jnp.exp2(d * rates) * grad_state
                    incoming[j][i] = passed
                    weighted = passed * prior
                    term = weighted * rates
                    rate_part = term if rate_part is None else rate_part + term
                    term = grad_state * b_now[i]
                    side_part = term if side_part is None else side_part + term
                    term = grad_state * du
                    in_sum[i] = term if in_sum[i] is None else in_sum[i] + term
                    term = posts[j][i] * gm
                    out_sum[i] = term if out_sum[i] is None else out_sum[i] + term
                    rate_total[j][i] = rate_total[j][i] + weighted * d
                    posts[j][i] = prior
                rate_parts[j][k] = rate_part
                side_parts[j][k] = side_part
            here = lane == base + k
            for i in range(halves):
                in_acc[i] = jnp.where(here, jnp.sum(in_sum[i], axis=1, keepdims=True), in_acc[i])
                out_acc[i] = jnp.where(here, jnp.sum(out_sum[i], axis=1, keepdims=True), out_acc[i])
        for j in range(tiles):
            cols = slice(j * LANES, (j + 1) * LANES)
            side = sublane_sums(side_parts[j])
            grad_delta_ref[pl.ds(base, 8), cols] = (
                sublane_sums(rate_parts[j]) * (1.0 / LOG2E) + u8[:, cols] * side
            )
            grad_act_ref[pl.ds(base, 8), cols] = d8[:, cols] * side
        return (
            tuple(tuple(s) for s in incoming),
            tuple(tuple(s) for s in posts),
            tuple(tuple(s) for s in rate_total),
            tuple(in_acc),
            tuple(out_acc),
        )

    empty = tuple(jnp.zeros((8, steps), jnp.float32) for _ in range(halves))
    incoming, posts, rate_total, in_acc, out_acc = lax.fori_loop(
        0,
        steps // 8,
        group,
        (tile_of(incoming_ref), tile_of(post_ref), tile_of(rate_total_ref), empty, empty),
    )
    for i in range(halves):
        stage_ref[in_rows + 8 * i : in_rows + 8 * i + 8, :] = in_acc[i]
        stage_ref[out_rows + 8 * i : out_rows + 8 * i + 8, :] = out_acc[i]
        for j in range(tiles):
            cols = slice(j * LANES, (j + 1) * LANES)
            incoming_ref[8 * i : 8 * i + 8, cols] = incoming[j][i]
            post_ref[8 * i : 8 * i + 8, cols] = posts[j][i]
            rate_total_ref[8 * i : 8 * i + 8, cols] = rate_total[j][i]

    grad_act_ref[...] += grad_ref[...] * small_ref[cuts.skip : cuts.skip + 1, :]
    grad_pre = grad_delta_ref[...] * sigmoid(pre_ref[...])
    rows_ref[0:1, :] += jnp.sum(grad_pre, axis=0, keepdims=True)
    grad_step_ref[...] += dot_nn(selected_ref[0, : cuts.rank, :], grad_pre, HIGHEST)
    stage_ref[: cuts.rank, :] = outer_cols(
        small_ref[cuts.step : cuts.step + cuts.rank, :], grad_pre, HIGHEST
    )
    part_ref[now] = stage_ref[...].astype(jnp.bfloat16)

    def partial_to(block):
        return remote(
            part_ref.at[block], partial_ref.at[own], send_rs.at[block], recv_rs.at[own], line, block
        )

    @pl.when(now != own)
    def _():
        partial_to(now).start()

    def total_to(k):
        return remote(
            total_ref.at[own], total_ref.at[own], send_ag.at[k], recv_ag.at[own], line,
            lax.rem(own + k, count),
        )

    @pl.when(now >= 2)
    def _():
        hand_over(now - 2)

    @pl.when(index == NEAR_AT)
    def _():
        scatter.send_near()

    @pl.when(index == FAR_AT)
    def _():
        scatter.send_far()

    @pl.when(index == PASS_AT)
    def _():
        scatter.pass_far()

    @pl.when(index == count - 1)
    def _():
        scatter.hand_over()

    @pl.when(index == jnp.minimum(count - 1 - own + 2, count - 1))
    def _():
        total = part_ref[own].astype(jnp.float32)
        for k in range(1, count):
            there = lax.rem(own + k, count)
            remote(
                part_ref.at[own], partial_ref.at[there], send_rs.at[own], recv_rs.at[there],
                line, there,
            ).wait_recv()
            total = total + partial_ref[there].astype(jnp.float32)
        total_ref[own] = total.astype(jnp.bfloat16)
        for k in range(1, count):
            total_to(k).start()

    @pl.when(index == count - 1)
    def _():
        for k in range(1, count):
            there = lax.rem(own + k, count)
            remote(
                total_ref.at[there], total_ref.at[there], send_ag.at[k], recv_ag.at[there],
                line, there,
            ).wait_recv()
        grad_selected_ref[...] = total_ref[...]
        all_out_ref[...] = all_ref[...]
        for k in range(1, half):
            along(k).wait_send()
        for i in range(half):
            across(2 * i + low).wait_send()
        for k in range(1, count):
            partial_to(lax.rem(own + k, count)).wait_send()
            total_to(k).wait_send()
        scatter.finish(expert_out_ref)


def scan_backward(
    count, cuts, grad_low, act, gate, mixed, pre, selected, small, weights, priors, end, expert
):
    length, inner = act.shape
    state = cuts.state
    block = length // count
    width = grad_low.shape[1]
    half = count // 2

    def back(t):
        return count - 1 - t

    rows = pl.BlockSpec((block, inner), lambda t: (back(t), 0))
    whole = pl.BlockSpec((state, inner), lambda t: (0, 0))
    dma = pltpu.SemaphoreType.DMA
    picked = (count, cuts.sent, block)
    return pl.pallas_call(
        functools.partial(scan_backward_kernel, count, cuts),
        grid=(count,),
        in_specs=[
            pl.BlockSpec((block, width), lambda t: (0, 0)),
            rows,
            rows,
            rows,
            rows,
            pl.BlockSpec((1, cuts.picks, block), lambda t: (back(t), 0, 0)),
            pl.BlockSpec(small.shape, lambda t: (0, 0)),
            pl.BlockSpec((inner, width), lambda t: (0, 2)),
            pl.BlockSpec((block, state, inner), lambda t: (back(t), 0, 0)),
            whole,
            pl.BlockSpec(expert.shape, lambda t: (0, 0, 0)),
        ],
        out_specs=[
            rows,
            rows,
            pl.BlockSpec((cuts.rank, inner), lambda t: (0, 0)),
            whole,
            pl.BlockSpec((8, inner), lambda t: (0, 0)),
            pl.BlockSpec(picked, lambda t: (0, 0, 0)),
            pl.BlockSpec((count, block, width), lambda t: (0, 0, 0)),
            pl.BlockSpec((expert.shape[1], 2 * expert.shape[2]), lambda t: (0, 0)),
        ],
        out_shape=[
            jax.ShapeDtypeStruct((length, inner), jnp.bfloat16),
            jax.ShapeDtypeStruct((length, inner), jnp.float32),
            jax.ShapeDtypeStruct((cuts.rank, inner), jnp.float32),
            jax.ShapeDtypeStruct((state, inner), jnp.float32),
            jax.ShapeDtypeStruct((8, inner), jnp.float32),
            jax.ShapeDtypeStruct(picked, jnp.bfloat16),
            jax.ShapeDtypeStruct((count, block, width), jnp.bfloat16),
            jax.ShapeDtypeStruct((expert.shape[1], 2 * expert.shape[2]), jnp.float32),
        ],
        scratch_shapes=[
            pltpu.VMEM((state, inner), jnp.float32),
            pltpu.VMEM((state, inner), jnp.float32),
            pltpu.VMEM((block, inner), jnp.float32),
            pltpu.VMEM((block, inner), jnp.float32),
            pltpu.VMEM((block, inner), jnp.float32),
            pltpu.VMEM((block * state, 2 * block), jnp.bfloat16),
            pltpu.VMEM((block * state, LANES), jnp.float32),
            pltpu.VMEM((block * state, LANES), jnp.float32),
            pltpu.VMEM((count, block, width), jnp.bfloat16),
            pltpu.VMEM(picked[1:], jnp.float32),
            *[pltpu.VMEM(picked, jnp.bfloat16)] * 3,
            dma((half,)), dma((half,)), dma((half,)), dma((half,)),
            dma((count,)), dma((count,)), dma((count,)), dma((count,)),
            *scatter_scratch(count, expert.shape[1], expert.shape[2]),
        ],
        compiler_params=pltpu.CompilerParams(
            collective_id=2, has_side_effects=True, vmem_limit_bytes=VMEM_LIMIT
        ),
        cost_estimate=pl.CostEstimate(
            flops=20 * length * state * inner,
            bytes_accessed=4 * length * inner * (state + 6),
            transcendentals=length * state * inner,
        ),
        name="scan_backward",
    )(grad_low, act, gate, mixed, pre, selected, small, weights, priors, end, expert)


def back_kernel(
    count, lines, cuts,
    grad_selected_ref, small_ref, weights_ref, ext_ref, sum_ref, grad_act_ref, grad_gate_ref,
    mixer_low_ref, normed_ref, grad_middle_ref, grad_step_ref, rate_total_ref, scan_rows_ref,
    vectors_ref, expert_ref, far_ref, x_ref, gain_ref, kept_ref,
    tokens_ref, input_ref, output_ref, select_ref, step_ref, decay_ref, taps_ref, conv_bias_ref,
    step_bias_ref, skip_ref, totals_ref, expert_out_ref,
    grad_sum_ref, grad_conv_ref, grad_small_ref, ours_ref, theirs_ref,
    send_v, recv_v, send_u, recv_u, other_ref, held_ref, swap_s, swap_r, *refs,
):
    scatter = Scatter(count, expert_ref, far_ref, other_ref, held_ref, swap_s, swap_r, refs[:6])
    relay = whole_relay("seq", count, refs[6:13])
    spread = whole_relay("dp", lines, refs[13:])
    line, own, _, _ = place()
    length, inner = sum_ref.shape
    width = normed_ref.shape[1]
    rows = length // count
    kernel = cuts.kernel
    shard = spread.part.shape[1]
    own_shard = output_ref.shape[0]
    greet(count, lines)
    scatter.pass_far()
    scatter.send_near()
    grad_small_ref[...] = jnp.zeros_like(grad_small_ref)
    grad_sum_ref[length:, :] = jnp.zeros((8, inner), jnp.float32)
    select = small_ref[: cuts.sent, :].astype(jnp.bfloat16)

    def first(b, carry):
        start = pl.multiple_of(b * rows, rows)
        grad_selected = grad_selected_ref[b]
        total = sum_ref[pl.ds(start, rows), :]
        sig = sigmoid(total)
        grad_act = grad_act_ref[pl.ds(start, rows), :] + inner_rows(grad_selected, select)
        grad_sum = grad_act * (sig * (1.0 + total * (1.0 - sig)))
        grad_sum_ref[pl.ds(start, rows), :] = grad_sum
        grad_small_ref[: cuts.sent, :] += dot_nn(
            grad_selected, (total * sig).astype(jnp.bfloat16)
        )
        window = ext_ref[pl.ds(start, rows + 8), :]
        for k in range(kernel):
            row = slice(cuts.taps + k, cuts.taps + k + 1)
            grad_small_ref[row, :] += jnp.sum(
                grad_sum * window[9 - kernel + k : 9 - kernel + k + rows], axis=0, keepdims=True
            )
        row = slice(cuts.conv_bias, cuts.conv_bias + 1)
        grad_small_ref[row, :] += jnp.sum(grad_sum, axis=0, keepdims=True)
        return carry

    lax.fori_loop(0, count, first, 0)

    def order(j):
        return j // 2 + lax.rem(j, 2) * (count // 2)

    def second(j, carry):
        b = order(j)
        start = pl.multiple_of(b * rows, rows)
        window = grad_sum_ref[pl.ds(start, rows + 8), :]
        grad_conv = None
        for k in range(kernel):
            tap = small_ref[cuts.taps + k : cuts.taps + k + 1, :]
            term = tap * window[kernel - 1 - k : kernel - 1 - k + rows]
            grad_conv = term if grad_conv is None else grad_conv + term
        grad_conv = grad_conv.astype(jnp.bfloat16)
        grad_conv_ref[pl.ds(start, rows), :] = grad_conv
        relay.part[b] = (
            dot_nn(grad_conv, weights_ref[:, :width])
            + dot_nn(grad_gate_ref[pl.ds(start, rows), :], weights_ref[:, width : 2 * width])
        ).astype(jnp.bfloat16)
        relay.made(b // 2, lax.rem(b, 2))
        return carry

    lax.fori_loop(0, count, second, 0)

    decay = slice(cuts.decay, cuts.decay + cuts.state)
    grad_small_ref[cuts.step : cuts.step + cuts.rank, :] = grad_step_ref[...]
    grad_small_ref[decay, :] = -rate_total_ref[...] * jnp.exp(small_ref[decay, :])
    grad_small_ref[cuts.step_bias : cuts.step_bias + 2, :] = scan_rows_ref[0:2, :]
    small_t = grad_small_ref[...].T
    for d in range(lines):
        spread.part[d, :, 3 * width :] = small_t[d * shard : (d + 1) * shard].astype(jnp.bfloat16)
    chunk = width // 3

    def pass_on(j, carry):
        b = order(j)
        relay.pass_on(b // 2, lax.rem(b, 2))
        return carry

    ours_ref[...] = vectors_ref[...]
    for left_ref, right_ref, place_at in (
        (mixer_low_ref, grad_middle_ref, 2 * width),
        (grad_conv_ref, normed_ref, 0),
        (grad_gate_ref, normed_ref, width),
    ):

        def columns(c, carry, left_ref=left_ref, right_ref=right_ref, place_at=place_at):
            here = pl.ds(pl.multiple_of(c * chunk, chunk), chunk)
            there = pl.ds(pl.multiple_of(place_at + c * chunk, chunk), chunk)
            grad = inner_rows(left_ref[...], right_ref[:, here])
            if place_at < 2 * width:
                ours_ref[0:1, here] += jnp.sum(
                    weights_ref[:, there].astype(jnp.float32) * grad, axis=0, keepdims=True
                )
            low = grad.astype(jnp.bfloat16)
            for d in range(lines):
                spread.part[d, :, there] = low[d * shard : (d + 1) * shard]
            return carry

        lax.fori_loop(0, 3, columns, 0)
        if place_at == 2 * width:
            lax.fori_loop(0, count, pass_on, 0)
    for d in range(lines):
        spread.made(d // 2, d % 2)
    scatter.hand_over()

    def sum_over(size, axis, send, recv):
        here = own if axis == "seq" else line

        def copy(k, slot):
            there = lax.rem(here + k, size)
            target = (line, there) if axis == "seq" else (there, own)
            return remote(ours_ref, theirs_ref.at[slot], send.at[k], recv.at[k], *target)

        base = 0 if axis == "seq" else count
        for k in range(1, size):
            copy(k, base + k).start()
        total = ours_ref[...]
        for k in range(1, size):
            copy(k, base + k).wait_recv()
            total = total + theirs_ref[base + k]
        for k in range(1, size):
            copy(k, base + k).wait_send()
        return total

    ours_ref[...] = sum_over(count, "seq", send_v, recv_v)
    for d in range(lines):
        spread.pass_on(d // 2, d % 2)
    totals_ref[...] = sum_over(lines, "dp", send_u, recv_u)
    x = x_ref[...]
    scale = lax.rsqrt(jnp.mean(x * x, axis=1, keepdims=True) + 1e-05)
    scaled = gain_ref[...] * relay.finish()
    tokens_ref[...] = (
        kept_ref[...]
        + scale * scaled
        - x * (scale * scale * scale) * jnp.mean(scaled * x, axis=1, keepdims=True)
    )
    total = spread.finish()
    input_ref[0] = total[:own_shard, :width]
    input_ref[1] = total[:own_shard, width : 2 * width]
    output_ref[...] = total[:own_shard, 2 * width : 3 * width]
    small = total[:, 3 * width :]
    select_ref[...] = small[:own_shard, : cuts.picks]
    small = jnp.concatenate(
        [small, jnp.zeros((LANES - shard, small.shape[1]), jnp.float32)], axis=0
    ).T
    for at, ref in (
        (cuts.step, step_ref),
        (cuts.decay, decay_ref),
        (cuts.taps, taps_ref),
        (cuts.conv_bias, conv_bias_ref),
        (cuts.step_bias, step_bias_ref),
        (cuts.skip, skip_ref),
    ):
        ref[...] = small[at : at + ref.shape[0], :own_shard]
    scatter.finish(expert_out_ref)


def back(
    count, lines, shard, own_shard, cuts, grad_selected, small, weights, ext, conv_sum, grad_act, grad_gate,
    mixer_low, normed, grad_middle, grad_step, rate_total, scan_rows, vectors, expert, far,
    x, gain, kept,
):
    length, inner = conv_sum.shape
    width = normed.shape[1]
    columns = weights.shape[1]
    rows = length // count
    vmem = pl.BlockSpec(memory_space=pltpu.VMEM)
    dma = pltpu.SemaphoreType.DMA
    args = (
        grad_selected, small, weights, ext, conv_sum, grad_act, grad_gate, mixer_low, normed,
        grad_middle, grad_step, rate_total, scan_rows, vectors, expert, far, x, gain, kept,
    )
    return pl.pallas_call(
        functools.partial(back_kernel, count, lines, cuts),
        in_specs=[vmem] * len(args),
        out_specs=[vmem] * 12,
        out_shape=[
            *[
                jax.ShapeDtypeStruct(shape, jnp.float32)
                for shape in (
                    (rows, width),
                    (2, own_shard, width),
                    (own_shard, width),
                    (own_shard, cuts.picks),
                    (cuts.rank, own_shard),
                    (cuts.state, own_shard),
                    (cuts.kernel, own_shard),
                    (1, own_shard),
                    (1, own_shard),
                    (1, own_shard),
                    vectors.shape,
                )
            ],
            jax.ShapeDtypeStruct((expert.shape[1], 2 * expert.shape[2]), jnp.float32),
        ],
        scratch_shapes=[
            pltpu.VMEM((length + 8, inner), jnp.float32),
            pltpu.VMEM((length, inner), jnp.bfloat16),
            pltpu.VMEM(small.shape, jnp.float32),
            pltpu.VMEM(vectors.shape, jnp.float32),
            pltpu.VMEM((count + lines, *vectors.shape), jnp.float32),
            dma((count,)), dma((count,)), dma((lines,)), dma((lines,)),
            *scatter_scratch(count, expert.shape[1], expert.shape[2]),
            *relay_scratch(count, rows, width),
            *relay_scratch(lines, shard, columns),
        ],
        compiler_params=pltpu.CompilerParams(
            collective_id=3, has_side_effects=True, vmem_limit_bytes=VMEM_LIMIT
        ),
        cost_estimate=pl.CostEstimate(
            flops=10 * length * width * inner,
            bytes_accessed=30 * length * inner,
            transcendentals=length * inner,
        ),
        name="back",
    )(*args)


LAG = 3
FAR_AT = 0
NEAR_AT = 2
PASS_AT = 4
SLOTS = 64


def gauss(values):
    return 0.5 * (1.0 + lax.erf(values * math.sqrt(0.5)))


def split_low(values):
    high = values.astype(jnp.bfloat16)
    return high, (values - high.astype(jnp.float32)).astype(jnp.bfloat16)


def experts_kernel(
    count, lines, experts,
    x_ref, mixer_ref, grad_ref, route_ref, gain_ref, router_ref,
    up_ref, down_ref,
    output_ref, grad_middle_ref, grad_low_ref, vectors_ref, grad_up_ref, grad_down_ref, far_up_ref,
    table_ref, back_table_ref, middle_ref, normed_ref, send_ref, rows_ref, made_ref, got_ref, act_ref, slope_ref, pre_ref,
    send_sem, recv_sem, home_s, home_r, far_s, far_r,
):
    line, own, _, _ = place()
    q, f, low = square()
    mate = seat_of(q, 1 - f, low)
    copies = lines // experts
    barrier = pltpu.get_barrier_semaphore()
    for d in range(1, lines):
        for where in (own, mate):
            pl.semaphore_signal(
                barrier, inc=1, device_id=(lax.rem(line + d, lines), where), device_id_type=MESH
            )
    partner = seat_of(q, f, 1 - low)
    for where in (mate, partner):
        pl.semaphore_signal(barrier, inc=1, device_id=(line, where), device_id_type=MESH)
    pl.semaphore_wait(barrier, 2 * lines)

    peers = [(j, d) for d in range(lines) for j in (1, 0) if (j, d) != (0, 0)]

    def out_copy(what, j, d):
        there = lax.rem(line + d, lines)
        return remote(
            send_ref.at[what, there // copies], rows_ref.at[what, j, line],
            send_sem.at[what, j, d], recv_sem.at[what, j, line],
            there, mate if j else own,
        )

    def arrived(what, j, d):
        from_line = lax.rem(line + d, lines)
        return remote(
            send_ref.at[what, 0], rows_ref.at[what, j, from_line],
            send_sem.at[what, j, d], recv_sem.at[what, j, from_line],
            from_line, mate if j else own,
        )

    def home_copy(what, j, d):
        there = lax.rem(line + d, lines)
        return remote(
            made_ref.at[what, j, there], got_ref.at[what, j, line],
            home_s.at[what, j, d], home_r.at[what, j, line],
            there, mate if j else own,
        )

    def came_home(what, j, d):
        from_line = lax.rem(line + d, lines)
        return remote(
            made_ref.at[what, j, 0], got_ref.at[what, j, from_line],
            home_s.at[what, j, d], home_r.at[what, j, from_line],
            from_line, mate if j else own,
        )

    middle = x_ref[...] + mixer_ref[...]
    middle_ref[...] = middle
    gain = gain_ref[...]
    scale = lax.rsqrt(jnp.mean(middle * middle, axis=1, keepdims=True) + 1e-05)
    normed = (middle * scale * gain).astype(jnp.bfloat16)
    normed_ref[...] = normed
    rows, width = middle.shape
    slots = SLOTS
    lane = lax.broadcasted_iota(jnp.int32, (rows, LANES), 1)
    route_along = jnp.broadcast_to(route_ref[...].astype(jnp.float32), (rows, rows))
    route_down = route_along.T[:, :LANES]
    chosen = (route_down == lane.astype(jnp.float32)).astype(jnp.float32)
    earlier = (
        lax.broadcasted_iota(jnp.int32, (rows, rows), 0)
        > lax.broadcasted_iota(jnp.int32, (rows, rows), 1)
    ).astype(jnp.bfloat16)
    before = dot_nn(earlier, chosen.astype(jnp.bfloat16))
    slot_down = route_down[:, :1] * slots + jnp.sum(before * chosen, axis=1, keepdims=True)
    slot_along = jnp.broadcast_to(slot_down, (rows, rows)).T[:1, :]
    table_ref[...] = (
        jnp.broadcast_to(slot_along, table_ref.shape)
        == lax.broadcasted_iota(jnp.int32, table_ref.shape, 0).astype(jnp.float32)
    ).astype(jnp.bfloat16)
    for e in range(experts):
        places = lax.broadcasted_iota(jnp.int32, (rows, slots), 1) + e * slots
        back_table_ref[e] = (
            jnp.broadcast_to(slot_down, (rows, slots)) == places.astype(jnp.float32)
        ).astype(jnp.bfloat16)

    def dispatch(what, values):
        sent = dot_nn(table_ref[...], values).astype(jnp.bfloat16)
        for e in range(experts):
            send_ref[what, e] = sent[e * slots : (e + 1) * slots]
        for j, d in peers:
            out_copy(what, j, d).start()
        rows_ref[what, 0, line] = send_ref[what, line // copies]

    dispatch(0, normed)
    router_f = jnp.concatenate(
        [
            router_ref[...].astype(jnp.float32),
            jnp.zeros((LANES - experts, width), jnp.float32),
        ],
        axis=0,
    )
    router = router_f.astype(jnp.bfloat16)
    logits = jnp.where(lane < experts, outer_cols(normed, router), -jnp.inf)
    grown = jnp.exp(logits - jnp.max(logits, axis=1, keepdims=True))
    probs = grown / jnp.sum(grown, axis=1, keepdims=True)
    gate = jnp.sum(chosen * probs, axis=1, keepdims=True)
    dispatch(1, (gate * grad_ref[...]).astype(jnp.bfloat16))

    total = 2 * lines * slots
    hidden = up_ref.shape[1]
    chunk = hidden // 3 if hidden % (3 * LANES) == 0 else hidden
    parts = hidden // chunk

    def rows_of(ref, what):
        return ref[what].reshape(total, width)

    def columns(c):
        return pl.ds(pl.multiple_of(c * chunk, LANES), chunk)

    for j, d in peers:
        arrived(0, j, d).wait_recv()

    def rise(c, carry):
        pre_ref[:, columns(c)] = dot_nn(rows_of(rows_ref, 0), up_ref[:, columns(c)])
        pre = pre_ref[:, columns(c)]
        half = gauss(pre)
        act_ref[:, columns(c)] = (pre * half).astype(jnp.bfloat16)
        pre_ref[:, columns(c)] = half + pre * (
            jnp.exp(-0.5 * pre * pre) * (1.0 / math.sqrt(2.0 * math.pi))
        )
        return carry

    lax.fori_loop(0, parts, rise, 0)

    wide = width // 3

    def send_home(what, left_ref, right_ref):
        def make(c, carry):
            here = pl.ds(pl.multiple_of(c * wide, LANES), wide)
            there = pl.ds(pl.multiple_of(c * wide, LANES), wide)
            made = outer_cols(left_ref[...], right_ref[there, :]).astype(jnp.bfloat16)
            made_ref[what, :, :, :, here] = made.reshape(2, lines, slots, wide)
            return carry

        lax.fori_loop(0, 3, make, 0)
        for j, d in peers:
            home_copy(what, j, d).start()
        got_ref[what, 0, line] = made_ref[what, 0, line]

    for j, d in peers:
        arrived(1, j, d).wait_recv()

    def fall(c, carry):
        slope_ref[:, columns(c)] = (
            dot_nn(rows_of(rows_ref, 1), down_ref[:, columns(c)]) * pre_ref[:, columns(c)]
        ).astype(jnp.bfloat16)
        return carry

    lax.fori_loop(0, parts, fall, 0)
    send_home(1, slope_ref, up_ref)
    send_home(0, act_ref, down_ref)

    pieces = grad_up_ref.shape[1]

    def weigh(c, carry):
        up = inner_rows(rows_of(rows_ref, 0), slope_ref[:, columns(c)]).astype(jnp.bfloat16)
        down = inner_rows(rows_of(rows_ref, 1), act_ref[:, columns(c)]).astype(jnp.bfloat16)
        grad_up_ref[:, :, columns(c)] = up.reshape(count, pieces, chunk)
        grad_down_ref[:, :, columns(c)] = down.reshape(count, pieces, chunk)
        return carry

    lax.fori_loop(0, parts, weigh, 0)

    far_copies = []
    for k in range(1, count // 4):
        i = lax.rem(q + k, count // 4)
        for j in (1, 0):
            far_copies.append(
                remote(
                    grad_up_ref.at[seat_of(i, lax.rem(f + j, 2), 1 - low)], far_up_ref.at[j, i],
                    far_s.at[j, i], far_r.at[j, i], line, partner,
                )
            )
            far_copies[-1].start()

    def home(what):
        for j, d in peers:
            came_home(what, j, d).wait_recv()
        both = None
        for e in range(experts):
            own_rows = None
            for c in range(copies):
                for j in range(2):
                    term = got_ref[what, j, e * copies + c].astype(jnp.float32)
                    own_rows = term if own_rows is None else own_rows + term
            high, rest = split_low(own_rows)
            here = back_table_ref[e]
            term = dot_nn(here, high) + dot_nn(here, rest)
            both = term if both is None else both + term
        return both

    grad = grad_ref[...]
    middle = middle_ref[...]
    picked = home(0)
    output_ref[...] = middle + gate * picked
    grad_gate = jnp.sum(grad * picked, axis=1, keepdims=True)
    grad_logits = gate * (chosen - probs) * grad_gate
    grad_normed = home(1) + dot_nn(grad_logits, router_f, HIGHEST)
    scaled = gain * grad_normed
    grad_middle = (
        grad
        + scale * scaled
        - middle * (scale * scale * scale) * jnp.mean(scaled * middle, axis=1, keepdims=True)
    )
    grad_middle_ref[...] = grad_middle
    grad_low_ref[...] = grad_middle.astype(jnp.bfloat16)
    vectors_ref[...] = jnp.zeros_like(vectors_ref)
    vectors_ref[1:2, :] = jnp.sum(grad_normed * middle * scale, axis=0, keepdims=True)
    vectors_ref[2 : 2 + experts, :] = inner_rows(
        grad_logits, normed_ref[...].astype(jnp.float32), HIGHEST
    )[:experts]
    for what in range(2):
        for j, d in peers:
            out_copy(what, j, d).wait_send()
            home_copy(what, j, d).wait_send()
    for copy in far_copies:
        copy.wait()


def run_experts(
    count, lines, experts, x, mixer, grad, route, gain, router, up, down
):
    rows, width = x.shape
    slots = SLOTS
    total = 2 * lines * slots
    hidden = up.shape[1]
    pieces = (count, up.shape[0] // count, hidden)
    vmem = pl.BlockSpec(memory_space=pltpu.VMEM)
    dma = pltpu.SemaphoreType.DMA
    args = (x, mixer, grad, route, gain, router, up, down)
    low = jnp.bfloat16
    return pl.pallas_call(
        functools.partial(experts_kernel, count, lines, experts),
        in_specs=[vmem] * len(args),
        out_specs=[vmem] * 7,
        out_shape=[
            jax.ShapeDtypeStruct((rows, width), jnp.float32),
            jax.ShapeDtypeStruct((rows, width), jnp.float32),
            jax.ShapeDtypeStruct((rows, width), low),
            jax.ShapeDtypeStruct((8, width), jnp.float32),
            jax.ShapeDtypeStruct(pieces, low),
            jax.ShapeDtypeStruct(pieces, low),
            jax.ShapeDtypeStruct((2, count // 4, *pieces[1:]), low),
        ],
        scratch_shapes=[
            pltpu.VMEM((experts * slots, rows), low),
            pltpu.VMEM((experts, rows, slots), low),
            pltpu.VMEM((rows, width), jnp.float32),
            pltpu.VMEM((rows, width), low),
            pltpu.VMEM((2, experts, slots, width), low),
            pltpu.VMEM((2, 2, lines, slots, width), low),
            pltpu.VMEM((2, 2, lines, slots, width), low),
            pltpu.VMEM((2, 2, lines, slots, width), low),
            pltpu.VMEM((total, hidden), low),
            pltpu.VMEM((total, hidden), low),
            pltpu.VMEM((total, hidden), jnp.float32),
            dma((2, 2, lines)), dma((2, 2, lines)), dma((2, 2, lines)), dma((2, 2, lines)),
            dma((2, count // 4)), dma((2, count // 4)),
        ],
        compiler_params=pltpu.CompilerParams(
            collective_id=4, has_side_effects=True, vmem_limit_bytes=VMEM_LIMIT
        ),
        cost_estimate=pl.CostEstimate(
            flops=12 * total * width * hidden,
            bytes_accessed=8 * width * hidden,
            transcendentals=2 * total * hidden,
        ),
        name="experts",
    )(*args)


def body(
    tokens,
    cotangent,
    routes,
    mixer_gain,
    input_proj,
    conv_weight,
    conv_bias,
    select_proj,
    step_proj,
    step_bias,
    decay_log,
    skip_gain,
    output_proj,
    expert_gain,
    router,
    expert_up,
    expert_down,
):
    rows = tokens.shape[1]
    width = tokens.shape[2]
    shard = input_proj.shape[2]
    rank = step_proj.shape[0]
    state = decay_log.shape[0]
    kernel = conv_weight.shape[0]
    picks = select_proj.shape[0]
    count = lax.axis_size("seq")
    lines = lax.axis_size("dp")
    shard_rows = -(-shard // 16) * 16
    cuts = Cuts(picks, rank, state, kernel)

    x_in = tokens.reshape(rows, width)
    gain_one = mixer_gain.astype(jnp.float32)
    small_pad = -(-cuts.rows // LANES) * LANES
    (normed_all, weights, small_all, conv_ext, conv_sum, conv_act, gate_branch, selected, up_cut) = (
        front(
            count, lines, cuts, shard_rows, small_pad,
            x_in, gain_one[None], input_proj.transpose(0, 2, 1), output_proj, select_proj.T,
            step_proj, decay_log, conv_weight, conv_bias[None], step_bias[None], skip_gain[None],
            expert_up,
        )
    )
    pre, mixed, mixer_low, priors, end, mixer_out, down_cut = scan_forward(
        count, cuts, width, conv_act, gate_branch, selected, small_all, weights, expert_down.T
    )

    experts = router.shape[0]
    (output, grad_middle, grad_middle_low, vectors, grad_up_low, grad_down_low, far_up) = run_experts(
        count,
        lines,
        experts,
        x_in,
        mixer_out,
        cotangent.reshape(rows, width),
        routes.reshape(1, rows),
        expert_gain.astype(jnp.float32)[None],
        router,
        up_cut.reshape(-1, up_cut.shape[2]),
        down_cut.reshape(-1, down_cut.shape[2]),
    )

    (grad_gate_branch, grad_act, grad_step_w, rate_total, scan_rows, grad_selected, grad_middle_all,
     grad_down_t) = (
        scan_backward(
            count, cuts, grad_middle_low, conv_act, gate_branch, mixed, pre, selected, small_all,
            weights, priors, end, grad_down_low,
        )
    )
    (grad_tokens, grad_input, grad_output, grad_select, grad_step, grad_decay, grad_taps,
     grad_conv_bias, grad_step_bias, grad_skip, totals, grad_up) = back(
        count, lines, shard_rows, shard, cuts, grad_selected, small_all, weights, conv_ext, conv_sum,
        grad_act, grad_gate_branch, mixer_low, normed_all.reshape(-1, width),
        grad_middle_all.reshape(-1, width), grad_step_w, rate_total, scan_rows, vectors,
        grad_up_low, far_up, x_in, gain_one[None], grad_middle,
    )
    return (
        output.reshape(tokens.shape),
        grad_tokens.reshape(tokens.shape),
        totals[0] / gain_one,
        grad_input.transpose(0, 2, 1),
        grad_taps,
        grad_conv_bias.reshape(shard),
        grad_select.T,
        grad_step,
        grad_step_bias.reshape(shard),
        grad_decay,
        grad_skip.reshape(shard),
        grad_output,
        totals[1],
        totals[2 : 2 + experts],
        grad_up,
        grad_down_t.T,
    )


def solution(mesh):
    both = ("dp", "seq")
    placed = (
        P("dp", "seq", None),
        P("dp", "seq", None),
        P("dp", "seq", None),
        P(),
        P(None, None, both),
        P(None, both),
        P(both),
        P(None, both),
        P(None, both),
        P(both),
        P(None, both),
        P(both),
        P(both, None),
        P(),
        P(),
        P("seq", "dp"),
        P("dp", "seq"),
    )
    return jax.shard_map(
        body,
        mesh=mesh,
        in_specs=placed,
        out_specs=(
            P("dp", "seq", None),
            P("dp", "seq", None),
            P(),
            P(None, None, both),
            P(None, both),
            P(both),
            P(None, both),
            P(None, both),
            P(both),
            P(None, both),
            P(both),
            P(both, None),
            P(),
            P(),
            P("seq", "dp"),
            P("dp", "seq"),
        ),
        check_vma=False,
    )
```

```python
import functools
import math

import jax
import jax.numpy as jnp
from jax import lax
from jax.experimental import pallas as pl
from jax.experimental.pallas import tpu as pltpu
from jax.sharding import PartitionSpec as P

CAP = 56
LANES = 128
TIME_BLOCK = 128
LOG2E = math.log2(math.e)

HIGHEST = lax.Precision.HIGHEST


def inner_rows(left, right, precision=None):
    return lax.dot_general(
        left,
        right,
        (((0,), (0,)), ((), ())),
        precision=precision,
        preferred_element_type=jnp.float32,
    )


def outer_cols(left, right, precision=None):
    return lax.dot_general(
        left,
        right,
        (((1,), (1,)), ((), ())),
        precision=precision,
        preferred_element_type=jnp.float32,
    )


def sublane_sums(parts):
    row = lax.broadcasted_iota(jnp.int32, parts[0].shape, 0)
    low4 = row < 4
    low2 = (row % 4) < 2
    low1 = (row % 2) < 1
    quads = []
    for k in range(4):
        a, b = parts[k], parts[k + 4]
        quads.append(jnp.where(low4, a, b) + pltpu.roll(jnp.where(low4, b, a), 4, 0))
    pairs = []
    for k in range(2):
        a, b = quads[k], quads[k + 2]
        pairs.append(
            jnp.where(low2, a, b) + jnp.where(low2, pltpu.roll(a, 6, 0), pltpu.roll(b, 2, 0))
        )
    a, b = pairs
    return jnp.where(low1, a, b) + jnp.where(low1, pltpu.roll(a, 7, 0), pltpu.roll(b, 1, 0))


MESH = pl.DeviceIdType.MESH
VMEM_LIMIT = 60 * 1024 * 1024


def dot_nn(left, right, precision=None):
    return lax.dot_general(
        left, right, (((1,), (0,)), ((), ())), precision=precision,
        preferred_element_type=jnp.float32,
    )


def place():
    own, line = lax.axis_index("seq"), lax.axis_index("dp")
    return line, own, own // 2, lax.rem(own, 2)


def remote(source, target, send_sem, recv_sem, line, position):
    return pltpu.make_async_remote_copy(
        src_ref=source,
        dst_ref=target,
        send_sem=send_sem,
        recv_sem=recv_sem,
        device_id=(line, position),
        device_id_type=MESH,
    )


def greet(count, lines=1):
    line, own, _, _ = place()
    barrier = pltpu.get_barrier_semaphore()
    for k in range(1, count):
        pl.semaphore_signal(
            barrier, inc=1, device_id=(line, lax.rem(own + k, count)), device_id_type=MESH
        )
    for k in range(1, lines):
        pl.semaphore_signal(
            barrier, inc=1, device_id=(lax.rem(line + k, lines), own), device_id_type=MESH
        )
    pl.semaphore_wait(barrier, count - 1 + lines - 1)


def sigmoid(values):
    return 1.0 / (1.0 + jnp.exp(-values))


def softplus(values):
    return jnp.maximum(values, 0.0) + jnp.log1p(jnp.exp(-jnp.abs(values)))


class Cuts:
    def __init__(self, picks, rank, state, kernel):
        self.picks, self.rank, self.state, self.kernel = picks, rank, state, kernel
        self.step = picks
        self.decay = self.step + rank
        self.taps = self.decay + state
        self.conv_bias = self.taps + kernel
        self.step_bias = self.conv_bias + 1
        self.skip = self.step_bias + 1
        self.rows = self.skip + 1
        self.sent = -(-picks // 16) * 16


class Relay:
    def __init__(self, axis, half, high, low, seat, block, refs):
        self.axis, self.half, self.high, self.low = axis, half, high, low
        self.seat, self.block = seat, block
        self.other = lax.axis_index("dp" if axis == "seq" else "seq")
        self.part, self.across, self.along = refs[:3]
        self.send_x, self.recv_x, self.send_hi, self.recv_hi = refs[3:]

    def remote(self, source, target, send_sem, recv_sem, position):
        if self.axis == "seq":
            return remote(source, target, send_sem, recv_sem, self.other, position)
        return remote(source, target, send_sem, recv_sem, position, self.other)

    def over(self, i, low):
        return self.remote(
            self.part.at[self.block(i, low)], self.across.at[i], self.send_x.at[i],
            self.recv_x.at[i], self.seat(self.high, 1 - self.low),
        )

    def on(self, i):
        k = lax.rem(i - self.high + self.half, self.half)
        return self.remote(
            self.across.at[i], self.along.at[k], self.send_hi.at[k], self.recv_hi.at[k],
            self.seat(i, self.low),
        )

    def made(self, i, low):
        @pl.when(low != self.low)
        def _():
            self.over(i, low).start()

    def summed(self, i):
        self.over(i, self.low).wait_recv()
        return self.part[self.block(i, self.low)].astype(jnp.float32) + self.across[i].astype(
            jnp.float32
        )

    def pass_on(self, i, low):
        @pl.when((low == self.low) & (i != self.high))
        def _():
            self.across[i] = self.summed(i).astype(jnp.bfloat16)
            self.on(i).start()

    def finish(self, sent=None):
        total = self.summed(self.high)
        for k in range(1, self.half):
            self.on(lax.rem(self.high + k, self.half)).wait_recv()
            total = total + self.along[k].astype(jnp.float32)
        for i in range(self.half) if sent is None else sent:
            self.over(i, 1 - self.low).wait_send()
        for k in range(1, self.half):
            self.on(lax.rem(self.high + k, self.half)).wait_send()
        return total


def whole_relay(axis, count, refs):
    own = lax.axis_index(axis)

    def seat(i, low):
        return 2 * i + low

    return Relay(axis, count // 2, own // 2, lax.rem(own, 2), seat, seat, refs)


def relay_scratch(count, rows, width, part=True):
    half = count // 2
    dma = pltpu.SemaphoreType.DMA
    own = [pltpu.VMEM((count, rows, width), jnp.bfloat16)] if part else []
    return own + [
        pltpu.VMEM((half, rows, width), jnp.bfloat16),
        pltpu.VMEM((half, rows, width), jnp.bfloat16),
        dma((half,)), dma((half,)), dma((half,)), dma((half,)),
    ]


def square():
    own = lax.axis_index("seq")
    return own // 4, lax.rem(own // 2, 2), lax.rem(own, 2)


def seat_of(q, f, low):
    return 4 * q + 2 * f + low


class Gather:
    def __init__(self, count, shard_ref, land_ref, swap_s, swap_r, line_s, line_r, pair_s, pair_r):
        self.line = lax.axis_index("dp")
        self.q, self.f, self.low = square()
        self.quarter = count // 4
        self.shard, self.land = shard_ref, land_ref
        self.swap_s, self.swap_r = swap_s, swap_r
        self.line_s, self.line_r, self.pair_s, self.pair_r = line_s, line_r, pair_s, pair_r
        self.cut = land_ref.shape[2]

    def columns(self, f):
        return pl.ds(pl.multiple_of(f * self.cut, LANES), self.cut)

    def piece(self, j, k, low):
        q = lax.rem(self.q - k + self.quarter, self.quarter)
        return seat_of(q, lax.rem(self.f + j, 2), low)

    def swap(self):
        own = self.piece(0, 0, self.low)
        return remote(
            self.shard.at[:, self.columns(1 - self.f)], self.land.at[own], self.swap_s, self.swap_r,
            self.line, self.piece(1, 0, self.low),
        )

    def along(self, j, k):
        piece = self.piece(j, 0, self.low)
        there = seat_of(lax.rem(self.q + k, self.quarter), self.f, self.low)
        return remote(
            self.land.at[piece], self.land.at[piece], self.line_s.at[j, k], self.line_r.at[j, k],
            self.line, there,
        )

    def pair(self, j, k, low):
        piece = self.piece(j, k, low)
        return remote(
            self.land.at[piece], self.land.at[piece], self.pair_s.at[j, k], self.pair_r.at[j, k],
            self.line, seat_of(self.q, self.f, 1 - self.low),
        )

    def start(self):
        self.swap().start()
        self.land[self.piece(0, 0, self.low)] = self.shard[:, self.columns(self.f)]

    def spread(self, j):
        if j == 1:
            mate = self.piece(1, 0, self.low)
            remote(
                self.land.at[mate], self.land.at[mate], self.swap_s, self.swap_r, self.line, mate
            ).wait_recv()
        for k in range(1, self.quarter):
            self.along(j, k).start()
        self.pair(j, 0, self.low).start()

    def arrive(self):
        for j in range(2):
            for k in range(1, self.quarter):
                piece = self.piece(j, k, self.low)
                remote(
                    self.land.at[piece], self.land.at[piece], self.line_s.at[j, k],
                    self.line_r.at[j, k], self.line, piece,
                ).wait_recv()

    def forward(self, j):
        for k in range(1, self.quarter):
            piece = self.piece(j, k, self.low)
            remote(
                self.land.at[piece], self.land.at[piece], self.line_s.at[j, k],
                self.line_r.at[j, k], self.line, piece,
            ).wait_recv()
            self.pair(j, k, self.low).start()

    def finish(self, passed=True):
        crossed = range(self.quarter) if passed else (0,)
        for j in range(2):
            for k in crossed:
                self.pair(j, k, 1 - self.low).wait_recv()
        self.swap().wait_send()
        for j in range(2):
            for k in range(1, self.quarter):
                self.along(j, k).wait_send()
            for k in crossed:
                self.pair(j, k, self.low).wait_send()


def gather_scratch(count):
    dma = pltpu.SemaphoreType.DMA
    quarter = count // 4
    return [dma, dma] + [dma((2, quarter)) for _ in range(4)]


class Scatter:
    def __init__(self, count, part_ref, far_ref, other_ref, held_ref, swap_s, swap_r, refs):
        self.line = lax.axis_index("dp")
        self.q, self.f, self.low = square()
        self.quarter = count // 4
        self.far, self.other, self.held = far_ref, other_ref, held_ref
        self.swap_s, self.swap_r = swap_s, swap_r
        self.relays = []
        for j in range(2):
            cut = lax.rem(self.f + j, 2)

            def seat(i, low):
                return seat_of(i, self.f, low)

            def block(i, low, cut=cut):
                return seat_of(i, cut, low)

            mine = tuple(ref.at[j] for ref in refs)
            self.relays.append(
                Relay("seq", self.quarter, self.q, self.low, seat, block, (part_ref, *mine))
            )

    def swap(self):
        return remote(
            self.held, self.other, self.swap_s, self.swap_r, self.line,
            seat_of(self.q, 1 - self.f, self.low),
        )

    def far_places(self):
        return [
            (j, lax.rem(self.q + k, self.quarter)) for k in range(1, self.quarter) for j in (1, 0)
        ]

    def send_far(self):
        for j, i in self.far_places():
            self.relays[j].over(i, 1 - self.low).start()

    def pass_far(self):
        for j, i in self.far_places():
            relay = self.relays[j]
            if self.far is None:
                relay.pass_on(i, self.low)
            else:
                both = relay.part[relay.block(i, self.low)].astype(jnp.float32) + self.far[
                    j, i
                ].astype(jnp.float32)
                relay.across[i] = both.astype(jnp.bfloat16)
                relay.on(i).start()

    def total(self, j):
        return self.relays[j].finish(None if self.far is None else [self.q])

    def send_near(self):
        for j in (1, 0):
            self.relays[j].over(self.q, 1 - self.low).start()

    def hand_over(self):
        self.held[...] = self.total(1).astype(jnp.bfloat16)
        self.swap().start()

    def finish(self, out_ref):
        cut = self.held.shape[1]
        out_ref[:, pl.ds(pl.multiple_of(self.f * cut, LANES), cut)] = self.total(0)
        self.swap().wait_recv()
        out_ref[:, pl.ds(pl.multiple_of((1 - self.f) * cut, LANES), cut)] = self.other[...].astype(
            jnp.float32
        )
        self.swap().wait_send()


def scatter_scratch(count, rows, cut):
    dma = pltpu.SemaphoreType.DMA
    quarter = count // 4
    return [
        pltpu.VMEM((rows, cut), jnp.bfloat16),
        pltpu.VMEM((rows, cut), jnp.bfloat16),
        dma, dma,
        pltpu.VMEM((2, quarter, rows, cut), jnp.bfloat16),
        pltpu.VMEM((2, quarter, rows, cut), jnp.bfloat16),
        *[dma((2, quarter)) for _ in range(4)],
    ]


def front_kernel(
    count, lines, cuts,
    x_ref, gain_ref, input_ref, output_ref, select_ref, step_ref, decay_ref, taps_ref, conv_bias_ref,
    step_bias_ref, skip_ref, expert_ref,
    all_ref, weights_ref, small_ref, ext_ref, sum_ref, act_ref, gate_ref, selected_ref, land_ref,
    normed_ref, packed_ref, table_ref, part_ref, partial_ref, total_ref,
    send_w, recv_w, send_up, send_down, recv_hi, send_x, recv_x, send_rs, recv_rs, send_ag, recv_ag,
    *gather_refs,
):
    line, own, high, low = place()
    half = count // 2
    gather = Gather(count, expert_ref, land_ref, *gather_refs)
    rows, width = x_ref.shape
    shard = packed_ref.shape[0]
    inner = weights_ref.shape[0]
    kernel = cuts.kernel
    partner = 2 * high + 1 - low

    own_shard = output_ref.shape[0]
    extra = jnp.zeros((shard - own_shard, width), jnp.float32)

    def padded(values):
        return jnp.concatenate([values.astype(jnp.float32), extra], axis=0).astype(jnp.bfloat16)

    packed_ref[:, :width] = padded(input_ref[0])
    packed_ref[:, width : 2 * width] = padded(input_ref[1])
    packed_ref[:, 2 * width : 3 * width] = padded(output_ref[...])
    table_ref[...] = jnp.zeros_like(table_ref)
    table_ref[:own_shard, : cuts.picks] = select_ref[...].astype(jnp.float32)
    picked = table_ref[:LANES, :].T
    table_ref[...] = jnp.zeros_like(table_ref)
    table_ref[:LANES, :] = picked
    for at, ref in (
        (cuts.step, step_ref),
        (cuts.decay, decay_ref),
        (cuts.taps, taps_ref),
        (cuts.conv_bias, conv_bias_ref),
        (cuts.step_bias, step_bias_ref),
        (cuts.skip, skip_ref),
    ):
        table_ref[at : at + ref.shape[0], :own_shard] = ref[...].astype(jnp.float32)
    packed_ref[:, 3 * width :] = table_ref[...].T[:shard].astype(jnp.bfloat16)
    x = x_ref[...]
    scale = lax.rsqrt(jnp.mean(x * x, axis=1, keepdims=True) + 1e-05)
    normed_ref[...] = (x * scale * gain_ref[...]).astype(jnp.bfloat16)
    greet(count, lines)

    copies = []
    shard_rows = pl.ds(pl.multiple_of(line * shard, 16), shard)
    def step_on(i, up):
        block = 2 * i + low
        return remote(
            all_ref.at[block], all_ref.at[block], (send_up if up else send_down).at[i],
            recv_hi.at[i], line, 2 * (high + (1 if up else -1)) + low,
        )

    def can_go(up):
        return high < half - 1 if up else high > 0

    all_ref[own] = normed_ref[...]
    for up in (True, False):

        @pl.when(can_go(up))
        def _(up=up):
            step_on(high, up).start()

    remote(all_ref.at[own], all_ref.at[own], send_x.at[high], recv_x.at[high], line, partner).start()
    for k in range(1, lines):
        copy = remote(
            packed_ref, weights_ref.at[shard_rows], send_w.at[k], recv_w.at[k],
            lax.rem(line + k, lines), own,
        )
        copy.start()
        copies.append(copy)
    gather.start()
    weights_ref[shard_rows, :] = packed_ref[...]
    if lines * shard < inner:
        weights_ref[lines * shard :, :] = jnp.zeros(
            (inner - lines * shard, weights_ref.shape[1]), weights_ref.dtype
        )
    ext_ref[0:8, :] = jnp.zeros((8, inner), jnp.float32)
    def cross(i):
        block = 2 * i + low
        return remote(
            all_ref.at[block], all_ref.at[block], send_x.at[i], recv_x.at[i], line, partner
        )

    for k in range(1, half):
        for up in (True, False):
            i = high - k if up else high + k

            @pl.when(i >= 0 if up else i < half)
            def _(i=i, up=up):
                step_on(i, up).wait_recv()

                @pl.when(can_go(up))
                def _():
                    step_on(i, up).start()

                cross(i).start()

    gather.spread(0)
    gather.spread(1)
    for k in range(1, lines):
        from_line = lax.rem(line - k + lines, lines)
        there = pl.ds(pl.multiple_of(from_line * shard, 16), shard)
        remote(
            packed_ref, weights_ref.at[there], send_w.at[k], recv_w.at[k], from_line, own
        ).wait_recv()
    small_ref[...] = weights_ref[:, 3 * width :].astype(jnp.float32).T
    for i in range(half):
        block = 2 * i + 1 - low
        remote(
            all_ref.at[block], all_ref.at[block], send_x.at[i], recv_x.at[i], line, partner
        ).wait_recv()

    def project(b, carry):
        start = pl.multiple_of(b * rows, rows)
        block = all_ref[b]
        ext_ref[pl.ds(pl.multiple_of(start + 8, 8), rows), :] = outer_cols(
            block, weights_ref[:, :width]
        )
        gate_ref[pl.ds(start, rows), :] = outer_cols(block, weights_ref[:, width : 2 * width])
        return carry

    lax.fori_loop(0, count, project, 0)

    def convolve(b, carry):
        start = pl.multiple_of(b * rows, rows)
        window = ext_ref[pl.ds(start, rows + 8), :]
        total = small_ref[cuts.conv_bias : cuts.conv_bias + 1, :]
        for k in range(kernel):
            tap = small_ref[cuts.taps + k : cuts.taps + k + 1, :]
            total = total + tap * window[9 - kernel + k : 9 - kernel + k + rows]
        act = total * sigmoid(total)
        sum_ref[pl.ds(start, rows), :] = total
        act_ref[pl.ds(start, rows), :] = act
        part_ref[b] = outer_cols(
            small_ref[: cuts.sent, :].astype(jnp.bfloat16), act.astype(jnp.bfloat16)
        ).astype(jnp.bfloat16)
        return carry

    lax.fori_loop(0, count, convolve, 0)

    for k in range(1, count):
        there = lax.rem(own + k, count)
        copy = remote(
            part_ref.at[there], partial_ref.at[k], send_rs.at[k], recv_rs.at[k], line, there
        )
        copy.start()
        copies.append(copy)
    total = part_ref[own].astype(jnp.float32)
    for k in range(1, count):
        remote(
            part_ref.at[own], partial_ref.at[k], send_rs.at[k], recv_rs.at[k], line, partner
        ).wait_recv()
        total = total + partial_ref[k].astype(jnp.float32)
    total_ref[own] = total.astype(jnp.bfloat16)
    for k in range(1, count):
        copy = remote(
            total_ref.at[own], total_ref.at[own], send_ag.at[k], recv_ag.at[k],
            line, lax.rem(own + k, count),
        )
        copy.start()
        copies.append(copy)
    gather.forward(0)
    gather.forward(1)
    for k in range(1, count):
        block = lax.rem(own - k + count, count)
        remote(
            total_ref.at[block], total_ref.at[block], send_ag.at[k], recv_ag.at[k],
            line, partner,
        ).wait_recv()
    selected_ref[...] = total_ref[...].astype(jnp.float32)[:, : cuts.picks]
    for copy in copies:
        copy.wait_send()
    for i in range(half):
        cross(i).wait_send()
        for up in (True, False):

            @pl.when(can_go(up) & (i <= high if up else i >= high))
            def _(i=i, up=up):
                step_on(i, up).wait_send()

    gather.finish()


def front(count, lines, cuts, shard, small, *args):
    rows, width = args[0].shape
    expert = args[-1]
    columns = 3 * width + small
    inner = -(-lines * shard // LANES) * LANES
    length = count * rows
    half = count // 2
    vmem = pl.BlockSpec(memory_space=pltpu.VMEM)

    def f32(*shape):
        return jax.ShapeDtypeStruct(shape, jnp.float32)

    dma = pltpu.SemaphoreType.DMA
    return pl.pallas_call(
        functools.partial(front_kernel, count, lines, cuts),
        in_specs=[vmem] * len(args),
        out_specs=[vmem] * 9,
        out_shape=[
            jax.ShapeDtypeStruct((count, rows, width), jnp.bfloat16),
            jax.ShapeDtypeStruct((inner, columns), jnp.bfloat16),
            f32(small, inner),
            f32(length + 8, inner),
            f32(length, inner),
            f32(length, inner),
            f32(length, inner),
            f32(count, cuts.picks, rows),
            jax.ShapeDtypeStruct((count, expert.shape[0], expert.shape[1] // 2), jnp.bfloat16),
        ],
        scratch_shapes=[
            pltpu.VMEM((rows, width), jnp.bfloat16),
            pltpu.VMEM((shard, columns), jnp.bfloat16),
            pltpu.VMEM((small, LANES), jnp.float32),
            *[pltpu.VMEM((count, cuts.sent, rows), jnp.bfloat16)] * 3,
            dma((lines,)), dma((lines,)), dma((half,)), dma((half,)), dma((half,)), dma((half,)),
            dma((half,)), dma((count,)), dma((count,)), dma((count,)), dma((count,)),
            *gather_scratch(count),
        ],
        compiler_params=pltpu.CompilerParams(
            collective_id=0, has_side_effects=True, vmem_limit_bytes=VMEM_LIMIT
        ),
        cost_estimate=pl.CostEstimate(
            flops=4 * length * width * inner,
            bytes_accessed=20 * length * inner,
            transcendentals=length * inner,
        ),
        name="front",
    )(*args)


def spread_lanes(values, wide_ref, out_ref):
    state, steps = values.shape
    high = values.astype(jnp.bfloat16).astype(jnp.float32)
    rest = values - high
    lane = lax.broadcasted_iota(jnp.int32, (state, steps), 1)

    def fill(g, carry):
        for k in range(8):
            t = g * 8 + k
            here = pl.ds(pl.multiple_of(t * state, state), state)
            mask = lane == t
            wide_ref[here, :steps] = jnp.where(mask, high, 0.0).astype(jnp.bfloat16)
            wide_ref[here, steps:] = jnp.where(mask, rest, 0.0).astype(jnp.bfloat16)
        return carry

    lax.fori_loop(0, steps // 8, fill, 0)
    ones = jnp.ones((2 * steps, LANES), jnp.bfloat16)
    out_ref[...] = dot_nn(wide_ref[...], ones)


def scan_forward_kernel(
    count, cuts,
    act_ref, gate_ref, selected_ref, small_ref, output_ref, expert_ref,
    pre_ref, mixed_ref, mixer_low_ref, prior_ref, end_ref, summed_ref, expert_out_ref,
    state_ref, delta_ref, scanned_ref, wide_ref, wide_in_ref, wide_out_ref, land_ref, *refs,
):
    steps, inner = act_ref.shape
    tiles = inner // LANES
    state = cuts.state
    halves = state // 8
    step = pl.program_id(0)
    relay = whole_relay("seq", count, refs[:7])
    gather = Gather(count, expert_ref, land_ref, *refs[7:])

    @pl.when(step == 0)
    def _():
        greet(count)
        gather.start()
        state_ref[...] = jnp.zeros_like(state_ref)

    @pl.when(step == 0)
    def _():
        gather.spread(0)

    @pl.when(step == 3)
    def _():
        gather.spread(1)

    rates2 = -LOG2E * jnp.exp(small_ref[cuts.decay : cuts.decay + state, :])
    pre = inner_rows(
        selected_ref[0, : cuts.rank, :],
        small_ref[cuts.step : cuts.step + cuts.rank, :],
        HIGHEST,
    ) + small_ref[cuts.step_bias : cuts.step_bias + 1, :]
    pre_ref[...] = pre
    delta_ref[...] = softplus(pre)
    in_rows = cuts.rank
    out_rows = cuts.rank + state
    spread_lanes(selected_ref[0, in_rows : in_rows + state, :], wide_ref, wide_in_ref)
    spread_lanes(selected_ref[0, out_rows : out_rows + state, :], wide_ref, wide_out_ref)

    def group(g, states):
        states = [list(s) for s in states]
        base = pl.multiple_of(g * 8, 8)
        d8 = delta_ref[pl.ds(base, 8), :]
        du8 = d8 * act_ref[pl.ds(base, 8), :]
        parts = [[None] * 8 for _ in range(tiles)]
        for k in range(8):
            rows_now = [pl.ds((base + k) * state + 8 * i, 8) for i in range(halves)]
            b_now = [wide_in_ref[here, :] for here in rows_now]
            c_now = [wide_out_ref[here, :] for here in rows_now]
            for j in range(tiles):
                cols = slice(j * LANES, (j + 1) * LANES)
                d = jnp.broadcast_to(d8[k : k + 1, cols], (8, LANES))
                du = jnp.broadcast_to(du8[k : k + 1, cols], (8, LANES))
                total = None
                for i in range(halves):
                    old = states[j][i]
                    prior_ref[base + k, 8 * i : 8 * i + 8, cols] = old
                    new = jnp.exp2(d * rates2[8 * i : 8 * i + 8, cols]) * old + b_now[i] * du
                    states[j][i] = new
                    term = c_now[i] * new
                    total = term if total is None else total + term
                parts[j][k] = total
        for j in range(tiles):
            scanned_ref[pl.ds(base, 8), j * LANES : (j + 1) * LANES] = sublane_sums(parts[j])
        return tuple(tuple(s) for s in states)

    first = tuple(
        tuple(
            state_ref[8 * i : 8 * i + 8, j * LANES : (j + 1) * LANES] for i in range(halves)
        )
        for j in range(tiles)
    )
    last = lax.fori_loop(0, steps // 8, group, first)
    for j in range(tiles):
        for i in range(halves):
            state_ref[8 * i : 8 * i + 8, j * LANES : (j + 1) * LANES] = last[j][i]
    end_ref[...] = state_ref[...]

    mixed = scanned_ref[...] + small_ref[cuts.skip : cuts.skip + 1, :] * act_ref[...]
    gate = gate_ref[...]
    low = (mixed * (gate * sigmoid(gate))).astype(jnp.bfloat16)
    mixed_ref[...] = mixed
    mixer_low_ref[...] = low
    relay.part[step] = dot_nn(low, output_ref[...]).astype(jnp.bfloat16)
    relay.made(step // 2, lax.rem(step, 2))

    def pass_on(block):
        relay.pass_on(block // 2, lax.rem(block, 2))

    @pl.when(step >= LAG)
    def _():
        pass_on(step - LAG)

    @pl.when(step == count - 1)
    def _():
        for late in range(LAG - 1, -1, -1):
            pass_on(step - late)
        gather.arrive()
        summed_ref[...] = relay.finish()
        gather.finish(False)
        expert_out_ref[...] = land_ref[...]


def scan_forward(count, cuts, width, act, gate, selected, small, weights, expert):
    length, inner = act.shape
    state = cuts.state
    block = length // count
    rows = pl.BlockSpec((block, inner), lambda t: (t, 0))
    whole = pl.BlockSpec((state, inner), lambda t: (0, 0))
    pieces = (count, expert.shape[0], expert.shape[1] // 2)
    return pl.pallas_call(
        functools.partial(scan_forward_kernel, count, cuts),
        grid=(count,),
        in_specs=[
            rows,
            rows,
            pl.BlockSpec((1, cuts.picks, block), lambda t: (t, 0, 0)),
            pl.BlockSpec(small.shape, lambda t: (0, 0)),
            pl.BlockSpec((inner, width), lambda t: (0, 2)),
            pl.BlockSpec(expert.shape, lambda t: (0, 0)),
        ],
        out_specs=[
            rows,
            rows,
            rows,
            pl.BlockSpec((block, state, inner), lambda t: (t, 0, 0)),
            whole,
            pl.BlockSpec((block, width), lambda t: (0, 0)),
            pl.BlockSpec(pieces, lambda t: (0, 0, 0)),
        ],
        out_shape=[
            jax.ShapeDtypeStruct((length, inner), jnp.float32),
            jax.ShapeDtypeStruct((length, inner), jnp.float32),
            jax.ShapeDtypeStruct((length, inner), jnp.bfloat16),
            jax.ShapeDtypeStruct((length, state, inner), jnp.float32),
            jax.ShapeDtypeStruct((state, inner), jnp.float32),
            jax.ShapeDtypeStruct((block, width), jnp.float32),
            jax.ShapeDtypeStruct(pieces, jnp.bfloat16),
        ],
        scratch_shapes=[
            pltpu.VMEM((state, inner), jnp.float32),
            pltpu.VMEM((block, inner), jnp.float32),
            pltpu.VMEM((block, inner), jnp.float32),
            pltpu.VMEM((block * state, 2 * block), jnp.bfloat16),
            pltpu.VMEM((block * state, LANES), jnp.float32),
            pltpu.VMEM((block * state, LANES), jnp.float32),
            pltpu.VMEM(pieces, jnp.bfloat16),
            *relay_scratch(count, block, width),
            *gather_scratch(count),
        ],
        compiler_params=pltpu.CompilerParams(
            collective_id=1, has_side_effects=True, vmem_limit_bytes=VMEM_LIMIT
        ),
        cost_estimate=pl.CostEstimate(
            flops=8 * length * state * inner,
            bytes_accessed=4 * length * inner * (state + 6),
            transcendentals=length * state * inner,
        ),
        name="scan_forward",
    )(act, gate, selected, small, weights, expert)


def scan_backward_kernel(
    count, cuts,
    own_ref, act_ref, gate_ref, mixed_ref, pre_ref, selected_ref, small_ref, output_ref,
    prior_ref, end_ref, expert_ref,
    grad_gate_ref, grad_act_ref, grad_step_ref, rate_total_ref, rows_ref, grad_selected_ref,
    all_out_ref, expert_out_ref,
    incoming_ref, post_ref, delta_ref, grad_ref, grad_delta_ref, wide_ref, wide_in_ref,
    wide_out_ref, all_ref,
    stage_ref, part_ref, partial_ref, total_ref,
    send_hi, recv_hi, send_x, recv_x, send_rs, recv_rs, send_ag, recv_ag,
    other_ref, held_ref, swap_s, swap_r, *scatter_refs,
):
    steps, inner = act_ref.shape
    tiles = inner // LANES
    state = cuts.state
    halves = state // 8
    lane = lax.broadcasted_iota(jnp.int32, (8, steps), 1)
    line, own, high, low = place()
    half = count // 2
    partner = 2 * high + 1 - low
    index = pl.program_id(0)
    now = count - 1 - index
    scatter = Scatter(
        count, expert_ref, None, other_ref, held_ref, swap_s, swap_r, scatter_refs
    )

    def along(k):
        return remote(
            own_ref, all_ref.at[own], send_hi.at[k], recv_hi.at[high], line,
            2 * lax.rem(high + k, half) + low,
        )

    def across(block):
        i = block // 2
        return remote(
            all_ref.at[block], all_ref.at[block], send_x.at[i], recv_x.at[i], line, partner
        )

    def came_along(block):
        i = block // 2
        return remote(
            all_ref.at[block], all_ref.at[block], send_hi.at[0], recv_hi.at[i], line, partner
        )

    def hand_over(block):
        @pl.when((lax.rem(block, 2) == low) & (block // 2 != high))
        def _():
            came_along(block).wait_recv()
            across(block).start()

    @pl.when(index == 0)
    def _():
        greet(count)
        all_ref[own] = own_ref[...]
        incoming_ref[...] = jnp.zeros_like(incoming_ref)
        post_ref[...] = end_ref[...]
        rate_total_ref[...] = jnp.zeros_like(rate_total_ref)
        grad_step_ref[...] = jnp.zeros_like(grad_step_ref)
        rows_ref[...] = jnp.zeros_like(rows_ref)
        stage_ref[...] = jnp.zeros_like(stage_ref)

    @pl.when(index == 0)
    def _():
        for k in range(1, half):
            along(k).start()
        across(own).start()

    @pl.when(index == 0)
    def _():
        hand_over(now - 0)
        hand_over(now - 1)

    @pl.when(lax.rem(now, 2) != low)
    def _():
        across(now).wait_recv()

    gate = gate_ref[...]
    gate_sig = sigmoid(gate)
    grad_y = outer_cols(all_ref[now], output_ref[...])
    grad_gate_ref[...] = (
        grad_y * mixed_ref[...] * (gate_sig * (1.0 + gate * (1.0 - gate_sig)))
    ).astype(jnp.bfloat16)
    grad_mixed = grad_y * (gate * gate_sig)
    grad_ref[...] = grad_mixed
    delta_ref[...] = softplus(pre_ref[...])
    rows_ref[1:2, :] += jnp.sum(grad_mixed * act_ref[...], axis=0, keepdims=True)
    rates2 = -LOG2E * jnp.exp(small_ref[cuts.decay : cuts.decay + state, :])
    in_rows = cuts.rank
    out_rows = cuts.rank + state
    spread_lanes(selected_ref[0, in_rows : in_rows + state, :], wide_ref, wide_in_ref)
    spread_lanes(selected_ref[0, out_rows : out_rows + state, :], wide_ref, wide_out_ref)

    def tile_of(ref):
        return tuple(
            tuple(ref[8 * i : 8 * i + 8, j * LANES : (j + 1) * LANES] for i in range(halves))
            for j in range(tiles)
        )

    def group(turn, carry):
        incoming, posts, rate_total, in_acc, out_acc = carry
        incoming = [list(s) for s in incoming]
        posts = [list(s) for s in posts]
        rate_total = [list(s) for s in rate_total]
        in_acc, out_acc = list(in_acc), list(out_acc)
        base = pl.multiple_of((steps // 8 - 1 - turn) * 8, 8)
        d8 = delta_ref[pl.ds(base, 8), :]
        u8 = act_ref[pl.ds(base, 8), :]
        du8 = d8 * u8
        g8 = grad_ref[pl.ds(base, 8), :]
        rate_parts = [[None] * 8 for _ in range(tiles)]
        side_parts = [[None] * 8 for _ in range(tiles)]
        for k in range(7, -1, -1):
            rows_now = [pl.ds((base + k) * state + 8 * i, 8) for i in range(halves)]
            b_now = [wide_in_ref[here, :] for here in rows_now]
            c_now = [wide_out_ref[here, :] for here in rows_now]
            in_sum = [None] * halves
            out_sum = [None] * halves
            for j in range(tiles):
                cols = slice(j * LANES, (j + 1) * LANES)
                d = jnp.broadcast_to(d8[k : k + 1, cols], (8, LANES))
                du = jnp.broadcast_to(du8[k : k + 1, cols], (8, LANES))
                gm = jnp.broadcast_to(g8[k : k + 1, cols], (8, LANES))
                rate_part = None
                side_part = None
                for i in range(halves):
                    prior = prior_ref[base + k, 8 * i : 8 * i + 8, cols]
                    rates = rates2[8 * i : 8 * i + 8, cols]
                    grad_state = c_now[i] * gm + incoming[j][i]
                    passed = jnp.exp2(d * rates) * grad_state
                    incoming[j][i] = passed
                    weighted = passed * prior
                    term = weighted * rates
                    rate_part = term if rate_part is None else rate_part + term
                    term = grad_state * b_now[i]
                    side_part = term if side_part is None else side_part + term
                    term = grad_state * du
                    in_sum[i] = term if in_sum[i] is None else in_sum[i] + term
                    term = posts[j][i] * gm
                    out_sum[i] = term if out_sum[i] is None else out_sum[i] + term
                    rate_total[j][i] = rate_total[j][i] + weighted * d
                    posts[j][i] = prior
                rate_parts[j][k] = rate_part
                side_parts[j][k] = side_part
            here = lane == base + k
            for i in range(halves):
                in_acc[i] = jnp.where(here, jnp.sum(in_sum[i], axis=1, keepdims=True), in_acc[i])
                out_acc[i] = jnp.where(here, jnp.sum(out_sum[i], axis=1, keepdims=True), out_acc[i])
        for j in range(tiles):
            cols = slice(j * LANES, (j + 1) * LANES)
            side = sublane_sums(side_parts[j])
            grad_delta_ref[pl.ds(base, 8), cols] = (
                sublane_sums(rate_parts[j]) * (1.0 / LOG2E) + u8[:, cols] * side
            )
            grad_act_ref[pl.ds(base, 8), cols] = d8[:, cols] * side
        return (
            tuple(tuple(s) for s in incoming),
            tuple(tuple(s) for s in posts),
            tuple(tuple(s) for s in rate_total),
            tuple(in_acc),
            tuple(out_acc),
        )

    empty = tuple(jnp.zeros((8, steps), jnp.float32) for _ in range(halves))
    incoming, posts, rate_total, in_acc, out_acc = lax.fori_loop(
        0,
        steps // 8,
        group,
        (tile_of(incoming_ref), tile_of(post_ref), tile_of(rate_total_ref), empty, empty),
    )
    for i in range(halves):
        stage_ref[in_rows + 8 * i : in_rows + 8 * i + 8, :] = in_acc[i]
        stage_ref[out_rows + 8 * i : out_rows + 8 * i + 8, :] = out_acc[i]
        for j in range(tiles):
            cols = slice(j * LANES, (j + 1) * LANES)
            incoming_ref[8 * i : 8 * i + 8, cols] = incoming[j][i]
            post_ref[8 * i : 8 * i + 8, cols] = posts[j][i]
            rate_total_ref[8 * i : 8 * i + 8, cols] = rate_total[j][i]

    grad_act_ref[...] += grad_ref[...] * small_ref[cuts.skip : cuts.skip + 1, :]
    grad_pre = grad_delta_ref[...] * sigmoid(pre_ref[...])
    rows_ref[0:1, :] += jnp.sum(grad_pre, axis=0, keepdims=True)
    grad_step_ref[...] += dot_nn(selected_ref[0, : cuts.rank, :], grad_pre, HIGHEST)
    stage_ref[: cuts.rank, :] = outer_cols(
        small_ref[cuts.step : cuts.step + cuts.rank, :], grad_pre, HIGHEST
    )
    part_ref[now] = stage_ref[...].astype(jnp.bfloat16)

    def partial_to(block):
        return remote(
            part_ref.at[block], partial_ref.at[own], send_rs.at[block], recv_rs.at[own], line, block
        )

    @pl.when(now != own)
    def _():
        partial_to(now).start()

    def total_to(k):
        return remote(
            total_ref.at[own], total_ref.at[own], send_ag.at[k], recv_ag.at[own], line,
            lax.rem(own + k, count),
        )

    @pl.when(now >= 2)
    def _():
        hand_over(now - 2)

    @pl.when(index == NEAR_AT)
    def _():
        scatter.send_near()

    @pl.when(index == FAR_AT)
    def _():
        scatter.send_far()

    @pl.when(index == PASS_AT)
    def _():
        scatter.pass_far()

    @pl.when(index == count - 1)
    def _():
        scatter.hand_over()

    @pl.when(index == jnp.minimum(count - 1 - own + 2, count - 1))
    def _():
        total = part_ref[own].astype(jnp.float32)
        for k in range(1, count):
            there = lax.rem(own + k, count)
            remote(
                part_ref.at[own], partial_ref.at[there], send_rs.at[own], recv_rs.at[there],
                line, there,
            ).wait_recv()
            total = total + partial_ref[there].astype(jnp.float32)
        total_ref[own] = total.astype(jnp.bfloat16)
        for k in range(1, count):
            total_to(k).start()

    @pl.when(index == count - 1)
    def _():
        for k in range(1, count):
            there = lax.rem(own + k, count)
            remote(
                total_ref.at[there], total_ref.at[there], send_ag.at[k], recv_ag.at[there],
                line, there,
            ).wait_recv()
        grad_selected_ref[...] = total_ref[...]
        all_out_ref[...] = all_ref[...]
        for k in range(1, half):
            along(k).wait_send()
        for i in range(half):
            across(2 * i + low).wait_send()
        for k in range(1, count):
            partial_to(lax.rem(own + k, count)).wait_send()
            total_to(k).wait_send()
        scatter.finish(expert_out_ref)


def scan_backward(
    count, cuts, grad_low, act, gate, mixed, pre, selected, small, weights, priors, end, expert
):
    length, inner = act.shape
    state = cuts.state
    block = length // count
    width = grad_low.shape[1]
    half = count // 2

    def back(t):
        return count - 1 - t

    rows = pl.BlockSpec((block, inner), lambda t: (back(t), 0))
    whole = pl.BlockSpec((state, inner), lambda t: (0, 0))
    dma = pltpu.SemaphoreType.DMA
    picked = (count, cuts.sent, block)
    return pl.pallas_call(
        functools.partial(scan_backward_kernel, count, cuts),
        grid=(count,),
        in_specs=[
            pl.BlockSpec((block, width), lambda t: (0, 0)),
            rows,
            rows,
            rows,
            rows,
            pl.BlockSpec((1, cuts.picks, block), lambda t: (back(t), 0, 0)),
            pl.BlockSpec(small.shape, lambda t: (0, 0)),
            pl.BlockSpec((inner, width), lambda t: (0, 2)),
            pl.BlockSpec((block, state, inner), lambda t: (back(t), 0, 0)),
            whole,
            pl.BlockSpec(expert.shape, lambda t: (0, 0, 0)),
        ],
        out_specs=[
            rows,
            rows,
            pl.BlockSpec((cuts.rank, inner), lambda t: (0, 0)),
            whole,
            pl.BlockSpec((8, inner), lambda t: (0, 0)),
            pl.BlockSpec(picked, lambda t: (0, 0, 0)),
            pl.BlockSpec((count, block, width), lambda t: (0, 0, 0)),
            pl.BlockSpec((expert.shape[1], 2 * expert.shape[2]), lambda t: (0, 0)),
        ],
        out_shape=[
            jax.ShapeDtypeStruct((length, inner), jnp.bfloat16),
            jax.ShapeDtypeStruct((length, inner), jnp.float32),
            jax.ShapeDtypeStruct((cuts.rank, inner), jnp.float32),
            jax.ShapeDtypeStruct((state, inner), jnp.float32),
            jax.ShapeDtypeStruct((8, inner), jnp.float32),
            jax.ShapeDtypeStruct(picked, jnp.bfloat16),
            jax.ShapeDtypeStruct((count, block, width), jnp.bfloat16),
            jax.ShapeDtypeStruct((expert.shape[1], 2 * expert.shape[2]), jnp.float32),
        ],
        scratch_shapes=[
            pltpu.VMEM((state, inner), jnp.float32),
            pltpu.VMEM((state, inner), jnp.float32),
            pltpu.VMEM((block, inner), jnp.float32),
            pltpu.VMEM((block, inner), jnp.float32),
            pltpu.VMEM((block, inner), jnp.float32),
            pltpu.VMEM((block * state, 2 * block), jnp.bfloat16),
            pltpu.VMEM((block * state, LANES), jnp.float32),
            pltpu.VMEM((block * state, LANES), jnp.float32),
            pltpu.VMEM((count, block, width), jnp.bfloat16),
            pltpu.VMEM(picked[1:], jnp.float32),
            *[pltpu.VMEM(picked, jnp.bfloat16)] * 3,
            dma((half,)), dma((half,)), dma((half,)), dma((half,)),
            dma((count,)), dma((count,)), dma((count,)), dma((count,)),
            *scatter_scratch(count, expert.shape[1], expert.shape[2]),
        ],
        compiler_params=pltpu.CompilerParams(
            collective_id=2, has_side_effects=True, vmem_limit_bytes=VMEM_LIMIT
        ),
        cost_estimate=pl.CostEstimate(
            flops=20 * length * state * inner,
            bytes_accessed=4 * length * inner * (state + 6),
            transcendentals=length * state * inner,
        ),
        name="scan_backward",
    )(grad_low, act, gate, mixed, pre, selected, small, weights, priors, end, expert)


def back_kernel(
    count, lines, cuts,
    grad_selected_ref, small_ref, weights_ref, ext_ref, sum_ref, grad_act_ref, grad_gate_ref,
    mixer_low_ref, normed_ref, grad_middle_ref, grad_step_ref, rate_total_ref, scan_rows_ref,
    vectors_ref, expert_ref, far_ref, x_ref, gain_ref, kept_ref,
    tokens_ref, input_ref, output_ref, select_ref, step_ref, decay_ref, taps_ref, conv_bias_ref,
    step_bias_ref, skip_ref, totals_ref, expert_out_ref,
    grad_sum_ref, grad_conv_ref, grad_small_ref, ours_ref, theirs_ref,
    send_v, recv_v, send_u, recv_u, other_ref, held_ref, swap_s, swap_r, *refs,
):
    scatter = Scatter(count, expert_ref, far_ref, other_ref, held_ref, swap_s, swap_r, refs[:6])
    relay = whole_relay("seq", count, refs[6:13])
    spread = whole_relay("dp", lines, refs[13:])
    line, own, _, _ = place()
    length, inner = sum_ref.shape
    width = normed_ref.shape[1]
    rows = length // count
    kernel = cuts.kernel
    shard = spread.part.shape[1]
    own_shard = output_ref.shape[0]
    greet(count, lines)
    scatter.pass_far()
    scatter.send_near()
    grad_small_ref[...] = jnp.zeros_like(grad_small_ref)
    grad_sum_ref[length:, :] = jnp.zeros((8, inner), jnp.float32)
    select = small_ref[: cuts.sent, :].astype(jnp.bfloat16)

    def first(b, carry):
        start = pl.multiple_of(b * rows, rows)
        grad_selected = grad_selected_ref[b]
        total = sum_ref[pl.ds(start, rows), :]
        sig = sigmoid(total)
        grad_act = grad_act_ref[pl.ds(start, rows), :] + inner_rows(grad_selected, select)
        grad_sum = grad_act * (sig * (1.0 + total * (1.0 - sig)))
        grad_sum_ref[pl.ds(start, rows), :] = grad_sum
        grad_small_ref[: cuts.sent, :] += dot_nn(
            grad_selected, (total * sig).astype(jnp.bfloat16)
        )
        window = ext_ref[pl.ds(start, rows + 8), :]
        for k in range(kernel):
            row = slice(cuts.taps + k, cuts.taps + k + 1)
            grad_small_ref[row, :] += jnp.sum(
                grad_sum * window[9 - kernel + k : 9 - kernel + k + rows], axis=0, keepdims=True
            )
        row = slice(cuts.conv_bias, cuts.conv_bias + 1)
        grad_small_ref[row, :] += jnp.sum(grad_sum, axis=0, keepdims=True)
        return carry

    lax.fori_loop(0, count, first, 0)

    def order(j):
        return j // 2 + lax.rem(j, 2) * (count // 2)

    def second(j, carry):
        b = order(j)
        start = pl.multiple_of(b * rows, rows)
        window = grad_sum_ref[pl.ds(start, rows + 8), :]
        grad_conv = None
        for k in range(kernel):
            tap = small_ref[cuts.taps + k : cuts.taps + k + 1, :]
            term = tap * window[kernel - 1 - k : kernel - 1 - k + rows]
            grad_conv = term if grad_conv is None else grad_conv + term
        grad_conv = grad_conv.astype(jnp.bfloat16)
        grad_conv_ref[pl.ds(start, rows), :] = grad_conv
        relay.part[b] = (
            dot_nn(grad_conv, weights_ref[:, :width])
            + dot_nn(grad_gate_ref[pl.ds(start, rows), :], weights_ref[:, width : 2 * width])
        ).astype(jnp.bfloat16)
        relay.made(b // 2, lax.rem(b, 2))
        return carry

    lax.fori_loop(0, count, second, 0)

    decay = slice(cuts.decay, cuts.decay + cuts.state)
    grad_small_ref[cuts.step : cuts.step + cuts.rank, :] = grad_step_ref[...]
    grad_small_ref[decay, :] = -rate_total_ref[...] * jnp.exp(small_ref[decay, :])
    grad_small_ref[cuts.step_bias : cuts.step_bias + 2, :] = scan_rows_ref[0:2, :]
    small_t = grad_small_ref[...].T
    for d in range(lines):
        spread.part[d, :, 3 * width :] = small_t[d * shard : (d + 1) * shard].astype(jnp.bfloat16)
    chunk = width // 3

    def pass_on(j, carry):
        b = order(j)
        relay.pass_on(b // 2, lax.rem(b, 2))
        return carry

    ours_ref[...] = vectors_ref[...]
    for left_ref, right_ref, place_at in (
        (mixer_low_ref, grad_middle_ref, 2 * width),
        (grad_conv_ref, normed_ref, 0),
        (grad_gate_ref, normed_ref, width),
    ):

        def columns(c, carry, left_ref=left_ref, right_ref=right_ref, place_at=place_at):
            here = pl.ds(pl.multiple_of(c * chunk, chunk), chunk)
            there = pl.ds(pl.multiple_of(place_at + c * chunk, chunk), chunk)
            grad = inner_rows(left_ref[...], right_ref[:, here])
            if place_at < 2 * width:
                ours_ref[0:1, here] += jnp.sum(
                    weights_ref[:, there].astype(jnp.float32) * grad, axis=0, keepdims=True
                )
            low = grad.astype(jnp.bfloat16)
            for d in range(lines):
                spread.part[d, :, there] = low[d * shard : (d + 1) * shard]
            return carry

        lax.fori_loop(0, 3, columns, 0)
        if place_at == 2 * width:
            lax.fori_loop(0, count, pass_on, 0)
    for d in range(lines):
        spread.made(d // 2, d % 2)
    scatter.hand_over()

    def sum_over(size, axis, send, recv):
        here = own if axis == "seq" else line

        def copy(k, slot):
            there = lax.rem(here + k, size)
            target = (line, there) if axis == "seq" else (there, own)
            return remote(ours_ref, theirs_ref.at[slot], send.at[k], recv.at[k], *target)

        base = 0 if axis == "seq" else count
        for k in range(1, size):
            copy(k, base + k).start()
        total = ours_ref[...]
        for k in range(1, size):
            copy(k, base + k).wait_recv()
            total = total + theirs_ref[base + k]
        for k in range(1, size):
            copy(k, base + k).wait_send()
        return total

    ours_ref[...] = sum_over(count, "seq", send_v, recv_v)
    for d in range(lines):
        spread.pass_on(d // 2, d % 2)
    totals_ref[...] = sum_over(lines, "dp", send_u, recv_u)
    x = x_ref[...]
    scale = lax.rsqrt(jnp.mean(x * x, axis=1, keepdims=True) + 1e-05)
    scaled = gain_ref[...] * relay.finish()
    tokens_ref[...] = (
        kept_ref[...]
        + scale * scaled
        - x * (scale * scale * scale) * jnp.mean(scaled * x, axis=1, keepdims=True)
    )
    total = spread.finish()
    input_ref[0] = total[:own_shard, :width]
    input_ref[1] = total[:own_shard, width : 2 * width]
    output_ref[...] = total[:own_shard, 2 * width : 3 * width]
    small = total[:, 3 * width :]
    select_ref[...] = small[:own_shard, : cuts.picks]
    small = jnp.concatenate(
        [small, jnp.zeros((LANES - shard, small.shape[1]), jnp.float32)], axis=0
    ).T
    for at, ref in (
        (cuts.step, step_ref),
        (cuts.decay, decay_ref),
        (cuts.taps, taps_ref),
        (cuts.conv_bias, conv_bias_ref),
        (cuts.step_bias, step_bias_ref),
        (cuts.skip, skip_ref),
    ):
        ref[...] = small[at : at + ref.shape[0], :own_shard]
    scatter.finish(expert_out_ref)


def back(
    count, lines, shard, own_shard, cuts, grad_selected, small, weights, ext, conv_sum, grad_act, grad_gate,
    mixer_low, normed, grad_middle, grad_step, rate_total, scan_rows, vectors, expert, far,
    x, gain, kept,
):
    length, inner = conv_sum.shape
    width = normed.shape[1]
    columns = weights.shape[1]
    rows = length // count
    vmem = pl.BlockSpec(memory_space=pltpu.VMEM)
    dma = pltpu.SemaphoreType.DMA
    args = (
        grad_selected, small, weights, ext, conv_sum, grad_act, grad_gate, mixer_low, normed,
        grad_middle, grad_step, rate_total, scan_rows, vectors, expert, far, x, gain, kept,
    )
    return pl.pallas_call(
        functools.partial(back_kernel, count, lines, cuts),
        in_specs=[vmem] * len(args),
        out_specs=[vmem] * 12,
        out_shape=[
            *[
                jax.ShapeDtypeStruct(shape, jnp.float32)
                for shape in (
                    (rows, width),
                    (2, own_shard, width),
                    (own_shard, width),
                    (own_shard, cuts.picks),
                    (cuts.rank, own_shard),
                    (cuts.state, own_shard),
                    (cuts.kernel, own_shard),
                    (1, own_shard),
                    (1, own_shard),
                    (1, own_shard),
                    vectors.shape,
                )
            ],
            jax.ShapeDtypeStruct((expert.shape[1], 2 * expert.shape[2]), jnp.float32),
        ],
        scratch_shapes=[
            pltpu.VMEM((length + 8, inner), jnp.float32),
            pltpu.VMEM((length, inner), jnp.bfloat16),
            pltpu.VMEM(small.shape, jnp.float32),
            pltpu.VMEM(vectors.shape, jnp.float32),
            pltpu.VMEM((count + lines, *vectors.shape), jnp.float32),
            dma((count,)), dma((count,)), dma((lines,)), dma((lines,)),
            *scatter_scratch(count, expert.shape[1], expert.shape[2]),
            *relay_scratch(count, rows, width),
            *relay_scratch(lines, shard, columns),
        ],
        compiler_params=pltpu.CompilerParams(
            collective_id=3, has_side_effects=True, vmem_limit_bytes=VMEM_LIMIT
        ),
        cost_estimate=pl.CostEstimate(
            flops=10 * length * width * inner,
            bytes_accessed=30 * length * inner,
            transcendentals=length * inner,
        ),
        name="back",
    )(*args)


LAG = 3
FAR_AT = 0
NEAR_AT = 2
PASS_AT = 4
SLOTS = 64


def gauss(values):
    return 0.5 * (1.0 + lax.erf(values * math.sqrt(0.5)))


def split_low(values):
    high = values.astype(jnp.bfloat16)
    return high, (values - high.astype(jnp.float32)).astype(jnp.bfloat16)


def experts_kernel(
    count, lines, experts,
    x_ref, mixer_ref, grad_ref, route_ref, gain_ref, router_ref,
    up_ref, held_ref,
    output_ref, grad_middle_ref, grad_low_ref, vectors_ref, grad_up_ref, grad_down_ref, far_up_ref,
    table_ref, back_table_ref, down_ref, middle_ref, normed_ref, send_ref, rows_ref, made_ref, got_ref, act_ref, slope_ref, pre_ref,
    send_sem, recv_sem, home_s, home_r, far_s, far_r,
    pass_s, pass_r,
):
    line, own, _, _ = place()
    q, f, low = square()
    mate = seat_of(q, 1 - f, low)
    copies = lines // experts
    barrier = pltpu.get_barrier_semaphore()
    for d in range(1, lines):
        for where in (own, mate):
            pl.semaphore_signal(
                barrier, inc=1, device_id=(lax.rem(line + d, lines), where), device_id_type=MESH
            )
    partner = seat_of(q, f, 1 - low)
    for where in (mate, partner):
        pl.semaphore_signal(barrier, inc=1, device_id=(line, where), device_id_type=MESH)
    pl.semaphore_wait(barrier, 2 * lines)

    quarter = count // 4
    piece_rows = held_ref.shape[0] // count

    def piece(j, k, member):
        at = seat_of(lax.rem(q - k + quarter, quarter), lax.rem(f + j, 2), member)
        return pl.ds(pl.multiple_of(at * piece_rows, piece_rows), piece_rows)

    def crossing(j, k, member):
        here = piece(j, k, member)
        return remote(
            held_ref.at[here], down_ref.at[here], pass_s.at[j, k], pass_r.at[j, k], line, partner
        )

    for j in range(2):
        for k in range(1, quarter):
            crossing(j, k, low).start()

    peers = [(j, d) for d in range(lines) for j in (1, 0) if (j, d) != (0, 0)]

    def out_copy(what, j, d):
        there = lax.rem(line + d, lines)
        return remote(
            send_ref.at[what, there // copies], rows_ref.at[what, j, line],
            send_sem.at[what, j, d], recv_sem.at[what, j, line],
            there, mate if j else own,
        )

    def arrived(what, j, d):
        from_line = lax.rem(line + d, lines)
        return remote(
            send_ref.at[what, 0], rows_ref.at[what, j, from_line],
            send_sem.at[what, j, d], recv_sem.at[what, j, from_line],
            from_line, mate if j else own,
        )

    def home_copy(what, j, d):
        there = lax.rem(line + d, lines)
        return remote(
            made_ref.at[what, j, there], got_ref.at[what, j, line],
            home_s.at[what, j, d], home_r.at[what, j, line],
            there, mate if j else own,
        )

    def came_home(what, j, d):
        from_line = lax.rem(line + d, lines)
        return remote(
            made_ref.at[what, j, 0], got_ref.at[what, j, from_line],
            home_s.at[what, j, d], home_r.at[what, j, from_line],
            from_line, mate if j else own,
        )

    middle = x_ref[...] + mixer_ref[...]
    middle_ref[...] = middle
    gain = gain_ref[...]
    scale = lax.rsqrt(jnp.mean(middle * middle, axis=1, keepdims=True) + 1e-05)
    normed = (middle * scale * gain).astype(jnp.bfloat16)
    normed_ref[...] = normed
    rows, width = middle.shape
    slots = SLOTS
    lane = lax.broadcasted_iota(jnp.int32, (rows, LANES), 1)
    route_along = jnp.broadcast_to(route_ref[...].astype(jnp.float32), (rows, rows))
    route_down = route_along.T[:, :LANES]
    chosen = (route_down == lane.astype(jnp.float32)).astype(jnp.float32)
    earlier = (
        lax.broadcasted_iota(jnp.int32, (rows, rows), 0)
        > lax.broadcasted_iota(jnp.int32, (rows, rows), 1)
    ).astype(jnp.bfloat16)
    before = dot_nn(earlier, chosen.astype(jnp.bfloat16))
    slot_down = route_down[:, :1] * slots + jnp.sum(before * chosen, axis=1, keepdims=True)
    slot_along = jnp.broadcast_to(slot_down, (rows, rows)).T[:1, :]
    table_ref[...] = (
        jnp.broadcast_to(slot_along, table_ref.shape)
        == lax.broadcasted_iota(jnp.int32, table_ref.shape, 0).astype(jnp.float32)
    ).astype(jnp.bfloat16)
    for e in range(experts):
        places = lax.broadcasted_iota(jnp.int32, (rows, slots), 1) + e * slots
        back_table_ref[e] = (
            jnp.broadcast_to(slot_down, (rows, slots)) == places.astype(jnp.float32)
        ).astype(jnp.bfloat16)

    def dispatch(what, values):
        sent = dot_nn(table_ref[...], values).astype(jnp.bfloat16)
        for e in range(experts):
            send_ref[what, e] = sent[e * slots : (e + 1) * slots]
        for j, d in peers:
            out_copy(what, j, d).start()
        rows_ref[what, 0, line] = send_ref[what, line // copies]

    dispatch(0, normed)
    router_f = jnp.concatenate(
        [
            router_ref[...].astype(jnp.float32),
            jnp.zeros((LANES - experts, width), jnp.float32),
        ],
        axis=0,
    )
    router = router_f.astype(jnp.bfloat16)
    logits = jnp.where(lane < experts, outer_cols(normed, router), -jnp.inf)
    grown = jnp.exp(logits - jnp.max(logits, axis=1, keepdims=True))
    probs = grown / jnp.sum(grown, axis=1, keepdims=True)
    gate = jnp.sum(chosen * probs, axis=1, keepdims=True)
    dispatch(1, (gate * grad_ref[...]).astype(jnp.bfloat16))

    total = 2 * lines * slots
    hidden = up_ref.shape[1]
    chunk = hidden // 3 if hidden % (3 * LANES) == 0 else hidden
    parts = hidden // chunk

    def rows_of(ref, what):
        return ref[what].reshape(total, width)

    def columns(c):
        return pl.ds(pl.multiple_of(c * chunk, LANES), chunk)

    for j in range(2):
        for k in range(quarter):
            here = piece(j, k, low)
            down_ref[here, :] = held_ref[here, :]
        here = piece(j, 0, 1 - low)
        down_ref[here, :] = held_ref[here, :]
    for j, d in peers:
        arrived(0, j, d).wait_recv()

    def rise(c, carry):
        pre_ref[:, columns(c)] = dot_nn(rows_of(rows_ref, 0), up_ref[:, columns(c)])
        pre = pre_ref[:, columns(c)]
        half = gauss(pre)
        act_ref[:, columns(c)] = (pre * half).astype(jnp.bfloat16)
        pre_ref[:, columns(c)] = half + pre * (
            jnp.exp(-0.5 * pre * pre) * (1.0 / math.sqrt(2.0 * math.pi))
        )
        return carry

    lax.fori_loop(0, parts, rise, 0)

    wide = width // 3

    def send_home(what, left_ref, right_ref):
        def make(c, carry):
            here = pl.ds(pl.multiple_of(c * wide, LANES), wide)
            there = pl.ds(pl.multiple_of(c * wide, LANES), wide)
            made = outer_cols(left_ref[...], right_ref[there, :]).astype(jnp.bfloat16)
            made_ref[what, :, :, :, here] = made.reshape(2, lines, slots, wide)
            return carry

        lax.fori_loop(0, 3, make, 0)
        for j, d in peers:
            home_copy(what, j, d).start()
        got_ref[what, 0, line] = made_ref[what, 0, line]

    for j, d in peers:
        arrived(1, j, d).wait_recv()
    for j in range(2):
        for k in range(1, quarter):
            crossing(j, k, 1 - low).wait_recv()

    def fall(c, carry):
        slope_ref[:, columns(c)] = (
            dot_nn(rows_of(rows_ref, 1), down_ref[:, columns(c)]) * pre_ref[:, columns(c)]
        ).astype(jnp.bfloat16)
        return carry

    lax.fori_loop(0, parts, fall, 0)
    send_home(1, slope_ref, up_ref)
    send_home(0, act_ref, down_ref)

    pieces = grad_up_ref.shape[1]

    def weigh(c, carry):
        up = inner_rows(rows_of(rows_ref, 0), slope_ref[:, columns(c)]).astype(jnp.bfloat16)
        down = inner_rows(rows_of(rows_ref, 1), act_ref[:, columns(c)]).astype(jnp.bfloat16)
        grad_up_ref[:, :, columns(c)] = up.reshape(count, pieces, chunk)
        grad_down_ref[:, :, columns(c)] = down.reshape(count, pieces, chunk)
        return carry

    lax.fori_loop(0, parts, weigh, 0)

    far_copies = []
    for k in range(1, count // 4):
        i = lax.rem(q + k, count // 4)
        for j in (1, 0):
            far_copies.append(
                remote(
                    grad_up_ref.at[seat_of(i, lax.rem(f + j, 2), 1 - low)], far_up_ref.at[j, i],
                    far_s.at[j, i], far_r.at[j, i], line, partner,
                )
            )
            far_copies[-1].start()

    def home(what):
        for j, d in peers:
            came_home(what, j, d).wait_recv()
        both = None
        for e in range(experts):
            own_rows = None
            for c in range(copies):
                for j in range(2):
                    term = got_ref[what, j, e * copies + c].astype(jnp.float32)
                    own_rows = term if own_rows is None else own_rows + term
            high, rest = split_low(own_rows)
            here = back_table_ref[e]
            term = dot_nn(here, high) + dot_nn(here, rest)
            both = term if both is None else both + term
        return both

    grad = grad_ref[...]
    middle = middle_ref[...]
    picked = home(0)
    output_ref[...] = middle + gate * picked
    grad_gate = jnp.sum(grad * picked, axis=1, keepdims=True)
    grad_logits = gate * (chosen - probs) * grad_gate
    grad_normed = home(1) + dot_nn(grad_logits, router_f, HIGHEST)
    scaled = gain * grad_normed
    grad_middle = (
        grad
        + scale * scaled
        - middle * (scale * scale * scale) * jnp.mean(scaled * middle, axis=1, keepdims=True)
    )
    grad_middle_ref[...] = grad_middle
    grad_low_ref[...] = grad_middle.astype(jnp.bfloat16)
    vectors_ref[...] = jnp.zeros_like(vectors_ref)
    vectors_ref[1:2, :] = jnp.sum(grad_normed * middle * scale, axis=0, keepdims=True)
    vectors_ref[2 : 2 + experts, :] = inner_rows(
        grad_logits, normed_ref[...].astype(jnp.float32), HIGHEST
    )[:experts]
    for what in range(2):
        for j, d in peers:
            out_copy(what, j, d).wait_send()
            home_copy(what, j, d).wait_send()
    for copy in far_copies:
        copy.wait()
    for j in range(2):
        for k in range(1, quarter):
            crossing(j, k, low).wait_send()


def run_experts(
    count, lines, experts, x, mixer, grad, route, gain, router, up, down
):
    rows, width = x.shape
    slots = SLOTS
    total = 2 * lines * slots
    hidden = up.shape[1]
    pieces = (count, up.shape[0] // count, hidden)
    vmem = pl.BlockSpec(memory_space=pltpu.VMEM)
    dma = pltpu.SemaphoreType.DMA
    args = (x, mixer, grad, route, gain, router, up, down)
    low = jnp.bfloat16
    return pl.pallas_call(
        functools.partial(experts_kernel, count, lines, experts),
        in_specs=[vmem] * len(args),
        out_specs=[vmem] * 7,
        out_shape=[
            jax.ShapeDtypeStruct((rows, width), jnp.float32),
            jax.ShapeDtypeStruct((rows, width), jnp.float32),
            jax.ShapeDtypeStruct((rows, width), low),
            jax.ShapeDtypeStruct((8, width), jnp.float32),
            jax.ShapeDtypeStruct(pieces, low),
            jax.ShapeDtypeStruct(pieces, low),
            jax.ShapeDtypeStruct((2, count // 4, *pieces[1:]), low),
        ],
        scratch_shapes=[
            pltpu.VMEM((experts * slots, rows), low),
            pltpu.VMEM((experts, rows, slots), low),
            pltpu.VMEM(down.shape, low),
            pltpu.VMEM((rows, width), jnp.float32),
            pltpu.VMEM((rows, width), low),
            pltpu.VMEM((2, experts, slots, width), low),
            pltpu.VMEM((2, 2, lines, slots, width), low),
            pltpu.VMEM((2, 2, lines, slots, width), low),
            pltpu.VMEM((2, 2, lines, slots, width), low),
            pltpu.VMEM((total, hidden), low),
            pltpu.VMEM((total, hidden), low),
            pltpu.VMEM((total, hidden), jnp.float32),
            dma((2, 2, lines)), dma((2, 2, lines)), dma((2, 2, lines)), dma((2, 2, lines)),
            dma((2, count // 4)), dma((2, count // 4)), dma((2, count // 4)), dma((2, count // 4)),
        ],
        compiler_params=pltpu.CompilerParams(
            collective_id=4, has_side_effects=True, vmem_limit_bytes=VMEM_LIMIT
        ),
        cost_estimate=pl.CostEstimate(
            flops=12 * total * width * hidden,
            bytes_accessed=8 * width * hidden,
            transcendentals=2 * total * hidden,
        ),
        name="experts",
    )(*args)


def body(
    tokens,
    cotangent,
    routes,
    mixer_gain,
    input_proj,
    conv_weight,
    conv_bias,
    select_proj,
    step_proj,
    step_bias,
    decay_log,
    skip_gain,
    output_proj,
    expert_gain,
    router,
    expert_up,
    expert_down,
):
    rows = tokens.shape[1]
    width = tokens.shape[2]
    shard = input_proj.shape[2]
    rank = step_proj.shape[0]
    state = decay_log.shape[0]
    kernel = conv_weight.shape[0]
    picks = select_proj.shape[0]
    count = lax.axis_size("seq")
    lines = lax.axis_size("dp")
    shard_rows = -(-shard // 16) * 16
    cuts = Cuts(picks, rank, state, kernel)

    x_in = tokens.reshape(rows, width)
    gain_one = mixer_gain.astype(jnp.float32)
    small_pad = -(-cuts.rows // LANES) * LANES
    (normed_all, weights, small_all, conv_ext, conv_sum, conv_act, gate_branch, selected, up_cut) = (
        front(
            count, lines, cuts, shard_rows, small_pad,
            x_in, gain_one[None], input_proj.transpose(0, 2, 1), output_proj, select_proj.T,
            step_proj, decay_log, conv_weight, conv_bias[None], step_bias[None], skip_gain[None],
            expert_up,
        )
    )
    pre, mixed, mixer_low, priors, end, mixer_out, down_cut = scan_forward(
        count, cuts, width, conv_act, gate_branch, selected, small_all, weights, expert_down.T
    )

    experts = router.shape[0]
    (output, grad_middle, grad_middle_low, vectors, grad_up_low, grad_down_low, far_up) = run_experts(
        count,
        lines,
        experts,
        x_in,
        mixer_out,
        cotangent.reshape(rows, width),
        routes.reshape(1, rows),
        expert_gain.astype(jnp.float32)[None],
        router,
        up_cut.reshape(-1, up_cut.shape[2]),
        down_cut.reshape(-1, down_cut.shape[2]),
    )

    (grad_gate_branch, grad_act, grad_step_w, rate_total, scan_rows, grad_selected, grad_middle_all,
     grad_down_t) = (
        scan_backward(
            count, cuts, grad_middle_low, conv_act, gate_branch, mixed, pre, selected, small_all,
            weights, priors, end, grad_down_low,
        )
    )
    (grad_tokens, grad_input, grad_output, grad_select, grad_step, grad_decay, grad_taps,
     grad_conv_bias, grad_step_bias, grad_skip, totals, grad_up) = back(
        count, lines, shard_rows, shard, cuts, grad_selected, small_all, weights, conv_ext, conv_sum,
        grad_act, grad_gate_branch, mixer_low, normed_all.reshape(-1, width),
        grad_middle_all.reshape(-1, width), grad_step_w, rate_total, scan_rows, vectors,
        grad_up_low, far_up, x_in, gain_one[None], grad_middle,
    )
    return (
        output.reshape(tokens.shape),
        grad_tokens.reshape(tokens.shape),
        totals[0] / gain_one,
        grad_input.transpose(0, 2, 1),
        grad_taps,
        grad_conv_bias.reshape(shard),
        grad_select.T,
        grad_step,
        grad_step_bias.reshape(shard),
        grad_decay,
        grad_skip.reshape(shard),
        grad_output,
        totals[1],
        totals[2 : 2 + experts],
        grad_up,
        grad_down_t.T,
    )


def solution(mesh):
    both = ("dp", "seq")
    placed = (
        P("dp", "seq", None),
        P("dp", "seq", None),
        P("dp", "seq", None),
        P(),
        P(None, None, both),
        P(None, both),
        P(both),
        P(None, both),
        P(None, both),
        P(both),
        P(None, both),
        P(both),
        P(both, None),
        P(),
        P(),
        P("seq", "dp"),
        P("dp", "seq"),
    )
    return jax.shard_map(
        body,
        mesh=mesh,
        in_specs=placed,
        out_specs=(
            P("dp", "seq", None),
            P("dp", "seq", None),
            P(),
            P(None, None, both),
            P(None, both),
            P(both),
            P(None, both),
            P(None, both),
            P(both),
            P(None, both),
            P(both),
            P(both, None),
            P(),
            P(),
            P("seq", "dp"),
            P("dp", "seq"),
        ),
        check_vma=False,
    )
```

```python
import functools
import math

import jax
import jax.numpy as jnp
from jax import lax
from jax.experimental import pallas as pl
from jax.experimental.pallas import tpu as pltpu
from jax.sharding import PartitionSpec as P

CAP = 56
LANES = 128
TIME_BLOCK = 128
LOG2E = math.log2(math.e)

HIGHEST = lax.Precision.HIGHEST


def inner_rows(left, right, precision=None):
    return lax.dot_general(
        left,
        right,
        (((0,), (0,)), ((), ())),
        precision=precision,
        preferred_element_type=jnp.float32,
    )


def outer_cols(left, right, precision=None):
    return lax.dot_general(
        left,
        right,
        (((1,), (1,)), ((), ())),
        precision=precision,
        preferred_element_type=jnp.float32,
    )


def sublane_sums(parts):
    row = lax.broadcasted_iota(jnp.int32, parts[0].shape, 0)
    low4 = row < 4
    low2 = (row % 4) < 2
    low1 = (row % 2) < 1
    quads = []
    for k in range(4):
        a, b = parts[k], parts[k + 4]
        quads.append(jnp.where(low4, a, b) + pltpu.roll(jnp.where(low4, b, a), 4, 0))
    pairs = []
    for k in range(2):
        a, b = quads[k], quads[k + 2]
        pairs.append(
            jnp.where(low2, a, b) + jnp.where(low2, pltpu.roll(a, 6, 0), pltpu.roll(b, 2, 0))
        )
    a, b = pairs
    return jnp.where(low1, a, b) + jnp.where(low1, pltpu.roll(a, 7, 0), pltpu.roll(b, 1, 0))


MESH = pl.DeviceIdType.MESH
VMEM_LIMIT = 60 * 1024 * 1024


def dot_nn(left, right, precision=None):
    return lax.dot_general(
        left, right, (((1,), (0,)), ((), ())), precision=precision,
        preferred_element_type=jnp.float32,
    )


def place():
    own, line = lax.axis_index("seq"), lax.axis_index("dp")
    return line, own, own // 2, lax.rem(own, 2)


def remote(source, target, send_sem, recv_sem, line, position):
    return pltpu.make_async_remote_copy(
        src_ref=source,
        dst_ref=target,
        send_sem=send_sem,
        recv_sem=recv_sem,
        device_id=(line, position),
        device_id_type=MESH,
    )


def greet(count, lines=1):
    line, own, _, _ = place()
    barrier = pltpu.get_barrier_semaphore()
    for k in range(1, count):
        pl.semaphore_signal(
            barrier, inc=1, device_id=(line, lax.rem(own + k, count)), device_id_type=MESH
        )
    for k in range(1, lines):
        pl.semaphore_signal(
            barrier, inc=1, device_id=(lax.rem(line + k, lines), own), device_id_type=MESH
        )
    pl.semaphore_wait(barrier, count - 1 + lines - 1)


def sigmoid(values):
    return 1.0 / (1.0 + jnp.exp(-values))


def softplus(values):
    return jnp.maximum(values, 0.0) + jnp.log1p(jnp.exp(-jnp.abs(values)))


class Cuts:
    def __init__(self, picks, rank, state, kernel):
        self.picks, self.rank, self.state, self.kernel = picks, rank, state, kernel
        self.step = picks
        self.decay = self.step + rank
        self.taps = self.decay + state
        self.conv_bias = self.taps + kernel
        self.step_bias = self.conv_bias + 1
        self.skip = self.step_bias + 1
        self.rows = self.skip + 1
        self.sent = -(-picks // 16) * 16


class Relay:
    def __init__(self, axis, half, high, low, seat, block, refs):
        self.axis, self.half, self.high, self.low = axis, half, high, low
        self.seat, self.block = seat, block
        self.other = lax.axis_index("dp" if axis == "seq" else "seq")
        self.part, self.across, self.along = refs[:3]
        self.send_x, self.recv_x, self.send_hi, self.recv_hi = refs[3:]

    def remote(self, source, target, send_sem, recv_sem, position):
        if self.axis == "seq":
            return remote(source, target, send_sem, recv_sem, self.other, position)
        return remote(source, target, send_sem, recv_sem, position, self.other)

    def over(self, i, low):
        return self.remote(
            self.part.at[self.block(i, low)], self.across.at[i], self.send_x.at[i],
            self.recv_x.at[i], self.seat(self.high, 1 - self.low),
        )

    def on(self, i):
        k = lax.rem(i - self.high + self.half, self.half)
        return self.remote(
            self.across.at[i], self.along.at[k], self.send_hi.at[k], self.recv_hi.at[k],
            self.seat(i, self.low),
        )

    def made(self, i, low):
        @pl.when(low != self.low)
        def _():
            self.over(i, low).start()

    def summed(self, i):
        self.over(i, self.low).wait_recv()
        return self.part[self.block(i, self.low)].astype(jnp.float32) + self.across[i].astype(
            jnp.float32
        )

    def pass_on(self, i, low):
        @pl.when((low == self.low) & (i != self.high))
        def _():
            self.across[i] = self.summed(i).astype(jnp.bfloat16)
            self.on(i).start()

    def finish(self, sent=None):
        total = self.summed(self.high)
        for k in range(1, self.half):
            self.on(lax.rem(self.high + k, self.half)).wait_recv()
            total = total + self.along[k].astype(jnp.float32)
        for i in range(self.half) if sent is None else sent:
            self.over(i, 1 - self.low).wait_send()
        for k in range(1, self.half):
            self.on(lax.rem(self.high + k, self.half)).wait_send()
        return total


def whole_relay(axis, count, refs):
    own = lax.axis_index(axis)

    def seat(i, low):
        return 2 * i + low

    return Relay(axis, count // 2, own // 2, lax.rem(own, 2), seat, seat, refs)


def relay_scratch(count, rows, width, part=True):
    half = count // 2
    dma = pltpu.SemaphoreType.DMA
    own = [pltpu.VMEM((count, rows, width), jnp.bfloat16)] if part else []
    return own + [
        pltpu.VMEM((half, rows, width), jnp.bfloat16),
        pltpu.VMEM((half, rows, width), jnp.bfloat16),
        dma((half,)), dma((half,)), dma((half,)), dma((half,)),
    ]


def square():
    own = lax.axis_index("seq")
    return own // 4, lax.rem(own // 2, 2), lax.rem(own, 2)


def seat_of(q, f, low):
    return 4 * q + 2 * f + low


class Gather:
    def __init__(self, count, shard_ref, land_ref, swap_s, swap_r, line_s, line_r, pair_s, pair_r):
        self.line = lax.axis_index("dp")
        self.q, self.f, self.low = square()
        self.quarter = count // 4
        self.shard, self.land = shard_ref, land_ref
        self.swap_s, self.swap_r = swap_s, swap_r
        self.line_s, self.line_r, self.pair_s, self.pair_r = line_s, line_r, pair_s, pair_r
        self.cut = land_ref.shape[2]

    def columns(self, f):
        return pl.ds(pl.multiple_of(f * self.cut, LANES), self.cut)

    def piece(self, j, k, low):
        q = lax.rem(self.q - k + self.quarter, self.quarter)
        return seat_of(q, lax.rem(self.f + j, 2), low)

    def swap(self):
        own = self.piece(0, 0, self.low)
        return remote(
            self.shard.at[:, self.columns(1 - self.f)], self.land.at[own], self.swap_s, self.swap_r,
            self.line, self.piece(1, 0, self.low),
        )

    def along(self, j, k):
        piece = self.piece(j, 0, self.low)
        there = seat_of(lax.rem(self.q + k, self.quarter), self.f, self.low)
        return remote(
            self.land.at[piece], self.land.at[piece], self.line_s.at[j, k], self.line_r.at[j, k],
            self.line, there,
        )

    def pair(self, j, k, low):
        piece = self.piece(j, k, low)
        return remote(
            self.land.at[piece], self.land.at[piece], self.pair_s.at[j, k], self.pair_r.at[j, k],
            self.line, seat_of(self.q, self.f, 1 - self.low),
        )

    def start(self):
        self.swap().start()
        self.land[self.piece(0, 0, self.low)] = self.shard[:, self.columns(self.f)]

    def spread(self, j):
        if j == 1:
            mate = self.piece(1, 0, self.low)
            remote(
                self.land.at[mate], self.land.at[mate], self.swap_s, self.swap_r, self.line, mate
            ).wait_recv()
        for k in range(1, self.quarter):
            self.along(j, k).start()
        self.pair(j, 0, self.low).start()

    def arrive(self):
        for j in range(2):
            for k in range(1, self.quarter):
                piece = self.piece(j, k, self.low)
                remote(
                    self.land.at[piece], self.land.at[piece], self.line_s.at[j, k],
                    self.line_r.at[j, k], self.line, piece,
                ).wait_recv()

    def forward(self, j):
        for k in range(1, self.quarter):
            piece = self.piece(j, k, self.low)
            remote(
                self.land.at[piece], self.land.at[piece], self.line_s.at[j, k],
                self.line_r.at[j, k], self.line, piece,
            ).wait_recv()
            self.pair(j, k, self.low).start()

    def finish(self, passed=True):
        crossed = range(self.quarter) if passed else (0,)
        for j in range(2):
            for k in crossed:
                self.pair(j, k, 1 - self.low).wait_recv()
        self.swap().wait_send()
        for j in range(2):
            for k in range(1, self.quarter):
                self.along(j, k).wait_send()
            for k in crossed:
                self.pair(j, k, self.low).wait_send()


def gather_scratch(count):
    dma = pltpu.SemaphoreType.DMA
    quarter = count // 4
    return [dma, dma] + [dma((2, quarter)) for _ in range(4)]


class Scatter:
    def __init__(self, count, part_ref, far_ref, other_ref, held_ref, swap_s, swap_r, refs):
        self.line = lax.axis_index("dp")
        self.q, self.f, self.low = square()
        self.quarter = count // 4
        self.far, self.other, self.held = far_ref, other_ref, held_ref
        self.swap_s, self.swap_r = swap_s, swap_r
        self.relays = []
        for j in range(2):
            cut = lax.rem(self.f + j, 2)

            def seat(i, low):
                return seat_of(i, self.f, low)

            def block(i, low, cut=cut):
                return seat_of(i, cut, low)

            mine = tuple(ref.at[j] for ref in refs)
            self.relays.append(
                Relay("seq", self.quarter, self.q, self.low, seat, block, (part_ref, *mine))
            )

    def swap(self):
        return remote(
            self.held, self.other, self.swap_s, self.swap_r, self.line,
            seat_of(self.q, 1 - self.f, self.low),
        )

    def far_places(self):
        return [
            (j, lax.rem(self.q + k, self.quarter)) for k in range(1, self.quarter) for j in (1, 0)
        ]

    def send_far(self):
        for j, i in self.far_places():
            self.relays[j].over(i, 1 - self.low).start()

    def pass_far(self):
        for j, i in self.far_places():
            relay = self.relays[j]
            if self.far is None:
                relay.pass_on(i, self.low)
            else:
                both = relay.part[relay.block(i, self.low)].astype(jnp.float32) + self.far[
                    j, i
                ].astype(jnp.float32)
                relay.across[i] = both.astype(jnp.bfloat16)
                relay.on(i).start()

    def total(self, j):
        return self.relays[j].finish(None if self.far is None else [self.q])

    def send_near(self):
        for j in (1, 0):
            self.relays[j].over(self.q, 1 - self.low).start()

    def hand_over(self):
        self.held[...] = self.total(1).astype(jnp.bfloat16)
        self.swap().start()

    def finish(self, out_ref):
        cut = self.held.shape[1]
        out_ref[:, pl.ds(pl.multiple_of(self.f * cut, LANES), cut)] = self.total(0)
        self.swap().wait_recv()
        out_ref[:, pl.ds(pl.multiple_of((1 - self.f) * cut, LANES), cut)] = self.other[...].astype(
            jnp.float32
        )
        self.swap().wait_send()


def scatter_scratch(count, rows, cut):
    dma = pltpu.SemaphoreType.DMA
    quarter = count // 4
    return [
        pltpu.VMEM((rows, cut), jnp.bfloat16),
        pltpu.VMEM((rows, cut), jnp.bfloat16),
        dma, dma,
        pltpu.VMEM((2, quarter, rows, cut), jnp.bfloat16),
        pltpu.VMEM((2, quarter, rows, cut), jnp.bfloat16),
        *[dma((2, quarter)) for _ in range(4)],
    ]


def front_kernel(
    count, lines, cuts,
    x_ref, gain_ref, input_ref, output_ref, select_ref, step_ref, decay_ref, taps_ref, conv_bias_ref,
    step_bias_ref, skip_ref, expert_ref,
    all_ref, weights_ref, small_ref, ext_ref, sum_ref, act_ref, gate_ref, selected_ref, land_ref,
    normed_ref, packed_ref, table_ref, part_ref, partial_ref, total_ref,
    send_w, recv_w, send_up, send_down, recv_hi, send_x, recv_x, send_rs, recv_rs, send_ag, recv_ag,
    *gather_refs,
):
    line, own, high, low = place()
    half = count // 2
    gather = Gather(count, expert_ref, land_ref, *gather_refs)
    rows, width = x_ref.shape
    shard = packed_ref.shape[0]
    inner = weights_ref.shape[0]
    kernel = cuts.kernel
    partner = 2 * high + 1 - low

    own_shard = output_ref.shape[0]
    extra = jnp.zeros((shard - own_shard, width), jnp.float32)

    def padded(values):
        return jnp.concatenate([values.astype(jnp.float32), extra], axis=0).astype(jnp.bfloat16)

    packed_ref[:, :width] = padded(input_ref[0])
    packed_ref[:, width : 2 * width] = padded(input_ref[1])
    packed_ref[:, 2 * width : 3 * width] = padded(output_ref[...])
    table_ref[...] = jnp.zeros_like(table_ref)
    table_ref[:own_shard, : cuts.picks] = select_ref[...].astype(jnp.float32)
    picked = table_ref[:LANES, :].T
    table_ref[...] = jnp.zeros_like(table_ref)
    table_ref[:LANES, :] = picked
    for at, ref in (
        (cuts.step, step_ref),
        (cuts.decay, decay_ref),
        (cuts.taps, taps_ref),
        (cuts.conv_bias, conv_bias_ref),
        (cuts.step_bias, step_bias_ref),
        (cuts.skip, skip_ref),
    ):
        table_ref[at : at + ref.shape[0], :own_shard] = ref[...].astype(jnp.float32)
    packed_ref[:, 3 * width :] = table_ref[...].T[:shard].astype(jnp.bfloat16)
    x = x_ref[...]
    scale = lax.rsqrt(jnp.mean(x * x, axis=1, keepdims=True) + 1e-05)
    normed_ref[...] = (x * scale * gain_ref[...]).astype(jnp.bfloat16)
    greet(count, lines)

    copies = []
    shard_rows = pl.ds(pl.multiple_of(line * shard, 16), shard)
    def step_on(i, up):
        block = 2 * i + low
        return remote(
            all_ref.at[block], all_ref.at[block], (send_up if up else send_down).at[i],
            recv_hi.at[i], line, 2 * (high + (1 if up else -1)) + low,
        )

    def can_go(up):
        return high < half - 1 if up else high > 0

    all_ref[own] = normed_ref[...]
    for up in (True, False):

        @pl.when(can_go(up))
        def _(up=up):
            step_on(high, up).start()

    remote(all_ref.at[own], all_ref.at[own], send_x.at[high], recv_x.at[high], line, partner).start()
    for k in range(1, lines):
        copy = remote(
            packed_ref, weights_ref.at[shard_rows], send_w.at[k], recv_w.at[k],
            lax.rem(line + k, lines), own,
        )
        copy.start()
        copies.append(copy)
    gather.start()
    weights_ref[shard_rows, :] = packed_ref[...]
    if lines * shard < inner:
        weights_ref[lines * shard :, :] = jnp.zeros(
            (inner - lines * shard, weights_ref.shape[1]), weights_ref.dtype
        )
    ext_ref[0:8, :] = jnp.zeros((8, inner), jnp.float32)
    def cross(i):
        block = 2 * i + low
        return remote(
            all_ref.at[block], all_ref.at[block], send_x.at[i], recv_x.at[i], line, partner
        )

    for k in range(1, half):
        for up in (True, False):
            i = high - k if up else high + k

            @pl.when(i >= 0 if up else i < half)
            def _(i=i, up=up):
                step_on(i, up).wait_recv()

                @pl.when(can_go(up))
                def _():
                    step_on(i, up).start()

                cross(i).start()

    gather.spread(0)
    gather.spread(1)
    for k in range(1, lines):
        from_line = lax.rem(line - k + lines, lines)
        there = pl.ds(pl.multiple_of(from_line * shard, 16), shard)
        remote(
            packed_ref, weights_ref.at[there], send_w.at[k], recv_w.at[k], from_line, own
        ).wait_recv()
    small_ref[...] = weights_ref[:, 3 * width :].astype(jnp.float32).T
    for i in range(half):
        block = 2 * i + 1 - low
        remote(
            all_ref.at[block], all_ref.at[block], send_x.at[i], recv_x.at[i], line, partner
        ).wait_recv()

    def project(b, carry):
        start = pl.multiple_of(b * rows, rows)
        block = all_ref[b]
        ext_ref[pl.ds(pl.multiple_of(start + 8, 8), rows), :] = outer_cols(
            block, weights_ref[:, :width]
        )
        gate_ref[pl.ds(start, rows), :] = outer_cols(block, weights_ref[:, width : 2 * width])
        return carry

    lax.fori_loop(0, count, project, 0)

    def convolve(b, carry):
        start = pl.multiple_of(b * rows, rows)
        window = ext_ref[pl.ds(start, rows + 8), :]
        total = small_ref[cuts.conv_bias : cuts.conv_bias + 1, :]
        for k in range(kernel):
            tap = small_ref[cuts.taps + k : cuts.taps + k + 1, :]
            total = total + tap * window[9 - kernel + k : 9 - kernel + k + rows]
        act = total * sigmoid(total)
        sum_ref[pl.ds(start, rows), :] = total
        act_ref[pl.ds(start, rows), :] = act
        part_ref[b] = outer_cols(
            small_ref[: cuts.sent, :].astype(jnp.bfloat16), act.astype(jnp.bfloat16)
        ).astype(jnp.bfloat16)
        return carry

    lax.fori_loop(0, count, convolve, 0)

    for k in range(1, count):
        there = lax.rem(own + k, count)
        copy = remote(
            part_ref.at[there], partial_ref.at[k], send_rs.at[k], recv_rs.at[k], line, there
        )
        copy.start()
        copies.append(copy)
    total = part_ref[own].astype(jnp.float32)
    for k in range(1, count):
        remote(
            part_ref.at[own], partial_ref.at[k], send_rs.at[k], recv_rs.at[k], line, partner
        ).wait_recv()
        total = total + partial_ref[k].astype(jnp.float32)
    total_ref[own] = total.astype(jnp.bfloat16)
    for k in range(1, count):
        copy = remote(
            total_ref.at[own], total_ref.at[own], send_ag.at[k], recv_ag.at[k],
            line, lax.rem(own + k, count),
        )
        copy.start()
        copies.append(copy)
    gather.forward(0)
    gather.forward(1)
    for k in range(1, count):
        block = lax.rem(own - k + count, count)
        remote(
            total_ref.at[block], total_ref.at[block], send_ag.at[k], recv_ag.at[k],
            line, partner,
        ).wait_recv()
    selected_ref[...] = total_ref[...].astype(jnp.float32)[:, : cuts.picks]
    for copy in copies:
        copy.wait_send()
    for i in range(half):
        cross(i).wait_send()
        for up in (True, False):

            @pl.when(can_go(up) & (i <= high if up else i >= high))
            def _(i=i, up=up):
                step_on(i, up).wait_send()

    gather.finish()


def front(count, lines, cuts, shard, small, *args):
    rows, width = args[0].shape
    expert = args[-1]
    columns = 3 * width + small
    inner = -(-lines * shard // LANES) * LANES
    length = count * rows
    half = count // 2
    vmem = pl.BlockSpec(memory_space=pltpu.VMEM)

    def f32(*shape):
        return jax.ShapeDtypeStruct(shape, jnp.float32)

    dma = pltpu.SemaphoreType.DMA
    return pl.pallas_call(
        functools.partial(front_kernel, count, lines, cuts),
        in_specs=[vmem] * len(args),
        out_specs=[vmem] * 9,
        out_shape=[
            jax.ShapeDtypeStruct((count, rows, width), jnp.bfloat16),
            jax.ShapeDtypeStruct((inner, columns), jnp.bfloat16),
            f32(small, inner),
            f32(length + 8, inner),
            f32(length, inner),
            f32(length, inner),
            f32(length, inner),
            f32(count, cuts.picks, rows),
            jax.ShapeDtypeStruct((count, expert.shape[0], expert.shape[1] // 2), jnp.bfloat16),
        ],
        scratch_shapes=[
            pltpu.VMEM((rows, width), jnp.bfloat16),
            pltpu.VMEM((shard, columns), jnp.bfloat16),
            pltpu.VMEM((small, LANES), jnp.float32),
            *[pltpu.VMEM((count, cuts.sent, rows), jnp.bfloat16)] * 3,
            dma((lines,)), dma((lines,)), dma((half,)), dma((half,)), dma((half,)), dma((half,)),
            dma((half,)), dma((count,)), dma((count,)), dma((count,)), dma((count,)),
            *gather_scratch(count),
        ],
        compiler_params=pltpu.CompilerParams(
            collective_id=0, has_side_effects=True, vmem_limit_bytes=VMEM_LIMIT
        ),
        cost_estimate=pl.CostEstimate(
            flops=4 * length * width * inner,
            bytes_accessed=20 * length * inner,
            transcendentals=length * inner,
        ),
        name="front",
    )(*args)


def spread_lanes(values, wide_ref, out_ref):
    state, steps = values.shape
    high = values.astype(jnp.bfloat16).astype(jnp.float32)
    rest = values - high
    lane = lax.broadcasted_iota(jnp.int32, (state, steps), 1)

    def fill(g, carry):
        for k in range(8):
            t = g * 8 + k
            here = pl.ds(pl.multiple_of(t * state, state), state)
            mask = lane == t
            wide_ref[here, :steps] = jnp.where(mask, high, 0.0).astype(jnp.bfloat16)
            wide_ref[here, steps:] = jnp.where(mask, rest, 0.0).astype(jnp.bfloat16)
        return carry

    lax.fori_loop(0, steps // 8, fill, 0)
    ones = jnp.ones((2 * steps, LANES), jnp.bfloat16)
    out_ref[...] = dot_nn(wide_ref[...], ones)


def scan_forward_kernel(
    count, cuts,
    act_ref, gate_ref, selected_ref, small_ref, output_ref, expert_ref,
    pre_ref, mixed_ref, mixer_low_ref, prior_ref, end_ref, summed_ref, expert_out_ref,
    state_ref, delta_ref, scanned_ref, wide_ref, wide_in_ref, wide_out_ref, land_ref, *refs,
):
    steps, inner = act_ref.shape
    tiles = inner // LANES
    state = cuts.state
    halves = state // 8
    step = pl.program_id(0)
    relay = whole_relay("seq", count, refs[:7])
    gather = Gather(count, expert_ref, land_ref, *refs[7:])

    @pl.when(step == 0)
    def _():
        greet(count)
        gather.start()
        state_ref[...] = jnp.zeros_like(state_ref)

    @pl.when(step == 0)
    def _():
        gather.spread(0)

    @pl.when(step == 3)
    def _():
        gather.spread(1)

    rates2 = -LOG2E * jnp.exp(small_ref[cuts.decay : cuts.decay + state, :])
    pre = inner_rows(
        selected_ref[0, : cuts.rank, :],
        small_ref[cuts.step : cuts.step + cuts.rank, :],
        HIGHEST,
    ) + small_ref[cuts.step_bias : cuts.step_bias + 1, :]
    pre_ref[...] = pre
    delta_ref[...] = softplus(pre)
    in_rows = cuts.rank
    out_rows = cuts.rank + state
    spread_lanes(selected_ref[0, in_rows : in_rows + state, :], wide_ref, wide_in_ref)
    spread_lanes(selected_ref[0, out_rows : out_rows + state, :], wide_ref, wide_out_ref)

    def group(g, states):
        states = [list(s) for s in states]
        base = pl.multiple_of(g * 8, 8)
        d8 = delta_ref[pl.ds(base, 8), :]
        du8 = d8 * act_ref[pl.ds(base, 8), :]
        parts = [[None] * 8 for _ in range(tiles)]
        for k in range(8):
            rows_now = [pl.ds((base + k) * state + 8 * i, 8) for i in range(halves)]
            b_now = [wide_in_ref[here, :] for here in rows_now]
            c_now = [wide_out_ref[here, :] for here in rows_now]
            for j in range(tiles):
                cols = slice(j * LANES, (j + 1) * LANES)
                d = jnp.broadcast_to(d8[k : k + 1, cols], (8, LANES))
                du = jnp.broadcast_to(du8[k : k + 1, cols], (8, LANES))
                total = None
                for i in range(halves):
                    old = states[j][i]
                    prior_ref[base + k, 8 * i : 8 * i + 8, cols] = old
                    new = jnp.exp2(d * rates2[8 * i : 8 * i + 8, cols]) * old + b_now[i] * du
                    states[j][i] = new
                    term = c_now[i] * new
                    total = term if total is None else total + term
                parts[j][k] = total
        for j in range(tiles):
            scanned_ref[pl.ds(base, 8), j * LANES : (j + 1) * LANES] = sublane_sums(parts[j])
        return tuple(tuple(s) for s in states)

    first = tuple(
        tuple(
            state_ref[8 * i : 8 * i + 8, j * LANES : (j + 1) * LANES] for i in range(halves)
        )
        for j in range(tiles)
    )
    last = lax.fori_loop(0, steps // 8, group, first)
    for j in range(tiles):
        for i in range(halves):
            state_ref[8 * i : 8 * i + 8, j * LANES : (j + 1) * LANES] = last[j][i]
    end_ref[...] = state_ref[...]

    mixed = scanned_ref[...] + small_ref[cuts.skip : cuts.skip + 1, :] * act_ref[...]
    gate = gate_ref[...]
    low = (mixed * (gate * sigmoid(gate))).astype(jnp.bfloat16)
    mixed_ref[...] = mixed
    mixer_low_ref[...] = low
    relay.part[step] = dot_nn(low, output_ref[...]).astype(jnp.bfloat16)
    relay.made(step // 2, lax.rem(step, 2))

    def pass_on(block):
        relay.pass_on(block // 2, lax.rem(block, 2))

    @pl.when(step >= LAG)
    def _():
        pass_on(step - LAG)

    @pl.when(step == count - 1)
    def _():
        for late in range(LAG - 1, -1, -1):
            pass_on(step - late)
        gather.arrive()
        summed_ref[...] = relay.finish()
        gather.finish(False)
        expert_out_ref[...] = land_ref[...]


def scan_forward(count, cuts, width, act, gate, selected, small, weights, expert):
    length, inner = act.shape
    state = cuts.state
    block = length // count
    rows = pl.BlockSpec((block, inner), lambda t: (t, 0))
    whole = pl.BlockSpec((state, inner), lambda t: (0, 0))
    pieces = (count, expert.shape[0], expert.shape[1] // 2)
    return pl.pallas_call(
        functools.partial(scan_forward_kernel, count, cuts),
        grid=(count,),
        in_specs=[
            rows,
            rows,
            pl.BlockSpec((1, cuts.picks, block), lambda t: (t, 0, 0)),
            pl.BlockSpec(small.shape, lambda t: (0, 0)),
            pl.BlockSpec((inner, width), lambda t: (0, 2)),
            pl.BlockSpec(expert.shape, lambda t: (0, 0)),
        ],
        out_specs=[
            rows,
            rows,
            rows,
            pl.BlockSpec((block, state, inner), lambda t: (t, 0, 0)),
            whole,
            pl.BlockSpec((block, width), lambda t: (0, 0)),
            pl.BlockSpec(pieces, lambda t: (0, 0, 0)),
        ],
        out_shape=[
            jax.ShapeDtypeStruct((length, inner), jnp.float32),
            jax.ShapeDtypeStruct((length, inner), jnp.float32),
            jax.ShapeDtypeStruct((length, inner), jnp.bfloat16),
            jax.ShapeDtypeStruct((length, state, inner), jnp.float32),
            jax.ShapeDtypeStruct((state, inner), jnp.float32),
            jax.ShapeDtypeStruct((block, width), jnp.float32),
            jax.ShapeDtypeStruct(pieces, jnp.bfloat16),
        ],
        scratch_shapes=[
            pltpu.VMEM((state, inner), jnp.float32),
            pltpu.VMEM((block, inner), jnp.float32),
            pltpu.VMEM((block, inner), jnp.float32),
            pltpu.VMEM((block * state, 2 * block), jnp.bfloat16),
            pltpu.VMEM((block * state, LANES), jnp.float32),
            pltpu.VMEM((block * state, LANES), jnp.float32),
            pltpu.VMEM(pieces, jnp.bfloat16),
            *relay_scratch(count, block, width),
            *gather_scratch(count),
        ],
        compiler_params=pltpu.CompilerParams(
            collective_id=1, has_side_effects=True, vmem_limit_bytes=VMEM_LIMIT
        ),
        cost_estimate=pl.CostEstimate(
            flops=8 * length * state * inner,
            bytes_accessed=4 * length * inner * (state + 6),
            transcendentals=length * state * inner,
        ),
        name="scan_forward",
    )(act, gate, selected, small, weights, expert)


def scan_backward_kernel(
    count, cuts,
    own_ref, act_ref, gate_ref, mixed_ref, pre_ref, selected_ref, small_ref, output_ref,
    prior_ref, end_ref, expert_ref,
    grad_gate_ref, grad_act_ref, grad_step_ref, rate_total_ref, rows_ref, grad_selected_ref,
    all_out_ref, expert_out_ref,
    incoming_ref, post_ref, delta_ref, grad_ref, grad_delta_ref, wide_ref, wide_in_ref,
    wide_out_ref, all_ref,
    stage_ref, part_ref, partial_ref, total_ref,
    send_hi, recv_hi, send_x, recv_x, send_rs, recv_rs, send_ag, recv_ag,
    other_ref, held_ref, swap_s, swap_r, *scatter_refs,
):
    steps, inner = act_ref.shape
    tiles = inner // LANES
    state = cuts.state
    halves = state // 8
    lane = lax.broadcasted_iota(jnp.int32, (8, steps), 1)
    line, own, high, low = place()
    half = count // 2
    partner = 2 * high + 1 - low
    index = pl.program_id(0)
    now = count - 1 - index
    scatter = Scatter(
        count, expert_ref, None, other_ref, held_ref, swap_s, swap_r, scatter_refs
    )

    def along(k):
        return remote(
            own_ref, all_ref.at[own], send_hi.at[k], recv_hi.at[high], line,
            2 * lax.rem(high + k, half) + low,
        )

    def across(block):
        i = block // 2
        return remote(
            all_ref.at[block], all_ref.at[block], send_x.at[i], recv_x.at[i], line, partner
        )

    def came_along(block):
        i = block // 2
        return remote(
            all_ref.at[block], all_ref.at[block], send_hi.at[0], recv_hi.at[i], line, partner
        )

    def hand_over(block):
        @pl.when((lax.rem(block, 2) == low) & (block // 2 != high))
        def _():
            came_along(block).wait_recv()
            across(block).start()

    @pl.when(index == 0)
    def _():
        greet(count)
        all_ref[own] = own_ref[...]
        incoming_ref[...] = jnp.zeros_like(incoming_ref)
        post_ref[...] = end_ref[...]
        rate_total_ref[...] = jnp.zeros_like(rate_total_ref)
        grad_step_ref[...] = jnp.zeros_like(grad_step_ref)
        rows_ref[...] = jnp.zeros_like(rows_ref)
        stage_ref[...] = jnp.zeros_like(stage_ref)

    @pl.when(index == 0)
    def _():
        for k in range(1, half):
            along(k).start()
        across(own).start()

    @pl.when(index == 0)
    def _():
        hand_over(now - 0)
        hand_over(now - 1)

    @pl.when(lax.rem(now, 2) != low)
    def _():
        across(now).wait_recv()

    gate = gate_ref[...]
    gate_sig = sigmoid(gate)
    grad_y = outer_cols(all_ref[now], output_ref[...])
    grad_gate_ref[...] = (
        grad_y * mixed_ref[...] * (gate_sig * (1.0 + gate * (1.0 - gate_sig)))
    ).astype(jnp.bfloat16)
    grad_mixed = grad_y * (gate * gate_sig)
    grad_ref[...] = grad_mixed
    delta_ref[...] = softplus(pre_ref[...])
    rows_ref[1:2, :] += jnp.sum(grad_mixed * act_ref[...], axis=0, keepdims=True)
    rates2 = -LOG2E * jnp.exp(small_ref[cuts.decay : cuts.decay + state, :])
    in_rows = cuts.rank
    out_rows = cuts.rank + state
    spread_lanes(selected_ref[0, in_rows : in_rows + state, :], wide_ref, wide_in_ref)
    spread_lanes(selected_ref[0, out_rows : out_rows + state, :], wide_ref, wide_out_ref)

    def tile_of(ref):
        return tuple(
            tuple(ref[8 * i : 8 * i + 8, j * LANES : (j + 1) * LANES] for i in range(halves))
            for j in range(tiles)
        )

    def group(turn, carry):
        incoming, posts, rate_total, in_acc, out_acc = carry
        incoming = [list(s) for s in incoming]
        posts = [list(s) for s in posts]
        rate_total = [list(s) for s in rate_total]
        in_acc, out_acc = list(in_acc), list(out_acc)
        base = pl.multiple_of((steps // 8 - 1 - turn) * 8, 8)
        d8 = delta_ref[pl.ds(base, 8), :]
        u8 = act_ref[pl.ds(base, 8), :]
        du8 = d8 * u8
        g8 = grad_ref[pl.ds(base, 8), :]
        rate_parts = [[None] * 8 for _ in range(tiles)]
        side_parts = [[None] * 8 for _ in range(tiles)]
        for k in range(7, -1, -1):
            rows_now = [pl.ds((base + k) * state + 8 * i, 8) for i in range(halves)]
            b_now = [wide_in_ref[here, :] for here in rows_now]
            c_now = [wide_out_ref[here, :] for here in rows_now]
            in_sum = [None] * halves
            out_sum = [None] * halves
            for j in range(tiles):
                cols = slice(j * LANES, (j + 1) * LANES)
                d = jnp.broadcast_to(d8[k : k + 1, cols], (8, LANES))
                du = jnp.broadcast_to(du8[k : k + 1, cols], (8, LANES))
                gm = jnp.broadcast_to(g8[k : k + 1, cols], (8, LANES))
                rate_part = None
                side_part = None
                for i in range(halves):
                    prior = prior_ref[base + k, 8 * i : 8 * i + 8, cols]
                    rates = rates2[8 * i : 8 * i + 8, cols]
                    grad_state = c_now[i] * gm + incoming[j][i]
                    passed = jnp.exp2(d * rates) * grad_state
                    incoming[j][i] = passed
                    weighted = passed * prior
                    term = weighted * rates
                    rate_part = term if rate_part is None else rate_part + term
                    term = grad_state * b_now[i]
                    side_part = term if side_part is None else side_part + term
                    term = grad_state * du
                    in_sum[i] = term if in_sum[i] is None else in_sum[i] + term
                    term = posts[j][i] * gm
                    out_sum[i] = term if out_sum[i] is None else out_sum[i] + term
                    rate_total[j][i] = rate_total[j][i] + weighted * d
                    posts[j][i] = prior
                rate_parts[j][k] = rate_part
                side_parts[j][k] = side_part
            here = lane == base + k
            for i in range(halves):
                in_acc[i] = jnp.where(here, jnp.sum(in_sum[i], axis=1, keepdims=True), in_acc[i])
                out_acc[i] = jnp.where(here, jnp.sum(out_sum[i], axis=1, keepdims=True), out_acc[i])
        for j in range(tiles):
            cols = slice(j * LANES, (j + 1) * LANES)
            side = sublane_sums(side_parts[j])
            grad_delta_ref[pl.ds(base, 8), cols] = (
                sublane_sums(rate_parts[j]) * (1.0 / LOG2E) + u8[:, cols] * side
            )
            grad_act_ref[pl.ds(base, 8), cols] = d8[:, cols] * side
        return (
            tuple(tuple(s) for s in incoming),
            tuple(tuple(s) for s in posts),
            tuple(tuple(s) for s in rate_total),
            tuple(in_acc),
            tuple(out_acc),
        )

    empty = tuple(jnp.zeros((8, steps), jnp.float32) for _ in range(halves))
    incoming, posts, rate_total, in_acc, out_acc = lax.fori_loop(
        0,
        steps // 8,
        group,
        (tile_of(incoming_ref), tile_of(post_ref), tile_of(rate_total_ref), empty, empty),
    )
    for i in range(halves):
        stage_ref[in_rows + 8 * i : in_rows + 8 * i + 8, :] = in_acc[i]
        stage_ref[out_rows + 8 * i : out_rows + 8 * i + 8, :] = out_acc[i]
        for j in range(tiles):
            cols = slice(j * LANES, (j + 1) * LANES)
            incoming_ref[8 * i : 8 * i + 8, cols] = incoming[j][i]
            post_ref[8 * i : 8 * i + 8, cols] = posts[j][i]
            rate_total_ref[8 * i : 8 * i + 8, cols] = rate_total[j][i]

    grad_act_ref[...] += grad_ref[...] * small_ref[cuts.skip : cuts.skip + 1, :]
    grad_pre = grad_delta_ref[...] * sigmoid(pre_ref[...])
    rows_ref[0:1, :] += jnp.sum(grad_pre, axis=0, keepdims=True)
    grad_step_ref[...] += dot_nn(selected_ref[0, : cuts.rank, :], grad_pre, HIGHEST)
    stage_ref[: cuts.rank, :] = outer_cols(
        small_ref[cuts.step : cuts.step + cuts.rank, :], grad_pre, HIGHEST
    )
    part_ref[now] = stage_ref[...].astype(jnp.bfloat16)

    def partial_to(block):
        return remote(
            part_ref.at[block], partial_ref.at[own], send_rs.at[block], recv_rs.at[own], line, block
        )

    @pl.when(now != own)
    def _():
        partial_to(now).start()

    def total_to(k):
        return remote(
            total_ref.at[own], total_ref.at[own], send_ag.at[k], recv_ag.at[own], line,
            lax.rem(own + k, count),
        )

    @pl.when(now >= 2)
    def _():
        hand_over(now - 2)

    @pl.when(index == NEAR_AT)
    def _():
        scatter.send_near()

    @pl.when(index == FAR_AT)
    def _():
        scatter.send_far()

    @pl.when(index == PASS_AT)
    def _():
        scatter.pass_far()

    @pl.when(index == count - 1)
    def _():
        scatter.hand_over()

    @pl.when(index == jnp.minimum(count - 1 - own + 2, count - 1))
    def _():
        total = part_ref[own].astype(jnp.float32)
        for k in range(1, count):
            there = lax.rem(own + k, count)
            remote(
                part_ref.at[own], partial_ref.at[there], send_rs.at[own], recv_rs.at[there],
                line, there,
            ).wait_recv()
            total = total + partial_ref[there].astype(jnp.float32)
        total_ref[own] = total.astype(jnp.bfloat16)
        for k in range(1, count):
            total_to(k).start()

    @pl.when(index == count - 1)
    def _():
        for k in range(1, count):
            there = lax.rem(own + k, count)
            remote(
                total_ref.at[there], total_ref.at[there], send_ag.at[k], recv_ag.at[there],
                line, there,
            ).wait_recv()
        grad_selected_ref[...] = total_ref[...]
        all_out_ref[...] = all_ref[...]
        for k in range(1, half):
            along(k).wait_send()
        for i in range(half):
            across(2 * i + low).wait_send()
        for k in range(1, count):
            partial_to(lax.rem(own + k, count)).wait_send()
            total_to(k).wait_send()
        scatter.finish(expert_out_ref)


def scan_backward(
    count, cuts, grad_low, act, gate, mixed, pre, selected, small, weights, priors, end, expert
):
    length, inner = act.shape
    state = cuts.state
    block = length // count
    width = grad_low.shape[1]
    half = count // 2

    def back(t):
        return count - 1 - t

    rows = pl.BlockSpec((block, inner), lambda t: (back(t), 0))
    whole = pl.BlockSpec((state, inner), lambda t: (0, 0))
    dma = pltpu.SemaphoreType.DMA
    picked = (count, cuts.sent, block)
    return pl.pallas_call(
        functools.partial(scan_backward_kernel, count, cuts),
        grid=(count,),
        in_specs=[
            pl.BlockSpec((block, width), lambda t: (0, 0)),
            rows,
            rows,
            rows,
            rows,
            pl.BlockSpec((1, cuts.picks, block), lambda t: (back(t), 0, 0)),
            pl.BlockSpec(small.shape, lambda t: (0, 0)),
            pl.BlockSpec((inner, width), lambda t: (0, 2)),
            pl.BlockSpec((block, state, inner), lambda t: (back(t), 0, 0)),
            whole,
            pl.BlockSpec(expert.shape, lambda t: (0, 0, 0)),
        ],
        out_specs=[
            rows,
            rows,
            pl.BlockSpec((cuts.rank, inner), lambda t: (0, 0)),
            whole,
            pl.BlockSpec((8, inner), lambda t: (0, 0)),
            pl.BlockSpec(picked, lambda t: (0, 0, 0)),
            pl.BlockSpec((count, block, width), lambda t: (0, 0, 0)),
            pl.BlockSpec((expert.shape[1], 2 * expert.shape[2]), lambda t: (0, 0)),
        ],
        out_shape=[
            jax.ShapeDtypeStruct((length, inner), jnp.bfloat16),
            jax.ShapeDtypeStruct((length, inner), jnp.float32),
            jax.ShapeDtypeStruct((cuts.rank, inner), jnp.float32),
            jax.ShapeDtypeStruct((state, inner), jnp.float32),
            jax.ShapeDtypeStruct((8, inner), jnp.float32),
            jax.ShapeDtypeStruct(picked, jnp.bfloat16),
            jax.ShapeDtypeStruct((count, block, width), jnp.bfloat16),
            jax.ShapeDtypeStruct((expert.shape[1], 2 * expert.shape[2]), jnp.float32),
        ],
        scratch_shapes=[
            pltpu.VMEM((state, inner), jnp.float32),
            pltpu.VMEM((state, inner), jnp.float32),
            pltpu.VMEM((block, inner), jnp.float32),
            pltpu.VMEM((block, inner), jnp.float32),
            pltpu.VMEM((block, inner), jnp.float32),
            pltpu.VMEM((block * state, 2 * block), jnp.bfloat16),
            pltpu.VMEM((block * state, LANES), jnp.float32),
            pltpu.VMEM((block * state, LANES), jnp.float32),
            pltpu.VMEM((count, block, width), jnp.bfloat16),
            pltpu.VMEM(picked[1:], jnp.float32),
            *[pltpu.VMEM(picked, jnp.bfloat16)] * 3,
            dma((half,)), dma((half,)), dma((half,)), dma((half,)),
            dma((count,)), dma((count,)), dma((count,)), dma((count,)),
            *scatter_scratch(count, expert.shape[1], expert.shape[2]),
        ],
        compiler_params=pltpu.CompilerParams(
            collective_id=2, has_side_effects=True, vmem_limit_bytes=VMEM_LIMIT
        ),
        cost_estimate=pl.CostEstimate(
            flops=20 * length * state * inner,
            bytes_accessed=4 * length * inner * (state + 6),
            transcendentals=length * state * inner,
        ),
        name="scan_backward",
    )(grad_low, act, gate, mixed, pre, selected, small, weights, priors, end, expert)


def back_kernel(
    count, lines, cuts,
    grad_selected_ref, small_ref, weights_ref, ext_ref, sum_ref, grad_act_ref, grad_gate_ref,
    mixer_low_ref, normed_ref, grad_middle_ref, grad_step_ref, rate_total_ref, scan_rows_ref,
    vectors_ref, expert_ref, far_ref, x_ref, gain_ref, kept_ref,
    tokens_ref, input_ref, output_ref, select_ref, step_ref, decay_ref, taps_ref, conv_bias_ref,
    step_bias_ref, skip_ref, totals_ref, expert_out_ref,
    grad_sum_ref, grad_conv_ref, grad_small_ref, ours_ref, theirs_ref,
    send_v, recv_v, send_u, recv_u, other_ref, held_ref, swap_s, swap_r, *refs,
):
    scatter = Scatter(count, expert_ref, far_ref, other_ref, held_ref, swap_s, swap_r, refs[:6])
    relay = whole_relay("seq", count, refs[6:13])
    spread = whole_relay("dp", lines, refs[13:])
    line, own, _, _ = place()
    length, inner = sum_ref.shape
    width = normed_ref.shape[1]
    rows = length // count
    kernel = cuts.kernel
    shard = spread.part.shape[1]
    own_shard = output_ref.shape[0]
    greet(count, lines)
    scatter.pass_far()
    scatter.send_near()
    grad_small_ref[...] = jnp.zeros_like(grad_small_ref)
    grad_sum_ref[length:, :] = jnp.zeros((8, inner), jnp.float32)
    select = small_ref[: cuts.sent, :].astype(jnp.bfloat16)

    def first(b, carry):
        start = pl.multiple_of(b * rows, rows)
        grad_selected = grad_selected_ref[b]
        total = sum_ref[pl.ds(start, rows), :]
        sig = sigmoid(total)
        grad_act = grad_act_ref[pl.ds(start, rows), :] + inner_rows(grad_selected, select)
        grad_sum = grad_act * (sig * (1.0 + total * (1.0 - sig)))
        grad_sum_ref[pl.ds(start, rows), :] = grad_sum
        grad_small_ref[: cuts.sent, :] += dot_nn(
            grad_selected, (total * sig).astype(jnp.bfloat16)
        )
        window = ext_ref[pl.ds(start, rows + 8), :]
        for k in range(kernel):
            row = slice(cuts.taps + k, cuts.taps + k + 1)
            grad_small_ref[row, :] += jnp.sum(
                grad_sum * window[9 - kernel + k : 9 - kernel + k + rows], axis=0, keepdims=True
            )
        row = slice(cuts.conv_bias, cuts.conv_bias + 1)
        grad_small_ref[row, :] += jnp.sum(grad_sum, axis=0, keepdims=True)
        return carry

    lax.fori_loop(0, count, first, 0)

    def order(j):
        return j // 2 + lax.rem(j, 2) * (count // 2)

    def second(j, carry):
        b = order(j)
        start = pl.multiple_of(b * rows, rows)
        window = grad_sum_ref[pl.ds(start, rows + 8), :]
        grad_conv = None
        for k in range(kernel):
            tap = small_ref[cuts.taps + k : cuts.taps + k + 1, :]
            term = tap * window[kernel - 1 - k : kernel - 1 - k + rows]
            grad_conv = term if grad_conv is None else grad_conv + term
        grad_conv = grad_conv.astype(jnp.bfloat16)
        grad_conv_ref[pl.ds(start, rows), :] = grad_conv
        relay.part[b] = (
            dot_nn(grad_conv, weights_ref[:, :width])
            + dot_nn(grad_gate_ref[pl.ds(start, rows), :], weights_ref[:, width : 2 * width])
        ).astype(jnp.bfloat16)
        relay.made(b // 2, lax.rem(b, 2))
        return carry

    lax.fori_loop(0, count, second, 0)

    decay = slice(cuts.decay, cuts.decay + cuts.state)
    grad_small_ref[cuts.step : cuts.step + cuts.rank, :] = grad_step_ref[...]
    grad_small_ref[decay, :] = -rate_total_ref[...] * jnp.exp(small_ref[decay, :])
    grad_small_ref[cuts.step_bias : cuts.step_bias + 2, :] = scan_rows_ref[0:2, :]
    small_t = grad_small_ref[...].T
    for d in range(lines):
        spread.part[d, :, 3 * width :] = small_t[d * shard : (d + 1) * shard].astype(jnp.bfloat16)
    chunk = width // 3

    def pass_on(j, carry):
        b = order(j)
        relay.pass_on(b // 2, lax.rem(b, 2))
        return carry

    ours_ref[...] = vectors_ref[...]
    for left_ref, right_ref, place_at in (
        (mixer_low_ref, grad_middle_ref, 2 * width),
        (grad_conv_ref, normed_ref, 0),
        (grad_gate_ref, normed_ref, width),
    ):

        def columns(c, carry, left_ref=left_ref, right_ref=right_ref, place_at=place_at):
            here = pl.ds(pl.multiple_of(c * chunk, chunk), chunk)
            there = pl.ds(pl.multiple_of(place_at + c * chunk, chunk), chunk)
            grad = inner_rows(left_ref[...], right_ref[:, here])
            if place_at < 2 * width:
                ours_ref[0:1, here] += jnp.sum(
                    weights_ref[:, there].astype(jnp.float32) * grad, axis=0, keepdims=True
                )
            low = grad.astype(jnp.bfloat16)
            for d in range(lines):
                spread.part[d, :, there] = low[d * shard : (d + 1) * shard]
            return carry

        lax.fori_loop(0, 3, columns, 0)
        if place_at == 2 * width:
            lax.fori_loop(0, count, pass_on, 0)
    for d in range(lines):
        spread.made(d // 2, d % 2)
    scatter.hand_over()

    def sum_over(size, axis, send, recv):
        here = own if axis == "seq" else line

        def copy(k, slot):
            there = lax.rem(here + k, size)
            target = (line, there) if axis == "seq" else (there, own)
            return remote(ours_ref, theirs_ref.at[slot], send.at[k], recv.at[k], *target)

        base = 0 if axis == "seq" else count
        for k in range(1, size):
            copy(k, base + k).start()
        total = ours_ref[...]
        for k in range(1, size):
            copy(k, base + k).wait_recv()
            total = total + theirs_ref[base + k]
        for k in range(1, size):
            copy(k, base + k).wait_send()
        return total

    ours_ref[...] = sum_over(count, "seq", send_v, recv_v)
    for d in range(lines):
        spread.pass_on(d // 2, d % 2)
    totals_ref[...] = sum_over(lines, "dp", send_u, recv_u)
    x = x_ref[...]
    scale = lax.rsqrt(jnp.mean(x * x, axis=1, keepdims=True) + 1e-05)
    scaled = gain_ref[...] * relay.finish()
    tokens_ref[...] = (
        kept_ref[...]
        + scale * scaled
        - x * (scale * scale * scale) * jnp.mean(scaled * x, axis=1, keepdims=True)
    )
    total = spread.finish()
    input_ref[0] = total[:own_shard, :width]
    input_ref[1] = total[:own_shard, width : 2 * width]
    output_ref[...] = total[:own_shard, 2 * width : 3 * width]
    small = total[:, 3 * width :]
    select_ref[...] = small[:own_shard, : cuts.picks]
    small = jnp.concatenate(
        [small, jnp.zeros((LANES - shard, small.shape[1]), jnp.float32)], axis=0
    ).T
    for at, ref in (
        (cuts.step, step_ref),
        (cuts.decay, decay_ref),
        (cuts.taps, taps_ref),
        (cuts.conv_bias, conv_bias_ref),
        (cuts.step_bias, step_bias_ref),
        (cuts.skip, skip_ref),
    ):
        ref[...] = small[at : at + ref.shape[0], :own_shard]
    scatter.finish(expert_out_ref)


def back(
    count, lines, shard, own_shard, cuts, grad_selected, small, weights, ext, conv_sum, grad_act, grad_gate,
    mixer_low, normed, grad_middle, grad_step, rate_total, scan_rows, vectors, expert, far,
    x, gain, kept,
):
    length, inner = conv_sum.shape
    width = normed.shape[1]
    columns = weights.shape[1]
    rows = length // count
    vmem = pl.BlockSpec(memory_space=pltpu.VMEM)
    dma = pltpu.SemaphoreType.DMA
    args = (
        grad_selected, small, weights, ext, conv_sum, grad_act, grad_gate, mixer_low, normed,
        grad_middle, grad_step, rate_total, scan_rows, vectors, expert, far, x, gain, kept,
    )
    return pl.pallas_call(
        functools.partial(back_kernel, count, lines, cuts),
        in_specs=[vmem] * len(args),
        out_specs=[vmem] * 12,
        out_shape=[
            *[
                jax.ShapeDtypeStruct(shape, jnp.float32)
                for shape in (
                    (rows, width),
                    (2, own_shard, width),
                    (own_shard, width),
                    (own_shard, cuts.picks),
                    (cuts.rank, own_shard),
                    (cuts.state, own_shard),
                    (cuts.kernel, own_shard),
                    (1, own_shard),
                    (1, own_shard),
                    (1, own_shard),
                    vectors.shape,
                )
            ],
            jax.ShapeDtypeStruct((expert.shape[1], 2 * expert.shape[2]), jnp.float32),
        ],
        scratch_shapes=[
            pltpu.VMEM((length + 8, inner), jnp.float32),
            pltpu.VMEM((length, inner), jnp.bfloat16),
            pltpu.VMEM(small.shape, jnp.float32),
            pltpu.VMEM(vectors.shape, jnp.float32),
            pltpu.VMEM((count + lines, *vectors.shape), jnp.float32),
            dma((count,)), dma((count,)), dma((lines,)), dma((lines,)),
            *scatter_scratch(count, expert.shape[1], expert.shape[2]),
            *relay_scratch(count, rows, width),
            *relay_scratch(lines, shard, columns),
        ],
        compiler_params=pltpu.CompilerParams(
            collective_id=3, has_side_effects=True, vmem_limit_bytes=VMEM_LIMIT
        ),
        cost_estimate=pl.CostEstimate(
            flops=10 * length * width * inner,
            bytes_accessed=30 * length * inner,
            transcendentals=length * inner,
        ),
        name="back",
    )(*args)


LAG = 3
FAR_AT = 0
NEAR_AT = 2
PASS_AT = 3
SLOTS = 64


def gauss(values):
    return 0.5 * (1.0 + lax.erf(values * math.sqrt(0.5)))


def split_low(values):
    high = values.astype(jnp.bfloat16)
    return high, (values - high.astype(jnp.float32)).astype(jnp.bfloat16)


def experts_kernel(
    count, lines, experts,
    x_ref, mixer_ref, grad_ref, route_ref, gain_ref, router_ref,
    up_ref, held_ref,
    output_ref, grad_middle_ref, grad_low_ref, vectors_ref, grad_up_ref, grad_down_ref, far_up_ref,
    table_ref, back_table_ref, down_ref, middle_ref, normed_ref, send_ref, rows_ref, made_ref, got_ref, act_ref, slope_ref, pre_ref,
    send_sem, recv_sem, home_s, home_r, far_s, far_r,
    pass_s, pass_r,
):
    line, own, _, _ = place()
    q, f, low = square()
    mate = seat_of(q, 1 - f, low)
    copies = lines // experts
    barrier = pltpu.get_barrier_semaphore()
    for d in range(1, lines):
        for where in (own, mate):
            pl.semaphore_signal(
                barrier, inc=1, device_id=(lax.rem(line + d, lines), where), device_id_type=MESH
            )
    partner = seat_of(q, f, 1 - low)
    for where in (mate, partner):
        pl.semaphore_signal(barrier, inc=1, device_id=(line, where), device_id_type=MESH)
    pl.semaphore_wait(barrier, 2 * lines)

    quarter = count // 4
    piece_rows = held_ref.shape[0] // count

    def piece(j, k, member):
        at = seat_of(lax.rem(q - k + quarter, quarter), lax.rem(f + j, 2), member)
        return pl.ds(pl.multiple_of(at * piece_rows, piece_rows), piece_rows)

    def crossing(j, k, member):
        here = piece(j, k, member)
        return remote(
            held_ref.at[here], down_ref.at[here], pass_s.at[j, k], pass_r.at[j, k], line, partner
        )

    for j in range(2):
        for k in range(1, quarter):
            crossing(j, k, low).start()

    peers = [(j, d) for d in range(lines) for j in (1, 0) if (j, d) != (0, 0)]

    def out_copy(what, j, d):
        there = lax.rem(line + d, lines)
        return remote(
            send_ref.at[what, there // copies], rows_ref.at[what, j, line],
            send_sem.at[what, j, d], recv_sem.at[what, j, line],
            there, mate if j else own,
        )

    def arrived(what, j, d):
        from_line = lax.rem(line + d, lines)
        return remote(
            send_ref.at[what, 0], rows_ref.at[what, j, from_line],
            send_sem.at[what, j, d], recv_sem.at[what, j, from_line],
            from_line, mate if j else own,
        )

    def home_copy(what, j, d):
        there = lax.rem(line + d, lines)
        return remote(
            made_ref.at[what, j, there], got_ref.at[what, j, line],
            home_s.at[what, j, d], home_r.at[what, j, line],
            there, mate if j else own,
        )

    def came_home(what, j, d):
        from_line = lax.rem(line + d, lines)
        return remote(
            made_ref.at[what, j, 0], got_ref.at[what, j, from_line],
            home_s.at[what, j, d], home_r.at[what, j, from_line],
            from_line, mate if j else own,
        )

    middle = x_ref[...] + mixer_ref[...]
    middle_ref[...] = middle
    gain = gain_ref[...]
    scale = lax.rsqrt(jnp.mean(middle * middle, axis=1, keepdims=True) + 1e-05)
    normed = (middle * scale * gain).astype(jnp.bfloat16)
    normed_ref[...] = normed
    rows, width = middle.shape
    slots = SLOTS
    lane = lax.broadcasted_iota(jnp.int32, (rows, LANES), 1)
    route_along = jnp.broadcast_to(route_ref[...].astype(jnp.float32), (rows, rows))
    route_down = route_along.T[:, :LANES]
    chosen = (route_down == lane.astype(jnp.float32)).astype(jnp.float32)
    earlier = (
        lax.broadcasted_iota(jnp.int32, (rows, rows), 0)
        > lax.broadcasted_iota(jnp.int32, (rows, rows), 1)
    ).astype(jnp.bfloat16)
    before = dot_nn(earlier, chosen.astype(jnp.bfloat16))
    slot_down = route_down[:, :1] * slots + jnp.sum(before * chosen, axis=1, keepdims=True)
    slot_along = jnp.broadcast_to(slot_down, (rows, rows)).T[:1, :]
    table_ref[...] = (
        jnp.broadcast_to(slot_along, table_ref.shape)
        == lax.broadcasted_iota(jnp.int32, table_ref.shape, 0).astype(jnp.float32)
    ).astype(jnp.bfloat16)
    for e in range(experts):
        places = lax.broadcasted_iota(jnp.int32, (rows, slots), 1) + e * slots
        back_table_ref[e] = (
            jnp.broadcast_to(slot_down, (rows, slots)) == places.astype(jnp.float32)
        ).astype(jnp.bfloat16)

    def dispatch(what, values):
        sent = dot_nn(table_ref[...], values).astype(jnp.bfloat16)
        for e in range(experts):
            send_ref[what, e] = sent[e * slots : (e + 1) * slots]
        for j, d in peers:
            out_copy(what, j, d).start()
        rows_ref[what, 0, line] = send_ref[what, line // copies]

    dispatch(0, normed)
    router_f = jnp.concatenate(
        [
            router_ref[...].astype(jnp.float32),
            jnp.zeros((LANES - experts, width), jnp.float32),
        ],
        axis=0,
    )
    router = router_f.astype(jnp.bfloat16)
    logits = jnp.where(lane < experts, outer_cols(normed, router), -jnp.inf)
    grown = jnp.exp(logits - jnp.max(logits, axis=1, keepdims=True))
    probs = grown / jnp.sum(grown, axis=1, keepdims=True)
    gate = jnp.sum(chosen * probs, axis=1, keepdims=True)
    dispatch(1, (gate * grad_ref[...]).astype(jnp.bfloat16))

    total = 2 * lines * slots
    hidden = up_ref.shape[1]
    chunk = hidden // 3 if hidden % (3 * LANES) == 0 else hidden
    parts = hidden // chunk

    def rows_of(ref, what):
        return ref[what].reshape(total, width)

    def columns(c):
        return pl.ds(pl.multiple_of(c * chunk, LANES), chunk)

    for j in range(2):
        for k in range(quarter):
            here = piece(j, k, low)
            down_ref[here, :] = held_ref[here, :]
        here = piece(j, 0, 1 - low)
        down_ref[here, :] = held_ref[here, :]
    for j, d in peers:
        arrived(0, j, d).wait_recv()

    def rise(c, carry):
        pre_ref[:, columns(c)] = dot_nn(rows_of(rows_ref, 0), up_ref[:, columns(c)])
        pre = pre_ref[:, columns(c)]
        half = gauss(pre)
        act_ref[:, columns(c)] = (pre * half).astype(jnp.bfloat16)
        pre_ref[:, columns(c)] = half + pre * (
            jnp.exp(-0.5 * pre * pre) * (1.0 / math.sqrt(2.0 * math.pi))
        )
        return carry

    lax.fori_loop(0, parts, rise, 0)

    wide = width // 3

    def send_home(what, left_ref, right_ref):
        def make(c, carry):
            here = pl.ds(pl.multiple_of(c * wide, LANES), wide)
            there = pl.ds(pl.multiple_of(c * wide, LANES), wide)
            made = outer_cols(left_ref[...], right_ref[there, :]).astype(jnp.bfloat16)
            made_ref[what, :, :, :, here] = made.reshape(2, lines, slots, wide)
            return carry

        lax.fori_loop(0, 3, make, 0)
        for j, d in peers:
            home_copy(what, j, d).start()
        got_ref[what, 0, line] = made_ref[what, 0, line]

    for j, d in peers:
        arrived(1, j, d).wait_recv()
    for j in range(2):
        for k in range(1, quarter):
            crossing(j, k, 1 - low).wait_recv()

    def fall(c, carry):
        slope_ref[:, columns(c)] = (
            dot_nn(rows_of(rows_ref, 1), down_ref[:, columns(c)]) * pre_ref[:, columns(c)]
        ).astype(jnp.bfloat16)
        return carry

    lax.fori_loop(0, parts, fall, 0)
    send_home(1, slope_ref, up_ref)
    pieces = grad_up_ref.shape[1]

    def weigh_up(c, carry):
        up = inner_rows(rows_of(rows_ref, 0), slope_ref[:, columns(c)]).astype(jnp.bfloat16)
        grad_up_ref[:, :, columns(c)] = up.reshape(count, pieces, chunk)
        return carry

    lax.fori_loop(0, parts, weigh_up, 0)

    far_copies = []
    for k in range(1, count // 4):
        i = lax.rem(q + k, count // 4)
        for j in (1, 0):
            far_copies.append(
                remote(
                    grad_up_ref.at[seat_of(i, lax.rem(f + j, 2), 1 - low)], far_up_ref.at[j, i],
                    far_s.at[j, i], far_r.at[j, i], line, partner,
                )
            )
            far_copies[-1].start()

    send_home(0, act_ref, down_ref)
    def weigh_down(c, carry):
        down = inner_rows(rows_of(rows_ref, 1), act_ref[:, columns(c)]).astype(jnp.bfloat16)
        grad_down_ref[:, :, columns(c)] = down.reshape(count, pieces, chunk)
        return carry

    lax.fori_loop(0, parts, weigh_down, 0)

    def home(what):
        for j, d in peers:
            came_home(what, j, d).wait_recv()
        both = None
        for e in range(experts):
            own_rows = None
            for c in range(copies):
                for j in range(2):
                    term = got_ref[what, j, e * copies + c].astype(jnp.float32)
                    own_rows = term if own_rows is None else own_rows + term
            high, rest = split_low(own_rows)
            here = back_table_ref[e]
            term = dot_nn(here, high) + dot_nn(here, rest)
            both = term if both is None else both + term
        return both

    grad = grad_ref[...]
    middle = middle_ref[...]
    picked = home(0)
    output_ref[...] = middle + gate * picked
    grad_gate = jnp.sum(grad * picked, axis=1, keepdims=True)
    grad_logits = gate * (chosen - probs) * grad_gate
    grad_normed = home(1) + dot_nn(grad_logits, router_f, HIGHEST)
    scaled = gain * grad_normed
    grad_middle = (
        grad
        + scale * scaled
        - middle * (scale * scale * scale) * jnp.mean(scaled * middle, axis=1, keepdims=True)
    )
    grad_middle_ref[...] = grad_middle
    grad_low_ref[...] = grad_middle.astype(jnp.bfloat16)
    vectors_ref[...] = jnp.zeros_like(vectors_ref)
    vectors_ref[1:2, :] = jnp.sum(grad_normed * middle * scale, axis=0, keepdims=True)
    vectors_ref[2 : 2 + experts, :] = inner_rows(
        grad_logits, normed_ref[...].astype(jnp.float32), HIGHEST
    )[:experts]
    for what in range(2):
        for j, d in peers:
            out_copy(what, j, d).wait_send()
            home_copy(what, j, d).wait_send()
    for copy in far_copies:
        copy.wait()
    for j in range(2):
        for k in range(1, quarter):
            crossing(j, k, low).wait_send()


def run_experts(
    count, lines, experts, x, mixer, grad, route, gain, router, up, down
):
    rows, width = x.shape
    slots = SLOTS
    total = 2 * lines * slots
    hidden = up.shape[1]
    pieces = (count, up.shape[0] // count, hidden)
    vmem = pl.BlockSpec(memory_space=pltpu.VMEM)
    dma = pltpu.SemaphoreType.DMA
    args = (x, mixer, grad, route, gain, router, up, down)
    low = jnp.bfloat16
    return pl.pallas_call(
        functools.partial(experts_kernel, count, lines, experts),
        in_specs=[vmem] * len(args),
        out_specs=[vmem] * 7,
        out_shape=[
            jax.ShapeDtypeStruct((rows, width), jnp.float32),
            jax.ShapeDtypeStruct((rows, width), jnp.float32),
            jax.ShapeDtypeStruct((rows, width), low),
            jax.ShapeDtypeStruct((8, width), jnp.float32),
            jax.ShapeDtypeStruct(pieces, low),
            jax.ShapeDtypeStruct(pieces, low),
            jax.ShapeDtypeStruct((2, count // 4, *pieces[1:]), low),
        ],
        scratch_shapes=[
            pltpu.VMEM((experts * slots, rows), low),
            pltpu.VMEM((experts, rows, slots), low),
            pltpu.VMEM(down.shape, low),
            pltpu.VMEM((rows, width), jnp.float32),
            pltpu.VMEM((rows, width), low),
            pltpu.VMEM((2, experts, slots, width), low),
            pltpu.VMEM((2, 2, lines, slots, width), low),
            pltpu.VMEM((2, 2, lines, slots, width), low),
            pltpu.VMEM((2, 2, lines, slots, width), low),
            pltpu.VMEM((total, hidden), low),
            pltpu.VMEM((total, hidden), low),
            pltpu.VMEM((total, hidden), jnp.float32),
            dma((2, 2, lines)), dma((2, 2, lines)), dma((2, 2, lines)), dma((2, 2, lines)),
            dma((2, count // 4)), dma((2, count // 4)), dma((2, count // 4)), dma((2, count // 4)),
        ],
        compiler_params=pltpu.CompilerParams(
            collective_id=4, has_side_effects=True, vmem_limit_bytes=VMEM_LIMIT
        ),
        cost_estimate=pl.CostEstimate(
            flops=12 * total * width * hidden,
            bytes_accessed=8 * width * hidden,
            transcendentals=2 * total * hidden,
        ),
        name="experts",
    )(*args)


def body(
    tokens,
    cotangent,
    routes,
    mixer_gain,
    input_proj,
    conv_weight,
    conv_bias,
    select_proj,
    step_proj,
    step_bias,
    decay_log,
    skip_gain,
    output_proj,
    expert_gain,
    router,
    expert_up,
    expert_down,
):
    rows = tokens.shape[1]
    width = tokens.shape[2]
    shard = input_proj.shape[2]
    rank = step_proj.shape[0]
    state = decay_log.shape[0]
    kernel = conv_weight.shape[0]
    picks = select_proj.shape[0]
    count = lax.axis_size("seq")
    lines = lax.axis_size("dp")
    shard_rows = -(-shard // 16) * 16
    cuts = Cuts(picks, rank, state, kernel)

    x_in = tokens.reshape(rows, width)
    gain_one = mixer_gain.astype(jnp.float32)
    small_pad = -(-cuts.rows // LANES) * LANES
    (normed_all, weights, small_all, conv_ext, conv_sum, conv_act, gate_branch, selected, up_cut) = (
        front(
            count, lines, cuts, shard_rows, small_pad,
            x_in, gain_one[None], input_proj.transpose(0, 2, 1), output_proj, select_proj.T,
            step_proj, decay_log, conv_weight, conv_bias[None], step_bias[None], skip_gain[None],
            expert_up,
        )
    )
    pre, mixed, mixer_low, priors, end, mixer_out, down_cut = scan_forward(
        count, cuts, width, conv_act, gate_branch, selected, small_all, weights, expert_down.T
    )

    experts = router.shape[0]
    (output, grad_middle, grad_middle_low, vectors, grad_up_low, grad_down_low, far_up) = run_experts(
        count,
        lines,
        experts,
        x_in,
        mixer_out,
        cotangent.reshape(rows, width),
        routes.reshape(1, rows),
        expert_gain.astype(jnp.float32)[None],
        router,
        up_cut.reshape(-1, up_cut.shape[2]),
        down_cut.reshape(-1, down_cut.shape[2]),
    )

    (grad_gate_branch, grad_act, grad_step_w, rate_total, scan_rows, grad_selected, grad_middle_all,
     grad_down_t) = (
        scan_backward(
            count, cuts, grad_middle_low, conv_act, gate_branch, mixed, pre, selected, small_all,
            weights, priors, end, grad_down_low,
        )
    )
    (grad_tokens, grad_input, grad_output, grad_select, grad_step, grad_decay, grad_taps,
     grad_conv_bias, grad_step_bias, grad_skip, totals, grad_up) = back(
        count, lines, shard_rows, shard, cuts, grad_selected, small_all, weights, conv_ext, conv_sum,
        grad_act, grad_gate_branch, mixer_low, normed_all.reshape(-1, width),
        grad_middle_all.reshape(-1, width), grad_step_w, rate_total, scan_rows, vectors,
        grad_up_low, far_up, x_in, gain_one[None], grad_middle,
    )
    return (
        output.reshape(tokens.shape),
        grad_tokens.reshape(tokens.shape),
        totals[0] / gain_one,
        grad_input.transpose(0, 2, 1),
        grad_taps,
        grad_conv_bias.reshape(shard),
        grad_select.T,
        grad_step,
        grad_step_bias.reshape(shard),
        grad_decay,
        grad_skip.reshape(shard),
        grad_output,
        totals[1],
        totals[2 : 2 + experts],
        grad_up,
        grad_down_t.T,
    )


def solution(mesh):
    both = ("dp", "seq")
    placed = (
        P("dp", "seq", None),
        P("dp", "seq", None),
        P("dp", "seq", None),
        P(),
        P(None, None, both),
        P(None, both),
        P(both),
        P(None, both),
        P(None, both),
        P(both),
        P(None, both),
        P(both),
        P(both, None),
        P(),
        P(),
        P("seq", "dp"),
        P("dp", "seq"),
    )
    return jax.shard_map(
        body,
        mesh=mesh,
        in_specs=placed,
        out_specs=(
            P("dp", "seq", None),
            P("dp", "seq", None),
            P(),
            P(None, None, both),
            P(None, both),
            P(both),
            P(None, both),
            P(None, both),
            P(both),
            P(None, both),
            P(both),
            P(both, None),
            P(),
            P(),
            P("seq", "dp"),
            P("dp", "seq"),
        ),
        check_vma=False,
    )
```
